32 devices in a mesh: section: 4 (over z), expert: 4 (over y, core), dp: 2 (over x).
Axes of the slice: x: 2, y: 2, z: 4, core: 2. Of those that a mesh axis runs over, the one named last changes fastest.
Arguments:
- tokens: bfloat16 [4096, 5120], P(('section', 'expert', 'dp')), may hold values from -6 to 6
- cotangent: bfloat16 [4096, 5120], P(('section', 'expert', 'dp')), may hold values from -6 to 6
- w_gate: bfloat16 [4, 5120, 2048], P('section', None, 'expert'), may hold values from -0.078125 to 0.078125
- w_up: bfloat16 [4, 5120, 2048], P('section', None, 'expert'), may hold values from -0.078125 to 0.078125
- w_down: bfloat16 [4, 2048, 5120], P('section', 'expert'), may hold values from -0.125 to 0.125
- routes: int32 [2, 4096, 4], P(None, ('section', 'expert', 'dp')), may hold values from 0 to 63, as said below
- gates: float32 [2, 4096, 4], P(None, ('section', 'expert', 'dp')), may hold values from 0.2 to 1
Outputs:
- tokens_grad: bfloat16 [4096, 5120], P(('section', 'expert', 'dp'))
- final_state: bfloat16 [4096, 5120], P(('section', 'expert', 'dp'))
- gate_grad: bfloat16 [4, 5120, 2048], P('section', None, 'expert')
- up_grad: bfloat16 [4, 5120, 2048], P('section', None, 'expert')
- down_grad: bfloat16 [4, 2048, 5120], P('section', 'expert')
The draws below stay inside these ranges and needn't reach their ends.
Inputs may be any that keep to these rules, and one draw needn't show every extreme that they name: `routes`: each row names 4 different experts. In each tick the 128 rows of one device name each expert below 1 in 1 to 10 rows, and for every tick and such expert all devices of some section and dp index name it in exactly 10 rows.
All inputs are finite; a program needn't handle non-finite values.
Results may differ from the reference program's by a relative error of at most 0.0095.
Values may be sent and summed in bfloat16 or wider, within the bound.
No kernel may reach another device: no remote copies, remote signals or barrier semaphores. Data moves between devices by JAX's collectives and lax.ppermute only.
A program may use at most 128 MiB of HBM per device.

```python
import math
import jax
import jax.numpy as jnp
from jax import lax

D = 5120
HID = 2048
EXPERTS_ALL = 64
EXP_W = 1
TOP = 4
CAP = 10
TICKS = 2
TOK_DEV = 128
GROUP = 4
H_DEV = 512
LAYERS = 4
TOKENS = 4096
N_SECTION = 4
N_EXPERT = 4
N_DP = 2


def draw_routes(key, part):
    key_list = jax.random.split(key, 5)
    blocks = TOKENS // TOK_DEV
    groups = N_SECTION * N_DP
    counts = jax.random.randint(key_list[0], (TICKS, blocks, EXP_W), 1, CAP + 1)
    full_group = jax.random.randint(key_list[1], (TICKS, 1, EXP_W), 0, groups)
    block_ids = jnp.arange(blocks, dtype=jnp.int32)
    group_of = block_ids // (N_EXPERT * N_DP) * N_DP + block_ids % N_DP
    counts = jnp.where(group_of[None, :, None] == full_group, CAP, counts)
    scores = jax.random.randint(key_list[2], (TICKS, blocks, EXP_W, TOK_DEV), 0, 2 ** 20) * TOK_DEV + jnp.arange(TOK_DEV, dtype=jnp.int32)
    ranks = jnp.argsort(jnp.argsort(scores, axis=-1), axis=-1)
    chosen = ranks < counts[..., None]
    chosen = jnp.transpose(chosen, (0, 1, 3, 2)).reshape(TICKS, TOKENS, EXP_W)
    others = EXPERTS_ALL - EXP_W
    filler_scores = jax.random.randint(key_list[3], (TICKS, TOKENS, others), 0, 2 ** 20) * others + jnp.arange(others, dtype=jnp.int32)
    fillers = lax.top_k(filler_scores, TOP)[1].astype(jnp.int32) + EXP_W
    columns = []
    for position in range(TOP):
        if position < EXP_W:
            columns.append(jnp.where(chosen[..., position], position, fillers[..., position]))
        else:
            columns.append(fillers[..., position])
    base_ids = jnp.stack(columns, axis=-1)
    rotation = jax.random.randint(key_list[4], (TICKS, TOKENS, 1), 0, TOP)
    column_order = (jnp.arange(TOP, dtype=jnp.int32)[None, None, :] + rotation) % TOP
    return jnp.take_along_axis(base_ids, column_order, axis=2).astype(jnp.int32)


def level_of(key, dims, shards, smallest, largest):
    level = 1.0
    for axis_at, shards_of in shards:
        steps = jax.random.uniform(jax.random.fold_in(jax.random.fold_in(key, 6), axis_at), (shards_of,), jnp.float32, smallest / len(shards), largest / len(shards))
        level = level * jnp.repeat(jnp.exp(steps), dims[axis_at] // shards_of).reshape((-1,) + (1,) * (len(dims) - 1 - axis_at))
    return level


def gaussian(rng, shape, deviation, reach, cuts=(), kind=jnp.bfloat16):
    gain = level_of(rng, shape, cuts, -0.22, 0.18) if cuts else 1.0
    array = jax.random.normal(rng, shape, jnp.float32) * deviation * gain
    return jnp.minimum(jnp.maximum(array, -reach), reach).astype(kind)


def setup_inputs(seed: int = 0) -> dict:
    streams_of = jax.random.split(jax.random.key(seed), 8)
    tokens = gaussian(streams_of[0], (TOKENS, D), 1.0, 6.0, ((0, 32),))
    cotangent = gaussian(streams_of[1], (TOKENS, D), 1.0, 6.0, ((0, 32),))
    w_gate = gaussian(streams_of[2], (LAYERS, D, EXP_W * HID), D ** -0.5, 0.078125, ((0, 4), (2, 4)))
    w_up = gaussian(streams_of[3], (LAYERS, D, EXP_W * HID), D ** -0.5, 0.078125, ((0, 4), (2, 4)))
    w_down = gaussian(streams_of[4], (LAYERS, EXP_W * HID, D), HID ** -0.5, 0.125, ((0, 4), (1, 4)))
    routes = draw_routes(jax.random.fold_in(streams_of[7], 71), 0)
    gates = jnp.clip(jnp.exp(math.log(1.0) - 1.609438 * jax.random.uniform(streams_of[6], (TICKS, TOKENS, TOP), jnp.float32) ** level_of(streams_of[6], (TICKS, TOKENS, TOP), ((1, 32),), -0.2, 0.2)), 0.2, 1.0)
    return dict(tokens=tokens, cotangent=cotangent, w_gate=w_gate, w_up=w_up, w_down=w_down, routes=routes, gates=gates)


EPSILON = 1e-06

def routing(route_ids, gate_vals):
    experts_here = jnp.arange(EXP_W, dtype=jnp.int32)
    matches = route_ids[..., None, :, :] == experts_here[:, None, None]
    marked = jnp.any(matches, axis=-1)
    weights = lax.optimization_barrier(jnp.sum(jnp.where(matches, gate_vals[..., None, :, :], 0.0), axis=-1)).astype(jnp.float32)
    places = jnp.cumsum(marked.astype(jnp.int32), axis=-1, dtype=jnp.int32) - 1
    capacity = jnp.arange(CAP, dtype=jnp.int32)
    select = (places[..., None, :] == capacity[:, None]) & marked[..., None, :]
    return (select.astype(jnp.float32), weights)

def normalize(current):
    values = current.astype(jnp.float32)
    inv_rms = lax.rsqrt(lax.optimization_barrier(jnp.mean(values * values, axis=-1, keepdims=True)) + EPSILON)
    return (values, inv_rms, (values * inv_rms).astype(jnp.bfloat16))

def slot_rows(select, rows):
    picked = jnp.einsum('edcr,edrx->edcx', select, rows.astype(jnp.float32), precision=lax.Precision.HIGHEST)
    picked = jnp.transpose(picked, (1, 0, 2, 3))
    return picked.reshape(picked.shape[0], -1, picked.shape[3])

def row_slots(select, slots):
    shaped = slots.reshape(slots.shape[0], select.shape[0], select.shape[2], slots.shape[2])
    shaped = jnp.transpose(shaped, (1, 0, 2, 3))
    return jnp.einsum('edcr,edcx->edrx', select, shaped, precision=lax.Precision.HIGHEST)

def expert_weights(w_gate, w_up, w_down, expert_index):
    first_col = expert_index * HID
    gate_part = w_gate[:, first_col:first_col + HID].astype(jnp.float32).reshape(D, GROUP, H_DEV)
    up_part = w_up[:, first_col:first_col + HID].astype(jnp.float32).reshape(D, GROUP, H_DEV)
    down_part = w_down[first_col:first_col + HID].astype(jnp.float32).reshape(GROUP, H_DEV, D)
    return (gate_part, up_part, down_part)

def section_forward(current, route_ids, gate_vals, w_gate, w_up, w_down):
    values, inv_rms, normed = normalize(current)
    select, weights = routing(route_ids, gate_vals)
    update = jnp.zeros(values.shape, jnp.float32)
    for expert_index in range(EXP_W):
        gate_part, up_part, down_part = expert_weights(w_gate, w_up, w_down, expert_index)
        chosen = select[:, :, expert_index]
        inputs = slot_rows(chosen, normed)
        pre_gate = jnp.einsum('psx,xqh->psqh', inputs, gate_part)
        pre_up = jnp.einsum('psx,xqh->psqh', inputs, up_part)
        gate_sig = jax.nn.sigmoid(pre_gate)
        activated = (pre_gate * gate_sig * pre_up).astype(jnp.bfloat16)
        partial_out = jnp.einsum('psqh,qhx->psqx', activated.astype(jnp.float32), down_part).astype(jnp.bfloat16)
        summed = lax.optimization_barrier(jnp.sum(partial_out.astype(jnp.float32), axis=2))
        update = update + weights[:, :, expert_index, :, None] * row_slots(chosen, summed)
    return (values + update).astype(jnp.bfloat16)

def section_backward(current, carried, route_ids, gate_vals, w_gate, w_up, w_down):
    values, inv_rms, normed = normalize(current)
    select, weights = routing(route_ids, gate_vals)
    cot_values = carried.astype(jnp.float32)
    grad_norm = jnp.zeros(values.shape, jnp.float32)
    grads_gate = []
    grads_up = []
    grads_down = []
    for expert_index in range(EXP_W):
        gate_part, up_part, down_part = expert_weights(w_gate, w_up, w_down, expert_index)
        chosen = select[:, :, expert_index]
        inputs = slot_rows(chosen, normed)
        pre_gate = jnp.einsum('psx,xqh->psqh', inputs, gate_part)
        pre_up = jnp.einsum('psx,xqh->psqh', inputs, up_part)
        gate_sig = jax.nn.sigmoid(pre_gate)
        silu_value = pre_gate * gate_sig
        activated = (silu_value * pre_up).astype(jnp.bfloat16)
        scaled = (weights[:, :, expert_index, :, None] * cot_values).astype(jnp.bfloat16)
        grad_slots = slot_rows(chosen, scaled)
        grad_act = jnp.einsum('psx,qhx->psqh', grad_slots, down_part)
        grad_gate = (grad_act * pre_up * gate_sig * (1.0 + pre_gate * (1.0 - gate_sig))).astype(jnp.bfloat16)
        grad_up = (grad_act * silu_value).astype(jnp.bfloat16)
        grads_down.append(jnp.einsum('psqh,psx->qhx', activated.astype(jnp.float32), grad_slots).reshape(HID, D))
        grads_gate.append(jnp.einsum('psx,psqh->xqh', inputs, grad_gate.astype(jnp.float32)).reshape(D, HID))
        grads_up.append(jnp.einsum('psx,psqh->xqh', inputs, grad_up.astype(jnp.float32)).reshape(D, HID))
        back_share = jnp.einsum('psqh,xqh->psqx', grad_gate.astype(jnp.float32), gate_part)
        back_share = back_share + jnp.einsum('psqh,xqh->psqx', grad_up.astype(jnp.float32), up_part)
        back_share = back_share.astype(jnp.bfloat16)
        grad_norm = grad_norm + row_slots(chosen, lax.optimization_barrier(jnp.sum(back_share.astype(jnp.float32), axis=2)))
    inner = lax.optimization_barrier(jnp.mean(grad_norm * values, axis=-1, keepdims=True))
    new_cot = (cot_values + inv_rms * grad_norm - inv_rms ** 3 * values * inner).astype(jnp.bfloat16)
    return (new_cot, jnp.concatenate(grads_gate, axis=1), jnp.concatenate(grads_up, axis=1), jnp.concatenate(grads_down, axis=0))

def reference(tokens, cotangent, w_gate, w_up, w_down, routes, gates):
    block_shape = (N_SECTION, N_EXPERT, N_DP, TOK_DEV, D)
    route_shape = (TICKS, N_SECTION, N_EXPERT, N_DP, TOK_DEV, TOP)
    route_blocks = routes.reshape(route_shape)
    gate_blocks = gates.reshape(route_shape)
    current = tokens.reshape(block_shape)
    history = []
    for tick_index in range(TICKS):
        history.append(current)
        updated = jnp.stack([section_forward(current[layer_index], route_blocks[tick_index, layer_index], gate_blocks[tick_index, layer_index], w_gate[layer_index], w_up[layer_index], w_down[layer_index]) for layer_index in range(N_SECTION)])
        current = jnp.roll(updated, 1, axis=0)
    carried = cotangent.reshape(block_shape)
    total_gate = [jnp.zeros((D, EXP_W * HID), jnp.float32) for layer_index in range(N_SECTION)]
    total_up = [jnp.zeros((D, EXP_W * HID), jnp.float32) for layer_index in range(N_SECTION)]
    total_down = [jnp.zeros((EXP_W * HID, D), jnp.float32) for layer_index in range(N_SECTION)]
    for tick_index in reversed(range(TICKS)):
        carried = jnp.roll(carried, -1, axis=0)
        entering = history[tick_index]
        new_rows = []
        for layer_index in range(N_SECTION):
            result_cot, grad_g, grad_u, grad_d = section_backward(entering[layer_index], carried[layer_index], route_blocks[tick_index, layer_index], gate_blocks[tick_index, layer_index], w_gate[layer_index], w_up[layer_index], w_down[layer_index])
            new_rows.append(result_cot)
            total_gate[layer_index] = total_gate[layer_index] + grad_g
            total_up[layer_index] = total_up[layer_index] + grad_u
            total_down[layer_index] = total_down[layer_index] + grad_d
        carried = jnp.stack(new_rows)
    return (carried.reshape(TOKENS, D), current.reshape(TOKENS, D), jnp.stack(total_gate).astype(jnp.bfloat16), jnp.stack(total_up).astype(jnp.bfloat16), jnp.stack(total_down).astype(jnp.bfloat16))
```

```python
import functools

import jax
import jax.numpy as jnp
from jax import lax
from jax.experimental import pallas as pl
from jax.experimental.pallas import tpu as pltpu
from jax.sharding import PartitionSpec as P

SLOTS = 16
TICKS = 2
EPSILON = 1e-06
F32 = jnp.float32
BF16 = jnp.bfloat16
VMEM_BIG = 48 * 1024 * 1024
VMEM_SMALL = 24 * 1024 * 1024
CHUNKS = 8


def shifted(block, axis, distance):
    size = lax.axis_size(axis)
    return lax.ppermute(block, axis, [((i - distance) % size, i) for i in range(size)])


def dot(a, b, ca=1, cb=0):
    return lax.dot_general(a, b, (((ca,), (cb,)), ((), ())), preferred_element_type=F32)


def call(kernel, outs, args, *, any_args=(), scratch=(), vmem=VMEM_SMALL, flops=0, extra=0):
    outs = [jax.ShapeDtypeStruct(s, d) for s, d in outs]
    moved = sum(a.size * a.dtype.itemsize for a in args) + sum(o.size * o.dtype.itemsize for o in outs)
    specs = [
        pl.BlockSpec(memory_space=pl.ANY if i in any_args else pltpu.VMEM) for i in range(len(args))
    ]
    return pl.pallas_call(
        kernel,
        out_shape=outs,
        in_specs=specs,
        out_specs=[pl.BlockSpec(memory_space=pltpu.VMEM) for _ in outs],
        scratch_shapes=list(scratch),
        compiler_params=pltpu.CompilerParams(vmem_limit_bytes=vmem),
        cost_estimate=pl.CostEstimate(flops=flops, bytes_accessed=moved + extra, transcendentals=0),
    )(*args)


def select_of(routes):
    hits = (routes == 0).astype(F32)
    marked = jnp.sum(hits, axis=0, keepdims=True)
    rows = routes.shape[1]
    before = lax.broadcasted_iota(jnp.int32, (rows, rows), 0) < lax.broadcasted_iota(
        jnp.int32, (rows, rows), 1
    )
    wide = jnp.broadcast_to(marked, (SLOTS, rows))
    places = dot(wide.astype(BF16), before.astype(F32).astype(BF16))
    slot = lax.broadcasted_iota(jnp.int32, (SLOTS, rows), 0).astype(F32)
    return jnp.where((places == slot) & (wide > 0.5), 1.0, 0.0), marked


def slot_gates(select, routes, gates):
    weights = jnp.sum(jnp.where(routes == 0, gates, 0.0), axis=0, keepdims=True)
    return jnp.sum(select * weights, axis=1, keepdims=True)


def pick(select, rows):
    return dot(select.astype(BF16), rows).astype(BF16)


def put(select, rows):
    return dot(select.astype(BF16), rows, 0, 0)


def inv_rms_of(values):
    return lax.rsqrt(jnp.mean(values * values, axis=-1, keepdims=True) + EPSILON)


def merged(select_to, select_from, fresh, old):
    same = dot(select_to.astype(BF16), select_from.astype(BF16), 1, 1)
    taken = jnp.sum(same, axis=1, keepdims=True)
    moved = dot(same.astype(BF16), fresh)
    return jnp.where(taken > 0.5, moved, old.astype(F32)).astype(BF16)


def first_rows_kernel(tokens, routes, raw, normed):
    select, _ = select_of(routes[0])
    rows = pick(select, tokens[...])
    raw[...] = rows
    values = rows.astype(F32)
    normed[...] = (values * inv_rms_of(values)).astype(BF16)


def other_rows_kernel(tokens, cotangent, next_routes, prev_routes, prev2_routes, t1, cot):
    t1[...] = pick(select_of(next_routes[0])[0], tokens[...])
    cot[:SLOTS] = pick(select_of(prev_routes[1])[0], cotangent[...])
    cot[SLOTS:] = pick(select_of(prev2_routes[0])[0], cotangent[...])


def scale_kernel(tick, rows, routes, gates, out):
    select, _ = select_of(routes[tick])
    weight = slot_gates(select, routes[tick], gates[tick])
    out[...] = (weight * rows[:SLOTS].astype(F32)).astype(BF16)


def norm_kernel(rows, out):
    values = rows[...].astype(F32)
    out[...] = (values * inv_rms_of(values)).astype(BF16)


def update_kernel(tick, n, *refs):
    parts, (raw, routes, gates), rest = refs[:n], refs[n : n + 3], refs[n + 3 :]
    select, _ = select_of(routes[tick])
    weight = slot_gates(select, routes[tick], gates[tick])
    total = parts[0][...].astype(F32)
    for p in parts[1:]:
        total = total + p[...].astype(F32)
    fresh = (raw[...].astype(F32) + weight * total).astype(BF16)
    if tick == 0:
        next_routes, t1, upd, onward = rest
        onward[...] = merged(select_of(next_routes[0])[0], select, fresh, t1[...])
    else:
        (upd,) = rest
    upd[...] = fresh


def state_grad(parts, h, c):
    total = parts[0][...].astype(F32)
    for p in parts[1:]:
        total = total + p[...].astype(F32)
    values = h.astype(F32)
    inv = inv_rms_of(values)
    inner = jnp.mean(total * values, axis=-1, keepdims=True)
    return (c.astype(F32) + inv * total - inv * inv * inv * values * inner).astype(BF16)


def grad1_kernel(n, *refs):
    parts, (h, cot, routes, prev_routes, upd, onward) = refs[:n], refs[n:]
    fresh = state_grad(parts, h[...], cot[:SLOTS])
    upd[...] = fresh
    onward[...] = merged(
        select_of(prev_routes[0])[0], select_of(routes[1])[0], fresh, cot[SLOTS:]
    )


def finish_grad_kernel(n, *refs):
    parts, (h, c, routes, upd1, next_routes, bulk, out) = refs[:n], refs[n:]
    fresh = state_grad(parts, h[...], c[...])
    first, _ = select_of(next_routes[0])
    second, _ = select_of(routes[0])
    place_rows(bulk, first, upd1[...], second, fresh, out)


def place_rows(bulk, first, rows1, second, rows2, out):
    ones = jnp.ones((SLOTS, 128), BF16)
    hit1 = put(first, ones)[:, :1] > 0.5
    hit2 = put(second, ones)[:, :1] > 0.5
    value = jnp.where(hit1, put(first, rows1), bulk[...].astype(F32))
    out[...] = jnp.where(hit2, put(second, rows2), value).astype(BF16)


def finish_state_kernel(bulk, upd0, prev2_routes, upd1, prev_routes, out):
    first, _ = select_of(prev2_routes[0])
    second, _ = select_of(prev_routes[1])
    place_rows(bulk, first, upd0[...], second, upd1[...], out)


def silu_grads(pre_gate, pre_up, grad_act):
    sig = jax.nn.sigmoid(pre_gate)
    grad_gate = (grad_act * pre_up * sig * (1.0 + pre_gate * (1.0 - sig))).astype(BF16)
    grad_up = (grad_act * (pre_gate * sig)).astype(BF16)
    return grad_gate, grad_up


def weight_copies(gate, up, down, gate_v, up_v, down_v, sems, rows, cols):
    out = []
    for c in range(CHUNKS):
        r = pl.ds(c * rows, rows)
        k = pl.ds(c * cols, cols)
        out.append(
            (
                pltpu.make_async_copy(gate.at[r], gate_v.at[r], sems.at[0, c]),
                pltpu.make_async_copy(up.at[r], up_v.at[r], sems.at[1, c]),
                pltpu.make_async_copy(down.at[:, k], down_v.at[:, k], sems.at[2, c]),
            )
        )
    return out


def gather_rows(blocks, whole):
    for i, b in enumerate(blocks):
        whole[i * SLOTS : (i + 1) * SLOTS] = b[...]


def spread_rows(value, blocks, cols):
    for i, b in enumerate(blocks):
        b[:, cols] = value[i * SLOTS : (i + 1) * SLOTS].astype(BF16)


def forward_kernel(n, *refs):
    blocks, (gate, up, down) = refs[:n], refs[n : n + 3]
    x, pre_gate, pre_up, act = refs[n + 3 : n + 7]
    parts = refs[n + 7 : 2 * n + 7]
    gate_v, up_v, down_v, sems = refs[2 * n + 7 :]
    width = gate.shape[0]
    step = width // CHUNKS
    copies = weight_copies(gate, up, down, gate_v, up_v, down_v, sems, step, step)
    for cg, cu, _ in copies:
        cg.start()
        cu.start()
    for _, _, cd in copies:
        cd.start()
    gather_rows(blocks, x)
    acc_g = jnp.zeros(pre_gate.shape, F32)
    acc_u = jnp.zeros(pre_up.shape, F32)
    for c, (cg, cu, _) in enumerate(copies):
        k = slice(c * step, (c + 1) * step)
        cg.wait()
        acc_g = acc_g + dot(x[:, k], gate_v[k])
        cu.wait()
        acc_u = acc_u + dot(x[:, k], up_v[k])
    pre_gate[...] = acc_g
    pre_up[...] = acc_u
    activated = (acc_g * jax.nn.sigmoid(acc_g) * acc_u).astype(BF16)
    act[...] = activated
    for c, (_, _, cd) in enumerate(copies):
        k = slice(c * step, (c + 1) * step)
        cd.wait()
        spread_rows(dot(activated, down_v[:, k]), parts, k)


def down_kernel(n, act, down, *parts):
    width = down.shape[1]
    step = width // CHUNKS
    for c in range(CHUNKS):
        k = slice(c * step, (c + 1) * step)
        spread_rows(dot(act[...], down[:, k]), parts, k)


def back_rows(gg, gu, gate_v, up_v, parts, step):
    for c in range(CHUNKS):
        k = slice(c * step, (c + 1) * step)
        spread_rows(dot(gg, gate_v[k], 1, 1) + dot(gu, up_v[k], 1, 1), parts, k)


def tick1_kernel(n, *refs):
    xs, gs, (gate, up, down) = refs[:n], refs[n : 2 * n], refs[2 * n : 2 * n + 3]
    x, g, act, grad_gate, grad_up = refs[2 * n + 3 : 2 * n + 8]
    parts = refs[2 * n + 8 : 3 * n + 8]
    gate_v, up_v, down_v, sems = refs[3 * n + 8 :]
    width = gate.shape[0]
    step = width // CHUNKS
    copies = weight_copies(gate, up, down, gate_v, up_v, down_v, sems, step, step)
    for three in copies:
        for c in three:
            c.start()
    gather_rows(xs, x)
    gather_rows(gs, g)
    acc_g = jnp.zeros(act.shape, F32)
    acc_u = jnp.zeros(act.shape, F32)
    acc_a = jnp.zeros(act.shape, F32)
    for c, (cg, cu, cd) in enumerate(copies):
        k = slice(c * step, (c + 1) * step)
        cg.wait()
        acc_g = acc_g + dot(x[:, k], gate_v[k])
        cu.wait()
        acc_u = acc_u + dot(x[:, k], up_v[k])
        cd.wait()
        acc_a = acc_a + dot(g[:, k], down_v[:, k], 1, 1)
    act[...] = (acc_g * jax.nn.sigmoid(acc_g) * acc_u).astype(BF16)
    gg, gu = silu_grads(acc_g, acc_u, acc_a)
    grad_gate[...] = gg
    grad_up[...] = gu
    back_rows(gg, gu, gate_v, up_v, parts, step)


def tick0_kernel(n, *refs):
    gs, (pre_gate, pre_up, gate, up, down) = refs[:n], refs[n : n + 5]
    g, grad_gate, grad_up = refs[n + 5 : n + 8]
    parts = refs[n + 8 : 2 * n + 8]
    gate_v, up_v, down_v, sems = refs[2 * n + 8 :]
    width = gate.shape[0]
    step = width // CHUNKS
    copies = weight_copies(gate, up, down, gate_v, up_v, down_v, sems, step, step)
    for _, _, cd in copies:
        cd.start()
    for cg, cu, _ in copies:
        cg.start()
        cu.start()
    gather_rows(gs, g)
    acc_a = jnp.zeros(pre_gate.shape, F32)
    for c, (_, _, cd) in enumerate(copies):
        k = slice(c * step, (c + 1) * step)
        cd.wait()
        acc_a = acc_a + dot(g[:, k], down_v[:, k], 1, 1)
    gg, gu = silu_grads(pre_gate[...], pre_up[...], acc_a)
    grad_gate[...] = gg
    grad_up[...] = gu
    for cg, cu, _ in copies:
        cg.wait()
        cu.wait()
    back_rows(gg, gu, gate_v, up_v, parts, step)


def weight_grad_kernel(m, *refs):
    xs, gs = refs[:m], refs[m : 2 * m]
    acts, ggs, gus = refs[2 * m : 3 * m], refs[3 * m : 4 * m], refs[4 * m : 5 * m]
    gate_out, up_out, down_out = refs[5 * m :]

    def whole(blocks):
        return jnp.concatenate([b[...] for b in blocks], axis=0)

    x_t = whole(xs).T
    gate_out[...] = dot(x_t, whole(ggs)).astype(BF16)
    up_out[...] = dot(x_t, whole(gus)).astype(BF16)
    down_out[...] = dot(whole(acts), whole(gs), 0, 0).astype(BF16)


def weight_grads(xs, gs, acts, ggs, gus):
    m = len(xs)
    rows, width = xs[0].shape
    hidden = acts[0].shape[1]
    step = width // CHUNKS
    wide = pl.BlockSpec((rows, step), lambda c: (0, c))
    narrow = pl.BlockSpec((rows, hidden), lambda c: (0, 0))
    return pl.pallas_call(
        functools.partial(weight_grad_kernel, m),
        grid=(CHUNKS,),
        out_shape=[
            jax.ShapeDtypeStruct((width, hidden), BF16),
            jax.ShapeDtypeStruct((width, hidden), BF16),
            jax.ShapeDtypeStruct((hidden, width), BF16),
        ],
        in_specs=[wide] * (2 * m) + [narrow] * (3 * m),
        out_specs=[
            pl.BlockSpec((step, hidden), lambda c: (c, 0)),
            pl.BlockSpec((step, hidden), lambda c: (c, 0)),
            pl.BlockSpec((hidden, step), lambda c: (0, c)),
        ],
        compiler_params=pltpu.CompilerParams(vmem_limit_bytes=VMEM_BIG),
        cost_estimate=pl.CostEstimate(
            flops=6 * m * rows * width * hidden,
            bytes_accessed=6 * width * hidden + 4 * m * rows * width,
            transcendentals=0,
        ),
    )(*xs, *gs, *acts, *ggs, *gus)


def from_group(block):
    n = lax.axis_size("expert")
    return [block] + [shifted(block, "expert", k) for k in range(1, n)]


def to_group(blocks):
    return [blocks[0]] + [shifted(b, "expert", -k) for k, b in enumerate(blocks) if k]


def copies_of(block):
    n = lax.axis_size("dp")
    return [block] + [shifted(block, "dp", k) for k in range(1, n)]


def shards(tokens, cotangent, w_gate, w_up, w_down, routes, gates):
    gate, up, down = w_gate[0], w_up[0], w_down[0]
    width, hidden = gate.shape
    n = lax.axis_size("expert")
    rows = n * SLOTS
    routes = jnp.transpose(routes, (0, 2, 1))
    gates = jnp.transpose(gates, (0, 2, 1))
    one = ((SLOTS, width), BF16)
    every = ((rows, width), BF16)
    wide = ((rows, hidden), BF16)
    wide32 = ((rows, hidden), F32)
    part = functools.partial
    weights_v = [
        pltpu.VMEM((width, hidden), BF16),
        pltpu.VMEM((width, hidden), BF16),
        pltpu.VMEM((hidden, width), BF16),
        pltpu.SemaphoreType.DMA((3, CHUNKS)),
    ]
    matmul = 2 * rows * width * hidden

    prev_routes = shifted(routes, "section", 1)
    next_routes = shifted(routes[1:], "section", -1)
    prev2_routes = shifted(routes[:1], "section", 2)
    bulk_state = shifted(tokens, "section", 2)
    bulk_grad = shifted(cotangent, "section", -2)

    raw0, normed0 = call(first_rows_kernel, [one, one], [tokens, routes])
    x0_blocks = from_group(normed0)
    t1, cot_rows = call(
        other_rows_kernel,
        [one, ((2 * SLOTS, width), BF16)],
        [tokens, cotangent, next_routes, prev_routes, prev2_routes],
    )
    cot_rows = shifted(cot_rows, "section", -1)
    x0, pre_gate0, pre_up0, act0, *parts = call(
        part(forward_kernel, n),
        [every, wide32, wide32, wide] + [one] * n,
        [*x0_blocks, gate, up, down],
        any_args=(n, n + 1, n + 2),
        scratch=weights_v,
        vmem=VMEM_BIG,
        flops=3 * matmul,
    )
    parts = to_group(parts)
    upd0, h1 = call(
        part(update_kernel, 0, n),
        [one, one],
        [*parts, raw0, routes, gates, next_routes, t1],
    )
    h1 = shifted(h1, "section", 1)
    upd0 = shifted(upd0, "section", 2)
    (g1_rows,) = call(part(scale_kernel, 1), [one], [cot_rows, routes, gates])
    g1_blocks = from_group(g1_rows)

    (normed1,) = call(norm_kernel, [one], [h1])
    x1_blocks = from_group(normed1)
    x1, g1, act1, gg1, gu1, *parts = call(
        part(tick1_kernel, n),
        [every, every, wide, wide, wide] + [one] * n,
        [*x1_blocks, *g1_blocks, gate, up, down],
        any_args=(2 * n, 2 * n + 1, 2 * n + 2),
        scratch=weights_v,
        vmem=VMEM_BIG,
        flops=5 * matmul,
    )
    parts = to_group(parts)
    outs1 = call(part(down_kernel, n), [one] * n, [act1, down], vmem=VMEM_BIG, flops=matmul)
    outs1 = to_group(outs1)
    cu1, c0 = call(
        part(grad1_kernel, n), [one, one], [*parts, h1, cot_rows, routes, prev_routes]
    )
    c0 = shifted(c0, "section", -1)
    cu1 = shifted(cu1, "section", -1)
    (upd1,) = call(part(update_kernel, 1, n), [one], [*outs1, h1, routes, gates])
    upd1 = shifted(upd1, "section", 1)

    (g0_rows,) = call(part(scale_kernel, 0), [one], [c0, routes, gates])
    g0_blocks = from_group(g0_rows)
    g0, gg0, gu0, *parts = call(
        part(tick0_kernel, n),
        [every, wide, wide] + [one] * n,
        [*g0_blocks, pre_gate0, pre_up0, gate, up, down],
        any_args=(n + 2, n + 3, n + 4),
        scratch=weights_v,
        vmem=VMEM_BIG,
        flops=3 * matmul,
    )
    parts = to_group(parts)
    gate_out, up_out, down_out = weight_grads(
        copies_of(x0) + copies_of(x1),
        copies_of(g0) + copies_of(g1),
        copies_of(act0) + copies_of(act1),
        copies_of(gg0) + copies_of(gg1),
        copies_of(gu0) + copies_of(gu1),
    )
    (state,) = call(
        finish_state_kernel,
        [(tokens.shape, BF16)],
        [bulk_state, upd0, prev2_routes, upd1, prev_routes],
    )
    (grad,) = call(
        part(finish_grad_kernel, n),
        [(tokens.shape, BF16)],
        [*parts, raw0, c0, routes, cu1, next_routes, bulk_grad],
    )
    return (grad, state, gate_out[None], up_out[None], down_out[None])


def solution(mesh):
    rows = P(("section", "expert", "dp"), None)
    slots = P(None, ("section", "expert", "dp"), None)
    cols = P("section", None, "expert")
    hidden = P("section", "expert", None)
    return jax.shard_map(
        shards,
        mesh=mesh,
        in_specs=(rows, rows, cols, cols, hidden, slots, slots),
        out_specs=(rows, rows, cols, cols, hidden),
        check_vma=False,
    )
```

```python
import functools

import jax
import jax.numpy as jnp
from jax import lax
from jax.experimental import pallas as pl
from jax.experimental.pallas import tpu as pltpu
from jax.sharding import PartitionSpec as P

CAP = 10
PACK = 8
PACKED = CAP * PACK
FIRST = 64
SECOND = 16
EPSILON = 1e-06
F32 = jnp.float32
BF16 = jnp.bfloat16
VMEM_BIG = 48 * 1024 * 1024
VMEM_SMALL = 24 * 1024 * 1024
COST_BYTES = 1024


def shifted(block, axis, distance):
    size = lax.axis_size(axis)
    return lax.ppermute(block, axis, [((i - distance) % size, i) for i in range(size)])


def dot(a, b, ca=1, cb=0):
    return lax.dot_general(a, b, (((ca,), (cb,)), ((), ())), preferred_element_type=F32)


def call(
    kernel, outs, args, *, any_args=(), any_outs=(), scratch=(), vmem=VMEM_SMALL, flops=0
):
    outs = [jax.ShapeDtypeStruct(s, d) for s, d in outs]
    anywhere = pl.BlockSpec(memory_space=pl.ANY)
    near = pl.BlockSpec(memory_space=pltpu.VMEM)
    return pl.pallas_call(
        kernel,
        out_shape=outs,
        in_specs=[anywhere if i in any_args else near for i in range(len(args))],
        out_specs=[anywhere if i in any_outs else near for i in range(len(outs))],
        scratch_shapes=list(scratch),
        compiler_params=pltpu.CompilerParams(vmem_limit_bytes=vmem),
        cost_estimate=pl.CostEstimate(flops=flops, bytes_accessed=COST_BYTES, transcendentals=0),
    )(*args)


def packed_index(shape, dim):
    place = lax.broadcasted_iota(jnp.int32, shape, dim).astype(F32)
    chunk = jnp.floor((place + 0.5) * (1.0 / CAP))
    return place - CAP * chunk, chunk


def select_of(routes):
    hits = (routes == 0).astype(F32)
    marked = jnp.sum(hits, axis=0, keepdims=True)
    rows = routes.shape[1]
    before = lax.broadcasted_iota(jnp.int32, (rows, rows), 0) < lax.broadcasted_iota(
        jnp.int32, (rows, rows), 1
    )
    wide = jnp.broadcast_to(marked, (PACKED, rows))
    places = dot(wide.astype(BF16), before.astype(F32).astype(BF16))
    slot, _ = packed_index((PACKED, rows), 0)
    return jnp.where((places == slot) & (wide > 0.5), 1.0, 0.0)


def slot_gates(select, routes, gates):
    weights = jnp.sum(jnp.where(routes == 0, gates, 0.0), axis=0, keepdims=True)
    return jnp.sum(select * weights, axis=1, keepdims=True)


def chunk_of(select, c):
    _, chunk = packed_index(select.shape, 0)
    return jnp.where(chunk == c, select, 0.0).astype(BF16)


def columns(c, width):
    return slice(c * (width // PACK), (c + 1) * (width // PACK))


def pick(select, rows):
    total = None
    at = 0
    for block in rows:
        end = at + block.shape[0]
        for c in range(PACK):
            part = dot(chunk_of(select[:, at:end], c), block[:, columns(c, block.shape[1])])
            total = part if total is None else total + part
        at = end
    return total


def over_chunks(row_sums):
    slot_r, _ = packed_index((PACKED, PACKED), 0)
    slot_c, _ = packed_index((PACKED, PACKED), 1)
    same = jnp.where(slot_r == slot_c, 1.0, 0.0)
    wide = jnp.broadcast_to(row_sums, (PACKED, 128))
    return jnp.dot(
        same, wide, precision=lax.Precision.HIGHEST, preferred_element_type=F32
    )[:, :1]


def mean_of(values):
    return over_chunks(jnp.sum(values, axis=-1, keepdims=True)) * (1.0 / (PACK * values.shape[1]))


def inv_rms_of(values):
    return lax.rsqrt(mean_of(values * values) + EPSILON)


def merged(select_to, select_from, fresh, old):
    same = dot(select_to.astype(BF16), select_from.astype(BF16), 1, 1)
    _, chunk_r = packed_index(same.shape, 0)
    _, chunk_c = packed_index(same.shape, 1)
    same = jnp.where(chunk_r == chunk_c, same, 0.0)
    taken = jnp.sum(same, axis=1, keepdims=True)
    return jnp.where(taken > 0.5, dot(same.astype(BF16), fresh), old).astype(BF16)


def summed(parts):
    total = parts[0][...].astype(F32)
    for p in parts[1:]:
        total = total + p[...].astype(F32)
    return total


def place_rows(bulk, first, rows1, second, rows2, out):
    ones = jnp.ones((PACKED, 128), BF16)
    hit1 = dot(chunk_of(first, 0), ones, 0, 0)[:, :1] > 0.5
    hit2 = dot(chunk_of(second, 0), ones, 0, 0)[:, :1] > 0.5
    width = out.shape[1]
    for c in range(PACK):
        k = columns(c, width)
        new1 = dot(chunk_of(first, c), rows1, 0, 0)
        new2 = dot(chunk_of(second, c), rows2, 0, 0)
        at = 0
        for block in bulk:
            r = slice(at, at + block.shape[0])
            at = r.stop
            value = jnp.where(hit1[r], new1[r], block[:, k].astype(F32))
            out[r, k] = jnp.where(hit2[r], new2[r], value).astype(BF16)


def first_rows_kernel(tokens, routes, cotangent, raw, normed, piece, sem):
    copy = pltpu.make_async_copy(cotangent.at[pl.ds(0, FIRST)], piece, sem)
    copy.start()
    values = pick(select_of(routes[0]), [tokens])
    raw[...] = values.astype(BF16)
    normed[...] = (values * inv_rms_of(values)).astype(BF16)
    copy.wait()


def other_rows_kernel(tokens, cotangent, next_routes, prev_routes, t1, cot):
    t1[...] = pick(select_of(next_routes[0]), [tokens]).astype(BF16)
    cot[...] = pick(select_of(prev_routes[0]), [cotangent]).astype(BF16)


def update0_kernel(n, *refs):
    parts, (raw, routes, gates, next_routes, t1, tokens) = refs[:n], refs[n : n + 6]
    upd, onward, piece, sem = refs[n + 9 :]
    copy = pltpu.make_async_copy(tokens.at[pl.ds(0, SECOND)], piece, sem)
    copy.start()
    select = select_of(routes[0])
    weight = slot_gates(select, routes[0], gates[0])
    fresh = (raw[...].astype(F32) + weight * summed(parts)).astype(BF16)
    onward[...] = merged(select_of(next_routes[0]), select, fresh, t1[...].astype(F32))
    upd[...] = fresh
    copy.wait()


def update1_kernel(n, *refs):
    parts, (h, routes, gates, upd) = refs[:n], refs[n:]
    select = select_of(routes[1])
    weight = slot_gates(select, routes[1], gates[1])
    upd[...] = (h[...].astype(F32) + weight * summed(parts)).astype(BF16)


def enter1_kernel(h, cot, routes, gates, cotangent, _, out, piece, sem):
    rows = cotangent.shape[0]
    copy = pltpu.make_async_copy(cotangent.at[pl.ds(FIRST, rows - FIRST)], piece, sem)
    copy.start()
    values = h[...].astype(F32)
    out[:PACKED] = (values * inv_rms_of(values)).astype(BF16)
    weight = slot_gates(select_of(routes[1]), routes[1], gates[1])
    out[PACKED:] = (weight * cot[...].astype(F32)).astype(BF16)
    copy.wait()


def state_grad(parts, h, c):
    total = summed(parts)
    values = h.astype(F32)
    inv = inv_rms_of(values)
    inner = mean_of(total * values)
    return (c.astype(F32) + inv * total - inv * inv * inv * values * inner).astype(BF16)


def grad1_kernel(n, *refs):
    parts, (h, cot, tokens) = refs[:n], refs[n : n + 3]
    upd, piece, sem = refs[n + 5 :]
    copy = pltpu.make_async_copy(tokens.at[pl.ds(SECOND, SECOND)], piece, sem)
    copy.start()
    upd[...] = state_grad(parts, h[...], cot[...])
    copy.wait()


def enter0_kernel(
    upd1, next_routes, routes, gates, bulk_a, bulk_b, tokens, _, c0, out, piece, sem
):
    left = tokens.shape[0] - 2 * SECOND
    copy = pltpu.make_async_copy(tokens.at[pl.ds(2 * SECOND, left)], piece, sem)
    copy.start()
    select = select_of(routes[0])
    old = pick(select, [bulk_a, bulk_b])
    rows = merged(select, select_of(next_routes[0]), upd1[...], old)
    c0[...] = rows
    out[...] = (slot_gates(select, routes[0], gates[0]) * rows.astype(F32)).astype(BF16)
    copy.wait()


def finish_grad_kernel(n, *refs):
    parts, (h, c, routes, upd1, next_routes, bulk_a, bulk_b, out) = refs[:n], refs[n:]
    fresh = state_grad(parts, h[...], c[...])
    place_rows(
        [bulk_a, bulk_b], select_of(next_routes[0]), upd1[...], select_of(routes[0]), fresh, out
    )


def finish_state_kernel(
    bulk_a, bulk_b, bulk_c, upd0, prev2_routes, upd1, prev_routes, out
):
    place_rows(
        [bulk_a, bulk_b, bulk_c],
        select_of(prev2_routes[0]),
        upd0[...],
        select_of(prev_routes[0]),
        upd1[...],
        out,
    )


def silu_grads(pre_gate, pre_up, grad_act):
    sig = jax.nn.sigmoid(pre_gate)
    grad_gate = (grad_act * pre_up * sig * (1.0 + pre_gate * (1.0 - sig))).astype(BF16)
    grad_up = (grad_act * (pre_gate * sig)).astype(BF16)
    return grad_gate, grad_up


def weight_copies(gate, up, down, gate_v, up_v, down_v, sems):
    out = []
    step = gate.shape[0] // PACK
    for c in range(PACK):
        r = pl.ds(c * step, step)
        out.append(
            (
                pltpu.make_async_copy(gate.at[r], gate_v.at[r], sems.at[0, c]),
                pltpu.make_async_copy(up.at[r], up_v.at[r], sems.at[1, c]),
                pltpu.make_async_copy(down.at[:, r], down_v.at[:, r], sems.at[2, c]),
            )
        )
    return out


def gather_rows(blocks, first, unpacked, whole32, whole):
    width = whole.shape[1]
    used = len(blocks) * CAP
    if used < whole.shape[0]:
        whole32[used:] = jnp.zeros((whole.shape[0] - used, width), F32)
    for i, b in enumerate(blocks):
        unpacked[i] = b[first : first + PACKED].astype(F32)
        for c in range(PACK):
            whole32[i * CAP : (i + 1) * CAP, columns(c, width)] = unpacked[
                i, c * CAP : (c + 1) * CAP
            ]
    whole[...] = whole32[...].astype(BF16)


def spread_rows(value, c, n, held, unpacked):
    held[...] = value
    for i in range(n):
        unpacked[i, c * CAP : (c + 1) * CAP] = held[i * CAP : (i + 1) * CAP]


def forward_kernel(n, *refs):
    blocks, (gate, up, down, _) = refs[:n], refs[n : n + 4]
    x, pre_gate, pre_up, act = refs[n + 4 : n + 8]
    parts = refs[n + 8 : 2 * n + 8]
    gate_v, up_v, down_v, sems, unpacked, whole32, held = refs[2 * n + 8 :]
    copies = weight_copies(gate, up, down, gate_v, up_v, down_v, sems)
    for cg, cu, _ in copies:
        cg.start()
        cu.start()
    for _, _, cd in copies:
        cd.start()
    gather_rows(blocks, 0, unpacked, whole32, x)
    acc_g = jnp.zeros(pre_gate.shape, F32)
    acc_u = jnp.zeros(pre_up.shape, F32)
    width = gate.shape[0]
    for c, (cg, cu, _) in enumerate(copies):
        k = columns(c, width)
        cg.wait()
        acc_g = acc_g + dot(x[:, k], gate_v[k])
        cu.wait()
        acc_u = acc_u + dot(x[:, k], up_v[k])
    pre_gate[...] = acc_g
    pre_up[...] = acc_u
    activated = (acc_g * jax.nn.sigmoid(acc_g) * acc_u).astype(BF16)
    act[...] = activated
    for c, (_, _, cd) in enumerate(copies):
        cd.wait()
        spread_rows(dot(activated, down_v[:, columns(c, width)]), c, n, held.at[c], unpacked)
    for i, p in enumerate(parts):
        p[...] = unpacked[i].astype(BF16)


def down_kernel(n, act, down, _, *refs):
    parts, (unpacked, held) = refs[:n], refs[n:]
    hidden = down.shape[0]
    for c in range(PACK):
        value = dot(act[:, hidden : 2 * hidden], down[:, columns(c, down.shape[1])])
        spread_rows(value, c, n, held.at[c], unpacked)
    for i, p in enumerate(parts):
        p[...] = unpacked[i].astype(BF16)


def back_rows(gg, gu, gate_v, up_v, held, unpacked, parts):
    n = len(parts)
    for c in range(PACK):
        k = columns(c, gate_v.shape[0])
        value = dot(gg, gate_v[k], 1, 1) + dot(gu, up_v[k], 1, 1)
        spread_rows(value, c, n, held.at[c], unpacked)
    for i, p in enumerate(parts):
        p[...] = unpacked[i].astype(BF16)


def tick1_kernel(n, *refs):
    blocks, (act0, gate, up, down, _) = refs[:n], refs[n : n + 5]
    xg, small = refs[n + 5 : n + 7]
    parts = refs[n + 7 : 2 * n + 7]
    gate_v, up_v, down_v, sems, unpacked, whole32, held, x, g = refs[2 * n + 7 :]
    copies = weight_copies(gate, up, down, gate_v, up_v, down_v, sems)
    for three in copies:
        for c in three:
            c.start()
    gather_rows(blocks, 0, unpacked, whole32.at[0], x)
    gather_rows(blocks, PACKED, unpacked, whole32.at[1], g)
    rows, hidden = act0.shape
    xg[:rows] = x[...]
    xg[rows:] = g[...]
    width = gate.shape[0]
    acc_g = jnp.zeros(act0.shape, F32)
    acc_u = jnp.zeros(act0.shape, F32)
    acc_a = jnp.zeros(act0.shape, F32)
    for c, (cg, cu, cd) in enumerate(copies):
        k = columns(c, width)
        cg.wait()
        acc_g = acc_g + dot(x[:, k], gate_v[k])
        cu.wait()
        acc_u = acc_u + dot(x[:, k], up_v[k])
        cd.wait()
        acc_a = acc_a + dot(g[:, k], down_v[:, k], 1, 1)
    gg, gu = silu_grads(acc_g, acc_u, acc_a)
    small[:, :hidden] = act0[...]
    small[:, hidden : 2 * hidden] = (acc_g * jax.nn.sigmoid(acc_g) * acc_u).astype(BF16)
    small[:, 2 * hidden : 3 * hidden] = gg
    small[:, 3 * hidden :] = gu
    back_rows(gg, gu, gate_v, up_v, held, unpacked, parts)


def tick0_kernel(n, *refs):
    blocks, (pre_gate, pre_up, gate, up, down, _) = refs[:n], refs[n : n + 6]
    g, small = refs[n + 6 : n + 8]
    parts = refs[n + 8 : 2 * n + 8]
    gate_v, up_v, down_v, sems, unpacked, whole32, held = refs[2 * n + 8 :]
    copies = weight_copies(gate, up, down, gate_v, up_v, down_v, sems)
    for _, _, cd in copies:
        cd.start()
    for cg, cu, _ in copies:
        cg.start()
        cu.start()
    gather_rows(blocks, 0, unpacked, whole32, g)
    hidden = pre_gate.shape[1]
    acc_a = jnp.zeros(pre_gate.shape, F32)
    for c, (_, _, cd) in enumerate(copies):
        k = columns(c, gate.shape[0])
        cd.wait()
        acc_a = acc_a + dot(g[:, k], down_v[:, k], 1, 1)
    gg, gu = silu_grads(pre_gate[...], pre_up[...], acc_a)
    small[:, :hidden] = gg
    small[:, hidden:] = gu
    for cg, cu, _ in copies:
        cg.wait()
        cu.wait()
    back_rows(gg, gu, gate_v, up_v, held, unpacked, parts)


def whole_of(blocks):
    return jnp.concatenate(blocks, axis=0)


def input_grad_kernel(m, *refs):
    x0, xg, small1, small0 = (refs[i * m : (i + 1) * m] for i in range(4))
    gate_out, up_out = refs[4 * m :]
    hidden = gate_out.shape[1]
    x_t = whole_of([b[...] for b in x0] + [b[...] for b in xg]).T
    gg = [b[:, :hidden] for b in small0] + [b[:, 2 * hidden : 3 * hidden] for b in small1]
    gu = [b[:, hidden:] for b in small0] + [b[:, 3 * hidden :] for b in small1]
    gate_out[...] = dot(x_t, whole_of(gg)).astype(BF16)
    up_out[...] = dot(x_t, whole_of(gu)).astype(BF16)


def down_grad_kernel(m, *refs):
    g0, xg, small1 = (refs[i * m : (i + 1) * m] for i in range(3))
    (down_out,) = refs[3 * m :]
    hidden = down_out.shape[0]
    act = [b[:, :hidden] for b in small1] + [b[:, hidden : 2 * hidden] for b in small1]
    grads = [b[...] for b in g0] + [b[...] for b in xg]
    down_out[...] = dot(whole_of(act), whole_of(grads), 0, 0).astype(BF16)


def input_grads(x0, xg, small1, small0):
    m = len(x0)
    rows, width = x0[0].shape
    hidden = small0[0].shape[1] // 2
    step = width // PACK
    wide = pl.BlockSpec((rows, step), lambda c: (0, c))
    whole = [pl.BlockSpec(a.shape, lambda c: (0, 0)) for a in small1 + small0]
    out = pl.BlockSpec((step, hidden), lambda c: (c, 0))
    return pl.pallas_call(
        functools.partial(input_grad_kernel, m),
        grid=(PACK,),
        out_shape=[jax.ShapeDtypeStruct((width, hidden), BF16)] * 2,
        in_specs=[wide] * (2 * m) + whole,
        out_specs=[out, out],
        compiler_params=pltpu.CompilerParams(vmem_limit_bytes=VMEM_SMALL),
        cost_estimate=pl.CostEstimate(flops=0, bytes_accessed=COST_BYTES, transcendentals=0),
    )(*x0, *xg, *small1, *small0)


def down_grads(g0, xg, small1):
    m = len(g0)
    rows, width = g0[0].shape
    hidden = small1[0].shape[1] // 4
    step = width // PACK
    wide = pl.BlockSpec((rows, step), lambda c: (0, c))
    second = pl.BlockSpec((rows, step), lambda c: (1, c))
    whole = [pl.BlockSpec(a.shape, lambda c: (0, 0)) for a in small1]
    return pl.pallas_call(
        functools.partial(down_grad_kernel, m),
        grid=(PACK,),
        out_shape=[jax.ShapeDtypeStruct((hidden, width), BF16)],
        in_specs=[wide] * m + [second] * m + whole,
        out_specs=[pl.BlockSpec((hidden, step), lambda c: (0, c))],
        compiler_params=pltpu.CompilerParams(vmem_limit_bytes=VMEM_SMALL),
        cost_estimate=pl.CostEstimate(flops=0, bytes_accessed=COST_BYTES, transcendentals=0),
    )(*g0, *xg, *small1)


def from_group(block):
    n = lax.axis_size("expert")
    return [block] + [shifted(block, "expert", k) for k in range(1, n)]


def to_group(blocks):
    return [blocks[0]] + [shifted(b, "expert", -k) for k, b in enumerate(blocks) if k]


def copies_of(block):
    n = lax.axis_size("dp")
    return [block] + [shifted(block, "dp", k) for k in range(1, n)]


def shards(tokens, cotangent, w_gate, w_up, w_down, routes, gates):
    gate, up, down = w_gate[0], w_up[0], w_down[0]
    width, hidden = gate.shape
    step = width // PACK
    own = tokens.shape[0]
    n = lax.axis_size("expert")
    rows = -(-n * CAP // 16) * 16
    routes = jnp.transpose(routes, (0, 2, 1))
    gates = jnp.transpose(gates, (0, 2, 1))
    one = ((PACKED, step), BF16)
    part = functools.partial
    scratch = [
        pltpu.VMEM((width, hidden), BF16),
        pltpu.VMEM((width, hidden), BF16),
        pltpu.VMEM((hidden, width), BF16),
        pltpu.SemaphoreType.DMA((3, PACK)),
        pltpu.VMEM((n, PACKED, step), F32),
        pltpu.VMEM((rows, width), F32),
        pltpu.VMEM((PACK, rows, step), F32),
    ]
    tick1_scratch = list(scratch)
    tick1_scratch[5] = pltpu.VMEM((2, rows, width), F32)
    tick1_scratch += [pltpu.VMEM((rows, width), BF16)] * 2
    matmul = 0

    next_routes = shifted(routes[1:], "section", -1)
    prev_routes = shifted(routes[1:], "section", 1)
    prev2_routes = shifted(routes[:1], "section", 2)

    raw0, normed0, piece = call(
        first_rows_kernel,
        [one, one, ((FIRST, width), BF16)],
        [tokens, routes, cotangent],
        any_args=(2,),
        any_outs=(2,),
        scratch=[pltpu.SemaphoreType.DMA],
    )
    cot_a = shifted(piece, "section", -2)
    x0_blocks = from_group(normed0)
    t1, cot1 = call(
        other_rows_kernel, [one, one], [tokens, cotangent, next_routes, prev_routes]
    )
    cot1 = shifted(cot1, "section", -1)
    x0, pre_gate0, pre_up0, act0, *parts = call(
        part(forward_kernel, n),
        [((rows, width), BF16), ((rows, hidden), F32), ((rows, hidden), F32)]
        + [((rows, hidden), BF16)]
        + [one] * n,
        [*x0_blocks, gate, up, down, t1],
        any_args=(n, n + 1, n + 2, n + 3),
        scratch=scratch,
        vmem=VMEM_BIG,
        flops=3 * matmul,
    )
    parts = to_group(parts)
    upd0, h1, piece = call(
        part(update0_kernel, n),
        [one, one, ((SECOND, width), BF16)],
        [*parts, raw0, routes, gates, next_routes, t1, tokens, cot_a, cot1, prev2_routes],
        any_args=(n + 5, n + 6, n + 7, n + 8),
        any_outs=(2,),
        scratch=[pltpu.SemaphoreType.DMA],
    )
    h1 = shifted(h1, "section", 1)
    tok_a = shifted(piece, "section", 2)
    upd0 = shifted(upd0, "section", 2)

    enter1, piece = call(
        enter1_kernel,
        [((2 * PACKED, step), BF16), ((own - FIRST, width), BF16)],
        [h1, cot1, routes, gates, cotangent, tok_a],
        any_args=(4, 5),
        any_outs=(1,),
        scratch=[pltpu.SemaphoreType.DMA],
    )
    cot_b = shifted(piece, "section", -2)
    blocks = from_group(enter1)
    x0_all = copies_of(x0)
    xg1, small1, *parts = call(
        part(tick1_kernel, n),
        [((2 * rows, width), BF16), ((rows, 4 * hidden), BF16)] + [one] * n,
        [*blocks, act0, gate, up, down, upd0],
        any_args=(n + 1, n + 2, n + 3, n + 4),
        scratch=tick1_scratch,
        vmem=VMEM_BIG,
        flops=5 * matmul,
    )
    parts = to_group(parts)
    upd1, piece = call(
        part(grad1_kernel, n),
        [one, ((SECOND, width), BF16)],
        [*parts, h1, cot1, tokens, cot_b, x0_all[-1]],
        any_args=(n + 2, n + 3, n + 4),
        any_outs=(1,),
        scratch=[pltpu.SemaphoreType.DMA],
    )
    upd1 = shifted(upd1, "section", -1)
    tok_b = shifted(piece, "section", 2)
    xg1_all = copies_of(xg1)

    c0, enter0, piece = call(
        enter0_kernel,
        [one, one, ((own - 2 * SECOND, width), BF16)],
        [upd1, next_routes, routes, gates, cot_a, cot_b, tokens, tok_b],
        any_args=(6, 7),
        any_outs=(2,),
        scratch=[pltpu.SemaphoreType.DMA],
    )
    tok_c = shifted(piece, "section", 2)
    blocks = from_group(enter0)
    g0, small0, *parts = call(
        part(tick0_kernel, n),
        [((rows, width), BF16), ((rows, 2 * hidden), BF16)] + [one] * n,
        [*blocks, pre_gate0, pre_up0, gate, up, down, xg1_all[-1]],
        any_args=(n + 2, n + 3, n + 4, n + 5),
        scratch=scratch,
        vmem=VMEM_BIG,
        flops=3 * matmul,
    )
    parts = to_group(parts)
    outs = call(
        part(down_kernel, n),
        [one] * n,
        [small1, down, small0],
        any_args=(2,),
        scratch=[scratch[4], scratch[6]],
        vmem=VMEM_BIG,
        flops=matmul,
    )
    outs = to_group(outs)
    (last1,) = call(part(update1_kernel, n), [one], [*outs, h1, routes, gates])
    last1 = shifted(last1, "section", 1)
    small1_all = copies_of(small1)
    gate_out, up_out = input_grads(x0_all, xg1_all, small1_all, copies_of(small0))
    (down_out,) = down_grads(copies_of(g0), xg1_all, small1_all)
    (grad,) = call(
        part(finish_grad_kernel, n),
        [(tokens.shape, BF16)],
        [*parts, raw0, c0, routes, upd1, next_routes, cot_a, cot_b],
    )
    (state,) = call(
        finish_state_kernel,
        [(tokens.shape, BF16)],
        [tok_a, tok_b, tok_c, upd0, prev2_routes, last1, prev_routes],
    )
    return (grad, state, gate_out[None], up_out[None], down_out[None])


def solution(mesh):
    rows = P(("section", "expert", "dp"), None)
    slots = P(None, ("section", "expert", "dp"), None)
    cols = P("section", None, "expert")
    hidden = P("section", "expert", None)
    return jax.shard_map(
        shards,
        mesh=mesh,
        in_specs=(rows, rows, cols, cols, hidden, slots, slots),
        out_specs=(rows, rows, cols, cols, hidden),
        check_vma=False,
    )
```

```python
import functools

import jax
import jax.numpy as jnp
from jax import lax
from jax.experimental import pallas as pl
from jax.experimental.pallas import tpu as pltpu
from jax.sharding import PartitionSpec as P

CAP = 10
PACK = 8
PACKED = CAP * PACK
FIRST = 48
EPSILON = 1e-06
F32 = jnp.float32
BF16 = jnp.bfloat16
VMEM_BIG = 48 * 1024 * 1024
VMEM_SMALL = 24 * 1024 * 1024
COST_BYTES = 1024


def shifted(block, axis, distance):
    size = lax.axis_size(axis)
    return lax.ppermute(block, axis, [((i - distance) % size, i) for i in range(size)])


def dot(a, b, ca=1, cb=0):
    return lax.dot_general(a, b, (((ca,), (cb,)), ((), ())), preferred_element_type=F32)


def call(
    kernel, outs, args, *, any_args=(), any_outs=(), scratch=(), vmem=VMEM_SMALL
):
    outs = [jax.ShapeDtypeStruct(s, d) for s, d in outs]
    anywhere = pl.BlockSpec(memory_space=pl.ANY)
    near = pl.BlockSpec(memory_space=pltpu.VMEM)
    return pl.pallas_call(
        kernel,
        out_shape=outs,
        in_specs=[anywhere if i in any_args else near for i in range(len(args))],
        out_specs=[anywhere if i in any_outs else near for i in range(len(outs))],
        scratch_shapes=list(scratch),
        compiler_params=pltpu.CompilerParams(vmem_limit_bytes=vmem),
        cost_estimate=pl.CostEstimate(flops=0, bytes_accessed=COST_BYTES, transcendentals=0),
    )(*args)


def packed_index(shape, dim):
    place = lax.broadcasted_iota(jnp.int32, shape, dim).astype(F32)
    chunk = jnp.floor((place + 0.5) * (1.0 / CAP))
    return place - CAP * chunk, chunk


def select_of(routes):
    hits = (routes == 0).astype(F32)
    marked = jnp.sum(hits, axis=0, keepdims=True)
    rows = routes.shape[1]
    before = lax.broadcasted_iota(jnp.int32, (rows, rows), 0) < lax.broadcasted_iota(
        jnp.int32, (rows, rows), 1
    )
    wide = jnp.broadcast_to(marked, (PACKED, rows))
    places = dot(wide.astype(BF16), before.astype(F32).astype(BF16))
    slot, _ = packed_index((PACKED, rows), 0)
    return jnp.where((places == slot) & (wide > 0.5), 1.0, 0.0)


def slot_gates(select, routes, gates):
    weights = jnp.sum(jnp.where(routes == 0, gates, 0.0), axis=0, keepdims=True)
    return jnp.sum(select * weights, axis=1, keepdims=True)


def chunk_of(select, c):
    _, chunk = packed_index(select.shape, 0)
    return jnp.where(chunk == c, select, 0.0).astype(BF16)


def columns(c, width):
    return slice(c * (width // PACK), (c + 1) * (width // PACK))


def pick(select, rows):
    total = None
    at = 0
    for block in rows:
        end = at + block.shape[0]
        for c in range(PACK):
            part = dot(chunk_of(select[:, at:end], c), block[:, columns(c, block.shape[1])])
            total = part if total is None else total + part
        at = end
    return total


def over_chunks(row_sums):
    slot_r, _ = packed_index((PACKED, PACKED), 0)
    slot_c, _ = packed_index((PACKED, PACKED), 1)
    same = jnp.where(slot_r == slot_c, 1.0, 0.0)
    wide = jnp.broadcast_to(row_sums, (PACKED, 128))
    return jnp.dot(
        same, wide, precision=lax.Precision.HIGHEST, preferred_element_type=F32
    )[:, :1]


def mean_of(values):
    return over_chunks(jnp.sum(values, axis=-1, keepdims=True)) * (1.0 / (PACK * values.shape[1]))


def inv_rms_of(values):
    return lax.rsqrt(mean_of(values * values) + EPSILON)


def merged(select_to, select_from, fresh, old):
    same = dot(select_to.astype(BF16), select_from.astype(BF16), 1, 1)
    _, chunk_r = packed_index(same.shape, 0)
    _, chunk_c = packed_index(same.shape, 1)
    same = jnp.where(chunk_r == chunk_c, same, 0.0)
    taken = jnp.sum(same, axis=1, keepdims=True)
    return jnp.where(taken > 0.5, dot(same.astype(BF16), fresh), old).astype(BF16)


def summed(parts):
    total = parts[0][...].astype(F32)
    for p in parts[1:]:
        total = total + p[...].astype(F32)
    return total


def place_rows(bulk, first, rows1, second, rows2, out):
    ones = jnp.ones((PACKED, 128), BF16)
    hit1 = dot(chunk_of(first, 0), ones, 0, 0)[:, :1] > 0.5
    hit2 = dot(chunk_of(second, 0), ones, 0, 0)[:, :1] > 0.5
    width = out.shape[1]
    for c in range(PACK):
        k = columns(c, width)
        new1 = dot(chunk_of(first, c), rows1, 0, 0)
        new2 = dot(chunk_of(second, c), rows2, 0, 0)
        at = 0
        for block in bulk:
            r = slice(at, at + block.shape[0])
            at = r.stop
            value = jnp.where(hit1[r], new1[r], block[:, k].astype(F32))
            out[r, k] = jnp.where(hit2[r], new2[r], value).astype(BF16)


def copy_rows(source, start, stop, piece, sem):
    copy = pltpu.make_async_copy(source.at[pl.ds(start, stop - start)], piece, sem)
    copy.start()
    return copy


def first_rows_kernel(
    tokens, cotangent, routes, next_routes, prev_routes, _, far, raw, normed, t1, cot, piece, sem
):
    copy = copy_rows(far, 0, FIRST, piece, sem)
    values = pick(select_of(routes[0]), [tokens])
    raw[...] = values.astype(BF16)
    normed[...] = (values * inv_rms_of(values)).astype(BF16)
    cot[...] = pick(select_of(prev_routes[0]), [cotangent]).astype(BF16)
    t1[...] = pick(select_of(next_routes[0]), [tokens]).astype(BF16)
    copy.wait()


def update0_kernel(n, *refs):
    parts, (raw, routes, gates, next_routes, t1) = refs[:n], refs[n : n + 5]
    upd, onward = refs[n + 7 :]
    select = select_of(routes[0])
    weight = slot_gates(select, routes[0], gates[0])
    fresh = (raw[...].astype(F32) + weight * summed(parts)).astype(BF16)
    onward[...] = merged(select_of(next_routes[0]), select, fresh, t1[...].astype(F32))
    upd[...] = fresh


def update1_kernel(n, *refs):
    parts, (h, routes, gates, upd) = refs[:n], refs[n:]
    select = select_of(routes[1])
    weight = slot_gates(select, routes[1], gates[1])
    upd[...] = (h[...].astype(F32) + weight * summed(parts)).astype(BF16)


def enter1_kernel(h, cot, routes, gates, cotangent, out, piece, sem):
    copy = copy_rows(cotangent, FIRST, cotangent.shape[0], piece, sem)
    values = h[...].astype(F32)
    out[:PACKED] = (values * inv_rms_of(values)).astype(BF16)
    weight = slot_gates(select_of(routes[1]), routes[1], gates[1])
    out[PACKED:] = (weight * cot[...].astype(F32)).astype(BF16)
    copy.wait()


def state_grad(parts, h, c):
    total = summed(parts)
    values = h.astype(F32)
    inv = inv_rms_of(values)
    inner = mean_of(total * values)
    return (c.astype(F32) + inv * total - inv * inv * inv * values * inner).astype(BF16)


def grad1_kernel(n, *refs):
    parts, (h, cot, upd) = refs[:n], refs[n:]
    upd[...] = state_grad(parts, h[...], cot[...])


def enter0_kernel(
    upd1, next_routes, routes, gates, bulk_a, bulk_b, tokens, _, __, c0, out, piece, sem
):
    copy = copy_rows(tokens, 0, tokens.shape[0], piece, sem)
    select = select_of(routes[0])
    old = pick(select, [bulk_a, bulk_b])
    rows = merged(select, select_of(next_routes[0]), upd1[...], old)
    c0[...] = rows
    out[...] = (slot_gates(select, routes[0], gates[0]) * rows.astype(F32)).astype(BF16)
    copy.wait()


def finish_grad_kernel(n, *refs):
    parts, (h, c, routes, upd1, next_routes, bulk_a, bulk_b, out) = refs[:n], refs[n:]
    fresh = state_grad(parts, h[...], c[...])
    place_rows(
        [bulk_a, bulk_b], select_of(next_routes[0]), upd1[...], select_of(routes[0]), fresh, out
    )


def finish_state_kernel(bulk, upd0, prev2_routes, upd1, prev_routes, out):
    place_rows(
        [bulk],
        select_of(prev2_routes[0]),
        upd0[...],
        select_of(prev_routes[0]),
        upd1[...],
        out,
    )


def silu_grads(pre_gate, pre_up, grad_act):
    sig = jax.nn.sigmoid(pre_gate)
    grad_gate = (grad_act * pre_up * sig * (1.0 + pre_gate * (1.0 - sig))).astype(BF16)
    grad_up = (grad_act * (pre_gate * sig)).astype(BF16)
    return grad_gate, grad_up


def weight_copies(gate, up, down, gate_v, up_v, down_v, sems):
    out = []
    step = gate.shape[0] // PACK
    for c in range(PACK):
        r = pl.ds(c * step, step)
        out.append(
            (
                pltpu.make_async_copy(gate.at[r], gate_v.at[r], sems.at[0, c]),
                pltpu.make_async_copy(up.at[r], up_v.at[r], sems.at[1, c]),
                pltpu.make_async_copy(down.at[:, r], down_v.at[:, r], sems.at[2, c]),
            )
        )
    return out


def gather_rows(blocks, first, unpacked, whole32, whole):
    width = whole.shape[1]
    used = len(blocks) * CAP
    if used < whole.shape[0]:
        whole32[used:] = jnp.zeros((whole.shape[0] - used, width), F32)
    for i, b in enumerate(blocks):
        unpacked[i] = b[first : first + PACKED].astype(F32)
        for c in range(PACK):
            whole32[i * CAP : (i + 1) * CAP, columns(c, width)] = unpacked[
                i, c * CAP : (c + 1) * CAP
            ]
    whole[...] = whole32[...].astype(BF16)


def spread_rows(value, c, n, held, unpacked):
    held[...] = value
    for i in range(n):
        unpacked[i, c * CAP : (c + 1) * CAP] = held[i * CAP : (i + 1) * CAP]


def forward_kernel(n, *refs):
    blocks, (gate, up, down, _) = refs[:n], refs[n : n + 4]
    x, pre_gate, pre_up, act = refs[n + 4 : n + 8]
    parts = refs[n + 8 : 2 * n + 8]
    gate_v, up_v, down_v, sems, unpacked, whole32, held = refs[2 * n + 8 :]
    copies = weight_copies(gate, up, down, gate_v, up_v, down_v, sems)
    for cg, cu, _ in copies:
        cg.start()
        cu.start()
    for _, _, cd in copies:
        cd.start()
    gather_rows(blocks, 0, unpacked, whole32, x)
    acc_g = jnp.zeros(pre_gate.shape, F32)
    acc_u = jnp.zeros(pre_up.shape, F32)
    width = gate.shape[0]
    for c, (cg, cu, _) in enumerate(copies):
        k = columns(c, width)
        cg.wait()
        acc_g = acc_g + dot(x[:, k], gate_v[k])
        cu.wait()
        acc_u = acc_u + dot(x[:, k], up_v[k])
    pre_gate[...] = acc_g
    pre_up[...] = acc_u
    activated = (acc_g * jax.nn.sigmoid(acc_g) * acc_u).astype(BF16)
    act[...] = activated
    for c, (_, _, cd) in enumerate(copies):
        cd.wait()
        spread_rows(dot(activated, down_v[:, columns(c, width)]), c, n, held.at[c], unpacked)
    for i, p in enumerate(parts):
        p[...] = unpacked[i].astype(BF16)


def down_kernel(n, act, down, _, *refs):
    parts, (unpacked, held) = refs[:n], refs[n:]
    hidden, width = down.shape
    for c in range(PACK):
        value = dot(act[:, width + hidden :], down[:, columns(c, width)])
        spread_rows(value, c, n, held.at[c], unpacked)
    for i, p in enumerate(parts):
        p[...] = unpacked[i].astype(BF16)


def back_rows(gg, gu, gate_v, up_v, held, unpacked, parts):
    n = len(parts)
    for c in range(PACK):
        k = columns(c, gate_v.shape[0])
        value = dot(gg, gate_v[k], 1, 1) + dot(gu, up_v[k], 1, 1)
        spread_rows(value, c, n, held.at[c], unpacked)
    for i, p in enumerate(parts):
        p[...] = unpacked[i].astype(BF16)


def tick1_kernel(n, *refs):
    blocks, (act0, gate, up, down, _) = refs[:n], refs[n : n + 5]
    x_act, g_grad = refs[n + 5 : n + 7]
    parts = refs[n + 7 : 2 * n + 7]
    gate_v, up_v, down_v, sems, unpacked, whole32, held, x, g = refs[2 * n + 7 :]
    copies = weight_copies(gate, up, down, gate_v, up_v, down_v, sems)
    for three in copies:
        for c in three:
            c.start()
    gather_rows(blocks, 0, unpacked, whole32.at[0], x)
    gather_rows(blocks, PACKED, unpacked, whole32.at[1], g)
    width, hidden = gate.shape
    x_act[:, :width] = x[...]
    x_act[:, width : width + hidden] = act0[...]
    g_grad[:, :width] = g[...]
    acc_g = jnp.zeros(act0.shape, F32)
    acc_u = jnp.zeros(act0.shape, F32)
    acc_a = jnp.zeros(act0.shape, F32)
    for c, (cg, cu, cd) in enumerate(copies):
        k = columns(c, width)
        cg.wait()
        acc_g = acc_g + dot(x[:, k], gate_v[k])
        cu.wait()
        acc_u = acc_u + dot(x[:, k], up_v[k])
        cd.wait()
        acc_a = acc_a + dot(g[:, k], down_v[:, k], 1, 1)
    gg, gu = silu_grads(acc_g, acc_u, acc_a)
    x_act[:, width + hidden :] = (acc_g * jax.nn.sigmoid(acc_g) * acc_u).astype(BF16)
    g_grad[:, width : width + hidden] = gg
    g_grad[:, width + hidden :] = gu
    back_rows(gg, gu, gate_v, up_v, held, unpacked, parts)


def tick0_kernel(n, *refs):
    blocks, (pre_gate, pre_up, gate, up, down) = refs[:n], refs[n : n + 5]
    (g_grad,) = refs[n + 5 : n + 6]
    parts = refs[n + 6 : 2 * n + 6]
    gate_v, up_v, down_v, sems, unpacked, whole32, held, g = refs[2 * n + 6 :]
    copies = weight_copies(gate, up, down, gate_v, up_v, down_v, sems)
    for _, _, cd in copies:
        cd.start()
    for cg, cu, _ in copies:
        cg.start()
        cu.start()
    gather_rows(blocks, 0, unpacked, whole32, g)
    width, hidden = gate.shape
    g_grad[:, :width] = g[...]
    acc_a = jnp.zeros(pre_gate.shape, F32)
    for c, (_, _, cd) in enumerate(copies):
        k = columns(c, width)
        cd.wait()
        acc_a = acc_a + dot(g[:, k], down_v[:, k], 1, 1)
    gg, gu = silu_grads(pre_gate[...], pre_up[...], acc_a)
    g_grad[:, width : width + hidden] = gg
    g_grad[:, width + hidden :] = gu
    for cg, cu, _ in copies:
        cg.wait()
        cu.wait()
    back_rows(gg, gu, gate_v, up_v, held, unpacked, parts)


def whole_of(blocks):
    return jnp.concatenate(blocks, axis=0)


def input_grad_kernel(m, *refs):
    x0, x1, gates0, ups0, gates1, ups1 = (refs[i * m : (i + 1) * m] for i in range(6))
    gate_out, up_out = refs[6 * m :]
    x_t = whole_of([b[...] for b in x0 + x1]).T
    gate_out[...] = dot(x_t, whole_of([b[...] for b in gates0 + gates1])).astype(BF16)
    up_out[...] = dot(x_t, whole_of([b[...] for b in ups0 + ups1])).astype(BF16)


def down_grad_kernel(m, *refs):
    g0, g1, act0, act1 = (refs[i * m : (i + 1) * m] for i in range(4))
    (down_out,) = refs[4 * m :]
    act = whole_of([b[...] for b in act0 + act1])
    down_out[...] = dot(act, whole_of([b[...] for b in g0 + g1]), 0, 0).astype(BF16)


def grads_call(kernel, wide, fixed, outs, out_block, out_index, hidden):
    rows = wide[0].shape[0]
    width = max(max(s) for s in outs)
    step = width // PACK
    return pl.pallas_call(
        kernel,
        grid=(PACK,),
        out_shape=[jax.ShapeDtypeStruct(s, BF16) for s in outs],
        in_specs=[pl.BlockSpec((rows, step), lambda c: (0, c)) for _ in wide]
        + [
            pl.BlockSpec((rows, hidden), functools.partial(lambda i, c: (0, i), at))
            for _, at in fixed
        ],
        out_specs=[pl.BlockSpec(out_block, out_index)] * len(outs),
        compiler_params=pltpu.CompilerParams(vmem_limit_bytes=VMEM_SMALL),
        cost_estimate=pl.CostEstimate(flops=0, bytes_accessed=COST_BYTES, transcendentals=0),
    )(*wide, *(a for a, _ in fixed))


def input_grads(x0, x_act1, g_grad0, g_grad1, width, hidden):
    first = width // hidden
    return grads_call(
        functools.partial(input_grad_kernel, len(x0)),
        x0 + x_act1,
        [(a, first) for a in g_grad0]
        + [(a, first + 1) for a in g_grad0]
        + [(a, first) for a in g_grad1]
        + [(a, first + 1) for a in g_grad1],
        [(width, hidden)] * 2,
        (width // PACK, hidden),
        lambda c: (c, 0),
        hidden,
    )


def down_grads(g_grad0, g_grad1, x_act1, width, hidden):
    first = width // hidden
    return grads_call(
        functools.partial(down_grad_kernel, len(g_grad0)),
        g_grad0 + g_grad1,
        [(a, first) for a in x_act1] + [(a, first + 1) for a in x_act1],
        [(hidden, width)],
        (hidden, width // PACK),
        lambda c: (0, c),
        hidden,
    )


def from_group(block):
    n = lax.axis_size("expert")
    return [block] + [shifted(block, "expert", k) for k in range(1, n)]


def to_group(blocks):
    return [blocks[0]] + [shifted(b, "expert", -k) for k, b in enumerate(blocks) if k]


def copies_of(block):
    n = lax.axis_size("dp")
    return [block] + [shifted(block, "dp", k) for k in range(1, n)]


def shards(tokens, cotangent, w_gate, w_up, w_down, routes, gates):
    gate, up, down = w_gate[0], w_up[0], w_down[0]
    width, hidden = gate.shape
    step = width // PACK
    own = tokens.shape[0]
    n = lax.axis_size("expert")
    rows = -(-n * CAP // 16) * 16
    routes = jnp.transpose(routes, (0, 2, 1))
    gates = jnp.transpose(gates, (0, 2, 1))
    one = ((PACKED, step), BF16)
    part = functools.partial
    scratch = [
        pltpu.VMEM((width, hidden), BF16),
        pltpu.VMEM((width, hidden), BF16),
        pltpu.VMEM((hidden, width), BF16),
        pltpu.SemaphoreType.DMA((3, PACK)),
        pltpu.VMEM((n, PACKED, step), F32),
        pltpu.VMEM((rows, width), F32),
        pltpu.VMEM((PACK, rows, step), F32),
    ]
    both = pltpu.VMEM((rows, width), BF16)
    tick1_scratch = [*scratch[:5], pltpu.VMEM((2, rows, width), F32), scratch[6], both, both]
    wide = ((rows, width + 2 * hidden), BF16)

    next_routes = shifted(routes[1:], "section", -1)
    prev_routes = shifted(routes[1:], "section", 1)
    prev2_routes = shifted(routes[:1], "section", 2)

    raw0, normed0, t1, cot1, piece = call(
        first_rows_kernel,
        [one, one, one, one, ((FIRST, width), BF16)],
        [tokens, cotangent, routes, next_routes, prev_routes, prev2_routes, cotangent],
        any_args=(5, 6),
        any_outs=(4,),
        scratch=[pltpu.SemaphoreType.DMA],
    )
    cot_a = shifted(piece, "section", -2)
    cot1 = shifted(cot1, "section", -1)
    blocks = from_group(normed0)
    x0, pre_gate0, pre_up0, act0, *parts = call(
        part(forward_kernel, n),
        [((rows, width), BF16), ((rows, hidden), F32), ((rows, hidden), F32)]
        + [((rows, hidden), BF16)]
        + [one] * n,
        [*blocks, gate, up, down, t1],
        any_args=(n, n + 1, n + 2, n + 3),
        scratch=scratch,
        vmem=VMEM_BIG,
    )
    parts = to_group(parts)
    upd0, h1 = call(
        part(update0_kernel, n),
        [one, one],
        [*parts, raw0, routes, gates, next_routes, t1, cot_a, cot1],
        any_args=(n + 5, n + 6),
    )
    h1 = shifted(h1, "section", 1)
    upd0 = shifted(upd0, "section", 2)

    enter1, piece = call(
        enter1_kernel,
        [((2 * PACKED, step), BF16), ((own - FIRST, width), BF16)],
        [h1, cot1, routes, gates, cotangent],
        any_args=(4,),
        any_outs=(1,),
        scratch=[pltpu.SemaphoreType.DMA],
    )
    cot_b = shifted(piece, "section", -2)
    blocks = from_group(enter1)
    x0_all = copies_of(x0)
    x_act1, g_grad1, *parts = call(
        part(tick1_kernel, n),
        [wide, wide] + [one] * n,
        [*blocks, act0, gate, up, down, x0_all[-1]],
        any_args=(n + 1, n + 2, n + 3, n + 4),
        scratch=tick1_scratch,
        vmem=VMEM_BIG,
    )
    parts = to_group(parts)
    (upd1,) = call(part(grad1_kernel, n), [one], [*parts, h1, cot1])
    outs = call(
        part(down_kernel, n),
        [one] * n,
        [x_act1, down, upd1],
        any_args=(2,),
        scratch=[scratch[4], scratch[6]],
        vmem=VMEM_BIG,
    )
    upd1 = shifted(upd1, "section", -1)
    x_act1_all, g_grad1_all = copies_of(x_act1), copies_of(g_grad1)

    c0, enter0, piece = call(
        enter0_kernel,
        [one, one, (tokens.shape, BF16)],
        [upd1, next_routes, routes, gates, cot_a, cot_b, tokens, outs[0], x_act1_all[-1]],
        any_args=(6, 7, 8),
        any_outs=(2,),
        scratch=[pltpu.SemaphoreType.DMA],
    )
    tok = shifted(piece, "section", 2)
    blocks = from_group(enter0)
    g_grad0, *parts = call(
        part(tick0_kernel, n),
        [wide] + [one] * n,
        [*blocks, pre_gate0, pre_up0, gate, up, down],
        any_args=(n + 2, n + 3, n + 4),
        scratch=scratch + [both],
        vmem=VMEM_BIG,
    )
    parts = to_group(parts)
    g_grad0_all = copies_of(g_grad0)
    (grad,) = call(
        part(finish_grad_kernel, n),
        [(tokens.shape, BF16)],
        [*parts, raw0, c0, routes, upd1, next_routes, cot_a, cot_b],
    )
    outs = to_group(outs)
    (last1,) = call(part(update1_kernel, n), [one], [*outs, h1, routes, gates])
    last1 = shifted(last1, "section", 1)
    gate_out, up_out = input_grads(x0_all, x_act1_all, g_grad0_all, g_grad1_all, width, hidden)
    (down_out,) = down_grads(g_grad0_all, g_grad1_all, x_act1_all, width, hidden)
    (state,) = call(
        finish_state_kernel,
        [(tokens.shape, BF16)],
        [tok, upd0, prev2_routes, last1, prev_routes],
    )
    return (grad, state, gate_out[None], up_out[None], down_out[None])


def solution(mesh):
    rows = P(("section", "expert", "dp"), None)
    slots = P(None, ("section", "expert", "dp"), None)
    cols = P("section", None, "expert")
    hidden = P("section", "expert", None)
    return jax.shard_map(
        shards,
        mesh=mesh,
        in_specs=(rows, rows, cols, cols, hidden, slots, slots),
        out_specs=(rows, rows, cols, cols, hidden),
        check_vma=False,
    )
```

```python
import functools

import jax
import jax.numpy as jnp
from jax import lax
from jax.experimental import pallas as pl
from jax.experimental.pallas import tpu as pltpu
from jax.sharding import PartitionSpec as P

CAP = 10
PACK = 8
PACKED = CAP * PACK
COT_PIECES = ((0, 32, 0, 8), (32, 64, 0, 8), (64, 128, 0, 3), (64, 128, 3, 8))
TOK_PIECES = ((0, 96, 0, 8), (96, 128, 0, 8))
EPSILON = 1e-06
F32 = jnp.float32
BF16 = jnp.bfloat16
VMEM_BIG = 48 * 1024 * 1024
VMEM_SMALL = 24 * 1024 * 1024
COST_BYTES = 1024


def shifted(block, axis, distance):
    size = lax.axis_size(axis)
    return lax.ppermute(block, axis, [((i - distance) % size, i) for i in range(size)])


def dot(a, b, ca=1, cb=0):
    return lax.dot_general(a, b, (((ca,), (cb,)), ((), ())), preferred_element_type=F32)


def call(
    kernel, outs, args, *, any_args=(), any_outs=(), scratch=(), vmem=VMEM_SMALL
):
    outs = [jax.ShapeDtypeStruct(s, d) for s, d in outs]
    anywhere = pl.BlockSpec(memory_space=pl.ANY)
    near = pl.BlockSpec(memory_space=pltpu.VMEM)
    return pl.pallas_call(
        kernel,
        out_shape=outs,
        in_specs=[anywhere if i in any_args else near for i in range(len(args))],
        out_specs=[anywhere if i in any_outs else near for i in range(len(outs))],
        scratch_shapes=list(scratch),
        compiler_params=pltpu.CompilerParams(vmem_limit_bytes=vmem),
        cost_estimate=pl.CostEstimate(flops=0, bytes_accessed=COST_BYTES, transcendentals=0),
    )(*args)


def packed_index(shape, dim):
    place = lax.broadcasted_iota(jnp.int32, shape, dim).astype(F32)
    chunk = jnp.floor((place + 0.5) * (1.0 / CAP))
    return place - CAP * chunk, chunk


def select_of(routes):
    hits = (routes == 0).astype(F32)
    marked = jnp.sum(hits, axis=0, keepdims=True)
    rows = routes.shape[1]
    before = lax.broadcasted_iota(jnp.int32, (rows, rows), 0) < lax.broadcasted_iota(
        jnp.int32, (rows, rows), 1
    )
    wide = jnp.broadcast_to(marked, (PACKED, rows))
    places = dot(wide.astype(BF16), before.astype(F32).astype(BF16))
    slot, _ = packed_index((PACKED, rows), 0)
    return jnp.where((places == slot) & (wide > 0.5), 1.0, 0.0)


def slot_gates(select, routes, gates):
    weights = jnp.sum(jnp.where(routes == 0, gates, 0.0), axis=0, keepdims=True)
    return jnp.sum(select * weights, axis=1, keepdims=True)


def chunk_of(select, c):
    _, chunk = packed_index(select.shape, 0)
    return jnp.where(chunk == c, select, 0.0).astype(BF16)


def columns(c, width):
    return slice(c * (width // PACK), (c + 1) * (width // PACK))


def pick(select, pieces):
    total = None
    for block, (r0, r1, c0, c1) in pieces:
        width = block.shape[1] // (c1 - c0)
        for c in range(c0, c1):
            columns_here = slice((c - c0) * width, (c - c0 + 1) * width)
            part = dot(chunk_of(select[:, r0:r1], c), block[:, columns_here])
            total = part if total is None else total + part
    return total


def whole_block(block):
    return [(block, (0, block.shape[0], 0, PACK))]


def over_chunks(row_sums):
    slot_r, _ = packed_index((PACKED, PACKED), 0)
    slot_c, _ = packed_index((PACKED, PACKED), 1)
    same = jnp.where(slot_r == slot_c, 1.0, 0.0)
    wide = jnp.broadcast_to(row_sums, (PACKED, 128))
    return jnp.dot(
        same, wide, precision=lax.Precision.HIGHEST, preferred_element_type=F32
    )[:, :1]


def mean_of(values):
    return over_chunks(jnp.sum(values, axis=-1, keepdims=True)) * (1.0 / (PACK * values.shape[1]))


def inv_rms_of(values):
    return lax.rsqrt(mean_of(values * values) + EPSILON)


def merged(select_to, select_from, fresh, old):
    same = dot(select_to.astype(BF16), select_from.astype(BF16), 1, 1)
    _, chunk_r = packed_index(same.shape, 0)
    _, chunk_c = packed_index(same.shape, 1)
    same = jnp.where(chunk_r == chunk_c, same, 0.0)
    taken = jnp.sum(same, axis=1, keepdims=True)
    return jnp.where(taken > 0.5, dot(same.astype(BF16), fresh), old).astype(BF16)


def summed(parts):
    total = parts[0][...].astype(F32)
    for p in parts[1:]:
        total = total + p[...].astype(F32)
    return total


def place_rows(pieces, first, rows1, second, rows2, out):
    ones = jnp.ones((PACKED, 128), BF16)
    hit1 = dot(chunk_of(first, 0), ones, 0, 0)[:, :1] > 0.5
    hit2 = dot(chunk_of(second, 0), ones, 0, 0)[:, :1] > 0.5
    width = out.shape[1] // PACK
    for c in range(PACK):
        new1 = dot(chunk_of(first, c), rows1, 0, 0)
        new2 = dot(chunk_of(second, c), rows2, 0, 0)
        for block, (r0, r1, c0, c1) in pieces:
            if c0 <= c < c1:
                old = block[:, (c - c0) * width : (c - c0 + 1) * width].astype(F32)
                value = jnp.where(hit1[r0:r1], new1[r0:r1], old)
                value = jnp.where(hit2[r0:r1], new2[r0:r1], value)
                out[r0:r1, columns(c, out.shape[1])] = value.astype(BF16)


def piece_copy(source, place, piece, sem):
    r0, r1, c0, c1 = place
    width = source.shape[1] // PACK
    block = source.at[pl.ds(r0, r1 - r0), pl.ds(c0 * width, (c1 - c0) * width)]
    copy = pltpu.make_async_copy(block, piece, sem)
    copy.start()
    return copy


def first_rows_kernel(tokens, routes, far, raw, normed, piece, sem):
    copy = piece_copy(far, COT_PIECES[0], piece, sem)
    values = pick(select_of(routes[0]), whole_block(tokens))
    raw[...] = values.astype(BF16)
    normed[...] = (values * inv_rms_of(values)).astype(BF16)
    copy.wait()


def other_rows_kernel(
    tokens, cotangent, next_routes, prev_routes, _, __, ___, far, t1, cot, piece, sem
):
    copy = piece_copy(far, COT_PIECES[1], piece, sem)
    cot[...] = pick(select_of(prev_routes[0]), whole_block(cotangent)).astype(BF16)
    t1[...] = pick(select_of(next_routes[0]), whole_block(tokens)).astype(BF16)
    copy.wait()


def update0_kernel(n, *refs):
    parts, (raw, routes, gates, next_routes, t1, cotangent) = refs[:n], refs[n : n + 6]
    upd, onward, piece, sem = refs[n + 6 :]
    copy = piece_copy(cotangent, COT_PIECES[2], piece, sem)
    select = select_of(routes[0])
    weight = slot_gates(select, routes[0], gates[0])
    fresh = (raw[...].astype(F32) + weight * summed(parts)).astype(BF16)
    onward[...] = merged(select_of(next_routes[0]), select, fresh, t1[...].astype(F32))
    upd[...] = fresh
    copy.wait()


def update1_kernel(n, *refs):
    parts, (h, routes, gates, upd) = refs[:n], refs[n:]
    select = select_of(routes[1])
    weight = slot_gates(select, routes[1], gates[1])
    upd[...] = (h[...].astype(F32) + weight * summed(parts)).astype(BF16)


def enter1_kernel(h, cot, routes, gates, cotangent, _, out, piece, sem):
    copy = piece_copy(cotangent, COT_PIECES[3], piece, sem)
    values = h[...].astype(F32)
    out[:PACKED] = (values * inv_rms_of(values)).astype(BF16)
    weight = slot_gates(select_of(routes[1]), routes[1], gates[1])
    out[PACKED:] = (weight * cot[...].astype(F32)).astype(BF16)
    copy.wait()


def state_grad(parts, h, c):
    total = summed(parts)
    values = h.astype(F32)
    inv = inv_rms_of(values)
    inner = mean_of(total * values)
    return (c.astype(F32) + inv * total - inv * inv * inv * values * inner).astype(BF16)


def grad1_kernel(n, *refs):
    parts, (h, cot, tokens, upd, piece, sem) = refs[:n], refs[n:]
    copy = piece_copy(tokens, TOK_PIECES[0], piece, sem)
    upd[...] = state_grad(parts, h[...], cot[...])
    copy.wait()


def enter0_kernel(m, upd1, next_routes, routes, gates, *refs):
    bulk, (tokens, _, c0, out, piece, sem) = refs[:m], refs[m:]
    copy = piece_copy(tokens, TOK_PIECES[1], piece, sem)
    select = select_of(routes[0])
    old = pick(select, list(zip(bulk, COT_PIECES)))
    rows = merged(select, select_of(next_routes[0]), upd1[...], old)
    c0[...] = rows
    out[...] = (slot_gates(select, routes[0], gates[0]) * rows.astype(F32)).astype(BF16)
    copy.wait()


def finish_grad_kernel(n, *refs):
    parts, (h, c, routes, upd1, next_routes, *bulk, out) = refs[:n], refs[n:]
    fresh = state_grad(parts, h[...], c[...])
    place_rows(
        list(zip(bulk, COT_PIECES)),
        select_of(next_routes[0]),
        upd1[...],
        select_of(routes[0]),
        fresh,
        out,
    )


def finish_state_kernel(first, rest, upd0, prev2_routes, upd1, prev_routes, out):
    place_rows(
        list(zip([first, rest], TOK_PIECES)),
        select_of(prev2_routes[0]),
        upd0[...],
        select_of(prev_routes[0]),
        upd1[...],
        out,
    )


def silu_grads(pre_gate, pre_up, grad_act):
    sig = jax.nn.sigmoid(pre_gate)
    grad_gate = (grad_act * pre_up * sig * (1.0 + pre_gate * (1.0 - sig))).astype(BF16)
    grad_up = (grad_act * (pre_gate * sig)).astype(BF16)
    return grad_gate, grad_up


def weight_copies(gate, up, down, gate_v, up_v, down_v, sems):
    out = []
    step = gate.shape[0] // PACK
    for c in range(PACK):
        r = pl.ds(c * step, step)
        out.append(
            (
                pltpu.make_async_copy(gate.at[r], gate_v.at[r], sems.at[0, c]),
                pltpu.make_async_copy(up.at[r], up_v.at[r], sems.at[1, c]),
                pltpu.make_async_copy(down.at[:, r], down_v.at[:, r], sems.at[2, c]),
            )
        )
    return out


def gather_rows(blocks, first, unpacked, whole32, whole):
    width = whole.shape[1]
    used = len(blocks) * CAP
    if used < whole.shape[0]:
        whole32[used:] = jnp.zeros((whole.shape[0] - used, width), F32)
    for i, b in enumerate(blocks):
        unpacked[i] = b[first : first + PACKED].astype(F32)
        for c in range(PACK):
            whole32[i * CAP : (i + 1) * CAP, columns(c, width)] = unpacked[
                i, c * CAP : (c + 1) * CAP
            ]
    whole[...] = whole32[...].astype(BF16)


def spread_rows(value, c, n, held, unpacked):
    held[...] = value
    for i in range(n):
        unpacked[i, c * CAP : (c + 1) * CAP] = held[i * CAP : (i + 1) * CAP]


def forward_kernel(n, *refs):
    blocks, (gate, up, down) = refs[:n], refs[n : n + 3]
    x, pre_gate, pre_up, act = refs[n + 3 : n + 7]
    parts = refs[n + 7 : 2 * n + 7]
    gate_v, up_v, down_v, sems, unpacked, whole32, held = refs[2 * n + 7 :]
    copies = weight_copies(gate, up, down, gate_v, up_v, down_v, sems)
    for cg, cu, _ in copies:
        cg.start()
        cu.start()
    for _, _, cd in copies:
        cd.start()
    gather_rows(blocks, 0, unpacked, whole32, x)
    acc_g = jnp.zeros(pre_gate.shape, F32)
    acc_u = jnp.zeros(pre_up.shape, F32)
    width = gate.shape[0]
    for c, (cg, cu, _) in enumerate(copies):
        k = columns(c, width)
        cg.wait()
        acc_g = acc_g + dot(x[:, k], gate_v[k])
        cu.wait()
        acc_u = acc_u + dot(x[:, k], up_v[k])
    pre_gate[...] = acc_g
    pre_up[...] = acc_u
    activated = (acc_g * jax.nn.sigmoid(acc_g) * acc_u).astype(BF16)
    act[...] = activated
    for c, (_, _, cd) in enumerate(copies):
        cd.wait()
        spread_rows(dot(activated, down_v[:, columns(c, width)]), c, n, held.at[c], unpacked)
    for i, p in enumerate(parts):
        p[...] = unpacked[i].astype(BF16)


def down_kernel(n, act, down, _, *refs):
    parts, (unpacked, held) = refs[:n], refs[n:]
    hidden, width = down.shape
    for c in range(PACK):
        value = dot(act[:, 2 * width + hidden :], down[:, columns(c, width)])
        spread_rows(value, c, n, held.at[c], unpacked)
    for i, p in enumerate(parts):
        p[...] = unpacked[i].astype(BF16)


def back_rows(gg, gu, gate_v, up_v, held, unpacked, parts):
    n = len(parts)
    for c in range(PACK):
        k = columns(c, gate_v.shape[0])
        value = dot(gg, gate_v[k], 1, 1) + dot(gu, up_v[k], 1, 1)
        spread_rows(value, c, n, held.at[c], unpacked)
    for i, p in enumerate(parts):
        p[...] = unpacked[i].astype(BF16)


def tick1_kernel(n, *refs):
    blocks, (x0, act0, gate, up, down, _) = refs[:n], refs[n : n + 6]
    x_act, g_grad = refs[n + 6 : n + 8]
    parts = refs[n + 8 : 2 * n + 8]
    gate_v, up_v, down_v, sems, unpacked, whole32, held, x, g = refs[2 * n + 8 :]
    copies = weight_copies(gate, up, down, gate_v, up_v, down_v, sems)
    for three in copies:
        for c in three:
            c.start()
    gather_rows(blocks, 0, unpacked, whole32.at[0], x)
    gather_rows(blocks, PACKED, unpacked, whole32.at[1], g)
    width, hidden = gate.shape
    x_act[:, :width] = x0[...]
    x_act[:, width : 2 * width] = x[...]
    x_act[:, 2 * width : 2 * width + hidden] = act0[...]
    g_grad[:, :width] = g[...]
    acc_g = jnp.zeros(act0.shape, F32)
    acc_u = jnp.zeros(act0.shape, F32)
    acc_a = jnp.zeros(act0.shape, F32)
    for c, (cg, cu, cd) in enumerate(copies):
        k = columns(c, width)
        cg.wait()
        acc_g = acc_g + dot(x[:, k], gate_v[k])
        cu.wait()
        acc_u = acc_u + dot(x[:, k], up_v[k])
        cd.wait()
        acc_a = acc_a + dot(g[:, k], down_v[:, k], 1, 1)
    gg, gu = silu_grads(acc_g, acc_u, acc_a)
    x_act[:, 2 * width + hidden :] = (acc_g * jax.nn.sigmoid(acc_g) * acc_u).astype(BF16)
    g_grad[:, width : width + hidden] = gg
    g_grad[:, width + hidden :] = gu
    back_rows(gg, gu, gate_v, up_v, held, unpacked, parts)


def tick0_kernel(n, *refs):
    blocks, (pre_gate, pre_up, gate, up, down) = refs[:n], refs[n : n + 5]
    (g_grad,) = refs[n + 5 : n + 6]
    parts = refs[n + 6 : 2 * n + 6]
    gate_v, up_v, down_v, sems, unpacked, whole32, held, g = refs[2 * n + 6 :]
    copies = weight_copies(gate, up, down, gate_v, up_v, down_v, sems)
    for _, _, cd in copies:
        cd.start()
    for cg, cu, _ in copies:
        cg.start()
        cu.start()
    gather_rows(blocks, 0, unpacked, whole32, g)
    width, hidden = gate.shape
    g_grad[:, :width] = g[...]
    acc_a = jnp.zeros(pre_gate.shape, F32)
    for c, (_, _, cd) in enumerate(copies):
        k = columns(c, width)
        cd.wait()
        acc_a = acc_a + dot(g[:, k], down_v[:, k], 1, 1)
    gg, gu = silu_grads(pre_gate[...], pre_up[...], acc_a)
    g_grad[:, width : width + hidden] = gg
    g_grad[:, width + hidden :] = gu
    for cg, cu, _ in copies:
        cg.wait()
        cu.wait()
    back_rows(gg, gu, gate_v, up_v, held, unpacked, parts)


def whole_of(blocks):
    return jnp.concatenate(blocks, axis=0)


def input_grad_kernel(m, *refs):
    x0, x1, gates0, ups0, gates1, ups1 = (refs[i * m : (i + 1) * m] for i in range(6))
    gate_out, up_out = refs[6 * m :]
    x_t = whole_of([b[...] for b in x0 + x1]).T
    gate_out[...] = dot(x_t, whole_of([b[...] for b in gates0 + gates1])).astype(BF16)
    up_out[...] = dot(x_t, whole_of([b[...] for b in ups0 + ups1])).astype(BF16)


def down_grad_kernel(m, *refs):
    g0, g1, act0, act1 = (refs[i * m : (i + 1) * m] for i in range(4))
    (down_out,) = refs[4 * m :]
    act = whole_of([b[...] for b in act0 + act1])
    down_out[...] = dot(act, whole_of([b[...] for b in g0 + g1]), 0, 0).astype(BF16)


def grads_call(kernel, wide, fixed, outs, out_block, out_index, hidden):
    rows = wide[0][0].shape[0]
    step = max(max(s) for s in outs) // PACK

    def chunked(at):
        return pl.BlockSpec((rows, step), lambda c: (0, at + c))

    def constant(at):
        return pl.BlockSpec((rows, hidden), lambda c: (0, at))

    return pl.pallas_call(
        kernel,
        grid=(PACK,),
        out_shape=[jax.ShapeDtypeStruct(s, BF16) for s in outs],
        in_specs=[chunked(at) for _, at in wide] + [constant(at) for _, at in fixed],
        out_specs=[pl.BlockSpec(out_block, out_index)] * len(outs),
        compiler_params=pltpu.CompilerParams(vmem_limit_bytes=VMEM_SMALL),
        cost_estimate=pl.CostEstimate(flops=0, bytes_accessed=COST_BYTES, transcendentals=0),
    )(*(a for a, _ in wide), *(a for a, _ in fixed))


def input_grads(x_act, g_grad0, g_grad1, width, hidden):
    first = width // hidden
    return grads_call(
        functools.partial(input_grad_kernel, len(x_act)),
        [(a, 0) for a in x_act] + [(a, PACK) for a in x_act],
        [(a, first) for a in g_grad0]
        + [(a, first + 1) for a in g_grad0]
        + [(a, first) for a in g_grad1]
        + [(a, first + 1) for a in g_grad1],
        [(width, hidden)] * 2,
        (width // PACK, hidden),
        lambda c: (c, 0),
        hidden,
    )


def down_grads(g_grad0, g_grad1, x_act, width, hidden):
    first = 2 * width // hidden
    return grads_call(
        functools.partial(down_grad_kernel, len(g_grad0)),
        [(a, 0) for a in g_grad0 + g_grad1],
        [(a, first) for a in x_act] + [(a, first + 1) for a in x_act],
        [(hidden, width)],
        (hidden, width // PACK),
        lambda c: (0, c),
        hidden,
    )


def from_group(block):
    n = lax.axis_size("expert")
    return [block] + [shifted(block, "expert", k) for k in range(1, n)]


def to_group(blocks):
    return [blocks[0]] + [shifted(b, "expert", -k) for k, b in enumerate(blocks) if k]


def copies_of(block):
    n = lax.axis_size("dp")
    return [block] + [shifted(block, "dp", k) for k in range(1, n)]


def shards(tokens, cotangent, w_gate, w_up, w_down, routes, gates):
    gate, up, down = w_gate[0], w_up[0], w_down[0]
    width, hidden = gate.shape
    step = width // PACK
    n = lax.axis_size("expert")
    rows = -(-n * CAP // 16) * 16
    routes = jnp.transpose(routes, (0, 2, 1))
    gates = jnp.transpose(gates, (0, 2, 1))
    one = ((PACKED, step), BF16)
    part = functools.partial
    scratch = [
        pltpu.VMEM((width, hidden), BF16),
        pltpu.VMEM((width, hidden), BF16),
        pltpu.VMEM((hidden, width), BF16),
        pltpu.SemaphoreType.DMA((3, PACK)),
        pltpu.VMEM((n, PACKED, step), F32),
        pltpu.VMEM((rows, width), F32),
        pltpu.VMEM((PACK, rows, step), F32),
    ]
    both = pltpu.VMEM((rows, width), BF16)
    tick1_scratch = [*scratch[:5], pltpu.VMEM((2, rows, width), F32), scratch[6], both, both]
    wide = ((rows, width + 2 * hidden), BF16)

    next_routes = shifted(routes[1:], "section", -1)
    prev_routes = shifted(routes[1:], "section", 1)
    prev2_routes = shifted(routes[:1], "section", 2)

    def shape_of(place):
        r0, r1, c0, c1 = place
        return ((r1 - r0, (c1 - c0) * step), BF16)

    cot_shapes = [shape_of(place) for place in COT_PIECES]
    tok_shapes = [shape_of(place) for place in TOK_PIECES]
    dma = [pltpu.SemaphoreType.DMA]

    raw0, normed0, piece = call(
        first_rows_kernel,
        [one, one, cot_shapes[0]],
        [tokens, routes, cotangent],
        any_args=(2,),
        any_outs=(2,),
        scratch=dma,
    )
    cot_parts = [shifted(piece, "section", -2)]
    blocks = from_group(normed0)
    x0, pre_gate0, pre_up0, act0, *parts = call(
        part(forward_kernel, n),
        [((rows, width), BF16), ((rows, hidden), F32), ((rows, hidden), F32)]
        + [((rows, hidden), BF16)]
        + [one] * n,
        [*blocks, gate, up, down],
        any_args=(n, n + 1, n + 2),
        scratch=scratch,
        vmem=VMEM_BIG,
    )
    t1, cot1, piece = call(
        other_rows_kernel,
        [one, one, cot_shapes[1]],
        [tokens, cotangent, next_routes, prev_routes, prev2_routes, act0, cot_parts[0], cotangent],
        any_args=(4, 5, 6, 7),
        any_outs=(2,),
        scratch=dma,
    )
    cot1 = shifted(cot1, "section", -1)
    cot_parts.append(shifted(piece, "section", -2))
    parts = to_group(parts)
    upd0, h1, piece = call(
        part(update0_kernel, n),
        [one, one, cot_shapes[2]],
        [*parts, raw0, routes, gates, next_routes, t1, cotangent],
        any_args=(n + 5,),
        any_outs=(2,),
        scratch=dma,
    )
    h1 = shifted(h1, "section", 1)
    cot_parts.append(shifted(piece, "section", -2))
    upd0 = shifted(upd0, "section", 2)

    enter1, piece = call(
        enter1_kernel,
        [((2 * PACKED, step), BF16), cot_shapes[3]],
        [h1, cot1, routes, gates, cotangent, cot_parts[1]],
        any_args=(4, 5),
        any_outs=(1,),
        scratch=dma,
    )
    cot_parts.append(shifted(piece, "section", -2))
    blocks = from_group(enter1)
    x_act, g_grad1, *parts = call(
        part(tick1_kernel, n),
        [((rows, 2 * (width + hidden)), BF16), wide] + [one] * n,
        [*blocks, x0, act0, gate, up, down, cot_parts[2]],
        any_args=(n + 2, n + 3, n + 4, n + 5),
        scratch=tick1_scratch,
        vmem=VMEM_BIG,
    )
    parts = to_group(parts)
    upd1, piece = call(
        part(grad1_kernel, n),
        [one, tok_shapes[0]],
        [*parts, h1, cot1, tokens],
        any_args=(n + 2,),
        any_outs=(1,),
        scratch=dma,
    )
    upd1_here = upd1
    upd1 = shifted(upd1, "section", -1)
    tok_parts = [shifted(piece, "section", 2)]
    outs = call(
        part(down_kernel, n),
        [one] * n,
        [x_act, down, upd1_here],
        any_args=(2,),
        scratch=[scratch[4], scratch[6]],
        vmem=VMEM_BIG,
    )
    x_act_all, g_grad1_all = copies_of(x_act), copies_of(g_grad1)

    m = len(cot_parts)
    c0, enter0, piece = call(
        part(enter0_kernel, m),
        [one, one, tok_shapes[1]],
        [upd1, next_routes, routes, gates, *cot_parts, tokens, outs[0]],
        any_args=(m + 4, m + 5),
        any_outs=(2,),
        scratch=dma,
    )
    tok_parts.append(shifted(piece, "section", 2))
    blocks = from_group(enter0)
    g_grad0, *parts = call(
        part(tick0_kernel, n),
        [wide] + [one] * n,
        [*blocks, pre_gate0, pre_up0, gate, up, down],
        any_args=(n + 2, n + 3, n + 4),
        scratch=scratch + [both],
        vmem=VMEM_BIG,
    )
    parts = to_group(parts)
    g_grad0_all = copies_of(g_grad0)
    (grad,) = call(
        part(finish_grad_kernel, n),
        [(tokens.shape, BF16)],
        [*parts, raw0, c0, routes, upd1, next_routes, *cot_parts],
    )
    outs = to_group(outs)
    (last1,) = call(part(update1_kernel, n), [one], [*outs, h1, routes, gates])
    last1 = shifted(last1, "section", 1)
    gate_out, up_out = input_grads(x_act_all, g_grad0_all, g_grad1_all, width, hidden)
    (down_out,) = down_grads(g_grad0_all, g_grad1_all, x_act_all, width, hidden)
    (state,) = call(
        finish_state_kernel,
        [(tokens.shape, BF16)],
        [*tok_parts, upd0, prev2_routes, last1, prev_routes],
    )
    return (grad, state, gate_out[None], up_out[None], down_out[None])


def solution(mesh):
    rows = P(("section", "expert", "dp"), None)
    slots = P(None, ("section", "expert", "dp"), None)
    cols = P("section", None, "expert")
    hidden = P("section", "expert", None)
    return jax.shard_map(
        shards,
        mesh=mesh,
        in_specs=(rows, rows, cols, cols, hidden, slots, slots),
        out_specs=(rows, rows, cols, cols, hidden),
        check_vma=False,
    )
```

```python
import functools

import jax
import jax.numpy as jnp
from jax import lax
from jax.experimental import pallas as pl
from jax.experimental.pallas import tpu as pltpu
from jax.sharding import PartitionSpec as P

CAP = 10
PACK = 8
PACKED = CAP * PACK
COT_PIECES = ((0, 32, 0, 8), (32, 64, 0, 8), (64, 128, 0, 3), (64, 128, 3, 8))
TOK_PIECES = ((0, 16, 0, 8), (16, 128, 0, 8))
EPSILON = 1e-06
F32 = jnp.float32
BF16 = jnp.bfloat16
VMEM_SMALL = 24 * 1024 * 1024
VMEM_LOAD = 44 * 1024 * 1024
VMEM_ALL = 60 * 1024 * 1024
COST_BYTES = 1024


def shifted(block, axis, distance):
    size = lax.axis_size(axis)
    return lax.ppermute(block, axis, [((i - distance) % size, i) for i in range(size)])


def dot(a, b, ca=1, cb=0):
    return lax.dot_general(a, b, (((ca,), (cb,)), ((), ())), preferred_element_type=F32)


def call(
    kernel, outs, args, *, any_args=(), any_outs=(), scratch=(), vmem=VMEM_SMALL
):
    outs = [jax.ShapeDtypeStruct(*o) if isinstance(o, tuple) else o for o in outs]
    anywhere = pl.BlockSpec(memory_space=pl.ANY)
    near = pl.BlockSpec(memory_space=pltpu.VMEM)
    return pl.pallas_call(
        kernel,
        out_shape=outs,
        in_specs=[anywhere if i in any_args else near for i in range(len(args))],
        out_specs=[anywhere if i in any_outs else near for i in range(len(outs))],
        scratch_shapes=list(scratch),
        compiler_params=pltpu.CompilerParams(vmem_limit_bytes=vmem),
        cost_estimate=pl.CostEstimate(flops=0, bytes_accessed=COST_BYTES, transcendentals=0),
    )(*args)


def packed_index(shape, dim):
    place = lax.broadcasted_iota(jnp.int32, shape, dim).astype(F32)
    chunk = jnp.floor((place + 0.5) * (1.0 / CAP))
    return place - CAP * chunk, chunk


def select_of(routes):
    hits = (routes == 0).astype(F32)
    marked = jnp.sum(hits, axis=0, keepdims=True)
    rows = routes.shape[1]
    before = lax.broadcasted_iota(jnp.int32, (rows, rows), 0) < lax.broadcasted_iota(
        jnp.int32, (rows, rows), 1
    )
    wide = jnp.broadcast_to(marked, (PACKED, rows))
    places = dot(wide.astype(BF16), before.astype(F32).astype(BF16))
    slot, _ = packed_index((PACKED, rows), 0)
    return jnp.where((places == slot) & (wide > 0.5), 1.0, 0.0)


def slot_gates(select, routes, gates):
    weights = jnp.sum(jnp.where(routes == 0, gates, 0.0), axis=0, keepdims=True)
    return jnp.sum(select * weights, axis=1, keepdims=True)


def chunk_of(select, c):
    _, chunk = packed_index(select.shape, 0)
    return jnp.where(chunk == c, select, 0.0).astype(BF16)


def columns(c, width):
    return slice(c * (width // PACK), (c + 1) * (width // PACK))


def pick(select, pieces):
    total = None
    for block, (r0, r1, c0, c1) in pieces:
        width = block.shape[1] // (c1 - c0)
        for c in range(c0, c1):
            columns_here = slice((c - c0) * width, (c - c0 + 1) * width)
            part = dot(chunk_of(select[:, r0:r1], c), block[:, columns_here])
            total = part if total is None else total + part
    return total


def whole_block(block):
    return [(block, (0, block.shape[0], 0, PACK))]


def over_chunks(row_sums):
    slot_r, _ = packed_index((PACKED, PACKED), 0)
    slot_c, _ = packed_index((PACKED, PACKED), 1)
    same = jnp.where(slot_r == slot_c, 1.0, 0.0)
    wide = jnp.broadcast_to(row_sums, (PACKED, 128))
    return jnp.dot(
        same, wide, precision=lax.Precision.HIGHEST, preferred_element_type=F32
    )[:, :1]


def mean_of(values):
    return over_chunks(jnp.sum(values, axis=-1, keepdims=True)) * (1.0 / (PACK * values.shape[1]))


def inv_rms_of(values):
    return lax.rsqrt(mean_of(values * values) + EPSILON)


def merged(select_to, select_from, fresh, old):
    same = dot(select_to.astype(BF16), select_from.astype(BF16), 1, 1)
    _, chunk_r = packed_index(same.shape, 0)
    _, chunk_c = packed_index(same.shape, 1)
    same = jnp.where(chunk_r == chunk_c, same, 0.0)
    taken = jnp.sum(same, axis=1, keepdims=True)
    return jnp.where(taken > 0.5, dot(same.astype(BF16), fresh), old).astype(BF16)


def summed(parts):
    total = parts[0][...].astype(F32)
    for p in parts[1:]:
        total = total + p[...].astype(F32)
    return total


def place_rows(pieces, first, rows1, second, rows2, out):
    ones = jnp.ones((PACKED, 128), BF16)
    hit1 = dot(chunk_of(first, 0), ones, 0, 0)[:, :1] > 0.5
    hit2 = dot(chunk_of(second, 0), ones, 0, 0)[:, :1] > 0.5
    width = out.shape[1] // PACK
    for c in range(PACK):
        new1 = dot(chunk_of(first, c), rows1, 0, 0)
        new2 = dot(chunk_of(second, c), rows2, 0, 0)
        for block, (r0, r1, c0, c1) in pieces:
            if c0 <= c < c1:
                old = block[:, (c - c0) * width : (c - c0 + 1) * width].astype(F32)
                value = jnp.where(hit1[r0:r1], new1[r0:r1], old)
                value = jnp.where(hit2[r0:r1], new2[r0:r1], value)
                out[r0:r1, columns(c, out.shape[1])] = value.astype(BF16)


def piece_copy(source, place, piece, sem):
    r0, r1, c0, c1 = place
    width = source.shape[1] // PACK
    block = source.at[pl.ds(r0, r1 - r0), pl.ds(c0 * width, (c1 - c0) * width)]
    copy = pltpu.make_async_copy(block, piece, sem)
    copy.start()
    return copy


def load_kernel(gate, up, down, gate_v, up_v, down_v, sems):
    step = gate.shape[0] // PACK
    copies = []
    for c in range(PACK):
        r = pl.ds(c * step, step)
        copies += [
            pltpu.make_async_copy(gate.at[r], gate_v.at[r], sems.at[0, c]),
            pltpu.make_async_copy(up.at[r], up_v.at[r], sems.at[1, c]),
            pltpu.make_async_copy(down.at[:, r], down_v.at[:, r], sems.at[2, c]),
        ]
    for copy in copies:
        copy.start()
    for copy in copies:
        copy.wait()


def first_rows_kernel(tokens, routes, cotangent, raw, normed, piece, sem, sems, held):
    copy = piece_copy(cotangent, COT_PIECES[0], piece, sem)
    fetches = []
    for c in range(PACK):
        k = columns(c, held.shape[1])
        fetches.append(pltpu.make_async_copy(tokens.at[:, k], held.at[:, k], sems.at[c]))
        fetches[-1].start()
    select = select_of(routes[0])
    for fetch in fetches:
        fetch.wait()
    values = pick(select, whole_block(held))
    raw[...] = values.astype(BF16)
    normed[...] = (values * inv_rms_of(values)).astype(BF16)
    copy.wait()


def other_rows_kernel(
    tokens, cotangent, next_routes, prev_routes, _, __, far, t1, cot, piece, sem
):
    copy = piece_copy(far, COT_PIECES[1], piece, sem)
    cot[...] = pick(select_of(prev_routes[0]), whole_block(cotangent)).astype(BF16)
    t1[...] = pick(select_of(next_routes[0]), whole_block(tokens)).astype(BF16)
    copy.wait()


def update0_kernel(n, *refs):
    parts, (raw, routes, gates, next_routes, t1, cotangent) = refs[:n], refs[n : n + 6]
    upd, onward, piece, sem = refs[n + 6 :]
    copy = piece_copy(cotangent, COT_PIECES[2], piece, sem)
    select = select_of(routes[0])
    weight = slot_gates(select, routes[0], gates[0])
    fresh = (raw[...].astype(F32) + weight * summed(parts)).astype(BF16)
    onward[...] = merged(select_of(next_routes[0]), select, fresh, t1[...].astype(F32))
    upd[...] = fresh
    copy.wait()


def update1_kernel(n, *refs):
    parts, (h, routes, gates, upd) = refs[:n], refs[n:]
    select = select_of(routes[1])
    weight = slot_gates(select, routes[1], gates[1])
    upd[...] = (h[...].astype(F32) + weight * summed(parts)).astype(BF16)


def enter1_kernel(h, cot, routes, gates, cotangent, _, out, piece, sem):
    copy = piece_copy(cotangent, COT_PIECES[3], piece, sem)
    values = h[...].astype(F32)
    out[:PACKED] = (values * inv_rms_of(values)).astype(BF16)
    weight = slot_gates(select_of(routes[1]), routes[1], gates[1])
    out[PACKED:] = (weight * cot[...].astype(F32)).astype(BF16)
    copy.wait()


def state_grad(parts, h, c):
    total = summed(parts)
    values = h.astype(F32)
    inv = inv_rms_of(values)
    inner = mean_of(total * values)
    return (c.astype(F32) + inv * total - inv * inv * inv * values * inner).astype(BF16)


def grad1_kernel(n, *refs):
    parts, (h, cot, upd) = refs[:n], refs[n:]
    upd[...] = state_grad(parts, h[...], cot[...])


def enter0_kernel(m, upd1, next_routes, routes, gates, *refs):
    bulk, (tokens, _, c0, out, piece, sem) = refs[:m], refs[m:]
    copy = piece_copy(tokens, TOK_PIECES[1], piece, sem)
    select = select_of(routes[0])
    old = pick(select, list(zip(bulk, COT_PIECES)))
    rows = merged(select, select_of(next_routes[0]), upd1[...], old)
    c0[...] = rows
    out[...] = (slot_gates(select, routes[0], gates[0]) * rows.astype(F32)).astype(BF16)
    copy.wait()


def finish_grad_kernel(n, *refs):
    parts, (h, c, routes, upd1, next_routes, *bulk, out) = refs[:n], refs[n:]
    fresh = state_grad(parts, h[...], c[...])
    place_rows(
        list(zip(bulk, COT_PIECES)),
        select_of(next_routes[0]),
        upd1[...],
        select_of(routes[0]),
        fresh,
        out,
    )


def finish_state_kernel(first, rest, upd0, prev2_routes, upd1, prev_routes, out):
    place_rows(
        list(zip([first, rest], TOK_PIECES)),
        select_of(prev2_routes[0]),
        upd0[...],
        select_of(prev_routes[0]),
        upd1[...],
        out,
    )


def silu_grads(pre_gate, pre_up, grad_act):
    sig = jax.nn.sigmoid(pre_gate)
    grad_gate = (grad_act * pre_up * sig * (1.0 + pre_gate * (1.0 - sig))).astype(BF16)
    grad_up = (grad_act * (pre_gate * sig)).astype(BF16)
    return grad_gate, grad_up


def gather_rows(blocks, first, unpacked, whole32, whole):
    width = whole.shape[1]
    used = len(blocks) * CAP
    if used < whole.shape[0]:
        whole32[used:] = jnp.zeros((whole.shape[0] - used, width), F32)
    for i, b in enumerate(blocks):
        unpacked[i] = b[first : first + PACKED].astype(F32)
        for c in range(PACK):
            whole32[i * CAP : (i + 1) * CAP, columns(c, width)] = unpacked[
                i, c * CAP : (c + 1) * CAP
            ]
    whole[...] = whole32[...].astype(BF16)


def spread_rows(value, c, n, held, unpacked):
    held[...] = value
    for i in range(n):
        unpacked[i, c * CAP : (c + 1) * CAP] = held[i * CAP : (i + 1) * CAP]


def forward_kernel(n, *refs):
    blocks, (gate, up, down) = refs[:n], refs[n : n + 3]
    x, pre_gate, pre_up, act = refs[n + 3 : n + 7]
    parts = refs[n + 7 : 2 * n + 7]
    unpacked, whole32, held = refs[2 * n + 7 :]
    gather_rows(blocks, 0, unpacked, whole32, x)
    acc_g = dot(x[...], gate[...])
    acc_u = dot(x[...], up[...])
    pre_gate[...] = acc_g
    pre_up[...] = acc_u
    activated = (acc_g * jax.nn.sigmoid(acc_g) * acc_u).astype(BF16)
    act[...] = activated
    out_rows(activated, down, held, unpacked, parts)


def out_rows(act, down, held, unpacked, parts):
    n = len(parts)
    for c in range(PACK):
        value = dot(act, down[:, columns(c, down.shape[1])])
        spread_rows(value, c, n, held.at[c], unpacked)
    for i, p in enumerate(parts):
        p[...] = unpacked[i].astype(BF16)


def down_kernel(n, act, down, _, *refs):
    parts, (unpacked, held) = refs[:n], refs[n:]
    hidden, width = down.shape
    out_rows(act[:, width + hidden :], down, held, unpacked, parts)


def back_rows(gg, gu, gate, up, held, unpacked, parts):
    n = len(parts)
    for c in range(PACK):
        k = columns(c, gate.shape[0])
        value = dot(gg, gate[k], 1, 1) + dot(gu, up[k], 1, 1)
        spread_rows(value, c, n, held.at[c], unpacked)
    for i, p in enumerate(parts):
        p[...] = unpacked[i].astype(BF16)


def tick1_kernel(n, *refs):
    blocks, (act0, gate, up, down, tokens, _) = refs[:n], refs[n : n + 6]
    x_act, g_grad, piece = refs[n + 6 : n + 9]
    parts = refs[n + 9 : 2 * n + 9]
    sem, unpacked, whole32, held, x, g = refs[2 * n + 9 :]
    copy = piece_copy(tokens, TOK_PIECES[0], piece, sem)
    gather_rows(blocks, 0, unpacked, whole32.at[0], x)
    gather_rows(blocks, PACKED, unpacked, whole32.at[1], g)
    width, hidden = gate.shape
    x_act[:, :width] = x[...]
    x_act[:, width : width + hidden] = act0[...]
    g_grad[:, :width] = g[...]
    acc_g = dot(x[...], gate[...])
    acc_u = dot(x[...], up[...])
    acc_a = dot(g[...], down[...], 1, 1)
    gg, gu = silu_grads(acc_g, acc_u, acc_a)
    x_act[:, width + hidden :] = (acc_g * jax.nn.sigmoid(acc_g) * acc_u).astype(BF16)
    g_grad[:, width : width + hidden] = gg
    g_grad[:, width + hidden :] = gu
    back_rows(gg, gu, gate, up, held, unpacked, parts)
    copy.wait()


def gather0_kernel(n, *refs):
    blocks, (g, unpacked, whole32) = refs[:n], refs[n:]
    gather_rows(blocks, 0, unpacked, whole32, g)


def tick0_kernel(n, *refs):
    g, pre_gate, pre_up, gate, up, down, small = refs[:7]
    parts = refs[7 : n + 7]
    unpacked, held = refs[n + 7 :]
    hidden = gate.shape[1]
    acc_a = dot(g[...], down[...], 1, 1)
    gg, gu = silu_grads(pre_gate[...], pre_up[...], acc_a)
    small[:, :hidden] = gg
    small[:, hidden:] = gu
    back_rows(gg, gu, gate, up, held, unpacked, parts)


def whole_of(blocks):
    return jnp.concatenate(blocks, axis=0)


def turn_kernel(m, *refs):
    x0, x1, act0, act1 = (refs[i * m : (i + 1) * m] for i in range(4))
    x_t, act_t = refs[4 * m :]
    x_t[...] = whole_of([b[...] for b in x0 + x1]).T

    @pl.when(pl.program_id(0) == 0)
    def _():
        act_t[...] = whole_of([b[...] for b in act0 + act1]).T


def weight_grad_kernel(m, x_t, act_t, *refs):
    g0, g1, small0, gates1, ups1 = (refs[i * m : (i + 1) * m] for i in range(5))
    gate_out, up_out, down_out = refs[5 * m :]
    hidden = gate_out.shape[1]
    gg = whole_of([b[:, :hidden] for b in small0] + [b[...] for b in gates1])
    gu = whole_of([b[:, hidden:] for b in small0] + [b[...] for b in ups1])
    gate_out[...] = dot(x_t[...], gg).astype(BF16)
    up_out[...] = dot(x_t[...], gu).astype(BF16)
    down_out[...] = dot(act_t[...], whole_of([b[...] for b in g0 + g1])).astype(BF16)


def chunked_call(kernel, ins, outs):
    return pl.pallas_call(
        kernel,
        grid=(PACK,),
        out_shape=[jax.ShapeDtypeStruct(s, BF16) for s, _, _ in outs],
        in_specs=[pl.BlockSpec(block, index) for _, block, index in ins],
        out_specs=[pl.BlockSpec(block, index) for _, block, index in outs],
        compiler_params=pltpu.CompilerParams(vmem_limit_bytes=VMEM_SMALL),
        cost_estimate=pl.CostEstimate(flops=0, bytes_accessed=COST_BYTES, transcendentals=0),
    )(*(a for a, _, _ in ins))


def constant(at):
    return lambda c: (0, at)


def chunk_at(at):
    return lambda c: (0, at + c)


def turned(x0, x_act, width, hidden):
    m = len(x_act)
    rows = x_act[0].shape[0]
    step = width // PACK
    first = width // hidden
    ins = [(a, (rows, step), chunk_at(0)) for a in x0 + x_act]
    ins += [(a, (rows, hidden), constant(at)) for at in (first, first + 1) for a in x_act]
    outs = [
        ((width, 2 * m * rows), (step, 2 * m * rows), lambda c: (c, 0)),
        ((hidden, 2 * m * rows), (hidden, 2 * m * rows), lambda c: (0, 0)),
    ]
    return chunked_call(functools.partial(turn_kernel, m), ins, outs)


def weight_grads(x_t, act_t, g0, g_grad1, small0, width, hidden):
    m = len(g0)
    rows = g0[0].shape[0]
    step = width // PACK
    first = width // hidden
    ins = [(x_t, (step, x_t.shape[1]), lambda c: (c, 0)), (act_t, act_t.shape, constant(0))]
    ins += [(a, (rows, step), chunk_at(0)) for a in g0 + g_grad1]
    ins += [(a, a.shape, constant(0)) for a in small0]
    ins += [(a, (rows, hidden), constant(at)) for at in (first, first + 1) for a in g_grad1]
    tall = ((width, hidden), (step, hidden), lambda c: (c, 0))
    outs = [tall, tall, ((hidden, width), (hidden, step), chunk_at(0))]
    return chunked_call(functools.partial(weight_grad_kernel, m), ins, outs)


def from_group(block):
    n = lax.axis_size("expert")
    return [block] + [shifted(block, "expert", k) for k in range(1, n)]


def to_group(blocks):
    return [blocks[0]] + [shifted(b, "expert", -k) for k, b in enumerate(blocks) if k]


def copies_of(block):
    n = lax.axis_size("dp")
    return [block] + [shifted(block, "dp", k) for k in range(1, n)]


def shards(tokens, cotangent, w_gate, w_up, w_down, routes, gates):
    gate, up, down = w_gate[0], w_up[0], w_down[0]
    width, hidden = gate.shape
    step = width // PACK
    n = lax.axis_size("expert")
    rows = -(-n * CAP // 16) * 16
    routes = jnp.transpose(routes, (0, 2, 1))
    gates = jnp.transpose(gates, (0, 2, 1))
    one = ((PACKED, step), BF16)
    part = functools.partial
    unpacked = pltpu.VMEM((n, PACKED, step), F32)
    flat32 = pltpu.VMEM((rows, width), F32)
    held = pltpu.VMEM((PACK, rows, step), F32)
    flat = pltpu.VMEM((rows, width), BF16)
    wide = ((rows, width + 2 * hidden), BF16)
    dma = [pltpu.SemaphoreType.DMA]

    next_routes = shifted(routes[1:], "section", -1)
    prev_routes = shifted(routes[1:], "section", 1)
    prev2_routes = shifted(routes[:1], "section", 2)

    def shape_of(place):
        r0, r1, c0, c1 = place
        return ((r1 - r0, (c1 - c0) * step), BF16)

    cot_shapes = [shape_of(place) for place in COT_PIECES]
    tok_shapes = [shape_of(place) for place in TOK_PIECES]

    raw0, normed0, piece = call(
        first_rows_kernel,
        [one, one, cot_shapes[0]],
        [tokens, routes, cotangent],
        any_args=(0, 2),
        any_outs=(2,),
        scratch=[*dma, pltpu.SemaphoreType.DMA((PACK,)), pltpu.VMEM(tokens.shape, BF16)],
        vmem=VMEM_ALL,
    )
    gate, up, down = call(
        load_kernel,
        [pltpu.VMEM(a.shape, BF16) for a in (gate, up, down)],
        [gate, up, down],
        any_args=(0, 1, 2),
        scratch=[pltpu.SemaphoreType.DMA((3, PACK))],
        vmem=VMEM_LOAD,
    )
    cot_parts = [shifted(piece, "section", -2)]
    blocks = from_group(normed0)
    x0, pre_gate0, pre_up0, act0, *parts = call(
        part(forward_kernel, n),
        [((rows, width), BF16), ((rows, hidden), F32), ((rows, hidden), F32)]
        + [((rows, hidden), BF16)]
        + [one] * n,
        [*blocks, gate, up, down],
        scratch=[unpacked, flat32, held],
    )
    t1, cot1, piece = call(
        other_rows_kernel,
        [one, one, cot_shapes[1]],
        [tokens, cotangent, next_routes, prev_routes, act0, cot_parts[0], cotangent],
        any_args=(4, 5, 6),
        any_outs=(2,),
        scratch=dma,
    )
    cot1 = shifted(cot1, "section", -1)
    x0_all = copies_of(x0)
    cot_parts.append(shifted(piece, "section", -2))
    parts = to_group(parts)
    upd0, h1, piece = call(
        part(update0_kernel, n),
        [one, one, cot_shapes[2]],
        [*parts, raw0, routes, gates, next_routes, t1, cotangent],
        any_args=(n + 5,),
        any_outs=(2,),
        scratch=dma,
    )
    h1 = shifted(h1, "section", 1)
    cot_parts.append(shifted(piece, "section", -2))
    upd0 = shifted(upd0, "section", 2)

    enter1, piece = call(
        enter1_kernel,
        [((2 * PACKED, step), BF16), cot_shapes[3]],
        [h1, cot1, routes, gates, cotangent, cot_parts[1]],
        any_args=(4, 5),
        any_outs=(1,),
        scratch=dma,
    )
    cot_parts.append(shifted(piece, "section", -2))
    blocks = from_group(enter1)
    x_act, g_grad1, piece, *parts = call(
        part(tick1_kernel, n),
        [wide, wide, tok_shapes[0]] + [one] * n,
        [*blocks, act0, gate, up, down, tokens, cot_parts[2]],
        any_args=(n + 4, n + 5),
        any_outs=(2,),
        scratch=[*dma, unpacked, pltpu.VMEM((2, rows, width), F32), held, flat, flat],
    )
    tok_parts = [shifted(piece, "section", 2)]
    parts = to_group(parts)
    (upd1,) = call(part(grad1_kernel, n), [one], [*parts, h1, cot1])
    upd1 = shifted(upd1, "section", -1)
    x_act_all, g_grad1_all = copies_of(x_act), copies_of(g_grad1)

    m = len(cot_parts)
    c0, enter0, piece = call(
        part(enter0_kernel, m),
        [one, one, tok_shapes[1]],
        [upd1, next_routes, routes, gates, *cot_parts, tokens, tok_parts[0]],
        any_args=(m + 4, m + 5),
        any_outs=(2,),
        scratch=dma,
    )
    tok_parts.append(shifted(piece, "section", 2))
    blocks = from_group(enter0)
    (g0,) = call(
        part(gather0_kernel, n), [((rows, width), BF16)], blocks, scratch=[unpacked, flat32]
    )
    g0_all = copies_of(g0)
    small0, *parts = call(
        part(tick0_kernel, n),
        [((rows, 2 * hidden), BF16)] + [one] * n,
        [g0, pre_gate0, pre_up0, gate, up, down],
        scratch=[unpacked, held],
    )
    parts = to_group(parts)
    (grad,) = call(
        part(finish_grad_kernel, n),
        [(tokens.shape, BF16)],
        [*parts, raw0, c0, routes, upd1, next_routes, *cot_parts],
    )
    outs = call(
        part(down_kernel, n),
        [one] * n,
        [x_act, down, small0],
        any_args=(2,),
        scratch=[unpacked, held],
    )
    outs = to_group(outs)
    (last1,) = call(part(update1_kernel, n), [one], [*outs, h1, routes, gates])
    last1 = shifted(last1, "section", 1)
    x_t, act_t = turned(x0_all, x_act_all, width, hidden)
    gate_out, up_out, down_out = weight_grads(
        x_t, act_t, g0_all, g_grad1_all, copies_of(small0), width, hidden
    )
    (state,) = call(
        finish_state_kernel,
        [(tokens.shape, BF16)],
        [*tok_parts, upd0, prev2_routes, last1, prev_routes],
    )
    return (grad, state, gate_out[None], up_out[None], down_out[None])


def solution(mesh):
    rows = P(("section", "expert", "dp"), None)
    slots = P(None, ("section", "expert", "dp"), None)
    cols = P("section", None, "expert")
    hidden = P("section", "expert", None)
    return jax.shard_map(
        shards,
        mesh=mesh,
        in_specs=(rows, rows, cols, cols, hidden, slots, slots),
        out_specs=(rows, rows, cols, cols, hidden),
        check_vma=False,
    )
```

```python
import functools

import jax
import jax.numpy as jnp
from jax import lax
from jax.experimental import pallas as pl
from jax.experimental.pallas import tpu as pltpu
from jax.sharding import PartitionSpec as P

CAP = 10
PACK = 8
PACKED = CAP * PACK
COT_PIECES = ((0, 48, 0, 8), (48, 64, 0, 8), (64, 128, 0, 8))
TOK_PIECES = ((0, 128, 0, 8),)
EPSILON = 1e-06
F32 = jnp.float32
BF16 = jnp.bfloat16
VMEM_SMALL = 24 * 1024 * 1024
VMEM_LOAD = 36 * 1024 * 1024
VMEM_ALL = 60 * 1024 * 1024
COST_BYTES = 1024


def shifted(block, axis, distance):
    size = lax.axis_size(axis)
    return lax.ppermute(block, axis, [((i - distance) % size, i) for i in range(size)])


def dot(a, b, ca=1, cb=0):
    return lax.dot_general(a, b, (((ca,), (cb,)), ((), ())), preferred_element_type=F32)


def call(
    kernel, outs, args, *, any_args=(), any_outs=(), scratch=(), vmem=VMEM_SMALL
):
    outs = [jax.ShapeDtypeStruct(*o) if isinstance(o, tuple) else o for o in outs]
    anywhere = pl.BlockSpec(memory_space=pl.ANY)
    near = pl.BlockSpec(memory_space=pltpu.VMEM)
    return pl.pallas_call(
        kernel,
        out_shape=outs,
        in_specs=[anywhere if i in any_args else near for i in range(len(args))],
        out_specs=[anywhere if i in any_outs else near for i in range(len(outs))],
        scratch_shapes=list(scratch),
        compiler_params=pltpu.CompilerParams(vmem_limit_bytes=vmem),
        cost_estimate=pl.CostEstimate(flops=0, bytes_accessed=COST_BYTES, transcendentals=0),
    )(*args)


def packed_index(shape, dim):
    place = lax.broadcasted_iota(jnp.int32, shape, dim).astype(F32)
    chunk = jnp.floor((place + 0.5) * (1.0 / CAP))
    return place - CAP * chunk, chunk


def select_of(routes):
    hits = (routes == 0).astype(F32)
    marked = jnp.sum(hits, axis=0, keepdims=True)
    rows = routes.shape[1]
    before = lax.broadcasted_iota(jnp.int32, (rows, rows), 0) < lax.broadcasted_iota(
        jnp.int32, (rows, rows), 1
    )
    wide = jnp.broadcast_to(marked, (PACKED, rows))
    places = dot(wide.astype(BF16), before.astype(F32).astype(BF16))
    slot, _ = packed_index((PACKED, rows), 0)
    return jnp.where((places == slot) & (wide > 0.5), 1.0, 0.0)


def slot_gates(select, routes, gates):
    weights = jnp.sum(jnp.where(routes == 0, gates, 0.0), axis=0, keepdims=True)
    return jnp.sum(select * weights, axis=1, keepdims=True)


def chunk_of(select, c):
    _, chunk = packed_index(select.shape, 0)
    return jnp.where(chunk == c, select, 0.0).astype(BF16)


def columns(c, width):
    return slice(c * (width // PACK), (c + 1) * (width // PACK))


def pick(select, pieces):
    total = None
    for block, (r0, r1, c0, c1) in pieces:
        width = block.shape[1] // (c1 - c0)
        for c in range(c0, c1):
            columns_here = slice((c - c0) * width, (c - c0 + 1) * width)
            part = dot(chunk_of(select[:, r0:r1], c), block[:, columns_here])
            total = part if total is None else total + part
    return total


def whole_block(block):
    return [(block, (0, block.shape[0], 0, PACK))]


def over_chunks(row_sums):
    slot_r, _ = packed_index((PACKED, PACKED), 0)
    slot_c, _ = packed_index((PACKED, PACKED), 1)
    same = jnp.where(slot_r == slot_c, 1.0, 0.0)
    wide = jnp.broadcast_to(row_sums, (PACKED, 128))
    return jnp.dot(
        same, wide, precision=lax.Precision.HIGHEST, preferred_element_type=F32
    )[:, :1]


def mean_of(values):
    return over_chunks(jnp.sum(values, axis=-1, keepdims=True)) * (1.0 / (PACK * values.shape[1]))


def inv_rms_of(values):
    return lax.rsqrt(mean_of(values * values) + EPSILON)


def merged(select_to, select_from, fresh, old):
    same = dot(select_to.astype(BF16), select_from.astype(BF16), 1, 1)
    _, chunk_r = packed_index(same.shape, 0)
    _, chunk_c = packed_index(same.shape, 1)
    same = jnp.where(chunk_r == chunk_c, same, 0.0)
    taken = jnp.sum(same, axis=1, keepdims=True)
    return jnp.where(taken > 0.5, dot(same.astype(BF16), fresh), old).astype(BF16)


def summed(parts):
    total = parts[0][...].astype(F32)
    for p in parts[1:]:
        total = total + p[...].astype(F32)
    return total


def place_rows(pieces, first, rows1, second, rows2, out):
    ones = jnp.ones((PACKED, 128), BF16)
    hit1 = dot(chunk_of(first, 0), ones, 0, 0)[:, :1] > 0.5
    hit2 = dot(chunk_of(second, 0), ones, 0, 0)[:, :1] > 0.5
    width = out.shape[1] // PACK
    for c in range(PACK):
        new1 = dot(chunk_of(first, c), rows1, 0, 0)
        new2 = dot(chunk_of(second, c), rows2, 0, 0)
        for block, (r0, r1, c0, c1) in pieces:
            if c0 <= c < c1:
                old = block[:, (c - c0) * width : (c - c0 + 1) * width].astype(F32)
                value = jnp.where(hit1[r0:r1], new1[r0:r1], old)
                value = jnp.where(hit2[r0:r1], new2[r0:r1], value)
                out[r0:r1, columns(c, out.shape[1])] = value.astype(BF16)


def piece_copy(source, place, piece, sem):
    r0, r1, c0, c1 = place
    width = source.shape[1] // PACK
    block = source.at[pl.ds(r0, r1 - r0), pl.ds(c0 * width, (c1 - c0) * width)]
    copy = pltpu.make_async_copy(block, piece, sem)
    copy.start()
    return copy


def first_rows_kernel(tokens, routes, cotangent, raw, normed, piece, sem, sems, held):
    copy = piece_copy(cotangent, COT_PIECES[0], piece, sem)
    fetches = []
    for c in range(PACK):
        k = columns(c, held.shape[1])
        fetches.append(pltpu.make_async_copy(tokens.at[:, k], held.at[:, k], sems.at[c]))
        fetches[-1].start()
    select = select_of(routes[0])
    for fetch in fetches:
        fetch.wait()
    values = pick(select, whole_block(held))
    raw[...] = values.astype(BF16)
    normed[...] = (values * inv_rms_of(values)).astype(BF16)
    copy.wait()


def other_rows_kernel(
    tokens, cotangent, next_routes, prev_routes, _, __, far, t1, cot, piece, sem
):
    copy = piece_copy(far, COT_PIECES[1], piece, sem)
    cot[...] = pick(select_of(prev_routes[0]), whole_block(cotangent)).astype(BF16)
    t1[...] = pick(select_of(next_routes[0]), whole_block(tokens)).astype(BF16)
    copy.wait()


def update0_kernel(n, *refs):
    parts, (raw, routes, gates, next_routes, t1, upd, onward) = refs[:n], refs[n:]
    select = select_of(routes[0])
    weight = slot_gates(select, routes[0], gates[0])
    fresh = (raw[...].astype(F32) + weight * summed(parts)).astype(BF16)
    onward[...] = merged(select_of(next_routes[0]), select, fresh, t1[...].astype(F32))
    upd[...] = fresh


def update1_kernel(n, *refs):
    parts, (h, routes, gates, upd) = refs[:n], refs[n:]
    select = select_of(routes[1])
    weight = slot_gates(select, routes[1], gates[1])
    upd[...] = (h[...].astype(F32) + weight * summed(parts)).astype(BF16)


def enter1_kernel(h, cot, routes, gates, cotangent, _, out, piece, sem):
    copy = piece_copy(cotangent, COT_PIECES[2], piece, sem)
    values = h[...].astype(F32)
    out[:PACKED] = (values * inv_rms_of(values)).astype(BF16)
    weight = slot_gates(select_of(routes[1]), routes[1], gates[1])
    out[PACKED:] = (weight * cot[...].astype(F32)).astype(BF16)
    copy.wait()


def state_grad(parts, h, c):
    total = summed(parts)
    values = h.astype(F32)
    inv = inv_rms_of(values)
    inner = mean_of(total * values)
    return (c.astype(F32) + inv * total - inv * inv * inv * values * inner).astype(BF16)


def grad1_kernel(n, *refs):
    parts, (h, cot, _, __, upd) = refs[:n], refs[n:]
    upd[...] = state_grad(parts, h[...], cot[...])


def enter0_kernel(m, upd1, next_routes, routes, gates, *refs):
    bulk, (tokens, _, c0, out, piece, sem) = refs[:m], refs[m:]
    copy = piece_copy(tokens, TOK_PIECES[0], piece, sem)
    select = select_of(routes[0])
    old = pick(select, list(zip(bulk, COT_PIECES)))
    rows = merged(select, select_of(next_routes[0]), upd1[...], old)
    c0[...] = rows
    out[...] = (slot_gates(select, routes[0], gates[0]) * rows.astype(F32)).astype(BF16)
    copy.wait()


def finish_grad_kernel(n, *refs):
    parts, (h, c, routes, upd1, next_routes, *bulk, out) = refs[:n], refs[n:]
    fresh = state_grad(parts, h[...], c[...])
    place_rows(
        list(zip(bulk, COT_PIECES)),
        select_of(next_routes[0]),
        upd1[...],
        select_of(routes[0]),
        fresh,
        out,
    )


def finish_state_kernel(bulk, upd0, prev2_routes, upd1, prev_routes, out):
    place_rows(
        list(zip([bulk], TOK_PIECES)),
        select_of(prev2_routes[0]),
        upd0[...],
        select_of(prev_routes[0]),
        upd1[...],
        out,
    )


def silu_grads(pre_gate, pre_up, grad_act):
    sig = jax.nn.sigmoid(pre_gate)
    grad_gate = (grad_act * pre_up * sig * (1.0 + pre_gate * (1.0 - sig))).astype(BF16)
    grad_up = (grad_act * (pre_gate * sig)).astype(BF16)
    return grad_gate, grad_up


def gather_rows(blocks, first, unpacked, whole32, whole):
    width = whole.shape[1]
    used = len(blocks) * CAP
    if used < whole.shape[0]:
        whole32[used:] = jnp.zeros((whole.shape[0] - used, width), F32)
    for i, b in enumerate(blocks):
        unpacked[i] = b[first : first + PACKED].astype(F32)
        for c in range(PACK):
            whole32[i * CAP : (i + 1) * CAP, columns(c, width)] = unpacked[
                i, c * CAP : (c + 1) * CAP
            ]
    whole[...] = whole32[...].astype(BF16)


def spread_rows(value, c, n, held, unpacked):
    held[...] = value
    for i in range(n):
        unpacked[i, c * CAP : (c + 1) * CAP] = held[i * CAP : (i + 1) * CAP]


def forward_kernel(n, *refs):
    blocks, (gate, up, down) = refs[:n], refs[n : n + 3]
    x, pre_gate, pre_up, act, gate_v, up_v, down_v = refs[n + 3 : n + 10]
    parts = refs[n + 10 : 2 * n + 10]
    sems, unpacked, whole32, held = refs[2 * n + 10 :]
    width = gate.shape[0]
    fetches = []
    for c in range(PACK):
        k = columns(c, width)
        fetches.append(
            (
                pltpu.make_async_copy(gate.at[k], gate_v.at[k], sems.at[0, c]),
                pltpu.make_async_copy(up.at[k], up_v.at[k], sems.at[1, c]),
                pltpu.make_async_copy(down.at[:, k], down_v.at[:, k], sems.at[2, c]),
            )
        )
    for fetch_g, fetch_u, _ in fetches:
        fetch_g.start()
        fetch_u.start()
    for _, _, fetch_d in fetches:
        fetch_d.start()
    gather_rows(blocks, 0, unpacked, whole32, x)
    acc_g = jnp.zeros(pre_gate.shape, F32)
    acc_u = jnp.zeros(pre_up.shape, F32)
    for c, (fetch_g, fetch_u, _) in enumerate(fetches):
        k = columns(c, width)
        fetch_g.wait()
        acc_g = acc_g + dot(x[:, k], gate_v[k])
        fetch_u.wait()
        acc_u = acc_u + dot(x[:, k], up_v[k])
    pre_gate[...] = acc_g
    pre_up[...] = acc_u
    activated = (acc_g * jax.nn.sigmoid(acc_g) * acc_u).astype(BF16)
    act[...] = activated
    for c, (_, _, fetch_d) in enumerate(fetches):
        fetch_d.wait()
        value = dot(activated, down_v[:, columns(c, width)])
        spread_rows(value, c, n, held.at[c], unpacked)
    for i, p in enumerate(parts):
        p[...] = unpacked[i].astype(BF16)


def out_rows(act, down, held, unpacked, parts):
    n = len(parts)
    for c in range(PACK):
        value = dot(act, down[:, columns(c, down.shape[1])])
        spread_rows(value, c, n, held.at[c], unpacked)
    for i, p in enumerate(parts):
        p[...] = unpacked[i].astype(BF16)


def down_kernel(n, act, down, _, *refs):
    parts, (unpacked, held) = refs[:n], refs[n:]
    hidden, width = down.shape
    out_rows(act[:, width + hidden :], down, held, unpacked, parts)


def back_rows(gg, gu, gate, up, held, unpacked, parts):
    n = len(parts)
    for c in range(PACK):
        k = columns(c, gate.shape[0])
        value = dot(gg, gate[k], 1, 1) + dot(gu, up[k], 1, 1)
        spread_rows(value, c, n, held.at[c], unpacked)
    for i, p in enumerate(parts):
        p[...] = unpacked[i].astype(BF16)


def tick1_kernel(n, *refs):
    blocks, (act0, gate, up, down) = refs[:n], refs[n : n + 4]
    x_act, g_grad = refs[n + 4 : n + 6]
    parts = refs[n + 6 : 2 * n + 6]
    unpacked, whole32, held, x, g = refs[2 * n + 6 :]
    gather_rows(blocks, 0, unpacked, whole32.at[0], x)
    gather_rows(blocks, PACKED, unpacked, whole32.at[1], g)
    width, hidden = gate.shape
    x_act[:, :width] = x[...]
    x_act[:, width : width + hidden] = act0[...]
    g_grad[:, :width] = g[...]
    acc_g = dot(x[...], gate[...])
    acc_u = dot(x[...], up[...])
    acc_a = dot(g[...], down[...], 1, 1)
    gg, gu = silu_grads(acc_g, acc_u, acc_a)
    x_act[:, width + hidden :] = (acc_g * jax.nn.sigmoid(acc_g) * acc_u).astype(BF16)
    g_grad[:, width : width + hidden] = gg
    g_grad[:, width + hidden :] = gu
    back_rows(gg, gu, gate, up, held, unpacked, parts)


def gather0_kernel(n, *refs):
    blocks, (g, unpacked, whole32) = refs[:n], refs[n:]
    gather_rows(blocks, 0, unpacked, whole32, g)


def tick0_kernel(n, *refs):
    g, pre_gate, pre_up, gate, up, down, small = refs[:7]
    parts = refs[7 : n + 7]
    unpacked, held = refs[n + 7 :]
    hidden = gate.shape[1]
    acc_a = dot(g[...], down[...], 1, 1)
    gg, gu = silu_grads(pre_gate[...], pre_up[...], acc_a)
    small[:, :hidden] = gg
    small[:, hidden:] = gu
    back_rows(gg, gu, gate, up, held, unpacked, parts)


def whole_of(blocks):
    return jnp.concatenate(blocks, axis=0)


def turn_kernel(m, *refs):
    x0, x1, act0, act1 = (refs[i * m : (i + 1) * m] for i in range(4))
    x_t, act_t = refs[4 * m :]
    x_t[...] = whole_of([b[...] for b in x0 + x1]).T

    @pl.when(pl.program_id(0) == 0)
    def _():
        act_t[...] = whole_of([b[...] for b in act0 + act1]).T


def weight_grad_kernel(m, x_t, act_t, *refs):
    g0, g1, small0, gates1, ups1 = (refs[i * m : (i + 1) * m] for i in range(5))
    gate_out, up_out, down_out = refs[5 * m :]
    hidden = gate_out.shape[1]
    gg = whole_of([b[:, :hidden] for b in small0] + [b[...] for b in gates1])
    gu = whole_of([b[:, hidden:] for b in small0] + [b[...] for b in ups1])
    gate_out[...] = dot(x_t[...], gg).astype(BF16)
    up_out[...] = dot(x_t[...], gu).astype(BF16)
    down_out[...] = dot(act_t[...], whole_of([b[...] for b in g0 + g1])).astype(BF16)


def chunked_call(kernel, ins, outs):
    return pl.pallas_call(
        kernel,
        grid=(PACK,),
        out_shape=[jax.ShapeDtypeStruct(s, BF16) for s, _, _ in outs],
        in_specs=[pl.BlockSpec(block, index) for _, block, index in ins],
        out_specs=[pl.BlockSpec(block, index) for _, block, index in outs],
        compiler_params=pltpu.CompilerParams(vmem_limit_bytes=VMEM_SMALL),
        cost_estimate=pl.CostEstimate(flops=0, bytes_accessed=COST_BYTES, transcendentals=0),
    )(*(a for a, _, _ in ins))


def constant(at):
    return lambda c: (0, at)


def chunk_at(at):
    return lambda c: (0, at + c)


def turned(x0, x_act, width, hidden):
    m = len(x_act)
    rows = x_act[0].shape[0]
    step = width // PACK
    first = width // hidden
    ins = [(a, (rows, step), chunk_at(0)) for a in x0 + x_act]
    ins += [(a, (rows, hidden), constant(at)) for at in (first, first + 1) for a in x_act]
    outs = [
        ((width, 2 * m * rows), (step, 2 * m * rows), lambda c: (c, 0)),
        ((hidden, 2 * m * rows), (hidden, 2 * m * rows), lambda c: (0, 0)),
    ]
    return chunked_call(functools.partial(turn_kernel, m), ins, outs)


def weight_grads(x_t, act_t, g0, g_grad1, small0, width, hidden):
    m = len(g0)
    rows = g0[0].shape[0]
    step = width // PACK
    first = width // hidden
    ins = [(x_t, (step, x_t.shape[1]), lambda c: (c, 0)), (act_t, act_t.shape, constant(0))]
    ins += [(a, (rows, step), chunk_at(0)) for a in g0 + g_grad1]
    ins += [(a, a.shape, constant(0)) for a in small0]
    ins += [(a, (rows, hidden), constant(at)) for at in (first, first + 1) for a in g_grad1]
    tall = ((width, hidden), (step, hidden), lambda c: (c, 0))
    outs = [tall, tall, ((hidden, width), (hidden, step), chunk_at(0))]
    return chunked_call(functools.partial(weight_grad_kernel, m), ins, outs)


def from_group(block):
    n = lax.axis_size("expert")
    return [block] + [shifted(block, "expert", k) for k in range(1, n)]


def to_group(blocks):
    return [blocks[0]] + [shifted(b, "expert", -k) for k, b in enumerate(blocks) if k]


def copies_of(block):
    n = lax.axis_size("dp")
    return [block] + [shifted(block, "dp", k) for k in range(1, n)]


def shards(tokens, cotangent, w_gate, w_up, w_down, routes, gates):
    gate, up, down = w_gate[0], w_up[0], w_down[0]
    width, hidden = gate.shape
    step = width // PACK
    n = lax.axis_size("expert")
    rows = -(-n * CAP // 16) * 16
    routes = jnp.transpose(routes, (0, 2, 1))
    gates = jnp.transpose(gates, (0, 2, 1))
    one = ((PACKED, step), BF16)
    part = functools.partial
    unpacked = pltpu.VMEM((n, PACKED, step), F32)
    flat32 = pltpu.VMEM((rows, width), F32)
    held = pltpu.VMEM((PACK, rows, step), F32)
    flat = pltpu.VMEM((rows, width), BF16)
    wide = ((rows, width + 2 * hidden), BF16)
    dma = [pltpu.SemaphoreType.DMA]

    next_routes = shifted(routes[1:], "section", -1)
    prev_routes = shifted(routes[1:], "section", 1)
    prev2_routes = shifted(routes[:1], "section", 2)

    def shape_of(place):
        r0, r1, c0, c1 = place
        return ((r1 - r0, (c1 - c0) * step), BF16)

    cot_shapes = [shape_of(place) for place in COT_PIECES]
    tok_shapes = [shape_of(place) for place in TOK_PIECES]

    raw0, normed0, piece = call(
        first_rows_kernel,
        [one, one, cot_shapes[0]],
        [tokens, routes, cotangent],
        any_args=(0, 2),
        scratch=[*dma, pltpu.SemaphoreType.DMA((PACK,)), pltpu.VMEM(tokens.shape, BF16)],
        vmem=VMEM_ALL,
    )
    cot_parts = [shifted(piece, "section", -2)]
    blocks = from_group(normed0)
    x0, pre_gate0, pre_up0, act0, gate, up, down, *parts = call(
        part(forward_kernel, n),
        [((rows, width), BF16), ((rows, hidden), F32), ((rows, hidden), F32)]
        + [((rows, hidden), BF16)]
        + [pltpu.VMEM(a.shape, BF16) for a in (gate, up, down)]
        + [one] * n,
        [*blocks, gate, up, down],
        any_args=(n, n + 1, n + 2),
        scratch=[pltpu.SemaphoreType.DMA((3, PACK)), unpacked, flat32, held],
        vmem=VMEM_LOAD,
    )
    t1, cot1, piece = call(
        other_rows_kernel,
        [one, one, cot_shapes[1]],
        [tokens, cotangent, next_routes, prev_routes, act0, cot_parts[0], cotangent],
        any_args=(4, 5, 6),
        any_outs=(2,),
        scratch=dma,
    )
    cot1 = shifted(cot1, "section", -1)
    x0_all = copies_of(x0)
    cot_parts.append(shifted(piece, "section", -2))
    parts = to_group(parts)
    upd0, h1 = call(
        part(update0_kernel, n), [one, one], [*parts, raw0, routes, gates, next_routes, t1]
    )
    h1 = shifted(h1, "section", 1)
    upd0 = shifted(upd0, "section", 2)

    enter1, piece = call(
        enter1_kernel,
        [((2 * PACKED, step), BF16), cot_shapes[2]],
        [h1, cot1, routes, gates, cotangent, cot_parts[1]],
        any_args=(4, 5),
        any_outs=(1,),
        scratch=dma,
    )
    cot_parts.append(shifted(piece, "section", -2))
    blocks = from_group(enter1)
    x_act, g_grad1, *parts = call(
        part(tick1_kernel, n),
        [wide, wide] + [one] * n,
        [*blocks, act0, gate, up, down],
        scratch=[unpacked, pltpu.VMEM((2, rows, width), F32), held, flat, flat],
    )
    parts = to_group(parts)
    (upd1,) = call(
        part(grad1_kernel, n),
        [one],
        [*parts, h1, cot1, x0_all[-1], cot_parts[2]],
        any_args=(n + 2, n + 3),
    )
    upd1 = shifted(upd1, "section", -1)
    x_act_all, g_grad1_all = copies_of(x_act), copies_of(g_grad1)

    m = len(cot_parts)
    c0, enter0, piece = call(
        part(enter0_kernel, m),
        [one, one, tok_shapes[0]],
        [upd1, next_routes, routes, gates, *cot_parts, tokens, x_act_all[-1]],
        any_args=(m + 4, m + 5),
        any_outs=(2,),
        scratch=dma,
    )
    tok_parts = [shifted(piece, "section", 2)]
    blocks = from_group(enter0)
    (g0,) = call(
        part(gather0_kernel, n), [((rows, width), BF16)], blocks, scratch=[unpacked, flat32]
    )
    g0_all = copies_of(g0)
    small0, *parts = call(
        part(tick0_kernel, n),
        [((rows, 2 * hidden), BF16)] + [one] * n,
        [g0, pre_gate0, pre_up0, gate, up, down],
        scratch=[unpacked, held],
    )
    parts = to_group(parts)
    (grad,) = call(
        part(finish_grad_kernel, n),
        [(tokens.shape, BF16)],
        [*parts, raw0, c0, routes, upd1, next_routes, *cot_parts],
    )
    outs = call(
        part(down_kernel, n),
        [one] * n,
        [x_act, down, small0],
        any_args=(2,),
        scratch=[unpacked, held],
    )
    outs = to_group(outs)
    (last1,) = call(part(update1_kernel, n), [one], [*outs, h1, routes, gates])
    last1 = shifted(last1, "section", 1)
    x_t, act_t = turned(x0_all, x_act_all, width, hidden)
    gate_out, up_out, down_out = weight_grads(
        x_t, act_t, g0_all, g_grad1_all, copies_of(small0), width, hidden
    )
    (state,) = call(
        finish_state_kernel,
        [(tokens.shape, BF16)],
        [*tok_parts, upd0, prev2_routes, last1, prev_routes],
    )
    return (grad, state, gate_out[None], up_out[None], down_out[None])


def solution(mesh):
    rows = P(("section", "expert", "dp"), None)
    slots = P(None, ("section", "expert", "dp"), None)
    cols = P("section", None, "expert")
    hidden = P("section", "expert", None)
    return jax.shard_map(
        shards,
        mesh=mesh,
        in_specs=(rows, rows, cols, cols, hidden, slots, slots),
        out_specs=(rows, rows, cols, cols, hidden),
        check_vma=False,
    )
```

```python
import functools

import jax
import jax.numpy as jnp
from jax import lax
from jax.experimental import pallas as pl
from jax.experimental.pallas import tpu as pltpu
from jax.sharding import PartitionSpec as P

CAP = 10
PACK = 8
PACKED = CAP * PACK
TOK_PIECES = ((0, 128, 0, 8),)
EPSILON = 1e-06
F32 = jnp.float32
BF16 = jnp.bfloat16
VMEM_SMALL = 24 * 1024 * 1024
VMEM_LOAD = 36 * 1024 * 1024
VMEM_ALL = 60 * 1024 * 1024
COST_BYTES = 1024


def shifted(block, axis, distance):
    size = lax.axis_size(axis)
    return lax.ppermute(block, axis, [((i - distance) % size, i) for i in range(size)])


def dot(a, b, ca=1, cb=0):
    return lax.dot_general(a, b, (((ca,), (cb,)), ((), ())), preferred_element_type=F32)


def call(
    kernel, outs, args, *, any_args=(), any_outs=(), scratch=(), vmem=VMEM_SMALL, aliases=None
):
    outs = [jax.ShapeDtypeStruct(*o) if isinstance(o, tuple) else o for o in outs]
    anywhere = pl.BlockSpec(memory_space=pl.ANY)
    near = pl.BlockSpec(memory_space=pltpu.VMEM)
    return pl.pallas_call(
        kernel,
        out_shape=outs,
        in_specs=[anywhere if i in any_args else near for i in range(len(args))],
        out_specs=[anywhere if i in any_outs else near for i in range(len(outs))],
        scratch_shapes=list(scratch),
        compiler_params=pltpu.CompilerParams(vmem_limit_bytes=vmem),
        cost_estimate=pl.CostEstimate(flops=0, bytes_accessed=COST_BYTES, transcendentals=0),
        input_output_aliases=aliases or {},
    )(*args)


def packed_index(shape, dim):
    place = lax.broadcasted_iota(jnp.int32, shape, dim).astype(F32)
    chunk = jnp.floor((place + 0.5) * (1.0 / CAP))
    return place - CAP * chunk, chunk


def select_of(routes):
    hits = (routes == 0).astype(F32)
    marked = jnp.sum(hits, axis=0, keepdims=True)
    rows = routes.shape[1]
    before = lax.broadcasted_iota(jnp.int32, (rows, rows), 0) < lax.broadcasted_iota(
        jnp.int32, (rows, rows), 1
    )
    wide = jnp.broadcast_to(marked, (PACKED, rows))
    places = dot(wide.astype(BF16), before.astype(F32).astype(BF16))
    slot, _ = packed_index((PACKED, rows), 0)
    return jnp.where((places == slot) & (wide > 0.5), 1.0, 0.0)


def slot_gates(select, routes, gates):
    weights = jnp.sum(jnp.where(routes == 0, gates, 0.0), axis=0, keepdims=True)
    return jnp.sum(select * weights, axis=1, keepdims=True)


def chunk_of(select, c):
    _, chunk = packed_index(select.shape, 0)
    return jnp.where(chunk == c, select, 0.0).astype(BF16)


def columns(c, width):
    return slice(c * (width // PACK), (c + 1) * (width // PACK))


def pick(select, pieces):
    total = None
    for block, (r0, r1, c0, c1) in pieces:
        width = block.shape[1] // (c1 - c0)
        for c in range(c0, c1):
            columns_here = slice((c - c0) * width, (c - c0 + 1) * width)
            part = dot(chunk_of(select[:, r0:r1], c), block[:, columns_here])
            total = part if total is None else total + part
    return total


def whole_block(block):
    return [(block, (0, block.shape[0], 0, PACK))]


def over_chunks(row_sums):
    slot_r, _ = packed_index((PACKED, PACKED), 0)
    slot_c, _ = packed_index((PACKED, PACKED), 1)
    same = jnp.where(slot_r == slot_c, 1.0, 0.0)
    wide = jnp.broadcast_to(row_sums, (PACKED, 128))
    return jnp.dot(
        same, wide, precision=lax.Precision.HIGHEST, preferred_element_type=F32
    )[:, :1]


def mean_of(values):
    return over_chunks(jnp.sum(values, axis=-1, keepdims=True)) * (1.0 / (PACK * values.shape[1]))


def inv_rms_of(values):
    return lax.rsqrt(mean_of(values * values) + EPSILON)


def merged(select_to, select_from, fresh, old):
    same = dot(select_to.astype(BF16), select_from.astype(BF16), 1, 1)
    _, chunk_r = packed_index(same.shape, 0)
    _, chunk_c = packed_index(same.shape, 1)
    same = jnp.where(chunk_r == chunk_c, same, 0.0)
    taken = jnp.sum(same, axis=1, keepdims=True)
    return jnp.where(taken > 0.5, dot(same.astype(BF16), fresh), old).astype(BF16)


def summed(parts):
    total = parts[0][...].astype(F32)
    for p in parts[1:]:
        total = total + p[...].astype(F32)
    return total


def place_rows(pieces, first, rows1, second, rows2, out):
    ones = jnp.ones((PACKED, 128), BF16)
    hit1 = dot(chunk_of(first, 0), ones, 0, 0)[:, :1] > 0.5
    hit2 = dot(chunk_of(second, 0), ones, 0, 0)[:, :1] > 0.5
    width = out.shape[1] // PACK
    for c in range(PACK):
        new1 = dot(chunk_of(first, c), rows1, 0, 0)
        new2 = dot(chunk_of(second, c), rows2, 0, 0)
        for block, (r0, r1, c0, c1) in pieces:
            if c0 <= c < c1:
                old = block[:, (c - c0) * width : (c - c0 + 1) * width].astype(F32)
                value = jnp.where(hit1[r0:r1], new1[r0:r1], old)
                value = jnp.where(hit2[r0:r1], new2[r0:r1], value)
                out[r0:r1, columns(c, out.shape[1])] = value.astype(BF16)


def piece_copy(source, place, piece, sem):
    r0, r1, c0, c1 = place
    width = source.shape[1] // PACK
    block = source.at[pl.ds(r0, r1 - r0), pl.ds(c0 * width, (c1 - c0) * width)]
    copy = pltpu.make_async_copy(block, piece, sem)
    copy.start()
    return copy


def first_rows_kernel(tokens, routes_far, raw, normed, sems, held, routes):
    fetch_routes = pltpu.make_async_copy(routes_far, routes, sems.at[PACK])
    fetch_routes.start()
    fetches = []
    for c in range(PACK):
        k = columns(c, held.shape[1])
        fetches.append(pltpu.make_async_copy(tokens.at[:, k], held.at[:, k], sems.at[c]))
        fetches[-1].start()
    fetch_routes.wait()
    select = select_of(routes[0])
    for fetch in fetches:
        fetch.wait()
    values = pick(select, whole_block(held))
    raw[...] = values.astype(BF16)
    normed[...] = (values * inv_rms_of(values)).astype(BF16)


def update0_kernel(n, *refs):
    parts, (raw, routes, gates, tokens, next_routes, upd, onward) = refs[:n], refs[n:]
    select = select_of(routes[0])
    select_next = select_of(next_routes[0])
    weight = slot_gates(select, routes[0], gates[0])
    fresh = (raw[...].astype(F32) + weight * summed(parts)).astype(BF16)
    old = pick(select_next, whole_block(tokens))
    onward[...] = merged(select_next, select, fresh, old)
    upd[...] = fresh


def grad_rows_kernel(bulk, routes, gates, cot, scaled):
    select = select_of(routes[1])
    values = pick(select, whole_block(bulk))
    cot[...] = values.astype(BF16)
    scaled[...] = (slot_gates(select, routes[1], gates[1]) * values).astype(BF16)


def update1_kernel(n, *refs):
    parts, (h, routes, gates, upd) = refs[:n], refs[n:]
    select = select_of(routes[1])
    weight = slot_gates(select, routes[1], gates[1])
    upd[...] = (h[...].astype(F32) + weight * summed(parts)).astype(BF16)


def enter1_kernel(h, scaled, _, out, __):
    values = h[...].astype(F32)
    out[:PACKED] = (values * inv_rms_of(values)).astype(BF16)
    out[PACKED:] = scaled[...]


def state_grad(parts, h, c):
    total = summed(parts)
    values = h.astype(F32)
    inv = inv_rms_of(values)
    inner = mean_of(total * values)
    return (c.astype(F32) + inv * total - inv * inv * inv * values * inner).astype(BF16)


def grad1_kernel(n, *refs):
    parts, (h, cot, _, upd) = refs[:n], refs[n:]
    upd[...] = state_grad(parts, h[...], cot[...])


def enter0_kernel(upd1, next_routes, routes, gates, bulk, tokens, _, c0, out, *refs):
    pieces, sems = refs[:-1], refs[-1]
    copies = [
        piece_copy(tokens, place, piece, sems.at[i])
        for i, (place, piece) in enumerate(zip(TOK_PIECES, pieces))
    ]
    select = select_of(routes[0])
    old = pick(select, whole_block(bulk))
    rows = merged(select, select_of(next_routes[0]), upd1[...], old)
    c0[...] = rows
    out[...] = (slot_gates(select, routes[0], gates[0]) * rows.astype(F32)).astype(BF16)
    for copy in copies:
        copy.wait()


def finish_grad_kernel(n, *refs):
    parts, (h, c, routes, upd1, next_routes, bulk, out) = refs[:n], refs[n:]
    fresh = state_grad(parts, h[...], c[...])
    place_rows(
        whole_block(bulk),
        select_of(next_routes[0]),
        upd1[...],
        select_of(routes[0]),
        fresh,
        out,
    )


def finish_state_kernel(m, *refs):
    bulk, (upd0, prev2_routes, upd1, prev_routes, out) = refs[:m], refs[m:]
    place_rows(
        list(zip(bulk, TOK_PIECES)),
        select_of(prev2_routes[0]),
        upd0[...],
        select_of(prev_routes[0]),
        upd1[...],
        out,
    )


def silu_grads(pre_gate, pre_up, grad_act):
    sig = jax.nn.sigmoid(pre_gate)
    grad_gate = (grad_act * pre_up * sig * (1.0 + pre_gate * (1.0 - sig))).astype(BF16)
    grad_up = (grad_act * (pre_gate * sig)).astype(BF16)
    return grad_gate, grad_up


def gather_rows(blocks, first, unpacked, whole32, whole):
    width = whole.shape[1]
    used = len(blocks) * CAP
    if used < whole.shape[0]:
        whole32[used:] = jnp.zeros((whole.shape[0] - used, width), F32)
    for i, b in enumerate(blocks):
        unpacked[i] = b[first : first + PACKED].astype(F32)
        for c in range(PACK):
            whole32[i * CAP : (i + 1) * CAP, columns(c, width)] = unpacked[
                i, c * CAP : (c + 1) * CAP
            ]
    whole[...] = whole32[...].astype(BF16)


def spread_rows(value, c, n, held, unpacked):
    held[...] = value
    for i in range(n):
        unpacked[i, c * CAP : (c + 1) * CAP] = held[i * CAP : (i + 1) * CAP]


def forward_kernel(n, *refs):
    blocks, (gate, up, down) = refs[:n], refs[n : n + 3]
    x, pre_gate, pre_up, act, gate_v, up_v, down_v = refs[n + 3 : n + 10]
    parts = refs[n + 10 : 2 * n + 10]
    sems, unpacked, whole32, held = refs[2 * n + 10 :]
    width = gate.shape[0]
    fetches = []
    for c in range(PACK):
        k = columns(c, width)
        fetches.append(
            (
                pltpu.make_async_copy(gate.at[k], gate_v.at[k], sems.at[0, c]),
                pltpu.make_async_copy(up.at[k], up_v.at[k], sems.at[1, c]),
                pltpu.make_async_copy(down.at[:, k], down_v.at[:, k], sems.at[2, c]),
            )
        )
    for fetch_g, fetch_u, _ in fetches:
        fetch_g.start()
        fetch_u.start()
    for _, _, fetch_d in fetches:
        fetch_d.start()
    gather_rows(blocks, 0, unpacked, whole32, x)
    acc_g = jnp.zeros(pre_gate.shape, F32)
    acc_u = jnp.zeros(pre_up.shape, F32)
    for c, (fetch_g, fetch_u, _) in enumerate(fetches):
        k = columns(c, width)
        fetch_g.wait()
        acc_g = acc_g + dot(x[:, k], gate_v[k])
        fetch_u.wait()
        acc_u = acc_u + dot(x[:, k], up_v[k])
    pre_gate[...] = acc_g
    pre_up[...] = acc_u
    activated = (acc_g * jax.nn.sigmoid(acc_g) * acc_u).astype(BF16)
    act[...] = activated
    for c, (_, _, fetch_d) in enumerate(fetches):
        fetch_d.wait()
        value = dot(activated, down_v[:, columns(c, width)])
        spread_rows(value, c, n, held.at[c], unpacked)
    for i, p in enumerate(parts):
        p[...] = unpacked[i].astype(BF16)


def out_rows(act, down, held, unpacked, parts):
    n = len(parts)
    for c in range(PACK):
        value = dot(act, down[:, columns(c, down.shape[1])])
        spread_rows(value, c, n, held.at[c], unpacked)
    for i, p in enumerate(parts):
        p[...] = unpacked[i].astype(BF16)


def down_kernel(n, act, down, _, *refs):
    parts, (unpacked, held) = refs[:n], refs[n:]
    hidden, width = down.shape
    out_rows(act[:, width + hidden :], down, held, unpacked, parts)


def back_rows(gg, gu, gate, up, held, unpacked, parts):
    n = len(parts)
    for c in range(PACK):
        k = columns(c, gate.shape[0])
        value = dot(gg, gate[k], 1, 1) + dot(gu, up[k], 1, 1)
        spread_rows(value, c, n, held.at[c], unpacked)
    for i, p in enumerate(parts):
        p[...] = unpacked[i].astype(BF16)


def tick1_kernel(n, *refs):
    blocks, (act0, gate, up, down) = refs[:n], refs[n : n + 4]
    x_act, g_grad = refs[n + 4 : n + 6]
    parts = refs[n + 6 : 2 * n + 6]
    unpacked, whole32, held, x, g = refs[2 * n + 6 :]
    gather_rows(blocks, 0, unpacked, whole32.at[0], x)
    gather_rows(blocks, PACKED, unpacked, whole32.at[1], g)
    width, hidden = gate.shape
    x_act[:, :width] = x[...]
    x_act[:, width : width + hidden] = act0[...]
    g_grad[:, :width] = g[...]
    acc_g = dot(x[...], gate[...])
    acc_u = dot(x[...], up[...])
    acc_a = dot(g[...], down[...], 1, 1)
    gg, gu = silu_grads(acc_g, acc_u, acc_a)
    x_act[:, width + hidden :] = (acc_g * jax.nn.sigmoid(acc_g) * acc_u).astype(BF16)
    g_grad[:, width : width + hidden] = gg
    g_grad[:, width + hidden :] = gu
    back_rows(gg, gu, gate, up, held, unpacked, parts)


def gather0_kernel(n, *refs):
    blocks, (g, unpacked, whole32) = refs[:n], refs[n:]
    gather_rows(blocks, 0, unpacked, whole32, g)


def tick0_kernel(n, *refs):
    g, pre_gate, pre_up, gate, up, down, small = refs[:7]
    parts = refs[7 : n + 7]
    unpacked, held = refs[n + 7 :]
    hidden = gate.shape[1]
    acc_a = dot(g[...], down[...], 1, 1)
    gg, gu = silu_grads(pre_gate[...], pre_up[...], acc_a)
    small[:, :hidden] = gg
    small[:, hidden:] = gu
    back_rows(gg, gu, gate, up, held, unpacked, parts)


def whole_of(blocks):
    return jnp.concatenate(blocks, axis=0)


def turn_kernel(m, *refs):
    x0, x1, act0, act1 = (refs[i * m : (i + 1) * m] for i in range(4))
    x_t, act_t = refs[4 * m :]
    x_t[...] = whole_of([b[...] for b in x0 + x1]).T

    @pl.when(pl.program_id(0) == 0)
    def _():
        act_t[...] = whole_of([b[...] for b in act0 + act1]).T


def weight_grad_kernel(m, x_t, act_t, *refs):
    g0, g1, small0, gates1, ups1 = (refs[i * m : (i + 1) * m] for i in range(5))
    gate_out, up_out, down_out = refs[5 * m :]
    hidden = gate_out.shape[1]
    gg = whole_of([b[:, :hidden] for b in small0] + [b[...] for b in gates1])
    gu = whole_of([b[:, hidden:] for b in small0] + [b[...] for b in ups1])
    gate_out[...] = dot(x_t[...], gg).astype(BF16)
    up_out[...] = dot(x_t[...], gu).astype(BF16)
    down_out[...] = dot(act_t[...], whole_of([b[...] for b in g0 + g1])).astype(BF16)


def chunked_call(kernel, ins, outs):
    return pl.pallas_call(
        kernel,
        grid=(PACK,),
        out_shape=[jax.ShapeDtypeStruct(s, BF16) for s, _, _ in outs],
        in_specs=[pl.BlockSpec(block, index) for _, block, index in ins],
        out_specs=[pl.BlockSpec(block, index) for _, block, index in outs],
        compiler_params=pltpu.CompilerParams(vmem_limit_bytes=VMEM_SMALL),
        cost_estimate=pl.CostEstimate(flops=0, bytes_accessed=COST_BYTES, transcendentals=0),
    )(*(a for a, _, _ in ins))


def constant(at):
    return lambda c: (0, at)


def chunk_at(at):
    return lambda c: (0, at + c)


def turned(x0, x_act, width, hidden):
    m = len(x_act)
    rows = x_act[0].shape[0]
    step = width // PACK
    first = width // hidden
    ins = [(a, (rows, step), chunk_at(0)) for a in x0 + x_act]
    ins += [(a, (rows, hidden), constant(at)) for at in (first, first + 1) for a in x_act]
    outs = [
        ((width, 2 * m * rows), (step, 2 * m * rows), lambda c: (c, 0)),
        ((hidden, 2 * m * rows), (hidden, 2 * m * rows), lambda c: (0, 0)),
    ]
    return chunked_call(functools.partial(turn_kernel, m), ins, outs)


def weight_grads(x_t, act_t, g0, g_grad1, small0, width, hidden):
    m = len(g0)
    rows = g0[0].shape[0]
    step = width // PACK
    first = width // hidden
    ins = [(x_t, (step, x_t.shape[1]), lambda c: (c, 0)), (act_t, act_t.shape, constant(0))]
    ins += [(a, (rows, step), chunk_at(0)) for a in g0 + g_grad1]
    ins += [(a, a.shape, constant(0)) for a in small0]
    ins += [(a, (rows, hidden), constant(at)) for at in (first, first + 1) for a in g_grad1]
    tall = ((width, hidden), (step, hidden), lambda c: (c, 0))
    outs = [tall, tall, ((hidden, width), (hidden, step), chunk_at(0))]
    return chunked_call(functools.partial(weight_grad_kernel, m), ins, outs)


def from_group(block):
    n = lax.axis_size("expert")
    return [block] + [shifted(block, "expert", k) for k in range(1, n)]


def to_group(blocks):
    return [blocks[0]] + [shifted(b, "expert", -k) for k, b in enumerate(blocks) if k]


def copies_of(block):
    n = lax.axis_size("dp")
    return [block] + [shifted(block, "dp", k) for k in range(1, n)]


def shards(tokens, cotangent, w_gate, w_up, w_down, routes, gates):
    gate, up, down = w_gate[0], w_up[0], w_down[0]
    width, hidden = gate.shape
    step = width // PACK
    n = lax.axis_size("expert")
    rows = -(-n * CAP // 16) * 16
    routes = jnp.transpose(routes, (0, 2, 1))
    gates = jnp.transpose(gates, (0, 2, 1))
    one = ((PACKED, step), BF16)
    part = functools.partial
    unpacked = pltpu.VMEM((n, PACKED, step), F32)
    flat32 = pltpu.VMEM((rows, width), F32)
    held = pltpu.VMEM((PACK, rows, step), F32)
    flat = pltpu.VMEM((rows, width), BF16)
    wide = ((rows, width + 2 * hidden), BF16)
    dma = [pltpu.SemaphoreType.DMA]

    cot1_all = shifted(cotangent, "section", -1)
    next_routes = shifted(routes[1:], "section", -1)
    prev_routes = shifted(routes[1:], "section", 1)
    prev2_routes = shifted(routes[:1], "section", 2)

    def shape_of(place):
        r0, r1, c0, c1 = place
        return ((r1 - r0, (c1 - c0) * step), BF16)

    tok_shapes = [shape_of(place) for place in TOK_PIECES]

    raw0, normed0 = call(
        first_rows_kernel,
        [one, one],
        [tokens, routes],
        any_args=(0, 1),
        scratch=[
            pltpu.SemaphoreType.DMA((PACK + 1,)),
            pltpu.VMEM(tokens.shape, BF16),
            pltpu.VMEM(routes.shape, jnp.int32),
        ],
        vmem=VMEM_ALL,
    )
    blocks = from_group(normed0)
    x0, pre_gate0, pre_up0, act0, gate, up, down, *parts = call(
        part(forward_kernel, n),
        [((rows, width), BF16), ((rows, hidden), F32), ((rows, hidden), F32)]
        + [((rows, hidden), BF16)]
        + [pltpu.VMEM(a.shape, BF16) for a in (gate, up, down)]
        + [one] * n,
        [*blocks, gate, up, down],
        any_args=(n, n + 1, n + 2),
        scratch=[pltpu.SemaphoreType.DMA((3, PACK)), unpacked, flat32, held],
        vmem=VMEM_LOAD,
    )
    x0_all = copies_of(x0)
    parts = to_group(parts)
    upd0, h1 = call(
        part(update0_kernel, n), [one, one], [*parts, raw0, routes, gates, tokens, next_routes]
    )
    h1 = shifted(h1, "section", 1)
    cot1, scaled1 = call(grad_rows_kernel, [one, one], [cot1_all, routes, gates])
    upd0 = shifted(upd0, "section", 2)

    enter1, cot1_all = call(
        enter1_kernel,
        [((2 * PACKED, step), BF16), (tokens.shape, BF16)],
        [h1, scaled1, cot1_all],
        any_args=(2,),
        any_outs=(1,),
        aliases={2: 1},
    )
    cot0_all = shifted(cot1_all, "section", -1)
    blocks = from_group(enter1)
    x_act, g_grad1, *parts = call(
        part(tick1_kernel, n),
        [wide, wide] + [one] * n,
        [*blocks, act0, gate, up, down],
        scratch=[unpacked, pltpu.VMEM((2, rows, width), F32), held, flat, flat],
    )
    parts = to_group(parts)
    (upd1,) = call(
        part(grad1_kernel, n),
        [one],
        [*parts, h1, cot1, x0_all[-1]],
        any_args=(n + 2,),
    )
    upd1 = shifted(upd1, "section", -1)
    x_act_all, g_grad1_all = copies_of(x_act), copies_of(g_grad1)

    c0, enter0, *pieces = call(
        enter0_kernel,
        [one, one, *tok_shapes],
        [upd1, next_routes, routes, gates, cot0_all, tokens, x_act_all[-1]],
        any_args=(5, 6),
        any_outs=tuple(range(2, 2 + len(tok_shapes))),
        scratch=[pltpu.SemaphoreType.DMA((len(tok_shapes),))],
    )
    tok_parts = [shifted(piece, "section", 2) for piece in pieces]
    blocks = from_group(enter0)
    (g0,) = call(
        part(gather0_kernel, n), [((rows, width), BF16)], blocks, scratch=[unpacked, flat32]
    )
    g0_all = copies_of(g0)
    small0, *parts = call(
        part(tick0_kernel, n),
        [((rows, 2 * hidden), BF16)] + [one] * n,
        [g0, pre_gate0, pre_up0, gate, up, down],
        scratch=[unpacked, held],
    )
    parts = to_group(parts)
    (grad,) = call(
        part(finish_grad_kernel, n),
        [(tokens.shape, BF16)],
        [*parts, raw0, c0, routes, upd1, next_routes, cot0_all],
    )
    outs = call(
        part(down_kernel, n),
        [one] * n,
        [x_act, down, small0],
        any_args=(2,),
        scratch=[unpacked, held],
    )
    outs = to_group(outs)
    (last1,) = call(part(update1_kernel, n), [one], [*outs, h1, routes, gates])
    last1 = shifted(last1, "section", 1)
    x_t, act_t = turned(x0_all, x_act_all, width, hidden)
    gate_out, up_out, down_out = weight_grads(
        x_t, act_t, g0_all, g_grad1_all, copies_of(small0), width, hidden
    )
    (state,) = call(
        part(finish_state_kernel, len(tok_parts)),
        [(tokens.shape, BF16)],
        [*tok_parts, upd0, prev2_routes, last1, prev_routes],
    )
    return (grad, state, gate_out[None], up_out[None], down_out[None])


def solution(mesh):
    rows = P(("section", "expert", "dp"), None)
    slots = P(None, ("section", "expert", "dp"), None)
    cols = P("section", None, "expert")
    hidden = P("section", "expert", None)
    return jax.shard_map(
        shards,
        mesh=mesh,
        in_specs=(rows, rows, cols, cols, hidden, slots, slots),
        out_specs=(rows, rows, cols, cols, hidden),
        check_vma=False,
    )
```

```python
import functools

import jax
import jax.numpy as jnp
from jax import lax
from jax.experimental import pallas as pl
from jax.experimental.pallas import tpu as pltpu
from jax.sharding import PartitionSpec as P

CAP = 10
PACK = 8
PACKED = CAP * PACK
EPSILON = 1e-06
F32 = jnp.float32
BF16 = jnp.bfloat16
VMEM_SMALL = 24 * 1024 * 1024
VMEM_LOAD = 36 * 1024 * 1024
VMEM_ALL = 60 * 1024 * 1024
COST_BYTES = 1024
EARLY = 1


def shifted(block, axis, distance):
    size = lax.axis_size(axis)
    return lax.ppermute(block, axis, [((i - distance) % size, i) for i in range(size)])


def dot(a, b, ca=1, cb=0):
    return lax.dot_general(a, b, (((ca,), (cb,)), ((), ())), preferred_element_type=F32)


def call(
    kernel, outs, args, *, any_args=(), any_outs=(), scratch=(), vmem=VMEM_SMALL, aliases=None
):
    outs = [jax.ShapeDtypeStruct(*o) if isinstance(o, tuple) else o for o in outs]
    anywhere = pl.BlockSpec(memory_space=pl.ANY)
    near = pl.BlockSpec(memory_space=pltpu.VMEM)
    return pl.pallas_call(
        kernel,
        out_shape=outs,
        in_specs=[anywhere if i in any_args else near for i in range(len(args))],
        out_specs=[anywhere if i in any_outs else near for i in range(len(outs))],
        scratch_shapes=list(scratch),
        compiler_params=pltpu.CompilerParams(vmem_limit_bytes=vmem),
        cost_estimate=pl.CostEstimate(flops=0, bytes_accessed=COST_BYTES, transcendentals=0),
        input_output_aliases=aliases or {},
    )(*args)


def packed_index(shape, dim):
    place = lax.broadcasted_iota(jnp.int32, shape, dim).astype(F32)
    chunk = jnp.floor((place + 0.5) * (1.0 / CAP))
    return place - CAP * chunk, chunk


def select_of(routes):
    hits = (routes == 0).astype(F32)
    marked = jnp.sum(hits, axis=0, keepdims=True)
    rows = routes.shape[1]
    before = lax.broadcasted_iota(jnp.int32, (rows, rows), 0) < lax.broadcasted_iota(
        jnp.int32, (rows, rows), 1
    )
    wide = jnp.broadcast_to(marked, (PACKED, rows))
    places = dot(wide.astype(BF16), before.astype(F32).astype(BF16))
    slot, _ = packed_index((PACKED, rows), 0)
    return jnp.where((places == slot) & (wide > 0.5), 1.0, 0.0)


def slot_gates(select, routes, gates):
    weights = jnp.sum(jnp.where(routes == 0, gates, 0.0), axis=0, keepdims=True)
    return jnp.sum(select * weights, axis=1, keepdims=True)


def chunk_of(select, c):
    _, chunk = packed_index(select.shape, 0)
    return jnp.where(chunk == c, select, 0.0).astype(BF16)


def columns(c, width):
    return slice(c * (width // PACK), (c + 1) * (width // PACK))


def pick(select, pieces):
    total = None
    for block, (r0, r1, c0, c1) in pieces:
        width = block.shape[1] // (c1 - c0)
        for c in range(c0, c1):
            columns_here = slice((c - c0) * width, (c - c0 + 1) * width)
            part = dot(chunk_of(select[:, r0:r1], c), block[:, columns_here])
            total = part if total is None else total + part
    return total


def whole_block(block):
    return [(block, (0, block.shape[0], 0, PACK))]


def over_chunks(row_sums):
    slot_r, _ = packed_index((PACKED, PACKED), 0)
    slot_c, _ = packed_index((PACKED, PACKED), 1)
    same = jnp.where(slot_r == slot_c, 1.0, 0.0)
    wide = jnp.broadcast_to(row_sums, (PACKED, 128))
    return jnp.dot(
        same, wide, precision=lax.Precision.HIGHEST, preferred_element_type=F32
    )[:, :1]


def mean_of(values):
    return over_chunks(jnp.sum(values, axis=-1, keepdims=True)) * (1.0 / (PACK * values.shape[1]))


def inv_rms_of(values):
    return lax.rsqrt(mean_of(values * values) + EPSILON)


def merged(select_to, select_from, fresh, old):
    same = dot(select_to.astype(BF16), select_from.astype(BF16), 1, 1)
    _, chunk_r = packed_index(same.shape, 0)
    _, chunk_c = packed_index(same.shape, 1)
    same = jnp.where(chunk_r == chunk_c, same, 0.0)
    taken = jnp.sum(same, axis=1, keepdims=True)
    return jnp.where(taken > 0.5, dot(same.astype(BF16), fresh), old).astype(BF16)


def summed(parts):
    total = parts[0][...].astype(F32)
    for p in parts[1:]:
        total = total + p[...].astype(F32)
    return total


def hit_rows(select):
    ones = jnp.ones((PACKED, 128), BF16)
    return dot(chunk_of(select, 0), ones, 0, 0)[:, :1] > 0.5


def placed(c, old, first, hit1, rows1, second, hit2, rows2):
    value = jnp.where(hit1, dot(chunk_of(first, c), rows1, 0, 0), old.astype(F32))
    return jnp.where(hit2, dot(chunk_of(second, c), rows2, 0, 0), value).astype(BF16)


def first_rows_kernel(tokens, routes_far, raw, normed, early, sems, held, routes):
    fetch_routes = pltpu.make_async_copy(routes_far, routes, sems.at[PACK])
    fetch_routes.start()
    fetches = []
    for c in range(PACK):
        k = columns(c, held.shape[1])
        fetches.append(pltpu.make_async_copy(tokens.at[:, k], held.at[:, k], sems.at[c]))
        fetches[-1].start()
    fetch_routes.wait()
    select = select_of(routes[0])
    for fetch in fetches:
        fetch.wait()
    values = pick(select, whole_block(held))
    raw[...] = values.astype(BF16)
    normed[...] = (values * inv_rms_of(values)).astype(BF16)
    height, width = held.shape
    for c in range(EARLY):
        early[c * height : (c + 1) * height] = held[:, columns(c, width)]


def update0_kernel(n, *refs):
    parts, (raw, routes, gates, tokens, next_routes, upd, onward) = refs[:n], refs[n:]
    select = select_of(routes[0])
    select_next = select_of(next_routes[0])
    weight = slot_gates(select, routes[0], gates[0])
    fresh = (raw[...].astype(F32) + weight * summed(parts)).astype(BF16)
    old = pick(select_next, whole_block(tokens))
    onward[...] = merged(select_next, select, fresh, old)
    upd[...] = fresh


def grad_rows_kernel(bulk, routes, gates, cot, scaled):
    select = select_of(routes[1])
    values = pick(select, whole_block(bulk))
    cot[...] = values.astype(BF16)
    scaled[...] = (slot_gates(select, routes[1], gates[1]) * values).astype(BF16)


def update1_kernel(n, *refs):
    parts, (h, routes, gates, upd) = refs[:n], refs[n:]
    select = select_of(routes[1])
    weight = slot_gates(select, routes[1], gates[1])
    upd[...] = (h[...].astype(F32) + weight * summed(parts)).astype(BF16)


def enter1_kernel(h, scaled, _, __, out, ___):
    values = h[...].astype(F32)
    out[:PACKED] = (values * inv_rms_of(values)).astype(BF16)
    out[PACKED:] = scaled[...]


def state_grad(parts, h, c):
    total = summed(parts)
    values = h.astype(F32)
    inv = inv_rms_of(values)
    inner = mean_of(total * values)
    return (c.astype(F32) + inv * total - inv * inv * inv * values * inner).astype(BF16)


def grad1_kernel(n, *refs):
    parts, (h, cot, upd) = refs[:n], refs[n:]
    upd[...] = state_grad(parts, h[...], cot[...])


def enter0_kernel(upd1, next_routes, routes, gates, bulk, tokens, c0, out, rest, sem):
    step = tokens.shape[1] // PACK
    copy = pltpu.make_async_copy(tokens.at[:, pl.ds(EARLY * step, (PACK - EARLY) * step)], rest, sem)
    copy.start()
    select = select_of(routes[0])
    old = pick(select, whole_block(bulk))
    rows = merged(select, select_of(next_routes[0]), upd1[...], old)
    c0[...] = rows
    out[...] = (slot_gates(select, routes[0], gates[0]) * rows.astype(F32)).astype(BF16)
    copy.wait()


def finish_grad_kernel(n, *refs):
    parts, (h, c, routes, upd1, next_routes, bulk, out) = refs[:n], refs[n:]
    fresh = state_grad(parts, h[...], c[...])
    first, second = select_of(next_routes[0]), select_of(routes[0])
    hit1, hit2 = hit_rows(first), hit_rows(second)
    for chunk in range(PACK):
        k = columns(chunk, out.shape[1])
        out[:, k] = placed(chunk, bulk[:, k], first, hit1, upd1[...], second, hit2, fresh)


def finish_state_kernel(
    early, rest, upd0, prev2_routes, upd1, prev_routes, out, ins, outs, in_sems, out_sems
):
    height, width = out.shape
    fetches = []
    for chunk in range(PACK - EARLY):
        k = columns(chunk, width)
        fetches.append(pltpu.make_async_copy(rest.at[:, k], ins.at[chunk], in_sems.at[chunk]))
        fetches[-1].start()
    first, second = select_of(prev2_routes[0]), select_of(prev_routes[0])
    hit1, hit2 = hit_rows(first), hit_rows(second)
    rows1, rows2 = upd0[...], upd1[...]
    stores = []
    for chunk in range(PACK):
        if chunk < EARLY:
            old = early[chunk * height : (chunk + 1) * height]
        else:
            fetches[chunk - EARLY].wait()
            old = ins[chunk - EARLY]
        outs[chunk] = placed(chunk, old, first, hit1, rows1, second, hit2, rows2)
        k = columns(chunk, width)
        stores.append(pltpu.make_async_copy(outs.at[chunk], out.at[:, k], out_sems.at[chunk]))
        stores[-1].start()
    for store in stores:
        store.wait()


def silu_grads(pre_gate, pre_up, grad_act):
    sig = jax.nn.sigmoid(pre_gate)
    grad_gate = (grad_act * pre_up * sig * (1.0 + pre_gate * (1.0 - sig))).astype(BF16)
    grad_up = (grad_act * (pre_gate * sig)).astype(BF16)
    return grad_gate, grad_up


def gather_rows(blocks, first, unpacked, whole32, whole):
    width = whole.shape[1]
    used = len(blocks) * CAP
    if used < whole.shape[0]:
        whole32[used:] = jnp.zeros((whole.shape[0] - used, width), F32)
    for i, b in enumerate(blocks):
        unpacked[i] = b[first : first + PACKED].astype(F32)
        for c in range(PACK):
            whole32[i * CAP : (i + 1) * CAP, columns(c, width)] = unpacked[
                i, c * CAP : (c + 1) * CAP
            ]
    whole[...] = whole32[...].astype(BF16)


def spread_rows(value, c, n, held, unpacked):
    held[...] = value
    for i in range(n):
        unpacked[i, c * CAP : (c + 1) * CAP] = held[i * CAP : (i + 1) * CAP]


def forward_kernel(n, *refs):
    blocks, (gate, up, down) = refs[:n], refs[n : n + 3]
    x, pre_gate, pre_up, act, gate_v, up_v, down_v = refs[n + 3 : n + 10]
    parts = refs[n + 10 : 2 * n + 10]
    sems, unpacked, whole32, held = refs[2 * n + 10 :]
    width = gate.shape[0]
    fetches = []
    for c in range(PACK):
        k = columns(c, width)
        fetches.append(
            (
                pltpu.make_async_copy(gate.at[k], gate_v.at[k], sems.at[0, c]),
                pltpu.make_async_copy(up.at[k], up_v.at[k], sems.at[1, c]),
                pltpu.make_async_copy(down.at[:, k], down_v.at[:, k], sems.at[2, c]),
            )
        )
    for fetch_g, fetch_u, _ in fetches:
        fetch_g.start()
        fetch_u.start()
    for _, _, fetch_d in fetches:
        fetch_d.start()
    gather_rows(blocks, 0, unpacked, whole32, x)
    acc_g = jnp.zeros(pre_gate.shape, F32)
    acc_u = jnp.zeros(pre_up.shape, F32)
    for c, (fetch_g, fetch_u, _) in enumerate(fetches):
        k = columns(c, width)
        fetch_g.wait()
        acc_g = acc_g + dot(x[:, k], gate_v[k])
        fetch_u.wait()
        acc_u = acc_u + dot(x[:, k], up_v[k])
    pre_gate[...] = acc_g
    pre_up[...] = acc_u
    activated = (acc_g * jax.nn.sigmoid(acc_g) * acc_u).astype(BF16)
    act[...] = activated
    for c, (_, _, fetch_d) in enumerate(fetches):
        fetch_d.wait()
        value = dot(activated, down_v[:, columns(c, width)])
        spread_rows(value, c, n, held.at[c], unpacked)
    for i, p in enumerate(parts):
        p[...] = unpacked[i].astype(BF16)


def out_rows(act, down, held, unpacked, parts):
    n = len(parts)
    for c in range(PACK):
        value = dot(act, down[:, columns(c, down.shape[1])])
        spread_rows(value, c, n, held.at[c], unpacked)
    for i, p in enumerate(parts):
        p[...] = unpacked[i].astype(BF16)


def down_kernel(n, act, down, _, *refs):
    parts, (unpacked, held) = refs[:n], refs[n:]
    hidden, width = down.shape
    out_rows(act[:, 3 * width + hidden : 3 * width + 2 * hidden], down, held, unpacked, parts)


def back_rows(gg, gu, gate, up, held, unpacked, parts):
    n = len(parts)
    for c in range(PACK):
        k = columns(c, gate.shape[0])
        value = dot(gg, gate[k], 1, 1) + dot(gu, up[k], 1, 1)
        spread_rows(value, c, n, held.at[c], unpacked)
    for i, p in enumerate(parts):
        p[...] = unpacked[i].astype(BF16)


def tick1_kernel(n, *refs):
    blocks, (x0, act0, gate, up, down) = refs[:n], refs[n : n + 5]
    (kept,) = refs[n + 5 : n + 6]
    parts = refs[n + 6 : 2 * n + 6]
    unpacked, whole32, held, x, g = refs[2 * n + 6 :]
    gather_rows(blocks, 0, unpacked, whole32.at[0], x)
    gather_rows(blocks, PACKED, unpacked, whole32.at[1], g)
    width, hidden = gate.shape
    kept[:, :width] = x0[...]
    kept[:, width : 2 * width] = x[...]
    kept[:, 2 * width : 3 * width] = g[...]
    narrow = [slice(3 * width + i * hidden, 3 * width + (i + 1) * hidden) for i in range(4)]
    kept[:, narrow[0]] = act0[...]
    acc_g = dot(x[...], gate[...])
    acc_u = dot(x[...], up[...])
    acc_a = dot(g[...], down[...], 1, 1)
    gg, gu = silu_grads(acc_g, acc_u, acc_a)
    kept[:, narrow[1]] = (acc_g * jax.nn.sigmoid(acc_g) * acc_u).astype(BF16)
    kept[:, narrow[2]] = gg
    kept[:, narrow[3]] = gu
    back_rows(gg, gu, gate, up, held, unpacked, parts)


def tick0_kernel(n, *refs):
    blocks, (pre_gate, pre_up, gate, up, down) = refs[:n], refs[n : n + 5]
    (g_grad,) = refs[n + 5 : n + 6]
    parts = refs[n + 6 : 2 * n + 6]
    unpacked, whole32, held, g = refs[2 * n + 6 :]
    gather_rows(blocks, 0, unpacked, whole32, g)
    width, hidden = gate.shape
    g_grad[:, :width] = g[...]
    acc_a = dot(g[...], down[...], 1, 1)
    gg, gu = silu_grads(pre_gate[...], pre_up[...], acc_a)
    g_grad[:, width : width + hidden] = gg
    g_grad[:, width + hidden :] = gu
    back_rows(gg, gu, gate, up, held, unpacked, parts)


def whole_of(blocks):
    return jnp.concatenate([b.astype(F32) for b in blocks], axis=0).astype(BF16)


def turn_kernel(m, *refs):
    x0, x1, act0, act1 = (refs[i * m : (i + 1) * m] for i in range(4))
    x_t, act_t = refs[4 * m :]
    x_t[...] = whole_of([b[...] for b in x0 + x1]).T

    @pl.when(pl.program_id(0) == 0)
    def _():
        act_t[...] = whole_of([b[...] for b in act0 + act1]).T


def down_grad_kernel(m, act_t, *refs):
    g0, g1, (down_out,) = refs[:m], refs[m : 2 * m], refs[2 * m :]
    down_out[...] = dot(act_t[...], whole_of([b[...] for b in g0 + g1])).astype(BF16)


def input_grad_kernel(m, x_t, *refs):
    gates0, ups0, gates1, ups1 = (refs[i * m : (i + 1) * m] for i in range(4))
    gate_out, up_out, both = refs[4 * m :]
    hidden = gate_out.shape[1]

    @pl.when(pl.program_id(0) == 0)
    def _():
        both[:, :hidden] = whole_of([b[...] for b in gates0 + gates1])
        both[:, hidden:] = whole_of([b[...] for b in ups0 + ups1])

    gate_out[...] = dot(x_t[...], both[:, :hidden]).astype(BF16)
    up_out[...] = dot(x_t[...], both[:, hidden:]).astype(BF16)


def chunked_call(kernel, ins, outs, scratch=()):
    return pl.pallas_call(
        kernel,
        grid=(PACK,),
        out_shape=[jax.ShapeDtypeStruct(s, BF16) for s, _, _ in outs],
        in_specs=[pl.BlockSpec(block, index) for _, block, index in ins],
        out_specs=[pl.BlockSpec(block, index) for _, block, index in outs],
        scratch_shapes=list(scratch),
        compiler_params=pltpu.CompilerParams(vmem_limit_bytes=VMEM_SMALL),
        cost_estimate=pl.CostEstimate(flops=0, bytes_accessed=COST_BYTES, transcendentals=0),
    )(*(a for a, _, _ in ins))


def constant(at):
    return lambda c: (0, at)


def chunk_at(at):
    return lambda c: (0, at + c)


def turned(kept, width, hidden):
    m = len(kept)
    rows = kept[0].shape[0]
    step = width // PACK
    first = 3 * width // hidden
    ins = [(a, (rows, step), chunk_at(at)) for at in (0, PACK) for a in kept]
    ins += [(a, (rows, hidden), constant(at)) for at in (first, first + 1) for a in kept]
    outs = [
        ((width, 2 * m * rows), (step, 2 * m * rows), lambda c: (c, 0)),
        ((hidden, 2 * m * rows), (hidden, 2 * m * rows), lambda c: (0, 0)),
    ]
    return chunked_call(functools.partial(turn_kernel, m), ins, outs)


def down_grads(act_t, g_grad0, kept, width, hidden):
    rows = kept[0].shape[0]
    step = width // PACK
    ins = [(act_t, act_t.shape, constant(0))]
    ins += [(a, (rows, step), chunk_at(0)) for a in g_grad0]
    ins += [(a, (rows, step), chunk_at(2 * PACK)) for a in kept]
    outs = [((hidden, width), (hidden, step), chunk_at(0))]
    return chunked_call(functools.partial(down_grad_kernel, len(kept)), ins, outs)


def input_grads(x_t, g_grad0, kept, width, hidden):
    m = len(kept)
    rows = kept[0].shape[0]
    step = width // PACK
    first, second = width // hidden, 3 * width // hidden + 2
    ins = [(x_t, (step, x_t.shape[1]), lambda c: (c, 0))]
    ins += [(a, (rows, hidden), constant(at)) for at in (first, first + 1) for a in g_grad0]
    ins += [(a, (rows, hidden), constant(at)) for at in (second, second + 1) for a in kept]
    tall = ((width, hidden), (step, hidden), lambda c: (c, 0))
    scratch = [pltpu.VMEM((2 * m * rows, 2 * hidden), BF16)]
    return chunked_call(functools.partial(input_grad_kernel, m), ins, [tall, tall], scratch)


def from_group(block):
    n = lax.axis_size("expert")
    return [block] + [shifted(block, "expert", k) for k in range(1, n)]


def to_group(blocks):
    return [blocks[0]] + [shifted(b, "expert", -k) for k, b in enumerate(blocks) if k]


def copies_of(block):
    n = lax.axis_size("dp")
    return [block] + [shifted(block, "dp", k) for k in range(1, n)]


def shards(tokens, cotangent, w_gate, w_up, w_down, routes, gates):
    gate, up, down = w_gate[0], w_up[0], w_down[0]
    width, hidden = gate.shape
    step = width // PACK
    n = lax.axis_size("expert")
    rows = -(-n * CAP // 8) * 8
    routes = jnp.transpose(routes, (0, 2, 1))
    gates = jnp.transpose(gates, (0, 2, 1))
    one = ((PACKED, step), BF16)
    part = functools.partial
    unpacked = pltpu.VMEM((n, PACKED, step), F32)
    flat32 = pltpu.VMEM((rows, width), F32)
    held = pltpu.VMEM((PACK, rows, step), F32)
    flat = pltpu.VMEM((rows, width), BF16)
    wide = ((rows, width + 2 * hidden), BF16)
    dma = [pltpu.SemaphoreType.DMA]

    cot1_all = shifted(cotangent, "section", -1)
    next_routes = shifted(routes[1:], "section", -1)
    prev_routes = shifted(routes[1:], "section", 1)
    prev2_routes = shifted(routes[:1], "section", 2)

    raw0, normed0, early = call(
        first_rows_kernel,
        [pltpu.VMEM(*one), pltpu.VMEM(*one), pltpu.VMEM((EARLY * tokens.shape[0], step), BF16)],
        [tokens, routes],
        any_args=(0, 1),
        scratch=[
            pltpu.SemaphoreType.DMA((PACK + 1,)),
            pltpu.VMEM(tokens.shape, BF16),
            pltpu.VMEM(routes.shape, jnp.int32),
        ],
        vmem=VMEM_ALL,
    )
    early = shifted(early, "section", 2)
    blocks = from_group(normed0)
    x0, pre_gate0, pre_up0, act0, gate, up, down, *parts = call(
        part(forward_kernel, n),
        [((rows, width), BF16), ((rows, hidden), F32), ((rows, hidden), F32)]
        + [((rows, hidden), BF16)]
        + [pltpu.VMEM(a.shape, BF16) for a in (gate, up, down)]
        + [one] * n,
        [*blocks, gate, up, down],
        any_args=(n, n + 1, n + 2),
        scratch=[pltpu.SemaphoreType.DMA((3, PACK)), unpacked, flat32, held],
        vmem=VMEM_LOAD,
    )
    parts = to_group(parts)
    upd0, h1 = call(
        part(update0_kernel, n), [one, one], [*parts, raw0, routes, gates, tokens, next_routes]
    )
    h1 = shifted(h1, "section", 1)
    cot1, scaled1 = call(grad_rows_kernel, [one, one], [cot1_all, routes, gates])
    upd0 = shifted(upd0, "section", 2)

    enter1, cot1_all = call(
        enter1_kernel,
        [((2 * PACKED, step), BF16), (tokens.shape, BF16)],
        [h1, scaled1, cot1_all, early],
        any_args=(2, 3),
        any_outs=(1,),
        aliases={2: 1},
    )
    cot0_all = shifted(cot1_all, "section", -1)
    blocks = from_group(enter1)
    kept, *parts = call(
        part(tick1_kernel, n),
        [((rows, 3 * width + 4 * hidden), BF16)] + [one] * n,
        [*blocks, x0, act0, gate, up, down],
        scratch=[unpacked, pltpu.VMEM((2, rows, width), F32), held, flat, flat],
    )
    parts = to_group(parts)
    (upd1,) = call(
        part(grad1_kernel, n),
        [one],
        [*parts, h1, cot1],
    )
    upd1 = shifted(upd1, "section", -1)
    kept_all = copies_of(kept)

    c0, enter0, rest = call(
        enter0_kernel,
        [one, one, ((tokens.shape[0], width - EARLY * step), BF16)],
        [upd1, next_routes, routes, gates, cot0_all, tokens],
        any_args=(5,),
        any_outs=(2,),
        scratch=[pltpu.SemaphoreType.DMA],
    )
    rest = shifted(rest, "section", 2)
    blocks = from_group(enter0)
    g_grad0, *parts = call(
        part(tick0_kernel, n),
        [wide] + [one] * n,
        [*blocks, pre_gate0, pre_up0, gate, up, down],
        scratch=[unpacked, flat32, held, flat],
    )
    parts = to_group(parts)
    g_grad0_all = copies_of(g_grad0)
    (grad,) = call(
        part(finish_grad_kernel, n),
        [(tokens.shape, BF16)],
        [*parts, raw0, c0, routes, upd1, next_routes, cot0_all],
    )
    outs = call(
        part(down_kernel, n),
        [one] * n,
        [kept, down, g_grad0],
        any_args=(2,),
        scratch=[unpacked, held],
    )
    outs = to_group(outs)
    (last1,) = call(part(update1_kernel, n), [one], [*outs, h1, routes, gates])
    last1 = shifted(last1, "section", 1)
    x_t, act_t = turned(kept_all, width, hidden)
    (down_out,) = down_grads(act_t, g_grad0_all, kept_all, width, hidden)
    gate_out, up_out = input_grads(x_t, g_grad0_all, kept_all, width, hidden)
    chunks = pltpu.VMEM((PACK, tokens.shape[0], step), BF16)
    (state,) = call(
        finish_state_kernel,
        [(tokens.shape, BF16)],
        [early, rest, upd0, prev2_routes, last1, prev_routes],
        any_args=(1,),
        any_outs=(0,),
        scratch=[
            chunks,
            chunks,
            pltpu.SemaphoreType.DMA((PACK,)),
            pltpu.SemaphoreType.DMA((PACK,)),
        ],
    )
    return (grad, state, gate_out[None], up_out[None], down_out[None])


def solution(mesh):
    rows = P(("section", "expert", "dp"), None)
    slots = P(None, ("section", "expert", "dp"), None)
    cols = P("section", None, "expert")
    hidden = P("section", "expert", None)
    return jax.shard_map(
        shards,
        mesh=mesh,
        in_specs=(rows, rows, cols, cols, hidden, slots, slots),
        out_specs=(rows, rows, cols, cols, hidden),
        check_vma=False,
    )
```

```python
import functools

import jax
import jax.numpy as jnp
from jax import lax
from jax.experimental import pallas as pl
from jax.experimental.pallas import tpu as pltpu
from jax.sharding import PartitionSpec as P

CAP = 10
PACK = 8
PACKED = CAP * PACK
EPSILON = 1e-06
F32 = jnp.float32
BF16 = jnp.bfloat16
VMEM_SMALL = 24 * 1024 * 1024
VMEM_LOAD = 36 * 1024 * 1024
VMEM_ALL = 60 * 1024 * 1024
COST_BYTES = 1024
EARLY = 1


def shifted(block, axis, distance):
    size = lax.axis_size(axis)
    return lax.ppermute(block, axis, [((i - distance) % size, i) for i in range(size)])


def dot(a, b, ca=1, cb=0):
    return lax.dot_general(a, b, (((ca,), (cb,)), ((), ())), preferred_element_type=F32)


def call(
    kernel, outs, args, *, any_args=(), any_outs=(), scratch=(), vmem=VMEM_SMALL, aliases=None
):
    outs = [jax.ShapeDtypeStruct(*o) if isinstance(o, tuple) else o for o in outs]
    anywhere = pl.BlockSpec(memory_space=pl.ANY)
    near = pl.BlockSpec(memory_space=pltpu.VMEM)
    return pl.pallas_call(
        kernel,
        out_shape=outs,
        in_specs=[anywhere if i in any_args else near for i in range(len(args))],
        out_specs=[anywhere if i in any_outs else near for i in range(len(outs))],
        scratch_shapes=list(scratch),
        compiler_params=pltpu.CompilerParams(vmem_limit_bytes=vmem),
        cost_estimate=pl.CostEstimate(flops=0, bytes_accessed=COST_BYTES, transcendentals=0),
        input_output_aliases=aliases or {},
    )(*args)


def packed_index(shape, dim):
    place = lax.broadcasted_iota(jnp.int32, shape, dim).astype(F32)
    chunk = jnp.floor((place + 0.5) * (1.0 / CAP))
    return place - CAP * chunk, chunk


def select_of(routes):
    hits = (routes == 0).astype(F32)
    marked = jnp.sum(hits, axis=0, keepdims=True)
    rows = routes.shape[1]
    before = lax.broadcasted_iota(jnp.int32, (rows, rows), 0) < lax.broadcasted_iota(
        jnp.int32, (rows, rows), 1
    )
    wide = jnp.broadcast_to(marked, (PACKED, rows))
    places = dot(wide.astype(BF16), before.astype(F32).astype(BF16))
    slot, _ = packed_index((PACKED, rows), 0)
    return jnp.where((places == slot) & (wide > 0.5), 1.0, 0.0)


def slot_gates(select, routes, gates):
    weights = jnp.sum(jnp.where(routes == 0, gates, 0.0), axis=0, keepdims=True)
    return jnp.sum(select * weights, axis=1, keepdims=True)


def chunk_of(select, c):
    _, chunk = packed_index(select.shape, 0)
    return jnp.where(chunk == c, select, 0.0).astype(BF16)


def columns(c, width):
    return slice(c * (width // PACK), (c + 1) * (width // PACK))


def pick(select, pieces):
    total = None
    for block, (r0, r1, c0, c1) in pieces:
        width = block.shape[1] // (c1 - c0)
        for c in range(c0, c1):
            columns_here = slice((c - c0) * width, (c - c0 + 1) * width)
            part = dot(chunk_of(select[:, r0:r1], c), block[:, columns_here])
            total = part if total is None else total + part
    return total


def whole_block(block):
    return [(block, (0, block.shape[0], 0, PACK))]


def over_chunks(row_sums):
    slot_r, _ = packed_index((PACKED, PACKED), 0)
    slot_c, _ = packed_index((PACKED, PACKED), 1)
    same = jnp.where(slot_r == slot_c, 1.0, 0.0)
    wide = jnp.broadcast_to(row_sums, (PACKED, 128))
    return jnp.dot(
        same, wide, precision=lax.Precision.HIGHEST, preferred_element_type=F32
    )[:, :1]


def mean_of(values):
    return over_chunks(jnp.sum(values, axis=-1, keepdims=True)) * (1.0 / (PACK * values.shape[1]))


def inv_rms_of(values):
    return lax.rsqrt(mean_of(values * values) + EPSILON)


def merged(select_to, select_from, fresh, old):
    same = dot(select_to.astype(BF16), select_from.astype(BF16), 1, 1)
    _, chunk_r = packed_index(same.shape, 0)
    _, chunk_c = packed_index(same.shape, 1)
    same = jnp.where(chunk_r == chunk_c, same, 0.0)
    taken = jnp.sum(same, axis=1, keepdims=True)
    return jnp.where(taken > 0.5, dot(same.astype(BF16), fresh), old).astype(BF16)


def summed(parts):
    total = parts[0][...].astype(F32)
    for p in parts[1:]:
        total = total + p[...].astype(F32)
    return total


def hit_rows(select):
    ones = jnp.ones((PACKED, 128), BF16)
    return dot(chunk_of(select, 0), ones, 0, 0)[:, :1] > 0.5


def placed(c, old, select, hit, rows):
    return jnp.where(hit, dot(chunk_of(select, c), rows, 0, 0), old.astype(F32)).astype(BF16)


def start_rows(source, target, sems):
    copies = []
    for i in range(source.shape[0] // 16):
        r = pl.ds(16 * i, 16)
        copies.append(pltpu.make_async_copy(source.at[r], target.at[r], sems.at[i]))
        copies[-1].start()
    return copies


def first_rows_kernel(tokens, routes_far, raw, normed, early, sems, held, routes):
    fetch_routes = pltpu.make_async_copy(routes_far, routes, sems.at[sems.shape[0] - 1])
    fetch_routes.start()
    fetches = start_rows(tokens, held, sems)
    fetch_routes.wait()
    select = select_of(routes[0])
    for fetch in fetches:
        fetch.wait()
    values = pick(select, whole_block(held))
    raw[...] = values.astype(BF16)
    normed[...] = (values * inv_rms_of(values)).astype(BF16)
    height, width = held.shape
    for c in range(EARLY):
        early[c * height : (c + 1) * height] = held[:, columns(c, width)]


def update0_kernel(n, *refs):
    parts, (raw, routes, gates, tokens, next_routes, upd, onward, part) = refs[:n], refs[n:]
    select = select_of(routes[0])
    select_next = select_of(next_routes[0])
    weight = slot_gates(select, routes[0], gates[0])
    fresh = (raw[...].astype(F32) + weight * summed(parts)).astype(BF16)
    old = pick(select_next, whole_block(tokens))
    onward[...] = merged(select_next, select, fresh, old)
    upd[...] = fresh
    part[...] = jnp.zeros(part.shape, BF16)
    part[: EARLY * CAP] = fresh[: EARLY * CAP]


def merge_kernel(tokens, upd, routes, out):
    select = select_of(routes[0])
    hit = hit_rows(select)
    width = tokens.shape[1]
    for c in range(EARLY, PACK):
        value = placed(c, tokens[:, columns(c, width)], select, hit, upd[...])
        out[:, columns(c - EARLY, width)] = value


def release_kernel(_, __, ___, ____):
    pass


def grad_rows_kernel(bulk, routes, gates, cot, scaled):
    select = select_of(routes[1])
    values = pick(select, whole_block(bulk))
    cot[...] = values.astype(BF16)
    scaled[...] = (slot_gates(select, routes[1], gates[1]) * values).astype(BF16)


def update1_kernel(n, *refs):
    parts, (h, routes, gates, upd) = refs[:n], refs[n:]
    select = select_of(routes[1])
    weight = slot_gates(select, routes[1], gates[1])
    upd[...] = (h[...].astype(F32) + weight * summed(parts)).astype(BF16)


def enter1_kernel(h, scaled, _, __, ___, ____, out, _____):
    values = h[...].astype(F32)
    out[:PACKED] = (values * inv_rms_of(values)).astype(BF16)
    out[PACKED:] = scaled[...]


def state_grad(parts, h, c):
    total = summed(parts)
    values = h.astype(F32)
    inv = inv_rms_of(values)
    inner = mean_of(total * values)
    return (c.astype(F32) + inv * total - inv * inv * inv * values * inner).astype(BF16)


def grad1_kernel(n, *refs):
    parts, (h, cot, upd) = refs[:n], refs[n:]
    upd[...] = state_grad(parts, h[...], cot[...])


def enter0_kernel(upd1, next_routes, routes, gates, bulk, _, c0, out):
    select = select_of(routes[0])
    old = pick(select, whole_block(bulk))
    rows = merged(select, select_of(next_routes[0]), upd1[...], old)
    c0[...] = rows
    out[...] = (slot_gates(select, routes[0], gates[0]) * rows.astype(F32)).astype(BF16)


def finish_grad_kernel(n, *refs):
    parts, (h, c, routes, upd1, next_routes, bulk, out) = refs[:n], refs[n:]
    fresh = state_grad(parts, h[...], c[...])
    first, second = select_of(next_routes[0]), select_of(routes[0])
    hit1, hit2 = hit_rows(first), hit_rows(second)
    for chunk in range(PACK):
        k = columns(chunk, out.shape[1])
        value = placed(chunk, bulk[:, k], first, hit1, upd1[...])
        out[:, k] = placed(chunk, value, second, hit2, fresh)


def finish_state_kernel(
    early, rest, part, prev2_routes, upd1, prev_routes, out, ins, outs, in_sems, out_sems
):
    fetches = start_rows(rest, ins, in_sems)
    height, width = out.shape
    first, second = select_of(prev2_routes[0]), select_of(prev_routes[0])
    hit1, hit2 = hit_rows(first), hit_rows(second)
    for c in range(EARLY):
        old = early[c * height : (c + 1) * height]
        rows = jnp.concatenate(
            [part[...].astype(F32), jnp.zeros((PACKED - part.shape[0], part.shape[1]), F32)], axis=0
        )
        value = placed(c, old, first, hit1, rows.astype(BF16))
        outs[:, columns(c, width)] = placed(c, value, second, hit2, upd1[...])
    for fetch in fetches:
        fetch.wait()
    for c in range(EARLY, PACK):
        value = ins[:, columns(c - EARLY, width)]
        outs[:, columns(c, width)] = placed(c, value, second, hit2, upd1[...])
    for store in start_rows(outs, out, out_sems):
        store.wait()


def silu_grads(pre_gate, pre_up, grad_act):
    sig = jax.nn.sigmoid(pre_gate)
    grad_gate = (grad_act * pre_up * sig * (1.0 + pre_gate * (1.0 - sig))).astype(BF16)
    grad_up = (grad_act * (pre_gate * sig)).astype(BF16)
    return grad_gate, grad_up


def gather_rows(blocks, first, unpacked, whole32, whole):
    width = whole.shape[1]
    used = len(blocks) * CAP
    if used < whole.shape[0]:
        whole32[used:] = jnp.zeros((whole.shape[0] - used, width), F32)
    for i, b in enumerate(blocks):
        unpacked[i] = b[first : first + PACKED].astype(F32)
        for c in range(PACK):
            whole32[i * CAP : (i + 1) * CAP, columns(c, width)] = unpacked[
                i, c * CAP : (c + 1) * CAP
            ]
    whole[...] = whole32[...].astype(BF16)


def spread_rows(value, c, n, held, unpacked):
    held[...] = value
    for i in range(n):
        unpacked[i, c * CAP : (c + 1) * CAP] = held[i * CAP : (i + 1) * CAP]


def forward_kernel(n, *refs):
    blocks, (gate, up, down) = refs[:n], refs[n : n + 3]
    x, pre_gate, pre_up, act, gate_v, up_v, down_v = refs[n + 3 : n + 10]
    parts = refs[n + 10 : 2 * n + 10]
    sems, unpacked, whole32, held = refs[2 * n + 10 :]
    width = gate.shape[0]
    fetches = []
    for c in range(PACK):
        k = columns(c, width)
        fetches.append(
            (
                pltpu.make_async_copy(gate.at[k], gate_v.at[k], sems.at[0, c]),
                pltpu.make_async_copy(up.at[k], up_v.at[k], sems.at[1, c]),
                pltpu.make_async_copy(down.at[:, k], down_v.at[:, k], sems.at[2, c]),
            )
        )
    for fetch_g, fetch_u, _ in fetches:
        fetch_g.start()
        fetch_u.start()
    for _, _, fetch_d in fetches:
        fetch_d.start()
    gather_rows(blocks, 0, unpacked, whole32, x)
    acc_g = jnp.zeros(pre_gate.shape, F32)
    acc_u = jnp.zeros(pre_up.shape, F32)
    for c, (fetch_g, fetch_u, _) in enumerate(fetches):
        k = columns(c, width)
        fetch_g.wait()
        acc_g = acc_g + dot(x[:, k], gate_v[k])
        fetch_u.wait()
        acc_u = acc_u + dot(x[:, k], up_v[k])
    pre_gate[...] = acc_g
    pre_up[...] = acc_u
    activated = (acc_g * jax.nn.sigmoid(acc_g) * acc_u).astype(BF16)
    act[...] = activated
    for c, (_, _, fetch_d) in enumerate(fetches):
        fetch_d.wait()
        value = dot(activated, down_v[:, columns(c, width)])
        spread_rows(value, c, n, held.at[c], unpacked)
    for i, p in enumerate(parts):
        p[...] = unpacked[i].astype(BF16)


def out_rows(act, down, held, unpacked, parts):
    n = len(parts)
    for c in range(PACK):
        value = dot(act, down[:, columns(c, down.shape[1])])
        spread_rows(value, c, n, held.at[c], unpacked)
    for i, p in enumerate(parts):
        p[...] = unpacked[i].astype(BF16)


def down_kernel(n, act, down, _, *refs):
    parts, (unpacked, held) = refs[:n], refs[n:]
    hidden, width = down.shape
    out_rows(act[:, 3 * width + hidden : 3 * width + 2 * hidden], down, held, unpacked, parts)


def back_rows(gg, gu, gate, up, held, unpacked, parts):
    n = len(parts)
    for c in range(PACK):
        k = columns(c, gate.shape[0])
        value = dot(gg, gate[k], 1, 1) + dot(gu, up[k], 1, 1)
        spread_rows(value, c, n, held.at[c], unpacked)
    for i, p in enumerate(parts):
        p[...] = unpacked[i].astype(BF16)


def tick1_kernel(n, *refs):
    blocks, (x0, act0, gate, up, down) = refs[:n], refs[n : n + 5]
    (kept,) = refs[n + 5 : n + 6]
    parts = refs[n + 6 : 2 * n + 6]
    unpacked, whole32, held, x, g = refs[2 * n + 6 :]
    gather_rows(blocks, 0, unpacked, whole32.at[0], x)
    gather_rows(blocks, PACKED, unpacked, whole32.at[1], g)
    width, hidden = gate.shape
    kept[:, :width] = x0[...]
    kept[:, width : 2 * width] = x[...]
    kept[:, 2 * width : 3 * width] = g[...]
    narrow = [slice(3 * width + i * hidden, 3 * width + (i + 1) * hidden) for i in range(4)]
    kept[:, narrow[0]] = act0[...]
    acc_g = dot(x[...], gate[...])
    acc_u = dot(x[...], up[...])
    acc_a = dot(g[...], down[...], 1, 1)
    gg, gu = silu_grads(acc_g, acc_u, acc_a)
    kept[:, narrow[1]] = (acc_g * jax.nn.sigmoid(acc_g) * acc_u).astype(BF16)
    kept[:, narrow[2]] = gg
    kept[:, narrow[3]] = gu
    back_rows(gg, gu, gate, up, held, unpacked, parts)


def tick0_kernel(n, *refs):
    blocks, (pre_gate, pre_up, gate, up, down) = refs[:n], refs[n : n + 5]
    (g_grad,) = refs[n + 5 : n + 6]
    parts = refs[n + 6 : 2 * n + 6]
    unpacked, whole32, held, g = refs[2 * n + 6 :]
    gather_rows(blocks, 0, unpacked, whole32, g)
    width, hidden = gate.shape
    g_grad[:, :width] = g[...]
    acc_a = dot(g[...], down[...], 1, 1)
    gg, gu = silu_grads(pre_gate[...], pre_up[...], acc_a)
    g_grad[:, width : width + hidden] = gg
    g_grad[:, width + hidden :] = gu
    back_rows(gg, gu, gate, up, held, unpacked, parts)


def whole_of(blocks):
    return jnp.concatenate([b.astype(F32) for b in blocks], axis=0).astype(BF16)


def turn_kernel(m, *refs):
    x0, x1, act0, act1 = (refs[i * m : (i + 1) * m] for i in range(4))
    x_t, act_t = refs[4 * m :]
    x_t[...] = whole_of([b[...] for b in x0 + x1]).T

    @pl.when(pl.program_id(0) == 0)
    def _():
        act_t[...] = whole_of([b[...] for b in act0 + act1]).T


def down_grad_kernel(m, act_t, *refs):
    g0, g1, (down_out,) = refs[:m], refs[m : 2 * m], refs[2 * m :]
    down_out[...] = dot(act_t[...], whole_of([b[...] for b in g0 + g1])).astype(BF16)


def input_grad_kernel(m, x_t, *refs):
    gates0, ups0, gates1, ups1 = (refs[i * m : (i + 1) * m] for i in range(4))
    gate_out, up_out, both = refs[4 * m :]
    hidden = gate_out.shape[1]

    @pl.when(pl.program_id(0) == 0)
    def _():
        both[:, :hidden] = whole_of([b[...] for b in gates0 + gates1])
        both[:, hidden:] = whole_of([b[...] for b in ups0 + ups1])

    gate_out[...] = dot(x_t[...], both[:, :hidden]).astype(BF16)
    up_out[...] = dot(x_t[...], both[:, hidden:]).astype(BF16)


def chunked_call(kernel, ins, outs, scratch=()):
    return pl.pallas_call(
        kernel,
        grid=(PACK,),
        out_shape=[jax.ShapeDtypeStruct(s, BF16) for s, _, _ in outs],
        in_specs=[pl.BlockSpec(block, index) for _, block, index in ins],
        out_specs=[pl.BlockSpec(block, index) for _, block, index in outs],
        scratch_shapes=list(scratch),
        compiler_params=pltpu.CompilerParams(vmem_limit_bytes=VMEM_SMALL),
        cost_estimate=pl.CostEstimate(flops=0, bytes_accessed=COST_BYTES, transcendentals=0),
    )(*(a for a, _, _ in ins))


def constant(at):
    return lambda c: (0, at)


def chunk_at(at):
    return lambda c: (0, at + c)


def turned(kept, width, hidden):
    m = len(kept)
    rows = kept[0].shape[0]
    step = width // PACK
    first = 3 * width // hidden
    ins = [(a, (rows, step), chunk_at(at)) for at in (0, PACK) for a in kept]
    ins += [(a, (rows, hidden), constant(at)) for at in (first, first + 1) for a in kept]
    outs = [
        ((width, 2 * m * rows), (step, 2 * m * rows), lambda c: (c, 0)),
        ((hidden, 2 * m * rows), (hidden, 2 * m * rows), lambda c: (0, 0)),
    ]
    return chunked_call(functools.partial(turn_kernel, m), ins, outs)


def down_grads(act_t, g_grad0, kept, width, hidden):
    rows = kept[0].shape[0]
    step = width // PACK
    ins = [(act_t, act_t.shape, constant(0))]
    ins += [(a, (rows, step), chunk_at(0)) for a in g_grad0]
    ins += [(a, (rows, step), chunk_at(2 * PACK)) for a in kept]
    outs = [((hidden, width), (hidden, step), chunk_at(0))]
    return chunked_call(functools.partial(down_grad_kernel, len(kept)), ins, outs)


def input_grads(x_t, g_grad0, kept, width, hidden):
    m = len(kept)
    rows = kept[0].shape[0]
    step = width // PACK
    first, second = width // hidden, 3 * width // hidden + 2
    ins = [(x_t, (step, x_t.shape[1]), lambda c: (c, 0))]
    ins += [(a, (rows, hidden), constant(at)) for at in (first, first + 1) for a in g_grad0]
    ins += [(a, (rows, hidden), constant(at)) for at in (second, second + 1) for a in kept]
    tall = ((width, hidden), (step, hidden), lambda c: (c, 0))
    scratch = [pltpu.VMEM((2 * m * rows, 2 * hidden), BF16)]
    return chunked_call(functools.partial(input_grad_kernel, m), ins, [tall, tall], scratch)


def from_group(block):
    n = lax.axis_size("expert")
    return [block] + [shifted(block, "expert", k) for k in range(1, n)]


def to_group(blocks):
    return [blocks[0]] + [shifted(b, "expert", -k) for k, b in enumerate(blocks) if k]


def copies_of(block):
    n = lax.axis_size("dp")
    return [block] + [shifted(block, "dp", k) for k in range(1, n)]


def shards(tokens, cotangent, w_gate, w_up, w_down, routes, gates):
    gate, up, down = w_gate[0], w_up[0], w_down[0]
    width, hidden = gate.shape
    step = width // PACK
    n = lax.axis_size("expert")
    rows = -(-n * CAP // 8) * 8
    routes = jnp.transpose(routes, (0, 2, 1))
    gates = jnp.transpose(gates, (0, 2, 1))
    one = ((PACKED, step), BF16)
    part = functools.partial
    unpacked = pltpu.VMEM((n, PACKED, step), F32)
    flat32 = pltpu.VMEM((rows, width), F32)
    held = pltpu.VMEM((PACK, rows, step), F32)
    flat = pltpu.VMEM((rows, width), BF16)
    wide = ((rows, width + 2 * hidden), BF16)
    dma = [pltpu.SemaphoreType.DMA]

    cot1_all = shifted(cotangent, "section", -1)
    next_routes = shifted(routes[1:], "section", -1)
    prev_routes = shifted(routes[1:], "section", 1)
    prev2_routes = shifted(routes[:1], "section", 2)

    raw0, normed0, early = call(
        first_rows_kernel,
        [pltpu.VMEM(*one), pltpu.VMEM(*one), ((EARLY * tokens.shape[0], step), BF16)],
        [tokens, routes],
        any_args=(0, 1),
        scratch=[
            pltpu.SemaphoreType.DMA((tokens.shape[0] // 16 + 1,)),
            pltpu.VMEM(tokens.shape, BF16),
            pltpu.VMEM(routes.shape, jnp.int32),
        ],
        vmem=VMEM_ALL,
    )
    early = shifted(early, "section", 2)
    blocks = from_group(normed0)
    x0, pre_gate0, pre_up0, act0, gate, up, down, *parts = call(
        part(forward_kernel, n),
        [((rows, width), BF16), ((rows, hidden), F32), ((rows, hidden), F32)]
        + [((rows, hidden), BF16)]
        + [pltpu.VMEM(a.shape, BF16) for a in (gate, up, down)]
        + [one] * n,
        [*blocks, gate, up, down],
        any_args=(n, n + 1, n + 2),
        scratch=[pltpu.SemaphoreType.DMA((3, PACK)), unpacked, flat32, held],
        vmem=VMEM_LOAD,
    )
    parts = to_group(parts)
    few = -(-EARLY * CAP // 16) * 16
    upd0, h1, part0 = call(
        part(update0_kernel, n),
        [one, one, ((few, step), BF16)],
        [*parts, raw0, routes, gates, tokens, next_routes],
    )
    h1 = shifted(h1, "section", 1)
    cot1, scaled1 = call(grad_rows_kernel, [one, one], [cot1_all, routes, gates])
    part0 = shifted(part0, "section", 2)
    (rest,) = call(
        merge_kernel,
        [((tokens.shape[0], width - EARLY * step), BF16)],
        [tokens, upd0, routes],
    )

    enter1, cot1_all = call(
        enter1_kernel,
        [((2 * PACKED, step), BF16), (tokens.shape, BF16)],
        [h1, scaled1, cot1_all, early, prev_routes, prev2_routes],
        any_args=(2, 3, 4, 5),
        any_outs=(1,),
        aliases={2: 1},
    )
    cot0_all = shifted(cot1_all, "section", -1)
    blocks = from_group(enter1)
    kept, *parts = call(
        part(tick1_kernel, n),
        [((rows, 3 * width + 4 * hidden), BF16)] + [one] * n,
        [*blocks, x0, act0, gate, up, down],
        scratch=[unpacked, pltpu.VMEM((2, rows, width), F32), held, flat, flat],
    )
    parts = to_group(parts)
    (upd1,) = call(
        part(grad1_kernel, n),
        [one],
        [*parts, h1, cot1],
    )
    upd1 = shifted(upd1, "section", -1)
    kept_all = copies_of(kept)

    (rest,) = call(
        release_kernel,
        [((tokens.shape[0], width - EARLY * step), BF16)],
        [rest, cot0_all, upd1],
        any_args=(0, 1, 2),
        any_outs=(0,),
        aliases={0: 0},
    )
    c0, enter0 = call(
        enter0_kernel,
        [one, one],
        [upd1, next_routes, routes, gates, cot0_all, rest],
        any_args=(5,),
    )
    rest = shifted(rest, "section", 2)
    blocks = from_group(enter0)
    g_grad0, *parts = call(
        part(tick0_kernel, n),
        [wide] + [one] * n,
        [*blocks, pre_gate0, pre_up0, gate, up, down],
        scratch=[unpacked, flat32, held, flat],
    )
    parts = to_group(parts)
    g_grad0_all = copies_of(g_grad0)
    (grad,) = call(
        part(finish_grad_kernel, n),
        [(tokens.shape, BF16)],
        [*parts, raw0, c0, routes, upd1, next_routes, cot0_all],
    )
    outs = call(
        part(down_kernel, n),
        [one] * n,
        [kept, down, g_grad0],
        any_args=(2,),
        scratch=[unpacked, held],
    )
    outs = to_group(outs)
    (last1,) = call(part(update1_kernel, n), [one], [*outs, h1, routes, gates])
    last1 = shifted(last1, "section", 1)
    x_t, act_t = turned(kept_all, width, hidden)
    (down_out,) = down_grads(act_t, g_grad0_all, kept_all, width, hidden)
    gate_out, up_out = input_grads(x_t, g_grad0_all, kept_all, width, hidden)
    blocks16 = pltpu.SemaphoreType.DMA((tokens.shape[0] // 16,))
    (state,) = call(
        finish_state_kernel,
        [(tokens.shape, BF16)],
        [early, rest, part0, prev2_routes, last1, prev_routes],
        any_args=(1,),
        any_outs=(0,),
        scratch=[
            pltpu.VMEM(rest.shape, BF16),
            pltpu.VMEM(tokens.shape, BF16),
            blocks16,
            blocks16,
        ],
    )
    return (grad, state, gate_out[None], up_out[None], down_out[None])


def solution(mesh):
    rows = P(("section", "expert", "dp"), None)
    slots = P(None, ("section", "expert", "dp"), None)
    cols = P("section", None, "expert")
    hidden = P("section", "expert", None)
    return jax.shard_map(
        shards,
        mesh=mesh,
        in_specs=(rows, rows, cols, cols, hidden, slots, slots),
        out_specs=(rows, rows, cols, cols, hidden),
        check_vma=False,
    )
```

```python
import functools

import jax
import jax.numpy as jnp
from jax import lax
from jax.experimental import pallas as pl
from jax.experimental.pallas import tpu as pltpu
from jax.sharding import PartitionSpec as P

CAP = 10
PACK = 8
PACKED = CAP * PACK
EPSILON = 1e-06
F32 = jnp.float32
BF16 = jnp.bfloat16
VMEM_SMALL = 24 * 1024 * 1024
VMEM_LOAD = 36 * 1024 * 1024
VMEM_ALL = 60 * 1024 * 1024
COST_BYTES = 1024
EARLY = 1


def shifted(block, axis, distance):
    size = lax.axis_size(axis)
    return lax.ppermute(block, axis, [((i - distance) % size, i) for i in range(size)])


def dot(a, b, ca=1, cb=0):
    return lax.dot_general(a, b, (((ca,), (cb,)), ((), ())), preferred_element_type=F32)


def call(
    kernel, outs, args, *, any_args=(), any_outs=(), scratch=(), vmem=VMEM_SMALL, aliases=None
):
    outs = [jax.ShapeDtypeStruct(*o) if isinstance(o, tuple) else o for o in outs]
    anywhere = pl.BlockSpec(memory_space=pl.ANY)
    near = pl.BlockSpec(memory_space=pltpu.VMEM)
    return pl.pallas_call(
        kernel,
        out_shape=outs,
        in_specs=[anywhere if i in any_args else near for i in range(len(args))],
        out_specs=[anywhere if i in any_outs else near for i in range(len(outs))],
        scratch_shapes=list(scratch),
        compiler_params=pltpu.CompilerParams(vmem_limit_bytes=vmem),
        cost_estimate=pl.CostEstimate(flops=0, bytes_accessed=COST_BYTES, transcendentals=0),
        input_output_aliases=aliases or {},
    )(*args)


def packed_index(shape, dim):
    place = lax.broadcasted_iota(jnp.int32, shape, dim).astype(F32)
    chunk = jnp.floor((place + 0.5) * (1.0 / CAP))
    return place - CAP * chunk, chunk


def select_of(routes):
    hits = (routes == 0).astype(F32)
    marked = jnp.sum(hits, axis=0, keepdims=True)
    rows = routes.shape[1]
    before = lax.broadcasted_iota(jnp.int32, (rows, rows), 0) < lax.broadcasted_iota(
        jnp.int32, (rows, rows), 1
    )
    wide = jnp.broadcast_to(marked, (PACKED, rows))
    places = dot(wide.astype(BF16), before.astype(F32).astype(BF16))
    slot, _ = packed_index((PACKED, rows), 0)
    return jnp.where((places == slot) & (wide > 0.5), 1.0, 0.0)


def slot_gates(select, routes, gates):
    weights = jnp.sum(jnp.where(routes == 0, gates, 0.0), axis=0, keepdims=True)
    return jnp.sum(select * weights, axis=1, keepdims=True)


def chunk_of(select, c):
    _, chunk = packed_index(select.shape, 0)
    return jnp.where(chunk == c, select, 0.0).astype(BF16)


def columns(c, width):
    return slice(c * (width // PACK), (c + 1) * (width // PACK))


def pick(select, pieces):
    total = None
    for block, (r0, r1, c0, c1) in pieces:
        width = block.shape[1] // (c1 - c0)
        for c in range(c0, c1):
            columns_here = slice((c - c0) * width, (c - c0 + 1) * width)
            part = dot(chunk_of(select[:, r0:r1], c), block[:, columns_here])
            total = part if total is None else total + part
    return total


def whole_block(block):
    return [(block, (0, block.shape[0], 0, PACK))]


def over_chunks(row_sums):
    slot_r, _ = packed_index((PACKED, PACKED), 0)
    slot_c, _ = packed_index((PACKED, PACKED), 1)
    same = jnp.where(slot_r == slot_c, 1.0, 0.0)
    wide = jnp.broadcast_to(row_sums, (PACKED, 128))
    return jnp.dot(
        same, wide, precision=lax.Precision.HIGHEST, preferred_element_type=F32
    )[:, :1]


def mean_of(values):
    return over_chunks(jnp.sum(values, axis=-1, keepdims=True)) * (1.0 / (PACK * values.shape[1]))


def inv_rms_of(values):
    return lax.rsqrt(mean_of(values * values) + EPSILON)


def merged(select_to, select_from, fresh, old):
    same = dot(select_to.astype(BF16), select_from.astype(BF16), 1, 1)
    _, chunk_r = packed_index(same.shape, 0)
    _, chunk_c = packed_index(same.shape, 1)
    same = jnp.where(chunk_r == chunk_c, same, 0.0)
    taken = jnp.sum(same, axis=1, keepdims=True)
    return jnp.where(taken > 0.5, dot(same.astype(BF16), fresh), old).astype(BF16)


def summed(parts):
    total = parts[0][...].astype(F32)
    for p in parts[1:]:
        total = total + p[...].astype(F32)
    return total


def hit_rows(select):
    ones = jnp.ones((PACKED, 128), BF16)
    return dot(chunk_of(select, 0), ones, 0, 0)[:, :1] > 0.5


def placed(c, old, select, hit, rows):
    return jnp.where(hit, dot(chunk_of(select, c), rows, 0, 0), old.astype(F32)).astype(BF16)


def start_rows(source, target, sems):
    copies = []
    for i in range(source.shape[0] // 16):
        r = pl.ds(16 * i, 16)
        copies.append(pltpu.make_async_copy(source.at[r], target.at[r], sems.at[i]))
        copies[-1].start()
    return copies


def first_rows_kernel(tokens, routes_far, raw, normed, early, sems, held, routes):
    fetch_routes = pltpu.make_async_copy(routes_far, routes, sems.at[sems.shape[0] - 1])
    fetch_routes.start()
    fetches = start_rows(tokens, held, sems)
    fetch_routes.wait()
    select = select_of(routes[0])
    for fetch in fetches:
        fetch.wait()
    values = pick(select, whole_block(held))
    raw[...] = values.astype(BF16)
    normed[...] = (values * inv_rms_of(values)).astype(BF16)
    height, width = held.shape
    for c in range(EARLY):
        early[c * height : (c + 1) * height] = held[:, columns(c, width)]


def update0_kernel(n, *refs):
    parts, (raw, routes, gates, tokens, next_routes, upd, onward, part) = refs[:n], refs[n:]
    select = select_of(routes[0])
    select_next = select_of(next_routes[0])
    weight = slot_gates(select, routes[0], gates[0])
    fresh = (raw[...].astype(F32) + weight * summed(parts)).astype(BF16)
    old = pick(select_next, whole_block(tokens))
    onward[...] = merged(select_next, select, fresh, old)
    upd[...] = fresh
    part[...] = jnp.zeros(part.shape, BF16)
    part[: EARLY * CAP] = fresh[: EARLY * CAP]


def merge_kernel(tokens, upd, routes, out):
    select = select_of(routes[0])
    hit = hit_rows(select)
    width = tokens.shape[1]
    for c in range(EARLY, PACK):
        value = placed(c, tokens[:, columns(c, width)], select, hit, upd[...])
        out[:, columns(c - EARLY, width)] = value


def release_kernel(_, __, ___, ____):
    pass


def grad_rows_kernel(bulk, routes, gates, cot, scaled):
    select = select_of(routes[1])
    values = pick(select, whole_block(bulk))
    cot[...] = values.astype(BF16)
    scaled[...] = (slot_gates(select, routes[1], gates[1]) * values).astype(BF16)


def update1_kernel(n, *refs):
    parts, (h, routes, gates, upd) = refs[:n], refs[n:]
    select = select_of(routes[1])
    weight = slot_gates(select, routes[1], gates[1])
    upd[...] = (h[...].astype(F32) + weight * summed(parts)).astype(BF16)


def enter1_kernel(h, scaled, *refs):
    out = refs[-2]
    values = h[...].astype(F32)
    out[:PACKED] = (values * inv_rms_of(values)).astype(BF16)
    out[PACKED:] = scaled[...]


def state_grad(parts, h, c):
    total = summed(parts)
    values = h.astype(F32)
    inv = inv_rms_of(values)
    inner = mean_of(total * values)
    return (c.astype(F32) + inv * total - inv * inv * inv * values * inner).astype(BF16)


def grad1_kernel(n, *refs):
    parts, (h, cot, upd) = refs[:n], refs[n:]
    upd[...] = state_grad(parts, h[...], cot[...])


def enter0_kernel(upd1, next_routes, routes, gates, bulk, _, c0, out):
    select = select_of(routes[0])
    old = pick(select, whole_block(bulk))
    rows = merged(select, select_of(next_routes[0]), upd1[...], old)
    c0[...] = rows
    out[...] = (slot_gates(select, routes[0], gates[0]) * rows.astype(F32)).astype(BF16)


def finish_grad_kernel(n, *refs):
    parts, (h, c, routes, upd1, next_routes, bulk, out) = refs[:n], refs[n:]
    fresh = state_grad(parts, h[...], c[...])
    first, second = select_of(next_routes[0]), select_of(routes[0])
    hit1, hit2 = hit_rows(first), hit_rows(second)
    for chunk in range(PACK):
        k = columns(chunk, out.shape[1])
        value = placed(chunk, bulk[:, k], first, hit1, upd1[...])
        out[:, k] = placed(chunk, value, second, hit2, fresh)


def finish_state_kernel(early, rest, part, prev2_routes, upd1, prev_routes, out, outs, sems):
    height, width = out.shape
    first, second = select_of(prev2_routes[0]), select_of(prev_routes[0])
    hit1, hit2 = hit_rows(first), hit_rows(second)
    rows = jnp.concatenate(
        [part[...].astype(F32), jnp.zeros((PACKED - part.shape[0], part.shape[1]), F32)], axis=0
    )
    for c in range(PACK):
        if c < EARLY:
            old = early[c * height : (c + 1) * height]
            value = placed(c, old, first, hit1, rows.astype(BF16))
        else:
            value = rest[:, columns(c - EARLY, width)]
        outs[:, columns(c, width)] = placed(c, value, second, hit2, upd1[...])
    for store in start_rows(outs, out, sems):
        store.wait()


def silu_grads(pre_gate, pre_up, grad_act):
    sig = jax.nn.sigmoid(pre_gate)
    grad_gate = (grad_act * pre_up * sig * (1.0 + pre_gate * (1.0 - sig))).astype(BF16)
    grad_up = (grad_act * (pre_gate * sig)).astype(BF16)
    return grad_gate, grad_up


def gather_rows(blocks, first, unpacked, whole32, whole):
    width = whole.shape[1]
    used = len(blocks) * CAP
    if used < whole.shape[0]:
        whole32[used:] = jnp.zeros((whole.shape[0] - used, width), F32)
    for i, b in enumerate(blocks):
        unpacked[i] = b[first : first + PACKED].astype(F32)
        for c in range(PACK):
            whole32[i * CAP : (i + 1) * CAP, columns(c, width)] = unpacked[
                i, c * CAP : (c + 1) * CAP
            ]
    whole[...] = whole32[...].astype(BF16)


def spread_rows(value, c, n, held, unpacked):
    held[...] = value
    for i in range(n):
        unpacked[i, c * CAP : (c + 1) * CAP] = held[i * CAP : (i + 1) * CAP]


def forward_kernel(n, *refs):
    blocks, (gate, up, down) = refs[:n], refs[n : n + 3]
    x, pre_gate, pre_up, act, gate_v, up_v, down_v = refs[n + 3 : n + 10]
    parts = refs[n + 10 : 2 * n + 10]
    sems, unpacked, whole32, held = refs[2 * n + 10 :]
    width = gate.shape[0]
    fetches = []
    for c in range(PACK):
        k = columns(c, width)
        fetches.append(
            (
                pltpu.make_async_copy(gate.at[k], gate_v.at[k], sems.at[0, c]),
                pltpu.make_async_copy(up.at[k], up_v.at[k], sems.at[1, c]),
                pltpu.make_async_copy(down.at[:, k], down_v.at[:, k], sems.at[2, c]),
            )
        )
    for fetch_g, fetch_u, _ in fetches:
        fetch_g.start()
        fetch_u.start()
    for _, _, fetch_d in fetches:
        fetch_d.start()
    gather_rows(blocks, 0, unpacked, whole32, x)
    acc_g = jnp.zeros(pre_gate.shape, F32)
    acc_u = jnp.zeros(pre_up.shape, F32)
    for c, (fetch_g, fetch_u, _) in enumerate(fetches):
        k = columns(c, width)
        fetch_g.wait()
        acc_g = acc_g + dot(x[:, k], gate_v[k])
        fetch_u.wait()
        acc_u = acc_u + dot(x[:, k], up_v[k])
    pre_gate[...] = acc_g
    pre_up[...] = acc_u
    activated = (acc_g * jax.nn.sigmoid(acc_g) * acc_u).astype(BF16)
    act[...] = activated
    for c, (_, _, fetch_d) in enumerate(fetches):
        fetch_d.wait()
        value = dot(activated, down_v[:, columns(c, width)])
        spread_rows(value, c, n, held.at[c], unpacked)
    for i, p in enumerate(parts):
        p[...] = unpacked[i].astype(BF16)


def out_rows(act, down, held, unpacked, parts):
    n = len(parts)
    for c in range(PACK):
        value = dot(act, down[:, columns(c, down.shape[1])])
        spread_rows(value, c, n, held.at[c], unpacked)
    for i, p in enumerate(parts):
        p[...] = unpacked[i].astype(BF16)


def down_kernel(n, act, down, _, *refs):
    parts, (unpacked, held) = refs[:n], refs[n:]
    hidden, width = down.shape
    out_rows(act[:, 3 * width + hidden : 3 * width + 2 * hidden], down, held, unpacked, parts)


def back_rows(gg, gu, gate, up, held, unpacked, parts):
    n = len(parts)
    for c in range(PACK):
        k = columns(c, gate.shape[0])
        value = dot(gg, gate[k], 1, 1) + dot(gu, up[k], 1, 1)
        spread_rows(value, c, n, held.at[c], unpacked)
    for i, p in enumerate(parts):
        p[...] = unpacked[i].astype(BF16)


def tick1_kernel(n, *refs):
    blocks, (x0, act0, gate, up, down) = refs[:n], refs[n : n + 5]
    (kept,) = refs[n + 5 : n + 6]
    parts = refs[n + 6 : 2 * n + 6]
    unpacked, whole32, held, x, g = refs[2 * n + 6 :]
    gather_rows(blocks, 0, unpacked, whole32.at[0], x)
    gather_rows(blocks, PACKED, unpacked, whole32.at[1], g)
    width, hidden = gate.shape
    kept[:, :width] = x0[...]
    kept[:, width : 2 * width] = x[...]
    kept[:, 2 * width : 3 * width] = g[...]
    narrow = [slice(3 * width + i * hidden, 3 * width + (i + 1) * hidden) for i in range(4)]
    kept[:, narrow[0]] = act0[...]
    acc_g = dot(x[...], gate[...])
    acc_u = dot(x[...], up[...])
    acc_a = dot(g[...], down[...], 1, 1)
    gg, gu = silu_grads(acc_g, acc_u, acc_a)
    kept[:, narrow[1]] = (acc_g * jax.nn.sigmoid(acc_g) * acc_u).astype(BF16)
    kept[:, narrow[2]] = gg
    kept[:, narrow[3]] = gu
    back_rows(gg, gu, gate, up, held, unpacked, parts)


def tick0_kernel(n, *refs):
    blocks, (pre_gate, pre_up, gate, up, down) = refs[:n], refs[n : n + 5]
    (g_grad,) = refs[n + 5 : n + 6]
    parts = refs[n + 6 : 2 * n + 6]
    unpacked, whole32, held, g = refs[2 * n + 6 :]
    gather_rows(blocks, 0, unpacked, whole32, g)
    width, hidden = gate.shape
    g_grad[:, :width] = g[...]
    acc_a = dot(g[...], down[...], 1, 1)
    gg, gu = silu_grads(pre_gate[...], pre_up[...], acc_a)
    g_grad[:, width : width + hidden] = gg
    g_grad[:, width + hidden :] = gu
    back_rows(gg, gu, gate, up, held, unpacked, parts)


def whole_of(blocks):
    return jnp.concatenate([b.astype(F32) for b in blocks], axis=0).astype(BF16)


def turn_kernel(m, *refs):
    x0, x1, act0, act1 = (refs[i * m : (i + 1) * m] for i in range(4))
    x_t, act_t = refs[4 * m :]
    x_t[...] = whole_of([b[...] for b in x0 + x1]).T

    @pl.when(pl.program_id(0) == 0)
    def _():
        act_t[...] = whole_of([b[...] for b in act0 + act1]).T


def down_grad_kernel(m, act_t, *refs):
    g0, g1, (down_out, both) = refs[:m], refs[m : 2 * m], refs[2 * m :]

    @pl.when(pl.program_id(0) == 0)
    def _():
        both[...] = whole_of([b[...] for b in g0 + g1])

    for c in range(PACK):
        k = columns(c, both.shape[1])
        down_out[:, k] = dot(act_t[...], both[:, k]).astype(BF16)


def input_grad_kernel(m, x_t, *refs):
    gates0, ups0, gates1, ups1 = (refs[i * m : (i + 1) * m] for i in range(4))
    gate_out, up_out, both = refs[4 * m :]
    hidden = gate_out.shape[1]

    @pl.when(pl.program_id(0) == 0)
    def _():
        both[:, :hidden] = whole_of([b[...] for b in gates0 + gates1])
        both[:, hidden:] = whole_of([b[...] for b in ups0 + ups1])

    gate_out[...] = dot(x_t[...], both[:, :hidden]).astype(BF16)
    up_out[...] = dot(x_t[...], both[:, hidden:]).astype(BF16)


def chunked_call(kernel, ins, outs, scratch=(), steps=PACK):
    return pl.pallas_call(
        kernel,
        grid=(steps,),
        out_shape=[jax.ShapeDtypeStruct(s, BF16) for s, _, _ in outs],
        in_specs=[pl.BlockSpec(block, index) for _, block, index in ins],
        out_specs=[pl.BlockSpec(block, index) for _, block, index in outs],
        scratch_shapes=list(scratch),
        compiler_params=pltpu.CompilerParams(vmem_limit_bytes=VMEM_SMALL),
        cost_estimate=pl.CostEstimate(flops=0, bytes_accessed=COST_BYTES, transcendentals=0),
    )(*(a for a, _, _ in ins))


def constant(at):
    return lambda c: (0, at)


def chunk_at(at):
    return lambda c: (0, at + c)


def turned(kept, width, hidden):
    m = len(kept)
    rows = kept[0].shape[0]
    step = width // PACK
    first = 3 * width // hidden
    ins = [(a, (rows, step), chunk_at(at)) for at in (0, PACK) for a in kept]
    ins += [(a, (rows, hidden), constant(at)) for at in (first, first + 1) for a in kept]
    outs = [
        ((width, 2 * m * rows), (step, 2 * m * rows), lambda c: (c, 0)),
        ((hidden, 2 * m * rows), (hidden, 2 * m * rows), lambda c: (0, 0)),
    ]
    return chunked_call(functools.partial(turn_kernel, m), ins, outs)


def down_grads(act_t, g_grad0, kept, width, hidden):
    m = len(kept)
    rows = kept[0].shape[0]
    block = max(hidden // 4, 16)
    ins = [(act_t, (block, act_t.shape[1]), lambda c: (c, 0))]
    ins += [(a, (rows, width), constant(0)) for a in g_grad0]
    ins += [(a, (rows, width), constant(2)) for a in kept]
    outs = [((hidden, width), (block, width), lambda c: (c, 0))]
    scratch = [pltpu.VMEM((2 * m * rows, width), BF16)]
    kernel = functools.partial(down_grad_kernel, m)
    return chunked_call(kernel, ins, outs, scratch, hidden // block)


def input_grads(x_t, g_grad0, kept, width, hidden):
    m = len(kept)
    rows = kept[0].shape[0]
    step = width // PACK
    first, second = width // hidden, 3 * width // hidden + 2
    ins = [(x_t, (step, x_t.shape[1]), lambda c: (c, 0))]
    ins += [(a, (rows, hidden), constant(at)) for at in (first, first + 1) for a in g_grad0]
    ins += [(a, (rows, hidden), constant(at)) for at in (second, second + 1) for a in kept]
    tall = ((width, hidden), (step, hidden), lambda c: (c, 0))
    scratch = [pltpu.VMEM((2 * m * rows, 2 * hidden), BF16)]
    return chunked_call(functools.partial(input_grad_kernel, m), ins, [tall, tall], scratch)


def from_group(block):
    n = lax.axis_size("expert")
    return [block] + [shifted(block, "expert", k) for k in range(1, n)]


def to_group(blocks):
    return [blocks[0]] + [shifted(b, "expert", -k) for k, b in enumerate(blocks) if k]


def copies_of(block):
    n = lax.axis_size("dp")
    return [block] + [shifted(block, "dp", k) for k in range(1, n)]


def shards(tokens, cotangent, w_gate, w_up, w_down, routes, gates):
    gate, up, down = w_gate[0], w_up[0], w_down[0]
    width, hidden = gate.shape
    step = width // PACK
    n = lax.axis_size("expert")
    rows = -(-n * CAP // 8) * 8
    routes = jnp.transpose(routes, (0, 2, 1))
    gates = jnp.transpose(gates, (0, 2, 1))
    one = ((PACKED, step), BF16)
    part = functools.partial
    unpacked = pltpu.VMEM((n, PACKED, step), F32)
    flat32 = pltpu.VMEM((rows, width), F32)
    held = pltpu.VMEM((PACK, rows, step), F32)
    flat = pltpu.VMEM((rows, width), BF16)
    wide = ((rows, width + 2 * hidden), BF16)
    dma = [pltpu.SemaphoreType.DMA]

    cot1_all = shifted(cotangent, "section", -1)
    next_routes = shifted(routes[1:], "section", -1)
    prev_routes = shifted(routes[1:], "section", 1)
    prev2_routes = shifted(routes[:1], "section", 2)

    raw0, normed0, early = call(
        first_rows_kernel,
        [pltpu.VMEM(*one), pltpu.VMEM(*one), ((EARLY * tokens.shape[0], step), BF16)],
        [tokens, routes],
        any_args=(0, 1),
        scratch=[
            pltpu.SemaphoreType.DMA((tokens.shape[0] // 16 + 1,)),
            pltpu.VMEM(tokens.shape, BF16),
            pltpu.VMEM(routes.shape, jnp.int32),
        ],
        vmem=VMEM_ALL,
    )
    early = shifted(early, "section", 2)
    blocks = from_group(normed0)
    x0, pre_gate0, pre_up0, act0, gate, up, down, *parts = call(
        part(forward_kernel, n),
        [((rows, width), BF16), ((rows, hidden), F32), ((rows, hidden), F32)]
        + [((rows, hidden), BF16)]
        + [pltpu.VMEM(a.shape, BF16) for a in (gate, up, down)]
        + [one] * n,
        [*blocks, gate, up, down],
        any_args=(n, n + 1, n + 2),
        scratch=[pltpu.SemaphoreType.DMA((3, PACK)), unpacked, flat32, held],
        vmem=VMEM_LOAD,
    )
    parts = to_group(parts)
    few = -(-EARLY * CAP // 16) * 16
    upd0, h1, part0 = call(
        part(update0_kernel, n),
        [one, one, ((few, step), BF16)],
        [*parts, raw0, routes, gates, tokens, next_routes],
    )
    h1 = shifted(h1, "section", 1)
    cot1, scaled1 = call(grad_rows_kernel, [one, one], [cot1_all, routes, gates])
    part0 = shifted(part0, "section", 2)
    (rest,) = call(
        merge_kernel,
        [((tokens.shape[0], width - EARLY * step), BF16)],
        [tokens, upd0, routes],
    )

    enter1, cot1_all = call(
        enter1_kernel,
        [((2 * PACKED, step), BF16), (tokens.shape, BF16)],
        [h1, scaled1, cot1_all, early, prev_routes, prev2_routes, part0],
        any_args=(2, 3, 4, 5, 6),
        any_outs=(1,),
        aliases={2: 1},
    )
    cot0_all = shifted(cot1_all, "section", -1)
    blocks = from_group(enter1)
    kept, *parts = call(
        part(tick1_kernel, n),
        [((rows, 3 * width + 4 * hidden), BF16)] + [one] * n,
        [*blocks, x0, act0, gate, up, down],
        scratch=[unpacked, pltpu.VMEM((2, rows, width), F32), held, flat, flat],
    )
    parts = to_group(parts)
    (upd1,) = call(
        part(grad1_kernel, n),
        [one],
        [*parts, h1, cot1],
    )
    upd1 = shifted(upd1, "section", -1)
    kept_all = copies_of(kept)

    (rest,) = call(
        release_kernel,
        [((tokens.shape[0], width - EARLY * step), BF16)],
        [rest, cot0_all, upd1],
        any_args=(0, 1, 2),
        any_outs=(0,),
        aliases={0: 0},
    )
    c0, enter0 = call(
        enter0_kernel,
        [one, one],
        [upd1, next_routes, routes, gates, cot0_all, rest],
        any_args=(5,),
    )
    rest = shifted(rest, "section", 2)
    blocks = from_group(enter0)
    g_grad0, *parts = call(
        part(tick0_kernel, n),
        [wide] + [one] * n,
        [*blocks, pre_gate0, pre_up0, gate, up, down],
        scratch=[unpacked, flat32, held, flat],
    )
    parts = to_group(parts)
    g_grad0_all = copies_of(g_grad0)
    (grad,) = call(
        part(finish_grad_kernel, n),
        [(tokens.shape, BF16)],
        [*parts, raw0, c0, routes, upd1, next_routes, cot0_all],
    )
    outs = call(
        part(down_kernel, n),
        [one] * n,
        [kept, down, g_grad0],
        any_args=(2,),
        scratch=[unpacked, held],
    )
    outs = to_group(outs)
    (last1,) = call(part(update1_kernel, n), [one], [*outs, h1, routes, gates])
    last1 = shifted(last1, "section", 1)
    x_t, act_t = turned(kept_all, width, hidden)
    (down_out,) = down_grads(act_t, g_grad0_all, kept_all, width, hidden)
    gate_out, up_out = input_grads(x_t, g_grad0_all, kept_all, width, hidden)
    (state,) = call(
        finish_state_kernel,
        [(tokens.shape, BF16)],
        [early, rest, part0, prev2_routes, last1, prev_routes],
        any_outs=(0,),
        scratch=[
            pltpu.VMEM(tokens.shape, BF16),
            pltpu.SemaphoreType.DMA((tokens.shape[0] // 16,)),
        ],
    )
    return (grad, state, gate_out[None], up_out[None], down_out[None])


def solution(mesh):
    rows = P(("section", "expert", "dp"), None)
    slots = P(None, ("section", "expert", "dp"), None)
    cols = P("section", None, "expert")
    hidden = P("section", "expert", None)
    return jax.shard_map(
        shards,
        mesh=mesh,
        in_specs=(rows, rows, cols, cols, hidden, slots, slots),
        out_specs=(rows, rows, cols, cols, hidden),
        check_vma=False,
    )
```

```python
import functools

import jax
import jax.numpy as jnp
from jax import lax
from jax.experimental import pallas as pl
from jax.experimental.pallas import tpu as pltpu
from jax.sharding import PartitionSpec as P

CAP = 10
PACK = 8
PACKED = CAP * PACK
EPSILON = 1e-06
F32 = jnp.float32
BF16 = jnp.bfloat16
VMEM_SMALL = 24 * 1024 * 1024
VMEM_LOAD = 36 * 1024 * 1024
VMEM_ALL = 60 * 1024 * 1024
COST_BYTES = 1024
TOP = 4
TAIL = 16
EARLY = 1


def shifted(block, axis, distance):
    size = lax.axis_size(axis)
    return lax.ppermute(block, axis, [((i - distance) % size, i) for i in range(size)])


def dot(a, b, ca=1, cb=0):
    return lax.dot_general(a, b, (((ca,), (cb,)), ((), ())), preferred_element_type=F32)


def call(
    kernel, outs, args, *, any_args=(), any_outs=(), scratch=(), vmem=VMEM_SMALL, aliases=None
):
    outs = [jax.ShapeDtypeStruct(*o) if isinstance(o, tuple) else o for o in outs]
    anywhere = pl.BlockSpec(memory_space=pl.ANY)
    near = pl.BlockSpec(memory_space=pltpu.VMEM)
    return pl.pallas_call(
        kernel,
        out_shape=outs,
        in_specs=[anywhere if i in any_args else near for i in range(len(args))],
        out_specs=[anywhere if i in any_outs else near for i in range(len(outs))],
        scratch_shapes=list(scratch),
        compiler_params=pltpu.CompilerParams(vmem_limit_bytes=vmem),
        cost_estimate=pl.CostEstimate(flops=0, bytes_accessed=COST_BYTES, transcendentals=0),
        input_output_aliases=aliases or {},
    )(*args)


def packed_index(shape, dim):
    place = lax.broadcasted_iota(jnp.int32, shape, dim).astype(F32)
    chunk = jnp.floor((place + 0.5) * (1.0 / CAP))
    return place - CAP * chunk, chunk


def select_of(routes):
    hits = (routes == 0).astype(F32)
    marked = jnp.sum(hits, axis=0, keepdims=True)
    rows = routes.shape[1]
    before = lax.broadcasted_iota(jnp.int32, (rows, rows), 0) < lax.broadcasted_iota(
        jnp.int32, (rows, rows), 1
    )
    wide = jnp.broadcast_to(marked, (PACKED, rows))
    places = dot(wide.astype(BF16), before.astype(F32).astype(BF16))
    slot, _ = packed_index((PACKED, rows), 0)
    return jnp.where((places == slot) & (wide > 0.5), 1.0, 0.0)


def slot_gates(select, routes, gates):
    weights = jnp.sum(jnp.where(routes == 0, gates, 0.0), axis=0, keepdims=True)
    return jnp.sum(select * weights, axis=1, keepdims=True)


def chunk_of(select, c):
    _, chunk = packed_index(select.shape, 0)
    return jnp.where(chunk == c, select, 0.0).astype(BF16)


def columns(c, width):
    return slice(c * (width // PACK), (c + 1) * (width // PACK))


def pick(select, pieces):
    total = None
    for block, (r0, r1, c0, c1) in pieces:
        width = block.shape[1] // (c1 - c0)
        for c in range(c0, c1):
            columns_here = slice((c - c0) * width, (c - c0 + 1) * width)
            part = dot(chunk_of(select[:, r0:r1], c), block[:, columns_here])
            total = part if total is None else total + part
    return total


def whole_block(block):
    return [(block, (0, block.shape[0], 0, PACK))]


def over_chunks(row_sums):
    slot_r, _ = packed_index((PACKED, PACKED), 0)
    slot_c, _ = packed_index((PACKED, PACKED), 1)
    same = jnp.where(slot_r == slot_c, 1.0, 0.0)
    wide = jnp.broadcast_to(row_sums, (PACKED, 128))
    return jnp.dot(
        same, wide, precision=lax.Precision.HIGHEST, preferred_element_type=F32
    )[:, :1]


def mean_of(values):
    return over_chunks(jnp.sum(values, axis=-1, keepdims=True)) * (1.0 / (PACK * values.shape[1]))


def inv_rms_of(values):
    return lax.rsqrt(mean_of(values * values) + EPSILON)


def merged(select_to, select_from, fresh, old):
    same = dot(select_to.astype(BF16), select_from.astype(BF16), 1, 1)
    _, chunk_r = packed_index(same.shape, 0)
    _, chunk_c = packed_index(same.shape, 1)
    same = jnp.where(chunk_r == chunk_c, same, 0.0)
    taken = jnp.sum(same, axis=1, keepdims=True)
    return jnp.where(taken > 0.5, dot(same.astype(BF16), fresh), old).astype(BF16)


def summed(parts):
    total = parts[0][...].astype(F32)
    for p in parts[1:]:
        total = total + p[...].astype(F32)
    return total


def hit_rows(select):
    ones = jnp.ones((PACKED, 128), BF16)
    return dot(chunk_of(select, 0), ones, 0, 0)[:, :1] > 0.5


def placed(c, old, select, hit, rows):
    return jnp.where(hit, dot(chunk_of(select, c), rows, 0, 0), old.astype(F32)).astype(BF16)


def start_rows(source, target, sems):
    copies = []
    for i in range(source.shape[0] // 16):
        r = pl.ds(16 * i, 16)
        copies.append(pltpu.make_async_copy(source.at[r], target.at[r], sems.at[i]))
        copies[-1].start()
    return copies


def first_rows_kernel(tokens, routes_far, raw, normed, early, sems, held, routes):
    fetch_routes = pltpu.make_async_copy(routes_far, routes, sems.at[sems.shape[0] - 1])
    fetch_routes.start()
    fetches = start_rows(tokens, held, sems)
    fetch_routes.wait()
    select = select_of(routes[0])
    for fetch in fetches:
        fetch.wait()
    values = pick(select, whole_block(held))
    raw[...] = values.astype(BF16)
    normed[...] = (values * inv_rms_of(values)).astype(BF16)
    height, width = held.shape
    for c in range(EARLY):
        early[c * height : (c + 1) * height] = held[:, columns(c, width)]


def update0_kernel(n, *refs):
    parts, (raw, routes, gates, tokens, next_routes, upd, onward) = refs[:n], refs[n:]
    select = select_of(routes[0])
    select_next = select_of(next_routes[0])
    weight = slot_gates(select, routes[0], gates[0])
    fresh = (raw[...].astype(F32) + weight * summed(parts)).astype(BF16)
    old = pick(select_next, whole_block(tokens))
    onward[:PACKED] = merged(select_next, select, fresh, old)
    names = routes[1].astype(F32)
    names = jnp.concatenate([names, jnp.full((TAIL - names.shape[0], names.shape[1]), 1.0)], 0)
    onward[PACKED:] = jnp.zeros((TAIL, onward.shape[1]), BF16)
    onward[PACKED:, : names.shape[1]] = names.astype(BF16)
    upd[...] = fresh


def merge_kernel(tokens, upd, routes, out, last):
    select = select_of(routes[0])
    hit = hit_rows(select)
    height, width = tokens.shape
    for c in range(EARLY, PACK):
        value = placed(c, tokens[:, columns(c, width)], select, hit, upd[...])
        out[(c - EARLY) * height : (c - EARLY + 1) * height] = value
    last[...] = jnp.zeros(last.shape, F32)
    last[:CAP] = upd[...].astype(F32)[:CAP]
    last[CAP : CAP + routes.shape[1], :height] = routes[0].astype(F32)
    out[(PACK - EARLY) * height :] = last[...].astype(BF16)


def release_kernel(*_):
    pass


def grad_rows_kernel(bulk, routes, gates, cot, scaled):
    select = select_of(routes[1])
    values = pick(select, whole_block(bulk))
    cot[...] = values.astype(BF16)
    scaled[...] = (slot_gates(select, routes[1], gates[1]) * values).astype(BF16)


def update1_kernel(n, *refs):
    parts, (h, routes, gates, upd) = refs[:n], refs[n:]
    select = select_of(routes[1])
    weight = slot_gates(select, routes[1], gates[1])
    upd[...] = (h[:PACKED].astype(F32) + weight * summed(parts)).astype(BF16)


def enter1_kernel(h, scaled, _, __, out, ___):
    values = h[:PACKED].astype(F32)
    out[:PACKED] = (values * inv_rms_of(values)).astype(BF16)
    out[PACKED:] = scaled[...]


def state_grad(parts, h, c):
    total = summed(parts)
    values = h.astype(F32)
    inv = inv_rms_of(values)
    inner = mean_of(total * values)
    return (c.astype(F32) + inv * total - inv * inv * inv * values * inner).astype(BF16)


def grad1_kernel(n, *refs):
    parts, (h, cot, upd) = refs[:n], refs[n:]
    upd[...] = state_grad(parts, h[:PACKED], cot[...])


def enter0_kernel(upd1, next_routes, routes, gates, bulk, _, c0, out):
    select = select_of(routes[0])
    old = pick(select, whole_block(bulk))
    rows = merged(select, select_of(next_routes[0]), upd1[...], old)
    c0[...] = rows
    out[...] = (slot_gates(select, routes[0], gates[0]) * rows.astype(F32)).astype(BF16)


def finish_grad_kernel(n, *refs):
    parts, (h, c, routes, upd1, next_routes, bulk, out) = refs[:n], refs[n:]
    fresh = state_grad(parts, h[...], c[...])
    first, second = select_of(next_routes[0]), select_of(routes[0])
    hit1, hit2 = hit_rows(first), hit_rows(second)
    for chunk in range(PACK):
        k = columns(chunk, out.shape[1])
        value = placed(chunk, bulk[:, k], first, hit1, upd1[...])
        out[:, k] = placed(chunk, value, second, hit2, fresh)


def finish_state_kernel(early, rest, upd1, h, out, outs, last, sems):
    height, width = out.shape
    at = (PACK - EARLY) * height
    last[...] = rest[at:].astype(F32)
    first = select_of(last[CAP : CAP + TOP, :height])
    second = select_of(h[PACKED:].astype(F32)[:TOP, :height])
    hit1, hit2 = hit_rows(first), hit_rows(second)
    rows = jnp.concatenate([last[...], jnp.zeros((PACKED - TAIL, last.shape[1]), F32)], axis=0)
    for c in range(PACK):
        if c < EARLY:
            value = placed(c, early[...], first, hit1, rows.astype(BF16))
        else:
            value = rest[(c - EARLY) * height : (c - EARLY + 1) * height]
        outs[:, columns(c, width)] = placed(c, value, second, hit2, upd1[...])
    for store in start_rows(outs, out, sems):
        store.wait()


def silu_grads(pre_gate, pre_up, grad_act):
    sig = jax.nn.sigmoid(pre_gate)
    grad_gate = (grad_act * pre_up * sig * (1.0 + pre_gate * (1.0 - sig))).astype(BF16)
    grad_up = (grad_act * (pre_gate * sig)).astype(BF16)
    return grad_gate, grad_up


def gather_rows(blocks, unpacked, whole32, whole):
    width = whole.shape[1]
    used = len(blocks) * CAP
    if used < whole.shape[0]:
        whole32[used:] = jnp.zeros((whole.shape[0] - used, width), F32)
    for i, b in enumerate(blocks):
        unpacked[i] = b[...].astype(F32)
        for c in range(PACK):
            whole32[i * CAP : (i + 1) * CAP, columns(c, width)] = unpacked[
                i, c * CAP : (c + 1) * CAP
            ]
    whole[...] = whole32[...].astype(BF16)


def spread_rows(value, c, n, held, unpacked):
    held[...] = value
    for i in range(n):
        unpacked[i, c * CAP : (c + 1) * CAP] = held[i * CAP : (i + 1) * CAP]


def forward_kernel(n, *refs):
    blocks, (gate, up, down) = refs[:n], refs[n : n + 3]
    x, pre_gate, pre_up, act, gate_v, up_v, down_v = refs[n + 3 : n + 10]
    parts = refs[n + 10 : 2 * n + 10]
    sems, unpacked, whole32, held = refs[2 * n + 10 :]
    width = gate.shape[0]
    fetches = []
    for c in range(PACK):
        k = columns(c, width)
        fetches.append(
            (
                pltpu.make_async_copy(gate.at[k], gate_v.at[k], sems.at[0, c]),
                pltpu.make_async_copy(up.at[k], up_v.at[k], sems.at[1, c]),
                pltpu.make_async_copy(down.at[:, k], down_v.at[:, k], sems.at[2, c]),
            )
        )
    for fetch_g, fetch_u, _ in fetches:
        fetch_g.start()
        fetch_u.start()
    for _, _, fetch_d in fetches:
        fetch_d.start()
    gather_rows(blocks, unpacked, whole32, x)
    acc_g = jnp.zeros(pre_gate.shape, F32)
    acc_u = jnp.zeros(pre_up.shape, F32)
    for c, (fetch_g, fetch_u, _) in enumerate(fetches):
        k = columns(c, width)
        fetch_g.wait()
        acc_g = acc_g + dot(x[:, k], gate_v[k])
        fetch_u.wait()
        acc_u = acc_u + dot(x[:, k], up_v[k])
    pre_gate[...] = acc_g
    pre_up[...] = acc_u
    activated = (acc_g * jax.nn.sigmoid(acc_g) * acc_u).astype(BF16)
    act[...] = activated
    for c, (_, _, fetch_d) in enumerate(fetches):
        fetch_d.wait()
        value = dot(activated, down_v[:, columns(c, width)])
        spread_rows(value, c, n, held.at[c], unpacked)
    for i, p in enumerate(parts):
        p[...] = unpacked[i].astype(BF16)


def out_rows(act, down, held, unpacked, parts):
    n = len(parts)
    for c in range(PACK):
        value = dot(act, down[:, columns(c, down.shape[1])])
        spread_rows(value, c, n, held.at[c], unpacked)
    for i, p in enumerate(parts):
        p[...] = unpacked[i].astype(BF16)


def down_kernel(n, act, down, _, *refs):
    parts, (unpacked, held) = refs[:n], refs[n:]
    hidden, width = down.shape
    out_rows(act[:, 3 * width + hidden : 3 * width + 2 * hidden], down, held, unpacked, parts)


def back_rows(gg, gu, gate, up, held, unpacked, parts):
    n = len(parts)
    for c in range(PACK):
        k = columns(c, gate.shape[0])
        value = dot(gg, gate[k], 1, 1) + dot(gu, up[k], 1, 1)
        spread_rows(value, c, n, held.at[c], unpacked)
    for i, p in enumerate(parts):
        p[...] = unpacked[i].astype(BF16)


def tick1_kernel(n, *refs):
    blocks, (x0, act0, gate, up, down) = refs[:n], refs[n : n + 5]
    (kept,) = refs[n + 5 : n + 6]
    parts = refs[n + 6 : 2 * n + 6]
    unpacked, whole32, held, x, g = refs[2 * n + 6 :]
    gather_rows([b.at[:PACKED] for b in blocks], unpacked, whole32.at[0], x)
    gather_rows([b.at[PACKED:] for b in blocks], unpacked, whole32.at[1], g)
    width, hidden = gate.shape
    kept[:, :width] = x0[...]
    kept[:, width : 2 * width] = x[...]
    kept[:, 2 * width : 3 * width] = g[...]
    narrow = [slice(3 * width + i * hidden, 3 * width + (i + 1) * hidden) for i in range(4)]
    kept[:, narrow[0]] = act0[...]
    acc_g = dot(x[...], gate[...])
    acc_u = dot(x[...], up[...])
    acc_a = dot(g[...], down[...], 1, 1)
    gg, gu = silu_grads(acc_g, acc_u, acc_a)
    kept[:, narrow[1]] = (acc_g * jax.nn.sigmoid(acc_g) * acc_u).astype(BF16)
    kept[:, narrow[2]] = gg
    kept[:, narrow[3]] = gu
    back_rows(gg, gu, gate, up, held, unpacked, parts)


def tick0_kernel(n, *refs):
    blocks, (pre_gate, pre_up, gate, up, down) = refs[:n], refs[n : n + 5]
    (g_grad,) = refs[n + 5 : n + 6]
    parts = refs[n + 6 : 2 * n + 6]
    unpacked, whole32, held, g = refs[2 * n + 6 :]
    gather_rows(blocks, unpacked, whole32, g)
    width, hidden = gate.shape
    g_grad[:, :width] = g[...]
    acc_a = dot(g[...], down[...], 1, 1)
    gg, gu = silu_grads(pre_gate[...], pre_up[...], acc_a)
    g_grad[:, width : width + hidden] = gg
    g_grad[:, width + hidden :] = gu
    back_rows(gg, gu, gate, up, held, unpacked, parts)


def whole_of(blocks):
    return jnp.concatenate([b.astype(F32) for b in blocks], axis=0).astype(BF16)


def turn_kernel(m, *refs):
    x0, x1, act0, act1 = (refs[i * m : (i + 1) * m] for i in range(4))
    x_t, act_t = refs[4 * m :]
    x_t[...] = whole_of([b[...] for b in x0 + x1]).T

    @pl.when(pl.program_id(0) == 0)
    def _():
        act_t[...] = whole_of([b[...] for b in act0 + act1]).T


def down_grad_kernel(m, act_t, *refs):
    g0, g1, (down_out, both) = refs[:m], refs[m : 2 * m], refs[2 * m :]

    @pl.when(pl.program_id(0) == 0)
    def _():
        both[...] = whole_of([b[...] for b in g0 + g1])

    for c in range(PACK):
        k = columns(c, both.shape[1])
        down_out[:, k] = dot(act_t[...], both[:, k]).astype(BF16)


def input_grad_kernel(m, x_t, *refs):
    gates0, ups0, gates1, ups1 = (refs[i * m : (i + 1) * m] for i in range(4))
    gate_out, up_out, both = refs[4 * m :]
    hidden = gate_out.shape[1]

    @pl.when(pl.program_id(0) == 0)
    def _():
        both[:, :hidden] = whole_of([b[...] for b in gates0 + gates1])
        both[:, hidden:] = whole_of([b[...] for b in ups0 + ups1])

    gate_out[...] = dot(x_t[...], both[:, :hidden]).astype(BF16)
    up_out[...] = dot(x_t[...], both[:, hidden:]).astype(BF16)


def chunked_call(kernel, ins, outs, scratch=(), steps=PACK):
    return pl.pallas_call(
        kernel,
        grid=(steps,),
        out_shape=[jax.ShapeDtypeStruct(s, BF16) for s, _, _ in outs],
        in_specs=[pl.BlockSpec(block, index) for _, block, index in ins],
        out_specs=[pl.BlockSpec(block, index) for _, block, index in outs],
        scratch_shapes=list(scratch),
        compiler_params=pltpu.CompilerParams(vmem_limit_bytes=VMEM_SMALL),
        cost_estimate=pl.CostEstimate(flops=0, bytes_accessed=COST_BYTES, transcendentals=0),
    )(*(a for a, _, _ in ins))


def constant(at):
    return lambda c: (0, at)


def chunk_at(at):
    return lambda c: (0, at + c)


def turned(kept, width, hidden):
    m = len(kept)
    rows = kept[0].shape[0]
    step = width // PACK
    first = 3 * width // hidden
    ins = [(a, (rows, step), chunk_at(at)) for at in (0, PACK) for a in kept]
    ins += [(a, (rows, hidden), constant(at)) for at in (first, first + 1) for a in kept]
    outs = [
        ((width, 2 * m * rows), (step, 2 * m * rows), lambda c: (c, 0)),
        ((hidden, 2 * m * rows), (hidden, 2 * m * rows), lambda c: (0, 0)),
    ]
    return chunked_call(functools.partial(turn_kernel, m), ins, outs)


def down_grads(act_t, g_grad0, kept, width, hidden):
    m = len(kept)
    rows = kept[0].shape[0]
    block = max(hidden // 4, 16)
    ins = [(act_t, (block, act_t.shape[1]), lambda c: (c, 0))]
    ins += [(a, (rows, width), constant(0)) for a in g_grad0]
    ins += [(a, (rows, width), constant(2)) for a in kept]
    outs = [((hidden, width), (block, width), lambda c: (c, 0))]
    scratch = [pltpu.VMEM((2 * m * rows, width), BF16)]
    kernel = functools.partial(down_grad_kernel, m)
    return chunked_call(kernel, ins, outs, scratch, hidden // block)


def input_grads(x_t, g_grad0, kept, width, hidden):
    m = len(kept)
    rows = kept[0].shape[0]
    step = width // PACK
    first, second = width // hidden, 3 * width // hidden + 2
    ins = [(x_t, (step, x_t.shape[1]), lambda c: (c, 0))]
    ins += [(a, (rows, hidden), constant(at)) for at in (first, first + 1) for a in g_grad0]
    ins += [(a, (rows, hidden), constant(at)) for at in (second, second + 1) for a in kept]
    tall = ((width, hidden), (step, hidden), lambda c: (c, 0))
    scratch = [pltpu.VMEM((2 * m * rows, 2 * hidden), BF16)]
    return chunked_call(functools.partial(input_grad_kernel, m), ins, [tall, tall], scratch)


def from_group(block):
    n = lax.axis_size("expert")
    return [block] + [shifted(block, "expert", k) for k in range(1, n)]


def to_group(blocks):
    return [blocks[0]] + [shifted(b, "expert", -k) for k, b in enumerate(blocks) if k]


def copies_of(block):
    n = lax.axis_size("dp")
    return [block] + [shifted(block, "dp", k) for k in range(1, n)]


def shards(tokens, cotangent, w_gate, w_up, w_down, routes, gates):
    gate, up, down = w_gate[0], w_up[0], w_down[0]
    width, hidden = gate.shape
    step = width // PACK
    n = lax.axis_size("expert")
    rows = -(-n * CAP // 8) * 8
    routes = jnp.transpose(routes, (0, 2, 1))
    gates = jnp.transpose(gates, (0, 2, 1))
    one = ((PACKED, step), BF16)
    part = functools.partial
    unpacked = pltpu.VMEM((n, PACKED, step), F32)
    flat32 = pltpu.VMEM((rows, width), F32)
    held = pltpu.VMEM((PACK, rows, step), F32)
    flat = pltpu.VMEM((rows, width), BF16)
    wide = ((rows, width + 2 * hidden), BF16)
    dma = [pltpu.SemaphoreType.DMA]

    cot1_all = shifted(cotangent, "section", -1)
    next_routes = shifted(routes[1:], "section", -1)

    raw0, normed0, early = call(
        first_rows_kernel,
        [pltpu.VMEM(*one), pltpu.VMEM(*one), ((EARLY * tokens.shape[0], step), BF16)],
        [tokens, routes],
        any_args=(0, 1),
        scratch=[
            pltpu.SemaphoreType.DMA((tokens.shape[0] // 16 + 1,)),
            pltpu.VMEM(tokens.shape, BF16),
            pltpu.VMEM(routes.shape, jnp.int32),
        ],
        vmem=VMEM_ALL,
    )
    early = shifted(early, "section", 2)
    blocks = from_group(normed0)
    x0, pre_gate0, pre_up0, act0, gate, up, down, *parts = call(
        part(forward_kernel, n),
        [((rows, width), BF16), ((rows, hidden), F32), ((rows, hidden), F32)]
        + [((rows, hidden), BF16)]
        + [pltpu.VMEM(a.shape, BF16) for a in (gate, up, down)]
        + [one] * n,
        [*blocks, gate, up, down],
        any_args=(n, n + 1, n + 2),
        scratch=[pltpu.SemaphoreType.DMA((3, PACK)), unpacked, flat32, held],
        vmem=VMEM_LOAD,
    )
    parts = to_group(parts)
    upd0, h1 = call(
        part(update0_kernel, n),
        [one, ((PACKED + TAIL, step), BF16)],
        [*parts, raw0, routes, gates, tokens, next_routes],
    )
    h1 = shifted(h1, "section", 1)
    (rest,) = call(
        merge_kernel,
        [(((PACK - EARLY) * tokens.shape[0] + TAIL, step), BF16)],
        [tokens, upd0, routes],
        scratch=[pltpu.VMEM((TAIL, step), F32)],
    )
    cot1, scaled1 = call(grad_rows_kernel, [one, one], [cot1_all, routes, gates])

    enter1, cot1_all = call(
        enter1_kernel,
        [((2 * PACKED, step), BF16), (tokens.shape, BF16)],
        [h1, scaled1, cot1_all, early],
        any_args=(2, 3),
        any_outs=(1,),
        aliases={2: 1},
    )
    cot0_all = shifted(cot1_all, "section", -1)
    blocks = from_group(enter1)
    kept, *parts = call(
        part(tick1_kernel, n),
        [((rows, 3 * width + 4 * hidden), BF16)] + [one] * n,
        [*blocks, x0, act0, gate, up, down],
        scratch=[unpacked, pltpu.VMEM((2, rows, width), F32), held, flat, flat],
    )
    parts = to_group(parts)
    (upd1,) = call(
        part(grad1_kernel, n),
        [one],
        [*parts, h1, cot1],
    )
    upd1 = shifted(upd1, "section", -1)
    kept_all = copies_of(kept)

    (rest,) = call(
        release_kernel,
        [(rest.shape, BF16)],
        [rest, cot0_all, upd1],
        any_args=(0, 1, 2),
        any_outs=(0,),
        aliases={0: 0},
    )
    c0, enter0 = call(
        enter0_kernel,
        [one, one],
        [upd1, next_routes, routes, gates, cot0_all, rest],
        any_args=(5,),
    )
    rest = shifted(rest, "section", 2)
    blocks = from_group(enter0)
    g_grad0, *parts = call(
        part(tick0_kernel, n),
        [wide] + [one] * n,
        [*blocks, pre_gate0, pre_up0, gate, up, down],
        scratch=[unpacked, flat32, held, flat],
    )
    parts = to_group(parts)
    g_grad0_all = copies_of(g_grad0)
    (grad,) = call(
        part(finish_grad_kernel, n),
        [(tokens.shape, BF16)],
        [*parts, raw0, c0, routes, upd1, next_routes, cot0_all],
    )
    outs = call(
        part(down_kernel, n),
        [one] * n,
        [kept, down, g_grad0],
        any_args=(2,),
        scratch=[unpacked, held],
    )
    outs = to_group(outs)
    (last1,) = call(part(update1_kernel, n), [one], [*outs, h1, routes, gates])
    last1 = shifted(last1, "section", 1)
    x_t, act_t = turned(kept_all, width, hidden)
    (down_out,) = down_grads(act_t, g_grad0_all, kept_all, width, hidden)
    gate_out, up_out = input_grads(x_t, g_grad0_all, kept_all, width, hidden)
    (state,) = call(
        finish_state_kernel,
        [(tokens.shape, BF16)],
        [early, rest, last1, h1],
        any_outs=(0,),
        scratch=[
            pltpu.VMEM(tokens.shape, BF16),
            pltpu.VMEM((TAIL, step), F32),
            pltpu.SemaphoreType.DMA((tokens.shape[0] // 16,)),
        ],
    )
    return (grad, state, gate_out[None], up_out[None], down_out[None])


def solution(mesh):
    rows = P(("section", "expert", "dp"), None)
    slots = P(None, ("section", "expert", "dp"), None)
    cols = P("section", None, "expert")
    hidden = P("section", "expert", None)
    return jax.shard_map(
        shards,
        mesh=mesh,
        in_specs=(rows, rows, cols, cols, hidden, slots, slots),
        out_specs=(rows, rows, cols, cols, hidden),
        check_vma=False,
    )
```

```python
import functools

import jax
import jax.numpy as jnp
from jax import lax
from jax.experimental import pallas as pl
from jax.experimental.pallas import tpu as pltpu
from jax.sharding import PartitionSpec as P

CAP = 10
PACK = 8
PACKED = CAP * PACK
EPSILON = 1e-06
F32 = jnp.float32
BF16 = jnp.bfloat16
VMEM_SMALL = 24 * 1024 * 1024
VMEM_LOAD = 36 * 1024 * 1024
VMEM_ALL = 60 * 1024 * 1024
COST_BYTES = 1024
TOP = 4
TAIL = 16
EARLY = 1


def shifted(block, axis, distance):
    size = lax.axis_size(axis)
    return lax.ppermute(block, axis, [((i - distance) % size, i) for i in range(size)])


def dot(a, b, ca=1, cb=0):
    return lax.dot_general(a, b, (((ca,), (cb,)), ((), ())), preferred_element_type=F32)


def call(
    kernel, outs, args, *, any_args=(), any_outs=(), scratch=(), vmem=VMEM_SMALL, aliases=None
):
    outs = [jax.ShapeDtypeStruct(*o) if isinstance(o, tuple) else o for o in outs]
    anywhere = pl.BlockSpec(memory_space=pl.ANY)
    near = pl.BlockSpec(memory_space=pltpu.VMEM)
    return pl.pallas_call(
        kernel,
        out_shape=outs,
        in_specs=[anywhere if i in any_args else near for i in range(len(args))],
        out_specs=[anywhere if i in any_outs else near for i in range(len(outs))],
        scratch_shapes=list(scratch),
        compiler_params=pltpu.CompilerParams(vmem_limit_bytes=vmem),
        cost_estimate=pl.CostEstimate(flops=0, bytes_accessed=COST_BYTES, transcendentals=0),
        input_output_aliases=aliases or {},
    )(*args)


def packed_index(shape, dim):
    place = lax.broadcasted_iota(jnp.int32, shape, dim).astype(F32)
    chunk = jnp.floor((place + 0.5) * (1.0 / CAP))
    return place - CAP * chunk, chunk


def select_of(routes):
    hits = (routes == 0).astype(F32)
    marked = jnp.sum(hits, axis=0, keepdims=True)
    rows = routes.shape[1]
    before = lax.broadcasted_iota(jnp.int32, (rows, rows), 0) < lax.broadcasted_iota(
        jnp.int32, (rows, rows), 1
    )
    wide = jnp.broadcast_to(marked, (PACKED, rows))
    places = dot(wide.astype(BF16), before.astype(F32).astype(BF16))
    slot, _ = packed_index((PACKED, rows), 0)
    return jnp.where((places == slot) & (wide > 0.5), 1.0, 0.0)


def slot_gates(select, routes, gates):
    weights = jnp.sum(jnp.where(routes == 0, gates, 0.0), axis=0, keepdims=True)
    return jnp.sum(select * weights, axis=1, keepdims=True)


def chunk_of(select, c):
    _, chunk = packed_index(select.shape, 0)
    return jnp.where(chunk == c, select, 0.0).astype(BF16)


def columns(c, width):
    return slice(c * (width // PACK), (c + 1) * (width // PACK))


def pick(select, pieces):
    total = None
    for block, (r0, r1, c0, c1) in pieces:
        width = block.shape[1] // (c1 - c0)
        for c in range(c0, c1):
            columns_here = slice((c - c0) * width, (c - c0 + 1) * width)
            part = dot(chunk_of(select[:, r0:r1], c), block[:, columns_here])
            total = part if total is None else total + part
    return total


def whole_block(block):
    return [(block, (0, block.shape[0], 0, PACK))]


def over_chunks(row_sums):
    slot_r, _ = packed_index((PACKED, PACKED), 0)
    slot_c, _ = packed_index((PACKED, PACKED), 1)
    same = jnp.where(slot_r == slot_c, 1.0, 0.0)
    wide = jnp.broadcast_to(row_sums, (PACKED, 128))
    return jnp.dot(
        same, wide, precision=lax.Precision.HIGHEST, preferred_element_type=F32
    )[:, :1]


def mean_of(values):
    return over_chunks(jnp.sum(values, axis=-1, keepdims=True)) * (1.0 / (PACK * values.shape[1]))


def inv_rms_of(values):
    return lax.rsqrt(mean_of(values * values) + EPSILON)


def merged(select_to, select_from, fresh, old):
    same = dot(select_to.astype(BF16), select_from.astype(BF16), 1, 1)
    _, chunk_r = packed_index(same.shape, 0)
    _, chunk_c = packed_index(same.shape, 1)
    same = jnp.where(chunk_r == chunk_c, same, 0.0)
    taken = jnp.sum(same, axis=1, keepdims=True)
    return jnp.where(taken > 0.5, dot(same.astype(BF16), fresh), old).astype(BF16)


def summed(parts):
    total = parts[0][...].astype(F32)
    for p in parts[1:]:
        total = total + p[...].astype(F32)
    return total


def hit_rows(select):
    ones = jnp.ones((PACKED, 128), BF16)
    return dot(chunk_of(select, 0), ones, 0, 0)[:, :1] > 0.5


def placed(c, old, select, hit, rows):
    return jnp.where(hit, dot(chunk_of(select, c), rows, 0, 0), old.astype(F32)).astype(BF16)


def start_rows(source, target, sems):
    copies = []
    for i in range(source.shape[0] // 16):
        r = pl.ds(16 * i, 16)
        copies.append(pltpu.make_async_copy(source.at[r], target.at[r], sems.at[i]))
        copies[-1].start()
    return copies


def first_rows_kernel(tokens, routes_far, raw, normed, early, sems, held, routes):
    fetch_routes = pltpu.make_async_copy(routes_far, routes, sems.at[sems.shape[0] - 1])
    fetch_routes.start()
    fetches = start_rows(tokens, held, sems)
    fetch_routes.wait()
    select = select_of(routes[0])
    for fetch in fetches:
        fetch.wait()
    values = pick(select, whole_block(held))
    raw[...] = values.astype(BF16)
    normed[...] = (values * inv_rms_of(values)).astype(BF16)
    height, width = held.shape
    for c in range(EARLY):
        early[c * height : (c + 1) * height] = held[:, columns(c, width)]


def update0_kernel(n, *refs):
    parts, (raw, routes, gates, tokens, next_routes, upd, onward) = refs[:n], refs[n:]
    select = select_of(routes[0])
    select_next = select_of(next_routes[0])
    weight = slot_gates(select, routes[0], gates[0])
    fresh = (raw[...].astype(F32) + weight * summed(parts)).astype(BF16)
    old = pick(select_next, whole_block(tokens))
    onward[...] = merged(select_next, select, fresh, old)
    upd[...] = fresh


def merge_kernel(tokens, upd, routes, next_routes, out, last):
    select = select_of(routes[0])
    hit = hit_rows(select)
    height, width = tokens.shape
    for c in range(EARLY, PACK):
        value = placed(c, tokens[:, columns(c, width)], select, hit, upd[...])
        out[(c - EARLY) * height : (c - EARLY + 1) * height] = value
    last[...] = jnp.zeros(last.shape, F32)
    last[:CAP] = upd[...].astype(F32)[:CAP]
    last[CAP : CAP + TOP, :height] = routes[0].astype(F32)
    last[CAP : CAP + TOP, height : 2 * height] = next_routes[0].astype(F32)
    out[(PACK - EARLY) * height :] = last[...].astype(BF16)


def release_kernel(*_):
    pass


def grad_rows_kernel(bulk, routes, gates, cot, scaled):
    select = select_of(routes[1])
    values = pick(select, whole_block(bulk))
    cot[...] = values.astype(BF16)
    scaled[...] = (slot_gates(select, routes[1], gates[1]) * values).astype(BF16)


def update1_kernel(n, *refs):
    parts, (h, routes, gates, upd) = refs[:n], refs[n:]
    select = select_of(routes[1])
    weight = slot_gates(select, routes[1], gates[1])
    upd[...] = (h[...].astype(F32) + weight * summed(parts)).astype(BF16)


def enter1_kernel(h, scaled, _, __, out, ___):
    values = h[...].astype(F32)
    out[:PACKED] = (values * inv_rms_of(values)).astype(BF16)
    out[PACKED:] = scaled[...]


def state_grad(parts, h, c):
    total = summed(parts)
    values = h.astype(F32)
    inv = inv_rms_of(values)
    inner = mean_of(total * values)
    return (c.astype(F32) + inv * total - inv * inv * inv * values * inner).astype(BF16)


def grad1_kernel(n, *refs):
    parts, (h, cot, upd) = refs[:n], refs[n:]
    upd[...] = state_grad(parts, h[...], cot[...])


def enter0_kernel(upd1, next_routes, routes, gates, bulk, _, c0, out):
    select = select_of(routes[0])
    old = pick(select, whole_block(bulk))
    rows = merged(select, select_of(next_routes[0]), upd1[...], old)
    c0[...] = rows
    out[...] = (slot_gates(select, routes[0], gates[0]) * rows.astype(F32)).astype(BF16)


def finish_grad_kernel(n, *refs):
    parts, (h, c, routes, upd1, next_routes, bulk, out) = refs[:n], refs[n:]
    fresh = state_grad(parts, h[...], c[...])
    first, second = select_of(next_routes[0]), select_of(routes[0])
    hit1, hit2 = hit_rows(first), hit_rows(second)
    for chunk in range(PACK):
        k = columns(chunk, out.shape[1])
        value = placed(chunk, bulk[:, k], first, hit1, upd1[...])
        out[:, k] = placed(chunk, value, second, hit2, fresh)


def finish_state_kernel(early, rest, upd1, out, outs, last, sems):
    height, width = out.shape
    at = (PACK - EARLY) * height
    last[...] = rest[at:].astype(F32)
    first = select_of(last[CAP : CAP + TOP, :height])
    second = select_of(last[CAP : CAP + TOP, height : 2 * height])
    hit1, hit2 = hit_rows(first), hit_rows(second)
    rows = jnp.concatenate([last[...], jnp.zeros((PACKED - TAIL, last.shape[1]), F32)], axis=0)
    rows1, rows2 = rows.astype(BF16), upd1[...]
    copies = []
    for r0 in range(0, height, height // 2):
        r = slice(r0, r0 + height // 2)
        for c in range(PACK):
            if c < EARLY:
                value = placed(c, early[r], first[:, r], hit1[r], rows1)
            else:
                start = (c - EARLY) * height + r0
                value = rest[start : start + height // 2]
            outs[r, columns(c, width)] = placed(c, value, second[:, r], hit2[r], rows2)
        for i in range(r0 // 16, r.stop // 16):
            b = pl.ds(16 * i, 16)
            copies.append(pltpu.make_async_copy(outs.at[b], out.at[b], sems.at[i]))
            copies[-1].start()
    for copy in copies:
        copy.wait()


def silu_grads(pre_gate, pre_up, grad_act):
    sig = jax.nn.sigmoid(pre_gate)
    grad_gate = (grad_act * pre_up * sig * (1.0 + pre_gate * (1.0 - sig))).astype(BF16)
    grad_up = (grad_act * (pre_gate * sig)).astype(BF16)
    return grad_gate, grad_up


def gather_rows(blocks, unpacked, whole32, whole):
    width = whole.shape[1]
    used = len(blocks) * CAP
    if used < whole.shape[0]:
        whole32[used:] = jnp.zeros((whole.shape[0] - used, width), F32)
    for i, b in enumerate(blocks):
        unpacked[i] = b[...].astype(F32)
        for c in range(PACK):
            whole32[i * CAP : (i + 1) * CAP, columns(c, width)] = unpacked[
                i, c * CAP : (c + 1) * CAP
            ]
    whole[...] = whole32[...].astype(BF16)


def spread_rows(value, c, n, held, unpacked):
    held[...] = value
    for i in range(n):
        unpacked[i, c * CAP : (c + 1) * CAP] = held[i * CAP : (i + 1) * CAP]


def forward_kernel(n, *refs):
    blocks, (gate, up, down) = refs[:n], refs[n : n + 3]
    x, pre_gate, pre_up, act, gate_v, up_v, down_v = refs[n + 3 : n + 10]
    parts = refs[n + 10 : 2 * n + 10]
    sems, unpacked, whole32, held = refs[2 * n + 10 :]
    width = gate.shape[0]
    fetches = []
    for c in range(PACK):
        k = columns(c, width)
        fetches.append(
            (
                pltpu.make_async_copy(gate.at[k], gate_v.at[k], sems.at[0, c]),
                pltpu.make_async_copy(up.at[k], up_v.at[k], sems.at[1, c]),
                pltpu.make_async_copy(down.at[:, k], down_v.at[:, k], sems.at[2, c]),
            )
        )
    for fetch_g, fetch_u, _ in fetches:
        fetch_g.start()
        fetch_u.start()
    for _, _, fetch_d in fetches:
        fetch_d.start()
    gather_rows(blocks, unpacked, whole32, x)
    acc_g = jnp.zeros(pre_gate.shape, F32)
    acc_u = jnp.zeros(pre_up.shape, F32)
    for c, (fetch_g, fetch_u, _) in enumerate(fetches):
        k = columns(c, width)
        fetch_g.wait()
        acc_g = acc_g + dot(x[:, k], gate_v[k])
        fetch_u.wait()
        acc_u = acc_u + dot(x[:, k], up_v[k])
    pre_gate[...] = acc_g
    pre_up[...] = acc_u
    activated = (acc_g * jax.nn.sigmoid(acc_g) * acc_u).astype(BF16)
    act[...] = activated
    for c, (_, _, fetch_d) in enumerate(fetches):
        fetch_d.wait()
        value = dot(activated, down_v[:, columns(c, width)])
        spread_rows(value, c, n, held.at[c], unpacked)
    for i, p in enumerate(parts):
        p[...] = unpacked[i].astype(BF16)


def out_rows(act, down, held, unpacked, parts):
    n = len(parts)
    for c in range(PACK):
        value = dot(act, down[:, columns(c, down.shape[1])])
        spread_rows(value, c, n, held.at[c], unpacked)
    for i, p in enumerate(parts):
        p[...] = unpacked[i].astype(BF16)


def down_kernel(n, act, down, _, *refs):
    parts, (unpacked, held) = refs[:n], refs[n:]
    hidden, width = down.shape
    out_rows(act[:, 3 * width + hidden : 3 * width + 2 * hidden], down, held, unpacked, parts)


def back_rows(gg, gu, gate, up, held, unpacked, parts):
    n = len(parts)
    for c in range(PACK):
        k = columns(c, gate.shape[0])
        value = dot(gg, gate[k], 1, 1) + dot(gu, up[k], 1, 1)
        spread_rows(value, c, n, held.at[c], unpacked)
    for i, p in enumerate(parts):
        p[...] = unpacked[i].astype(BF16)


def tick1_kernel(n, *refs):
    blocks, (x0, act0, gate, up, down) = refs[:n], refs[n : n + 5]
    (kept,) = refs[n + 5 : n + 6]
    parts = refs[n + 6 : 2 * n + 6]
    unpacked, whole32, held, x, g = refs[2 * n + 6 :]
    gather_rows([b.at[:PACKED] for b in blocks], unpacked, whole32.at[0], x)
    gather_rows([b.at[PACKED:] for b in blocks], unpacked, whole32.at[1], g)
    width, hidden = gate.shape
    kept[:, :width] = x0[...]
    kept[:, width : 2 * width] = x[...]
    kept[:, 2 * width : 3 * width] = g[...]
    narrow = [slice(3 * width + i * hidden, 3 * width + (i + 1) * hidden) for i in range(4)]
    kept[:, narrow[0]] = act0[...]
    acc_g = dot(x[...], gate[...])
    acc_u = dot(x[...], up[...])
    acc_a = dot(g[...], down[...], 1, 1)
    gg, gu = silu_grads(acc_g, acc_u, acc_a)
    kept[:, narrow[1]] = (acc_g * jax.nn.sigmoid(acc_g) * acc_u).astype(BF16)
    kept[:, narrow[2]] = gg
    kept[:, narrow[3]] = gu
    back_rows(gg, gu, gate, up, held, unpacked, parts)


def tick0_kernel(n, *refs):
    blocks, (pre_gate, pre_up, gate, up, down) = refs[:n], refs[n : n + 5]
    (g_grad,) = refs[n + 5 : n + 6]
    parts = refs[n + 6 : 2 * n + 6]
    unpacked, whole32, held, g = refs[2 * n + 6 :]
    gather_rows(blocks, unpacked, whole32, g)
    width, hidden = gate.shape
    g_grad[:, :width] = g[...]
    acc_a = dot(g[...], down[...], 1, 1)
    gg, gu = silu_grads(pre_gate[...], pre_up[...], acc_a)
    g_grad[:, width : width + hidden] = gg
    g_grad[:, width + hidden :] = gu
    back_rows(gg, gu, gate, up, held, unpacked, parts)


def whole_of(blocks):
    return jnp.concatenate([b.astype(F32) for b in blocks], axis=0).astype(BF16)


def turn_kernel(m, *refs):
    x0, x1, act0, act1 = (refs[i * m : (i + 1) * m] for i in range(4))
    x_t, act_t = refs[4 * m :]
    x_t[...] = whole_of([b[...] for b in x0 + x1]).T

    @pl.when(pl.program_id(0) == 0)
    def _():
        act_t[...] = whole_of([b[...] for b in act0 + act1]).T


def down_grad_kernel(m, act_t, *refs):
    g0, g1, (down_out, both) = refs[:m], refs[m : 2 * m], refs[2 * m :]

    @pl.when(pl.program_id(0) == 0)
    def _():
        both[...] = whole_of([b[...] for b in g0 + g1])

    for c in range(PACK):
        k = columns(c, both.shape[1])
        down_out[:, k] = dot(act_t[...], both[:, k]).astype(BF16)


def input_grad_kernel(m, x_t, *refs):
    gates0, ups0, gates1, ups1 = (refs[i * m : (i + 1) * m] for i in range(4))
    gate_out, up_out, both = refs[4 * m :]
    hidden = gate_out.shape[1]

    @pl.when(pl.program_id(0) == 0)
    def _():
        both[:, :hidden] = whole_of([b[...] for b in gates0 + gates1])
        both[:, hidden:] = whole_of([b[...] for b in ups0 + ups1])

    gate_out[...] = dot(x_t[...], both[:, :hidden]).astype(BF16)
    up_out[...] = dot(x_t[...], both[:, hidden:]).astype(BF16)


def chunked_call(kernel, ins, outs, scratch=(), steps=PACK):
    return pl.pallas_call(
        kernel,
        grid=(steps,),
        out_shape=[jax.ShapeDtypeStruct(s, BF16) for s, _, _ in outs],
        in_specs=[pl.BlockSpec(block, index) for _, block, index in ins],
        out_specs=[pl.BlockSpec(block, index) for _, block, index in outs],
        scratch_shapes=list(scratch),
        compiler_params=pltpu.CompilerParams(vmem_limit_bytes=VMEM_SMALL),
        cost_estimate=pl.CostEstimate(flops=0, bytes_accessed=COST_BYTES, transcendentals=0),
    )(*(a for a, _, _ in ins))


def constant(at):
    return lambda c: (0, at)


def chunk_at(at):
    return lambda c: (0, at + c)


def turned(kept, width, hidden):
    m = len(kept)
    rows = kept[0].shape[0]
    step = width // PACK
    first = 3 * width // hidden
    ins = [(a, (rows, step), chunk_at(at)) for at in (0, PACK) for a in kept]
    ins += [(a, (rows, hidden), constant(at)) for at in (first, first + 1) for a in kept]
    outs = [
        ((width, 2 * m * rows), (step, 2 * m * rows), lambda c: (c, 0)),
        ((hidden, 2 * m * rows), (hidden, 2 * m * rows), lambda c: (0, 0)),
    ]
    return chunked_call(functools.partial(turn_kernel, m), ins, outs)


def down_grads(act_t, g_grad0, kept, width, hidden):
    m = len(kept)
    rows = kept[0].shape[0]
    block = max(hidden // 4, 16)
    ins = [(act_t, (block, act_t.shape[1]), lambda c: (c, 0))]
    ins += [(a, (rows, width), constant(0)) for a in g_grad0]
    ins += [(a, (rows, width), constant(2)) for a in kept]
    outs = [((hidden, width), (block, width), lambda c: (c, 0))]
    scratch = [pltpu.VMEM((2 * m * rows, width), BF16)]
    kernel = functools.partial(down_grad_kernel, m)
    return chunked_call(kernel, ins, outs, scratch, hidden // block)


def input_grads(x_t, g_grad0, kept, width, hidden):
    m = len(kept)
    rows = kept[0].shape[0]
    step = width // PACK
    first, second = width // hidden, 3 * width // hidden + 2
    ins = [(x_t, (step, x_t.shape[1]), lambda c: (c, 0))]
    ins += [(a, (rows, hidden), constant(at)) for at in (first, first + 1) for a in g_grad0]
    ins += [(a, (rows, hidden), constant(at)) for at in (second, second + 1) for a in kept]
    tall = ((width, hidden), (step, hidden), lambda c: (c, 0))
    scratch = [pltpu.VMEM((2 * m * rows, 2 * hidden), BF16)]
    return chunked_call(functools.partial(input_grad_kernel, m), ins, [tall, tall], scratch)


def from_group(block):
    n = lax.axis_size("expert")
    return [block] + [shifted(block, "expert", k) for k in range(1, n)]


def to_group(blocks):
    return [blocks[0]] + [shifted(b, "expert", -k) for k, b in enumerate(blocks) if k]


def copies_of(block):
    n = lax.axis_size("dp")
    return [block] + [shifted(block, "dp", k) for k in range(1, n)]


def shards(tokens, cotangent, w_gate, w_up, w_down, routes, gates):
    gate, up, down = w_gate[0], w_up[0], w_down[0]
    width, hidden = gate.shape
    step = width // PACK
    n = lax.axis_size("expert")
    rows = -(-n * CAP // 8) * 8
    routes = jnp.transpose(routes, (0, 2, 1))
    gates = jnp.transpose(gates, (0, 2, 1))
    one = ((PACKED, step), BF16)
    part = functools.partial
    unpacked = pltpu.VMEM((n, PACKED, step), F32)
    flat32 = pltpu.VMEM((rows, width), F32)
    held = pltpu.VMEM((PACK, rows, step), F32)
    flat = pltpu.VMEM((rows, width), BF16)
    wide = ((rows, width + 2 * hidden), BF16)
    dma = [pltpu.SemaphoreType.DMA]

    cot1_all = shifted(cotangent, "section", -1)
    next_routes = shifted(routes[1:], "section", -1)

    raw0, normed0, early = call(
        first_rows_kernel,
        [pltpu.VMEM(*one), pltpu.VMEM(*one), ((EARLY * tokens.shape[0], step), BF16)],
        [tokens, routes],
        any_args=(0, 1),
        scratch=[
            pltpu.SemaphoreType.DMA((tokens.shape[0] // 16 + 1,)),
            pltpu.VMEM(tokens.shape, BF16),
            pltpu.VMEM(routes.shape, jnp.int32),
        ],
        vmem=VMEM_ALL,
    )
    early = shifted(early, "section", 2)
    blocks = from_group(normed0)
    x0, pre_gate0, pre_up0, act0, gate, up, down, *parts = call(
        part(forward_kernel, n),
        [((rows, width), BF16), ((rows, hidden), F32), ((rows, hidden), F32)]
        + [((rows, hidden), BF16)]
        + [pltpu.VMEM(a.shape, BF16) for a in (gate, up, down)]
        + [one] * n,
        [*blocks, gate, up, down],
        any_args=(n, n + 1, n + 2),
        scratch=[pltpu.SemaphoreType.DMA((3, PACK)), unpacked, flat32, held],
        vmem=VMEM_LOAD,
    )
    parts = to_group(parts)
    upd0, h1 = call(
        part(update0_kernel, n),
        [one, one],
        [*parts, raw0, routes, gates, tokens, next_routes],
    )
    h1 = shifted(h1, "section", 1)
    (rest,) = call(
        merge_kernel,
        [(((PACK - EARLY) * tokens.shape[0] + TAIL, step), BF16)],
        [tokens, upd0, routes, next_routes],
        scratch=[pltpu.VMEM((TAIL, step), F32)],
    )
    cot1, scaled1 = call(grad_rows_kernel, [one, one], [cot1_all, routes, gates])

    enter1, cot1_all = call(
        enter1_kernel,
        [((2 * PACKED, step), BF16), (tokens.shape, BF16)],
        [h1, scaled1, cot1_all, early],
        any_args=(2, 3),
        any_outs=(1,),
        aliases={2: 1},
    )
    cot0_all = shifted(cot1_all, "section", -1)
    blocks = from_group(enter1)
    kept, *parts = call(
        part(tick1_kernel, n),
        [((rows, 3 * width + 4 * hidden), BF16)] + [one] * n,
        [*blocks, x0, act0, gate, up, down],
        scratch=[unpacked, pltpu.VMEM((2, rows, width), F32), held, flat, flat],
    )
    parts = to_group(parts)
    (upd1,) = call(
        part(grad1_kernel, n),
        [one],
        [*parts, h1, cot1],
    )
    upd1 = shifted(upd1, "section", -1)
    kept_all = copies_of(kept)

    (rest,) = call(
        release_kernel,
        [(rest.shape, BF16)],
        [rest, cot0_all, upd1],
        any_args=(0, 1, 2),
        any_outs=(0,),
        aliases={0: 0},
    )
    c0, enter0 = call(
        enter0_kernel,
        [one, one],
        [upd1, next_routes, routes, gates, cot0_all, rest],
        any_args=(5,),
    )
    rest = shifted(rest, "section", 2)
    blocks = from_group(enter0)
    g_grad0, *parts = call(
        part(tick0_kernel, n),
        [wide] + [one] * n,
        [*blocks, pre_gate0, pre_up0, gate, up, down],
        scratch=[unpacked, flat32, held, flat],
    )
    parts = to_group(parts)
    g_grad0_all = copies_of(g_grad0)
    (grad,) = call(
        part(finish_grad_kernel, n),
        [(tokens.shape, BF16)],
        [*parts, raw0, c0, routes, upd1, next_routes, cot0_all],
    )
    outs = call(
        part(down_kernel, n),
        [one] * n,
        [kept, down, g_grad0],
        any_args=(2,),
        scratch=[unpacked, held],
    )
    outs = to_group(outs)
    (last1,) = call(part(update1_kernel, n), [one], [*outs, h1, routes, gates])
    last1 = shifted(last1, "section", 1)
    x_t, act_t = turned(kept_all, width, hidden)
    (down_out,) = down_grads(act_t, g_grad0_all, kept_all, width, hidden)
    gate_out, up_out = input_grads(x_t, g_grad0_all, kept_all, width, hidden)
    (state,) = call(
        finish_state_kernel,
        [(tokens.shape, BF16)],
        [early, rest, last1],
        any_outs=(0,),
        scratch=[
            pltpu.VMEM(tokens.shape, BF16),
            pltpu.VMEM((TAIL, step), F32),
            pltpu.SemaphoreType.DMA((tokens.shape[0] // 16,)),
        ],
    )
    return (grad, state, gate_out[None], up_out[None], down_out[None])


def solution(mesh):
    rows = P(("section", "expert", "dp"), None)
    slots = P(None, ("section", "expert", "dp"), None)
    cols = P("section", None, "expert")
    hidden = P("section", "expert", None)
    return jax.shard_map(
        shards,
        mesh=mesh,
        in_specs=(rows, rows, cols, cols, hidden, slots, slots),
        out_specs=(rows, rows, cols, cols, hidden),
        check_vma=False,
    )
```

```python
import functools

import jax
import jax.numpy as jnp
from jax import lax
from jax.experimental import pallas as pl
from jax.experimental.pallas import tpu as pltpu
from jax.sharding import PartitionSpec as P

CAP = 10
PACK = 8
PACKED = CAP * PACK
EPSILON = 1e-06
F32 = jnp.float32
BF16 = jnp.bfloat16
VMEM_SMALL = 24 * 1024 * 1024
VMEM_LOAD = 36 * 1024 * 1024
VMEM_ALL = 60 * 1024 * 1024
COST_BYTES = 1024
TOP = 4
TAIL = 16
EARLY = 1


def shifted(block, axis, distance):
    size = lax.axis_size(axis)
    return lax.ppermute(block, axis, [((i - distance) % size, i) for i in range(size)])


def dot(a, b, ca=1, cb=0):
    return lax.dot_general(a, b, (((ca,), (cb,)), ((), ())), preferred_element_type=F32)


def call(
    kernel, outs, args, *, any_args=(), any_outs=(), scratch=(), vmem=VMEM_SMALL, aliases=None
):
    outs = [jax.ShapeDtypeStruct(*o) if isinstance(o, tuple) else o for o in outs]
    anywhere = pl.BlockSpec(memory_space=pl.ANY)
    near = pl.BlockSpec(memory_space=pltpu.VMEM)
    return pl.pallas_call(
        kernel,
        out_shape=outs,
        in_specs=[anywhere if i in any_args else near for i in range(len(args))],
        out_specs=[anywhere if i in any_outs else near for i in range(len(outs))],
        scratch_shapes=list(scratch),
        compiler_params=pltpu.CompilerParams(vmem_limit_bytes=vmem),
        cost_estimate=pl.CostEstimate(flops=0, bytes_accessed=COST_BYTES, transcendentals=0),
        input_output_aliases=aliases or {},
    )(*args)


def packed_index(shape, dim):
    place = lax.broadcasted_iota(jnp.int32, shape, dim).astype(F32)
    chunk = jnp.floor((place + 0.5) * (1.0 / CAP))
    return place - CAP * chunk, chunk


def select_of(routes):
    hits = (routes == 0).astype(F32)
    marked = jnp.sum(hits, axis=0, keepdims=True)
    rows = routes.shape[1]
    before = lax.broadcasted_iota(jnp.int32, (rows, rows), 0) < lax.broadcasted_iota(
        jnp.int32, (rows, rows), 1
    )
    wide = jnp.broadcast_to(marked, (PACKED, rows))
    places = dot(wide.astype(BF16), before.astype(F32).astype(BF16))
    slot, _ = packed_index((PACKED, rows), 0)
    return jnp.where((places == slot) & (wide > 0.5), 1.0, 0.0)


def slot_gates(select, routes, gates):
    weights = jnp.sum(jnp.where(routes == 0, gates, 0.0), axis=0, keepdims=True)
    return jnp.sum(select * weights, axis=1, keepdims=True)


def chunk_of(select, c):
    _, chunk = packed_index(select.shape, 0)
    return jnp.where(chunk == c, select, 0.0).astype(BF16)


def columns(c, width):
    return slice(c * (width // PACK), (c + 1) * (width // PACK))


def pick(select, pieces):
    total = None
    for block, (r0, r1, c0, c1) in pieces:
        width = block.shape[1] // (c1 - c0)
        for c in range(c0, c1):
            columns_here = slice((c - c0) * width, (c - c0 + 1) * width)
            part = dot(chunk_of(select[:, r0:r1], c), block[:, columns_here])
            total = part if total is None else total + part
    return total


def whole_block(block):
    return [(block, (0, block.shape[0], 0, PACK))]


def over_chunks(row_sums):
    slot_r, _ = packed_index((PACKED, PACKED), 0)
    slot_c, _ = packed_index((PACKED, PACKED), 1)
    same = jnp.where(slot_r == slot_c, 1.0, 0.0)
    wide = jnp.broadcast_to(row_sums, (PACKED, 128))
    return jnp.dot(
        same, wide, precision=lax.Precision.HIGHEST, preferred_element_type=F32
    )[:, :1]


def mean_of(values):
    return over_chunks(jnp.sum(values, axis=-1, keepdims=True)) * (1.0 / (PACK * values.shape[1]))


def inv_rms_of(values):
    return lax.rsqrt(mean_of(values * values) + EPSILON)


def merged(select_to, select_from, fresh, old):
    same = dot(select_to.astype(BF16), select_from.astype(BF16), 1, 1)
    _, chunk_r = packed_index(same.shape, 0)
    _, chunk_c = packed_index(same.shape, 1)
    same = jnp.where(chunk_r == chunk_c, same, 0.0)
    taken = jnp.sum(same, axis=1, keepdims=True)
    return jnp.where(taken > 0.5, dot(same.astype(BF16), fresh), old).astype(BF16)


def summed(parts):
    total = parts[0][...].astype(F32)
    for p in parts[1:]:
        total = total + p[...].astype(F32)
    return total


def hit_rows(select):
    ones = jnp.ones((PACKED, 128), BF16)
    return dot(chunk_of(select, 0), ones, 0, 0)[:, :1] > 0.5


def placed(c, old, select, hit, rows):
    return jnp.where(hit, dot(chunk_of(select, c), rows, 0, 0), old.astype(F32)).astype(BF16)


def start_rows(source, target, sems):
    copies = []
    for i in range(source.shape[0] // 16):
        r = pl.ds(16 * i, 16)
        copies.append(pltpu.make_async_copy(source.at[r], target.at[r], sems.at[i]))
        copies[-1].start()
    return copies


def first_rows_kernel(tokens, routes_far, raw, normed, early, sems, held, routes):
    fetch_routes = pltpu.make_async_copy(routes_far, routes, sems.at[sems.shape[0] - 1])
    fetch_routes.start()
    fetches = start_rows(tokens, held, sems)
    fetch_routes.wait()
    select = select_of(routes[0])
    for fetch in fetches:
        fetch.wait()
    values = pick(select, whole_block(held))
    raw[...] = values.astype(BF16)
    normed[...] = (values * inv_rms_of(values)).astype(BF16)
    height, width = held.shape
    for c in range(EARLY):
        early[c * height : (c + 1) * height] = held[:, columns(c, width)]


def update0_kernel(n, *refs):
    parts, (raw, routes, gates, tokens, next_routes, upd, onward) = refs[:n], refs[n:]
    select = select_of(routes[0])
    select_next = select_of(next_routes[0])
    weight = slot_gates(select, routes[0], gates[0])
    fresh = (raw[...].astype(F32) + weight * summed(parts)).astype(BF16)
    old = pick(select_next, whole_block(tokens))
    onward[...] = merged(select_next, select, fresh, old)
    upd[...] = fresh


def merge_kernel(tokens, upd, routes, next_routes, out, last):
    select = select_of(routes[0])
    hit = hit_rows(select)
    height, width = tokens.shape
    for c in range(EARLY, PACK):
        value = placed(c, tokens[:, columns(c, width)], select, hit, upd[...])
        out[(c - EARLY) * height : (c - EARLY + 1) * height] = value
    last[...] = jnp.zeros(last.shape, F32)
    last[:CAP] = upd[...].astype(F32)[:CAP]
    last[CAP : CAP + TOP, :height] = routes[0].astype(F32)
    last[CAP : CAP + TOP, height : 2 * height] = next_routes[0].astype(F32)
    out[(PACK - EARLY) * height :] = last[...].astype(BF16)


def release_kernel(*_):
    pass


def grad_rows_kernel(bulk, routes, gates, cot, scaled):
    select = select_of(routes[1])
    values = pick(select, whole_block(bulk))
    cot[...] = values.astype(BF16)
    scaled[...] = (slot_gates(select, routes[1], gates[1]) * values).astype(BF16)


def update1_kernel(n, *refs):
    parts, (h, routes, gates, upd) = refs[:n], refs[n:]
    select = select_of(routes[1])
    weight = slot_gates(select, routes[1], gates[1])
    upd[...] = (h[...].astype(F32) + weight * summed(parts)).astype(BF16)


def enter1_kernel(h, scaled, out):
    values = h[...].astype(F32)
    out[:PACKED] = (values * inv_rms_of(values)).astype(BF16)
    out[PACKED:] = scaled[...]


def state_grad(parts, h, c):
    total = summed(parts)
    values = h.astype(F32)
    inv = inv_rms_of(values)
    inner = mean_of(total * values)
    return (c.astype(F32) + inv * total - inv * inv * inv * values * inner).astype(BF16)


def grad1_kernel(n, *refs):
    parts, (h, cot, upd) = refs[:n], refs[n:]
    upd[...] = state_grad(parts, h[...], cot[...])


def enter0_kernel(upd1, next_routes, routes, gates, bulk, _, c0, out):
    select = select_of(routes[0])
    old = pick(select, whole_block(bulk))
    rows = merged(select, select_of(next_routes[0]), upd1[...], old)
    c0[...] = rows
    out[...] = (slot_gates(select, routes[0], gates[0]) * rows.astype(F32)).astype(BF16)


def finish_grad_kernel(n, *refs):
    parts, (h, c, routes, upd1, next_routes, bulk, out) = refs[:n], refs[n:]
    fresh = state_grad(parts, h[...], c[...])
    first, second = select_of(next_routes[0]), select_of(routes[0])
    hit1, hit2 = hit_rows(first), hit_rows(second)
    for chunk in range(PACK):
        k = columns(chunk, out.shape[1])
        value = placed(chunk, bulk[:, k], first, hit1, upd1[...])
        out[:, k] = placed(chunk, value, second, hit2, fresh)


def prepare_state_kernel(early, rest, out, turned_select, hit, last):
    height, width = out.shape
    at = (PACK - EARLY) * height
    last[...] = rest[at:].astype(F32)
    first = select_of(last[CAP : CAP + TOP, :height])
    second = select_of(last[CAP : CAP + TOP, height : 2 * height])
    rows = jnp.concatenate([last[...], jnp.zeros((PACKED - TAIL, last.shape[1]), F32)], axis=0)
    out[:, columns(0, width)] = placed(0, early[...], first, hit_rows(first), rows.astype(BF16))
    for c in range(EARLY, PACK):
        out[:, columns(c, width)] = rest[(c - EARLY) * height : (c - EARLY + 1) * height]
    turned_select[...] = second.T
    ones = jnp.ones((PACKED, 128), BF16)
    hit[...] = dot(chunk_of(second, 0), ones, 0, 0)


def finish_state_kernel(base, turned_select, hit, upd1, out, outs, sems):
    height, width = out.shape
    _, chunk = packed_index(turned_select.shape, 1)
    copies = []
    for r0 in range(0, height, height // 2):
        r = slice(r0, r0 + height // 2)
        taken = hit[r, :1] > 0.5
        for c in range(PACK):
            k = columns(c, width)
            select = jnp.where(chunk[r] == c, turned_select[r], 0.0).astype(BF16)
            value = jnp.where(taken, dot(select, upd1[...]), base[r, k].astype(F32))
            outs[r, k] = value.astype(BF16)
        for i in range(r0 // 16, r.stop // 16):
            b = pl.ds(16 * i, 16)
            copies.append(pltpu.make_async_copy(outs.at[b], out.at[b], sems.at[i]))
            copies[-1].start()
    for copy in copies:
        copy.wait()


def silu_grads(pre_gate, pre_up, grad_act):
    sig = jax.nn.sigmoid(pre_gate)
    grad_gate = (grad_act * pre_up * sig * (1.0 + pre_gate * (1.0 - sig))).astype(BF16)
    grad_up = (grad_act * (pre_gate * sig)).astype(BF16)
    return grad_gate, grad_up


def gather_rows(blocks, unpacked, whole32, whole):
    width = whole.shape[1]
    used = len(blocks) * CAP
    if used < whole.shape[0]:
        whole32[used:] = jnp.zeros((whole.shape[0] - used, width), F32)
    for i, b in enumerate(blocks):
        unpacked[i] = b[...].astype(F32)
        for c in range(PACK):
            whole32[i * CAP : (i + 1) * CAP, columns(c, width)] = unpacked[
                i, c * CAP : (c + 1) * CAP
            ]
    whole[...] = whole32[...].astype(BF16)


def spread_rows(value, c, n, held, unpacked):
    held[...] = value
    for i in range(n):
        unpacked[i, c * CAP : (c + 1) * CAP] = held[i * CAP : (i + 1) * CAP]


def forward_kernel(n, *refs):
    blocks, (gate, up, down) = refs[:n], refs[n : n + 3]
    x, pre_gate, pre_up, act, gate_v, up_v, down_v = refs[n + 3 : n + 10]
    parts = refs[n + 10 : 2 * n + 10]
    sems, unpacked, whole32, held = refs[2 * n + 10 :]
    width = gate.shape[0]
    fetches = []
    for c in range(PACK):
        k = columns(c, width)
        fetches.append(
            (
                pltpu.make_async_copy(gate.at[k], gate_v.at[k], sems.at[0, c]),
                pltpu.make_async_copy(up.at[k], up_v.at[k], sems.at[1, c]),
                pltpu.make_async_copy(down.at[:, k], down_v.at[:, k], sems.at[2, c]),
            )
        )
    for fetch_g, fetch_u, _ in fetches:
        fetch_g.start()
        fetch_u.start()
    for _, _, fetch_d in fetches:
        fetch_d.start()
    gather_rows(blocks, unpacked, whole32, x)
    acc_g = jnp.zeros(pre_gate.shape, F32)
    acc_u = jnp.zeros(pre_up.shape, F32)
    for c, (fetch_g, fetch_u, _) in enumerate(fetches):
        k = columns(c, width)
        fetch_g.wait()
        acc_g = acc_g + dot(x[:, k], gate_v[k])
        fetch_u.wait()
        acc_u = acc_u + dot(x[:, k], up_v[k])
    pre_gate[...] = acc_g
    pre_up[...] = acc_u
    activated = (acc_g * jax.nn.sigmoid(acc_g) * acc_u).astype(BF16)
    act[...] = activated
    for c, (_, _, fetch_d) in enumerate(fetches):
        fetch_d.wait()
        value = dot(activated, down_v[:, columns(c, width)])
        spread_rows(value, c, n, held.at[c], unpacked)
    for i, p in enumerate(parts):
        p[...] = unpacked[i].astype(BF16)


def out_rows(act, down, held, unpacked, parts):
    n = len(parts)
    for c in range(PACK):
        value = dot(act, down[:, columns(c, down.shape[1])])
        spread_rows(value, c, n, held.at[c], unpacked)
    for i, p in enumerate(parts):
        p[...] = unpacked[i].astype(BF16)


def down_kernel(n, act, down, _, *refs):
    parts, (unpacked, held) = refs[:n], refs[n:]
    hidden, width = down.shape
    out_rows(act[:, 3 * width + hidden : 3 * width + 2 * hidden], down, held, unpacked, parts)


def back_rows(gg, gu, gate, up, held, unpacked, parts):
    n = len(parts)
    for c in range(PACK):
        k = columns(c, gate.shape[0])
        value = dot(gg, gate[k], 1, 1) + dot(gu, up[k], 1, 1)
        spread_rows(value, c, n, held.at[c], unpacked)
    for i, p in enumerate(parts):
        p[...] = unpacked[i].astype(BF16)


def tick1_kernel(n, *refs):
    blocks, (x0, act0, gate, up, down) = refs[:n], refs[n : n + 5]
    (kept,) = refs[n + 5 : n + 6]
    parts = refs[n + 6 : 2 * n + 6]
    unpacked, whole32, held, x, g = refs[2 * n + 6 :]
    gather_rows([b.at[:PACKED] for b in blocks], unpacked, whole32.at[0], x)
    gather_rows([b.at[PACKED:] for b in blocks], unpacked, whole32.at[1], g)
    width, hidden = gate.shape
    kept[:, :width] = x0[...]
    kept[:, width : 2 * width] = x[...]
    kept[:, 2 * width : 3 * width] = g[...]
    narrow = [slice(3 * width + i * hidden, 3 * width + (i + 1) * hidden) for i in range(4)]
    kept[:, narrow[0]] = act0[...]
    acc_g = dot(x[...], gate[...])
    acc_u = dot(x[...], up[...])
    acc_a = dot(g[...], down[...], 1, 1)
    gg, gu = silu_grads(acc_g, acc_u, acc_a)
    kept[:, narrow[1]] = (acc_g * jax.nn.sigmoid(acc_g) * acc_u).astype(BF16)
    kept[:, narrow[2]] = gg
    kept[:, narrow[3]] = gu
    back_rows(gg, gu, gate, up, held, unpacked, parts)


def tick0_kernel(n, *refs):
    blocks, (pre_gate, pre_up, gate, up, down) = refs[:n], refs[n : n + 5]
    (g_grad,) = refs[n + 5 : n + 6]
    parts = refs[n + 6 : 2 * n + 6]
    unpacked, whole32, held, g = refs[2 * n + 6 :]
    gather_rows(blocks, unpacked, whole32, g)
    width, hidden = gate.shape
    g_grad[:, :width] = g[...]
    acc_a = dot(g[...], down[...], 1, 1)
    gg, gu = silu_grads(pre_gate[...], pre_up[...], acc_a)
    g_grad[:, width : width + hidden] = gg
    g_grad[:, width + hidden :] = gu
    back_rows(gg, gu, gate, up, held, unpacked, parts)


def whole_of(blocks):
    return jnp.concatenate([b.astype(F32) for b in blocks], axis=0).astype(BF16)


def turn_kernel(m, *refs):
    x0, x1, act0, act1 = (refs[i * m : (i + 1) * m] for i in range(4))
    x_t, act_t = refs[4 * m :]
    x_t[...] = whole_of([b[...] for b in x0 + x1]).T

    @pl.when(pl.program_id(0) == 0)
    def _():
        act_t[...] = whole_of([b[...] for b in act0 + act1]).T


def down_grad_kernel(m, act_t, *refs):
    g0, g1, (down_out, both) = refs[:m], refs[m : 2 * m], refs[2 * m :]

    @pl.when(pl.program_id(0) == 0)
    def _():
        both[...] = whole_of([b[...] for b in g0 + g1])

    for c in range(PACK):
        k = columns(c, both.shape[1])
        down_out[:, k] = dot(act_t[...], both[:, k]).astype(BF16)


def input_grad_kernel(m, x_t, *refs):
    gates0, ups0, gates1, ups1 = (refs[i * m : (i + 1) * m] for i in range(4))
    gate_out, up_out, both = refs[4 * m :]
    hidden = gate_out.shape[1]

    @pl.when(pl.program_id(0) == 0)
    def _():
        both[:, :hidden] = whole_of([b[...] for b in gates0 + gates1])
        both[:, hidden:] = whole_of([b[...] for b in ups0 + ups1])

    gate_out[...] = dot(x_t[...], both[:, :hidden]).astype(BF16)
    up_out[...] = dot(x_t[...], both[:, hidden:]).astype(BF16)


def chunked_call(kernel, ins, outs, scratch=(), steps=PACK):
    return pl.pallas_call(
        kernel,
        grid=(steps,),
        out_shape=[jax.ShapeDtypeStruct(s, BF16) for s, _, _ in outs],
        in_specs=[pl.BlockSpec(block, index) for _, block, index in ins],
        out_specs=[pl.BlockSpec(block, index) for _, block, index in outs],
        scratch_shapes=list(scratch),
        compiler_params=pltpu.CompilerParams(vmem_limit_bytes=VMEM_SMALL),
        cost_estimate=pl.CostEstimate(flops=0, bytes_accessed=COST_BYTES, transcendentals=0),
    )(*(a for a, _, _ in ins))


def constant(at):
    return lambda c: (0, at)


def chunk_at(at):
    return lambda c: (0, at + c)


def turned(kept, width, hidden):
    m = len(kept)
    rows = kept[0].shape[0]
    step = width // PACK
    first = 3 * width // hidden
    ins = [(a, (rows, step), chunk_at(at)) for at in (0, PACK) for a in kept]
    ins += [(a, (rows, hidden), constant(at)) for at in (first, first + 1) for a in kept]
    outs = [
        ((width, 2 * m * rows), (step, 2 * m * rows), lambda c: (c, 0)),
        ((hidden, 2 * m * rows), (hidden, 2 * m * rows), lambda c: (0, 0)),
    ]
    return chunked_call(functools.partial(turn_kernel, m), ins, outs)


def down_grads(act_t, g_grad0, kept, width, hidden):
    m = len(kept)
    rows = kept[0].shape[0]
    block = max(hidden // 4, 16)
    ins = [(act_t, (block, act_t.shape[1]), lambda c: (c, 0))]
    ins += [(a, (rows, width), constant(0)) for a in g_grad0]
    ins += [(a, (rows, width), constant(2)) for a in kept]
    outs = [((hidden, width), (block, width), lambda c: (c, 0))]
    scratch = [pltpu.VMEM((2 * m * rows, width), BF16)]
    kernel = functools.partial(down_grad_kernel, m)
    return chunked_call(kernel, ins, outs, scratch, hidden // block)


def input_grads(x_t, g_grad0, kept, width, hidden):
    m = len(kept)
    rows = kept[0].shape[0]
    step = width // PACK
    first, second = width // hidden, 3 * width // hidden + 2
    ins = [(x_t, (step, x_t.shape[1]), lambda c: (c, 0))]
    ins += [(a, (rows, hidden), constant(at)) for at in (first, first + 1) for a in g_grad0]
    ins += [(a, (rows, hidden), constant(at)) for at in (second, second + 1) for a in kept]
    tall = ((width, hidden), (step, hidden), lambda c: (c, 0))
    scratch = [pltpu.VMEM((2 * m * rows, 2 * hidden), BF16)]
    return chunked_call(functools.partial(input_grad_kernel, m), ins, [tall, tall], scratch)


def from_group(block):
    n = lax.axis_size("expert")
    return [block] + [shifted(block, "expert", k) for k in range(1, n)]


def to_group(blocks):
    return [blocks[0]] + [shifted(b, "expert", -k) for k, b in enumerate(blocks) if k]


def copies_of(block):
    n = lax.axis_size("dp")
    return [block] + [shifted(block, "dp", k) for k in range(1, n)]


def shards(tokens, cotangent, w_gate, w_up, w_down, routes, gates):
    gate, up, down = w_gate[0], w_up[0], w_down[0]
    width, hidden = gate.shape
    step = width // PACK
    n = lax.axis_size("expert")
    rows = -(-n * CAP // 8) * 8
    routes = jnp.transpose(routes, (0, 2, 1))
    gates = jnp.transpose(gates, (0, 2, 1))
    one = ((PACKED, step), BF16)
    part = functools.partial
    unpacked = pltpu.VMEM((n, PACKED, step), F32)
    flat32 = pltpu.VMEM((rows, width), F32)
    held = pltpu.VMEM((PACK, rows, step), F32)
    flat = pltpu.VMEM((rows, width), BF16)
    wide = ((rows, width + 2 * hidden), BF16)
    dma = [pltpu.SemaphoreType.DMA]

    cot1_all = shifted(cotangent, "section", -1)
    next_routes = shifted(routes[1:], "section", -1)

    raw0, normed0, early = call(
        first_rows_kernel,
        [pltpu.VMEM(*one), pltpu.VMEM(*one), ((EARLY * tokens.shape[0], step), BF16)],
        [tokens, routes],
        any_args=(0, 1),
        scratch=[
            pltpu.SemaphoreType.DMA((tokens.shape[0] // 16 + 1,)),
            pltpu.VMEM(tokens.shape, BF16),
            pltpu.VMEM(routes.shape, jnp.int32),
        ],
        vmem=VMEM_ALL,
    )
    early = shifted(early, "section", 2)
    blocks = from_group(normed0)
    x0, pre_gate0, pre_up0, act0, gate, up, down, *parts = call(
        part(forward_kernel, n),
        [((rows, width), BF16), ((rows, hidden), F32), ((rows, hidden), F32)]
        + [((rows, hidden), BF16)]
        + [pltpu.VMEM(a.shape, BF16) for a in (gate, up, down)]
        + [one] * n,
        [*blocks, gate, up, down],
        any_args=(n, n + 1, n + 2),
        scratch=[pltpu.SemaphoreType.DMA((3, PACK)), unpacked, flat32, held],
        vmem=VMEM_LOAD,
    )
    parts = to_group(parts)
    upd0, h1 = call(
        part(update0_kernel, n),
        [one, one],
        [*parts, raw0, routes, gates, tokens, next_routes],
    )
    h1 = shifted(h1, "section", 1)
    (rest,) = call(
        merge_kernel,
        [(((PACK - EARLY) * tokens.shape[0] + TAIL, step), BF16)],
        [tokens, upd0, routes, next_routes],
        scratch=[pltpu.VMEM((TAIL, step), F32)],
    )
    cot1, scaled1 = call(grad_rows_kernel, [one, one], [cot1_all, routes, gates])

    (enter1,) = call(
        enter1_kernel,
        [((2 * PACKED, step), BF16)],
        [h1, scaled1],
    )
    (cot1_all,) = call(
        release_kernel,
        [(tokens.shape, BF16)],
        [cot1_all, h1, scaled1, early],
        any_args=(0, 1, 2, 3),
        any_outs=(0,),
        aliases={0: 0},
    )
    cot0_all = shifted(cot1_all, "section", -1)
    blocks = from_group(enter1)
    kept, *parts = call(
        part(tick1_kernel, n),
        [((rows, 3 * width + 4 * hidden), BF16)] + [one] * n,
        [*blocks, x0, act0, gate, up, down],
        scratch=[unpacked, pltpu.VMEM((2, rows, width), F32), held, flat, flat],
    )
    parts = to_group(parts)
    (upd1,) = call(
        part(grad1_kernel, n),
        [one],
        [*parts, h1, cot1],
    )
    upd1 = shifted(upd1, "section", -1)
    kept_all = copies_of(kept)

    (rest,) = call(
        release_kernel,
        [(rest.shape, BF16)],
        [rest, cot0_all, upd1],
        any_args=(0, 1, 2),
        any_outs=(0,),
        aliases={0: 0},
    )
    c0, enter0 = call(
        enter0_kernel,
        [one, one],
        [upd1, next_routes, routes, gates, cot0_all, rest],
        any_args=(5,),
    )
    rest = shifted(rest, "section", 2)
    blocks = from_group(enter0)
    g_grad0, *parts = call(
        part(tick0_kernel, n),
        [wide] + [one] * n,
        [*blocks, pre_gate0, pre_up0, gate, up, down],
        scratch=[unpacked, flat32, held, flat],
    )
    parts = to_group(parts)
    g_grad0_all = copies_of(g_grad0)
    (grad,) = call(
        part(finish_grad_kernel, n),
        [(tokens.shape, BF16)],
        [*parts, raw0, c0, routes, upd1, next_routes, cot0_all],
    )
    outs = call(
        part(down_kernel, n),
        [one] * n,
        [kept, down, g_grad0],
        any_args=(2,),
        scratch=[unpacked, held],
    )
    outs = to_group(outs)
    (last1,) = call(part(update1_kernel, n), [one], [*outs, h1, routes, gates])
    last1 = shifted(last1, "section", 1)
    x_t, act_t = turned(kept_all, width, hidden)
    (down_out,) = down_grads(act_t, g_grad0_all, kept_all, width, hidden)
    gate_out, up_out = input_grads(x_t, g_grad0_all, kept_all, width, hidden)
    height = tokens.shape[0]
    base, turned_select, hit = call(
        prepare_state_kernel,
        [
            pltpu.VMEM(tokens.shape, BF16),
            pltpu.VMEM((height, PACKED), F32),
            pltpu.VMEM((height, 128), F32),
        ],
        [early, rest],
        scratch=[pltpu.VMEM((TAIL, step), F32)],
    )
    (state,) = call(
        finish_state_kernel,
        [(tokens.shape, BF16)],
        [base, turned_select, hit, last1],
        any_outs=(0,),
        scratch=[pltpu.VMEM(tokens.shape, BF16), pltpu.SemaphoreType.DMA((height // 16,))],
    )
    return (grad, state, gate_out[None], up_out[None], down_out[None])


def solution(mesh):
    rows = P(("section", "expert", "dp"), None)
    slots = P(None, ("section", "expert", "dp"), None)
    cols = P("section", None, "expert")
    hidden = P("section", "expert", None)
    return jax.shard_map(
        shards,
        mesh=mesh,
        in_specs=(rows, rows, cols, cols, hidden, slots, slots),
        out_specs=(rows, rows, cols, cols, hidden),
        check_vma=False,
    )
```

```python
import functools

import jax
import jax.numpy as jnp
from jax import lax
from jax.experimental import pallas as pl
from jax.experimental.pallas import tpu as pltpu
from jax.sharding import PartitionSpec as P

CAP = 10
PACK = 8
PACKED = CAP * PACK
EPSILON = 1e-06
F32 = jnp.float32
BF16 = jnp.bfloat16
VMEM_SMALL = 24 * 1024 * 1024
VMEM_LOAD = 36 * 1024 * 1024
VMEM_ALL = 60 * 1024 * 1024
COST_BYTES = 1024
TOP = 4
TAIL = 16
EARLY = 1


def shifted(block, axis, distance):
    size = lax.axis_size(axis)
    return lax.ppermute(block, axis, [((i - distance) % size, i) for i in range(size)])


def dot(a, b, ca=1, cb=0):
    return lax.dot_general(a, b, (((ca,), (cb,)), ((), ())), preferred_element_type=F32)


def call(
    kernel, outs, args, *, any_args=(), any_outs=(), scratch=(), vmem=VMEM_SMALL, aliases=None
):
    outs = [jax.ShapeDtypeStruct(*o) if isinstance(o, tuple) else o for o in outs]
    anywhere = pl.BlockSpec(memory_space=pl.ANY)
    near = pl.BlockSpec(memory_space=pltpu.VMEM)
    return pl.pallas_call(
        kernel,
        out_shape=outs,
        in_specs=[anywhere if i in any_args else near for i in range(len(args))],
        out_specs=[anywhere if i in any_outs else near for i in range(len(outs))],
        scratch_shapes=list(scratch),
        compiler_params=pltpu.CompilerParams(vmem_limit_bytes=vmem),
        cost_estimate=pl.CostEstimate(flops=0, bytes_accessed=COST_BYTES, transcendentals=0),
        input_output_aliases=aliases or {},
    )(*args)


def packed_index(shape, dim):
    place = lax.broadcasted_iota(jnp.int32, shape, dim).astype(F32)
    chunk = jnp.floor((place + 0.5) * (1.0 / CAP))
    return place - CAP * chunk, chunk


def select_of(routes):
    hits = (routes == 0).astype(F32)
    marked = jnp.sum(hits, axis=0, keepdims=True)
    rows = routes.shape[1]
    before = lax.broadcasted_iota(jnp.int32, (rows, rows), 0) < lax.broadcasted_iota(
        jnp.int32, (rows, rows), 1
    )
    wide = jnp.broadcast_to(marked, (PACKED, rows))
    places = dot(wide.astype(BF16), before.astype(F32).astype(BF16))
    slot, _ = packed_index((PACKED, rows), 0)
    return jnp.where((places == slot) & (wide > 0.5), 1.0, 0.0)


def slot_gates(select, routes, gates):
    weights = jnp.sum(jnp.where(routes == 0, gates, 0.0), axis=0, keepdims=True)
    return jnp.sum(select * weights, axis=1, keepdims=True)


def chunk_of(select, c):
    _, chunk = packed_index(select.shape, 0)
    return jnp.where(chunk == c, select, 0.0).astype(BF16)


def columns(c, width):
    return slice(c * (width // PACK), (c + 1) * (width // PACK))


def pick(select, pieces):
    total = None
    for block, (r0, r1, c0, c1) in pieces:
        width = block.shape[1] // (c1 - c0)
        for c in range(c0, c1):
            columns_here = slice((c - c0) * width, (c - c0 + 1) * width)
            part = dot(chunk_of(select[:, r0:r1], c), block[:, columns_here])
            total = part if total is None else total + part
    return total


def whole_block(block):
    return [(block, (0, block.shape[0], 0, PACK))]


def over_chunks(row_sums):
    slot_r, _ = packed_index((PACKED, PACKED), 0)
    slot_c, _ = packed_index((PACKED, PACKED), 1)
    same = jnp.where(slot_r == slot_c, 1.0, 0.0)
    wide = jnp.broadcast_to(row_sums, (PACKED, 128))
    return jnp.dot(
        same, wide, precision=lax.Precision.HIGHEST, preferred_element_type=F32
    )[:, :1]


def mean_of(values):
    return over_chunks(jnp.sum(values, axis=-1, keepdims=True)) * (1.0 / (PACK * values.shape[1]))


def inv_rms_of(values):
    return lax.rsqrt(mean_of(values * values) + EPSILON)


def merged(select_to, select_from, fresh, old):
    same = dot(select_to.astype(BF16), select_from.astype(BF16), 1, 1)
    _, chunk_r = packed_index(same.shape, 0)
    _, chunk_c = packed_index(same.shape, 1)
    same = jnp.where(chunk_r == chunk_c, same, 0.0)
    taken = jnp.sum(same, axis=1, keepdims=True)
    return jnp.where(taken > 0.5, dot(same.astype(BF16), fresh), old).astype(BF16)


def summed(parts):
    total = parts[0][...].astype(F32)
    for p in parts[1:]:
        total = total + p[...].astype(F32)
    return total


def hit_rows(select):
    ones = jnp.ones((PACKED, 128), BF16)
    return dot(chunk_of(select, 0), ones, 0, 0)[:, :1] > 0.5


def placed(c, old, select, hit, rows):
    return jnp.where(hit, dot(chunk_of(select, c), rows, 0, 0), old.astype(F32)).astype(BF16)


def start_rows(source, target, sems):
    copies = []
    for i in range(source.shape[0] // 16):
        r = pl.ds(16 * i, 16)
        copies.append(pltpu.make_async_copy(source.at[r], target.at[r], sems.at[i]))
        copies[-1].start()
    return copies


def first_rows_kernel(tokens, routes_far, raw, normed, early, sems, held, routes):
    fetch_routes = pltpu.make_async_copy(routes_far, routes, sems.at[sems.shape[0] - 1])
    fetch_routes.start()
    fetches = start_rows(tokens, held, sems)
    fetch_routes.wait()
    select = select_of(routes[0])
    for fetch in fetches:
        fetch.wait()
    values = pick(select, whole_block(held))
    raw[...] = values.astype(BF16)
    normed[...] = (values * inv_rms_of(values)).astype(BF16)
    height, width = held.shape
    for c in range(EARLY):
        early[c * height : (c + 1) * height] = held[:, columns(c, width)]


def update0_kernel(n, *refs):
    parts, (raw, routes, gates, tokens, next_routes, upd, onward) = refs[:n], refs[n:]
    select = select_of(routes[0])
    select_next = select_of(next_routes[0])
    weight = slot_gates(select, routes[0], gates[0])
    fresh = (raw[...].astype(F32) + weight * summed(parts)).astype(BF16)
    old = pick(select_next, whole_block(tokens))
    onward[...] = merged(select_next, select, fresh, old)
    upd[...] = fresh


def merge_kernel(tokens, upd, routes, next_routes, out, last):
    select = select_of(routes[0])
    hit = hit_rows(select)
    height, width = tokens.shape
    for c in range(EARLY, PACK):
        value = placed(c, tokens[:, columns(c, width)], select, hit, upd[...])
        out[(c - EARLY) * height : (c - EARLY + 1) * height] = value
    last[...] = jnp.zeros(last.shape, F32)
    last[:CAP] = upd[...].astype(F32)[:CAP]
    last[CAP : CAP + TOP, :height] = routes[0].astype(F32)
    last[CAP : CAP + TOP, height : 2 * height] = next_routes[0].astype(F32)
    out[(PACK - EARLY) * height :] = last[...].astype(BF16)


def release_kernel(*_):
    pass


def grad_rows_kernel(bulk, routes, gates, cot, scaled):
    select = select_of(routes[1])
    values = pick(select, whole_block(bulk))
    cot[...] = values.astype(BF16)
    scaled[...] = (slot_gates(select, routes[1], gates[1]) * values).astype(BF16)


def update1_kernel(n, *refs):
    parts, (h, routes, gates, upd) = refs[:n], refs[n:]
    select = select_of(routes[1])
    weight = slot_gates(select, routes[1], gates[1])
    upd[...] = (h[...].astype(F32) + weight * summed(parts)).astype(BF16)


def enter1_kernel(h, scaled, out):
    values = h[...].astype(F32)
    out[:PACKED] = (values * inv_rms_of(values)).astype(BF16)
    out[PACKED:] = scaled[...]


def state_grad(parts, h, c):
    total = summed(parts)
    values = h.astype(F32)
    inv = inv_rms_of(values)
    inner = mean_of(total * values)
    return (c.astype(F32) + inv * total - inv * inv * inv * values * inner).astype(BF16)


def grad1_kernel(n, *refs):
    parts, (h, cot, upd) = refs[:n], refs[n:]
    upd[...] = state_grad(parts, h[...], cot[...])


def enter0_kernel(upd1, next_routes, routes, gates, bulk, _, c0, out):
    select = select_of(routes[0])
    old = pick(select, whole_block(bulk))
    rows = merged(select, select_of(next_routes[0]), upd1[...], old)
    c0[...] = rows
    out[...] = (slot_gates(select, routes[0], gates[0]) * rows.astype(F32)).astype(BF16)


def finish_grad_kernel(n, *refs):
    parts, (h, c, routes, upd1, next_routes, bulk, out) = refs[:n], refs[n:]
    fresh = state_grad(parts, h[...], c[...])
    first, second = select_of(next_routes[0]), select_of(routes[0])
    hit1, hit2 = hit_rows(first), hit_rows(second)
    for chunk in range(PACK):
        k = columns(chunk, out.shape[1])
        value = placed(chunk, bulk[:, k], first, hit1, upd1[...])
        out[:, k] = placed(chunk, value, second, hit2, fresh)


def prepare_state_kernel(early, rest, out, turned_select, hit, last):
    height, width = out.shape
    at = (PACK - EARLY) * height
    last[...] = rest[at:].astype(F32)
    first = select_of(last[CAP : CAP + TOP, :height])
    second = select_of(last[CAP : CAP + TOP, height : 2 * height])
    rows = jnp.concatenate([last[...], jnp.zeros((PACKED - TAIL, last.shape[1]), F32)], axis=0)
    out[:, columns(0, width)] = placed(0, early[...], first, hit_rows(first), rows.astype(BF16))
    for c in range(EARLY, PACK):
        out[:, columns(c, width)] = rest[(c - EARLY) * height : (c - EARLY + 1) * height]
    turned_select[...] = second.T
    ones = jnp.ones((PACKED, 128), BF16)
    hit[...] = dot(chunk_of(second, 0), ones, 0, 0)


def finish_state_kernel(base, turned_select, hit, upd1, out, outs, sems):
    height, width = out.shape
    _, chunk = packed_index(turned_select.shape, 1)
    copies = []
    for r0 in range(0, height, height // 2):
        r = slice(r0, r0 + height // 2)
        taken = hit[r, :1] > 0.5
        for c in range(PACK):
            k = columns(c, width)
            select = jnp.where(chunk[r] == c, turned_select[r], 0.0).astype(BF16)
            value = jnp.where(taken, dot(select, upd1[...]), base[r, k].astype(F32))
            outs[r, k] = value.astype(BF16)
        for i in range(r0 // 16, r.stop // 16):
            b = pl.ds(16 * i, 16)
            copies.append(pltpu.make_async_copy(outs.at[b], out.at[b], sems.at[i]))
            copies[-1].start()
    for copy in copies:
        copy.wait()


def silu_grads(pre_gate, pre_up, grad_act):
    sig = jax.nn.sigmoid(pre_gate)
    grad_gate = (grad_act * pre_up * sig * (1.0 + pre_gate * (1.0 - sig))).astype(BF16)
    grad_up = (grad_act * (pre_gate * sig)).astype(BF16)
    return grad_gate, grad_up


def gather_rows(blocks, unpacked, whole32, whole):
    width = whole.shape[1]
    used = len(blocks) * CAP
    if used < whole.shape[0]:
        whole32[used:] = jnp.zeros((whole.shape[0] - used, width), F32)
    for i, b in enumerate(blocks):
        unpacked[i] = b[...].astype(F32)
        for c in range(PACK):
            whole32[i * CAP : (i + 1) * CAP, columns(c, width)] = unpacked[
                i, c * CAP : (c + 1) * CAP
            ]
    whole[...] = whole32[...].astype(BF16)


def spread_rows(value, c, n, held, unpacked):
    held[...] = value
    for i in range(n):
        unpacked[i, c * CAP : (c + 1) * CAP] = held[i * CAP : (i + 1) * CAP]


def forward_kernel(n, *refs):
    blocks, (gate, up, down) = refs[:n], refs[n : n + 3]
    x, pre_gate, pre_up, act, gate_v, up_v, down_v = refs[n + 3 : n + 10]
    parts = refs[n + 10 : 2 * n + 10]
    sems, unpacked, whole32, held = refs[2 * n + 10 :]
    width = gate.shape[0]
    fetches = []
    for c in range(PACK):
        k = columns(c, width)
        fetches.append(
            (
                pltpu.make_async_copy(gate.at[k], gate_v.at[k], sems.at[0, c]),
                pltpu.make_async_copy(up.at[k], up_v.at[k], sems.at[1, c]),
                pltpu.make_async_copy(down.at[:, k], down_v.at[:, k], sems.at[2, c]),
            )
        )
    for fetch_g, fetch_u, _ in fetches:
        fetch_g.start()
        fetch_u.start()
    for _, _, fetch_d in fetches:
        fetch_d.start()
    gather_rows(blocks, unpacked, whole32, x)
    acc_g = jnp.zeros(pre_gate.shape, F32)
    acc_u = jnp.zeros(pre_up.shape, F32)
    for c, (fetch_g, fetch_u, _) in enumerate(fetches):
        k = columns(c, width)
        fetch_g.wait()
        acc_g = acc_g + dot(x[:, k], gate_v[k])
        fetch_u.wait()
        acc_u = acc_u + dot(x[:, k], up_v[k])
    pre_gate[...] = acc_g
    pre_up[...] = acc_u
    activated = (acc_g * jax.nn.sigmoid(acc_g) * acc_u).astype(BF16)
    act[...] = activated
    for c, (_, _, fetch_d) in enumerate(fetches):
        fetch_d.wait()
        value = dot(activated, down_v[:, columns(c, width)])
        spread_rows(value, c, n, held.at[c], unpacked)
    for i, p in enumerate(parts):
        p[...] = unpacked[i].astype(BF16)


def out_rows(act, down, held, unpacked, parts):
    n = len(parts)
    for c in range(PACK):
        value = dot(act, down[:, columns(c, down.shape[1])])
        spread_rows(value, c, n, held.at[c], unpacked)
    for i, p in enumerate(parts):
        p[...] = unpacked[i].astype(BF16)


def down_kernel(n, act, down, _, *refs):
    parts, (unpacked, held) = refs[:n], refs[n:]
    hidden, width = down.shape
    out_rows(act[:, 3 * width + hidden : 3 * width + 2 * hidden], down, held, unpacked, parts)


def back_rows(gg, gu, gate, up, held, unpacked, parts):
    n = len(parts)
    for c in range(PACK):
        k = columns(c, gate.shape[0])
        value = dot(gg, gate[k], 1, 1) + dot(gu, up[k], 1, 1)
        spread_rows(value, c, n, held.at[c], unpacked)
    for i, p in enumerate(parts):
        p[...] = unpacked[i].astype(BF16)


def tick1_kernel(n, *refs):
    blocks, (x0, act0, gate, up, down) = refs[:n], refs[n : n + 5]
    (kept,) = refs[n + 5 : n + 6]
    parts = refs[n + 6 : 2 * n + 6]
    unpacked, whole32, held, x, g = refs[2 * n + 6 :]
    gather_rows([b.at[:PACKED] for b in blocks], unpacked, whole32.at[0], x)
    gather_rows([b.at[PACKED:] for b in blocks], unpacked, whole32.at[1], g)
    width, hidden = gate.shape
    kept[:, :width] = x0[...]
    kept[:, width : 2 * width] = x[...]
    kept[:, 2 * width : 3 * width] = g[...]
    narrow = [slice(3 * width + i * hidden, 3 * width + (i + 1) * hidden) for i in range(4)]
    kept[:, narrow[0]] = act0[...]
    acc_g = dot(x[...], gate[...])
    acc_u = dot(x[...], up[...])
    acc_a = dot(g[...], down[...], 1, 1)
    gg, gu = silu_grads(acc_g, acc_u, acc_a)
    kept[:, narrow[1]] = (acc_g * jax.nn.sigmoid(acc_g) * acc_u).astype(BF16)
    kept[:, narrow[2]] = gg
    kept[:, narrow[3]] = gu
    back_rows(gg, gu, gate, up, held, unpacked, parts)


def tick0_kernel(n, *refs):
    blocks, (pre_gate, pre_up, gate, up, down) = refs[:n], refs[n : n + 5]
    (g_grad,) = refs[n + 5 : n + 6]
    parts = refs[n + 6 : 2 * n + 6]
    unpacked, whole32, held, g = refs[2 * n + 6 :]
    gather_rows(blocks, unpacked, whole32, g)
    width, hidden = gate.shape
    g_grad[:, :width] = g[...]
    acc_a = dot(g[...], down[...], 1, 1)
    gg, gu = silu_grads(pre_gate[...], pre_up[...], acc_a)
    g_grad[:, width : width + hidden] = gg
    g_grad[:, width + hidden :] = gu
    back_rows(gg, gu, gate, up, held, unpacked, parts)


def whole_of(blocks):
    return jnp.concatenate([b.astype(F32) for b in blocks], axis=0).astype(BF16)


def turn_kernel(m, *refs):
    x0, x1, act0, act1 = (refs[i * m : (i + 1) * m] for i in range(4))
    x_t, act_t = refs[4 * m :]
    x_t[...] = whole_of([b[...] for b in x0 + x1]).T

    @pl.when(pl.program_id(0) == 0)
    def _():
        act_t[...] = whole_of([b[...] for b in act0 + act1]).T


def down_grad_kernel(m, act_t, *refs):
    g0, g1, (down_out, both) = refs[:m], refs[m : 2 * m], refs[2 * m :]

    @pl.when(pl.program_id(0) == 0)
    def _():
        both[...] = whole_of([b[...] for b in g0 + g1])

    for c in range(PACK):
        k = columns(c, both.shape[1])
        down_out[:, k] = dot(act_t[...], both[:, k]).astype(BF16)


def input_grad_kernel(m, x_t, *refs):
    gates0, ups0, gates1, ups1 = (refs[i * m : (i + 1) * m] for i in range(4))
    gate_out, up_out, both = refs[4 * m :]
    hidden = gate_out.shape[1]

    @pl.when(pl.program_id(0) == 0)
    def _():
        both[:, :hidden] = whole_of([b[...] for b in gates0 + gates1])
        both[:, hidden:] = whole_of([b[...] for b in ups0 + ups1])

    gate_out[...] = dot(x_t[...], both[:, :hidden]).astype(BF16)
    up_out[...] = dot(x_t[...], both[:, hidden:]).astype(BF16)


def chunked_call(kernel, ins, outs, scratch=(), steps=PACK):
    return pl.pallas_call(
        kernel,
        grid=(steps,),
        out_shape=[jax.ShapeDtypeStruct(s, BF16) for s, _, _ in outs],
        in_specs=[pl.BlockSpec(block, index) for _, block, index in ins],
        out_specs=[pl.BlockSpec(block, index) for _, block, index in outs],
        scratch_shapes=list(scratch),
        compiler_params=pltpu.CompilerParams(vmem_limit_bytes=VMEM_SMALL),
        cost_estimate=pl.CostEstimate(flops=0, bytes_accessed=COST_BYTES, transcendentals=0),
    )(*(a for a, _, _ in ins))


def constant(at):
    return lambda c: (0, at)


def chunk_at(at):
    return lambda c: (0, at + c)


def turned(kept, width, hidden):
    m = len(kept)
    rows = kept[0].shape[0]
    step = width // PACK
    first = 3 * width // hidden
    ins = [(a, (rows, step), chunk_at(at)) for at in (0, PACK) for a in kept]
    ins += [(a, (rows, hidden), constant(at)) for at in (first, first + 1) for a in kept]
    outs = [
        ((width, 2 * m * rows), (step, 2 * m * rows), lambda c: (c, 0)),
        ((hidden, 2 * m * rows), (hidden, 2 * m * rows), lambda c: (0, 0)),
    ]
    return chunked_call(functools.partial(turn_kernel, m), ins, outs)


def down_grads(act_t, g_grad0, kept, width, hidden):
    m = len(kept)
    rows = kept[0].shape[0]
    block = max(hidden // 4, 16)
    ins = [(act_t, (block, act_t.shape[1]), lambda c: (c, 0))]
    ins += [(a, (rows, width), constant(0)) for a in g_grad0]
    ins += [(a, (rows, width), constant(2)) for a in kept]
    outs = [((hidden, width), (block, width), lambda c: (c, 0))]
    scratch = [pltpu.VMEM((2 * m * rows, width), BF16)]
    kernel = functools.partial(down_grad_kernel, m)
    return chunked_call(kernel, ins, outs, scratch, hidden // block)


def input_grads(x_t, g_grad0, kept, width, hidden):
    m = len(kept)
    rows = kept[0].shape[0]
    step = width // PACK
    first, second = width // hidden, 3 * width // hidden + 2
    ins = [(x_t, (step, x_t.shape[1]), lambda c: (c, 0))]
    ins += [(a, (rows, hidden), constant(at)) for at in (first, first + 1) for a in g_grad0]
    ins += [(a, (rows, hidden), constant(at)) for at in (second, second + 1) for a in kept]
    tall = ((width, hidden), (step, hidden), lambda c: (c, 0))
    scratch = [pltpu.VMEM((2 * m * rows, 2 * hidden), BF16)]
    return chunked_call(functools.partial(input_grad_kernel, m), ins, [tall, tall], scratch)


def from_group(block):
    n = lax.axis_size("expert")
    return [block] + [shifted(block, "expert", k) for k in range(1, n)]


def to_group(blocks):
    return [blocks[0]] + [shifted(b, "expert", -k) for k, b in enumerate(blocks) if k]


def copies_of(block):
    n = lax.axis_size("dp")
    return [block] + [shifted(block, "dp", k) for k in range(1, n)]


def shards(tokens, cotangent, w_gate, w_up, w_down, routes, gates):
    gate, up, down = w_gate[0], w_up[0], w_down[0]
    width, hidden = gate.shape
    step = width // PACK
    n = lax.axis_size("expert")
    rows = -(-n * CAP // 16) * 16
    routes = jnp.transpose(routes, (0, 2, 1))
    gates = jnp.transpose(gates, (0, 2, 1))
    one = ((PACKED, step), BF16)
    part = functools.partial
    unpacked = pltpu.VMEM((n, PACKED, step), F32)
    flat32 = pltpu.VMEM((rows, width), F32)
    held = pltpu.VMEM((PACK, rows, step), F32)
    flat = pltpu.VMEM((rows, width), BF16)
    wide = ((rows, width + 2 * hidden), BF16)
    dma = [pltpu.SemaphoreType.DMA]

    cot1_all = shifted(cotangent, "section", -1)
    next_routes = shifted(routes[1:], "section", -1)

    raw0, normed0, early = call(
        first_rows_kernel,
        [pltpu.VMEM(*one), pltpu.VMEM(*one), ((EARLY * tokens.shape[0], step), BF16)],
        [tokens, routes],
        any_args=(0, 1),
        scratch=[
            pltpu.SemaphoreType.DMA((tokens.shape[0] // 16 + 1,)),
            pltpu.VMEM(tokens.shape, BF16),
            pltpu.VMEM(routes.shape, jnp.int32),
        ],
        vmem=VMEM_ALL,
    )
    early = shifted(early, "section", 2)
    blocks = from_group(normed0)
    x0, pre_gate0, pre_up0, act0, gate, up, down, *parts = call(
        part(forward_kernel, n),
        [((rows, width), BF16), ((rows, hidden), F32), ((rows, hidden), F32)]
        + [((rows, hidden), BF16)]
        + [pltpu.VMEM(a.shape, BF16) for a in (gate, up, down)]
        + [one] * n,
        [*blocks, gate, up, down],
        any_args=(n, n + 1, n + 2),
        scratch=[pltpu.SemaphoreType.DMA((3, PACK)), unpacked, flat32, held],
        vmem=VMEM_LOAD,
    )
    parts = to_group(parts)
    upd0, h1 = call(
        part(update0_kernel, n),
        [one, one],
        [*parts, raw0, routes, gates, tokens, next_routes],
    )
    h1 = shifted(h1, "section", 1)
    (rest,) = call(
        merge_kernel,
        [(((PACK - EARLY) * tokens.shape[0] + TAIL, step), BF16)],
        [tokens, upd0, routes, next_routes],
        scratch=[pltpu.VMEM((TAIL, step), F32)],
    )
    cot1, scaled1 = call(grad_rows_kernel, [one, one], [cot1_all, routes, gates])

    (enter1,) = call(
        enter1_kernel,
        [((2 * PACKED, step), BF16)],
        [h1, scaled1],
    )
    (cot1_all,) = call(
        release_kernel,
        [(tokens.shape, BF16)],
        [cot1_all, h1, scaled1, early],
        any_args=(0, 1, 2, 3),
        any_outs=(0,),
        aliases={0: 0},
    )
    cot0_all = shifted(cot1_all, "section", -1)
    blocks = from_group(enter1)
    kept, *parts = call(
        part(tick1_kernel, n),
        [((rows, 3 * width + 4 * hidden), BF16)] + [one] * n,
        [*blocks, x0, act0, gate, up, down],
        scratch=[unpacked, pltpu.VMEM((2, rows, width), F32), held, flat, flat],
    )
    parts = to_group(parts)
    (upd1,) = call(
        part(grad1_kernel, n),
        [one],
        [*parts, h1, cot1],
    )
    upd1 = shifted(upd1, "section", -1)
    kept_all = copies_of(kept)

    (rest,) = call(
        release_kernel,
        [(rest.shape, BF16)],
        [rest, cot0_all, upd1],
        any_args=(0, 1, 2),
        any_outs=(0,),
        aliases={0: 0},
    )
    c0, enter0 = call(
        enter0_kernel,
        [one, one],
        [upd1, next_routes, routes, gates, cot0_all, rest],
        any_args=(5,),
    )
    rest = shifted(rest, "section", 2)
    blocks = from_group(enter0)
    g_grad0, *parts = call(
        part(tick0_kernel, n),
        [wide] + [one] * n,
        [*blocks, pre_gate0, pre_up0, gate, up, down],
        scratch=[unpacked, flat32, held, flat],
    )
    parts = to_group(parts)
    g_grad0_all = copies_of(g_grad0)
    (grad,) = call(
        part(finish_grad_kernel, n),
        [(tokens.shape, BF16)],
        [*parts, raw0, c0, routes, upd1, next_routes, cot0_all],
    )
    outs = call(
        part(down_kernel, n),
        [one] * n,
        [kept, down, g_grad0],
        any_args=(2,),
        scratch=[unpacked, held],
    )
    outs = to_group(outs)
    (last1,) = call(part(update1_kernel, n), [one], [*outs, h1, routes, gates])
    last1 = shifted(last1, "section", 1)
    x_t, act_t = turned(kept_all, width, hidden)
    (down_out,) = down_grads(act_t, g_grad0_all, kept_all, width, hidden)
    gate_out, up_out = input_grads(x_t, g_grad0_all, kept_all, width, hidden)
    height = tokens.shape[0]
    base, turned_select, hit = call(
        prepare_state_kernel,
        [
            pltpu.VMEM(tokens.shape, BF16),
            pltpu.VMEM((height, PACKED), F32),
            pltpu.VMEM((height, 128), F32),
        ],
        [early, rest],
        scratch=[pltpu.VMEM((TAIL, step), F32)],
    )
    (state,) = call(
        finish_state_kernel,
        [(tokens.shape, BF16)],
        [base, turned_select, hit, last1],
        any_outs=(0,),
        scratch=[pltpu.VMEM(tokens.shape, BF16), pltpu.SemaphoreType.DMA((height // 16,))],
    )
    return (grad, state, gate_out[None], up_out[None], down_out[None])


def solution(mesh):
    rows = P(("section", "expert", "dp"), None)
    slots = P(None, ("section", "expert", "dp"), None)
    cols = P("section", None, "expert")
    hidden = P("section", "expert", None)
    return jax.shard_map(
        shards,
        mesh=mesh,
        in_specs=(rows, rows, cols, cols, hidden, slots, slots),
        out_specs=(rows, rows, cols, cols, hidden),
        check_vma=False,
    )
```

```python
import functools

import jax
import jax.numpy as jnp
from jax import lax
from jax.experimental import pallas as pl
from jax.experimental.pallas import tpu as pltpu
from jax.sharding import PartitionSpec as P

CAP = 10
PACK = 8
PACKED = CAP * PACK
EPSILON = 1e-06
F32 = jnp.float32
BF16 = jnp.bfloat16
VMEM_SMALL = 24 * 1024 * 1024
VMEM_LOAD = 36 * 1024 * 1024
VMEM_ALL = 60 * 1024 * 1024
COST_BYTES = 1024
TOP = 4
TAIL = 16
EARLY = 1


def shifted(block, axis, distance):
    size = lax.axis_size(axis)
    return lax.ppermute(block, axis, [((i - distance) % size, i) for i in range(size)])


def dot(a, b, ca=1, cb=0):
    return lax.dot_general(a, b, (((ca,), (cb,)), ((), ())), preferred_element_type=F32)


def call(
    kernel, outs, args, *, any_args=(), any_outs=(), scratch=(), vmem=VMEM_SMALL, aliases=None
):
    outs = [jax.ShapeDtypeStruct(*o) if isinstance(o, tuple) else o for o in outs]
    anywhere = pl.BlockSpec(memory_space=pl.ANY)
    near = pl.BlockSpec(memory_space=pltpu.VMEM)
    return pl.pallas_call(
        kernel,
        out_shape=outs,
        in_specs=[anywhere if i in any_args else near for i in range(len(args))],
        out_specs=[anywhere if i in any_outs else near for i in range(len(outs))],
        scratch_shapes=list(scratch),
        compiler_params=pltpu.CompilerParams(vmem_limit_bytes=vmem),
        cost_estimate=pl.CostEstimate(flops=0, bytes_accessed=COST_BYTES, transcendentals=0),
        input_output_aliases=aliases or {},
    )(*args)


def packed_index(shape, dim):
    place = lax.broadcasted_iota(jnp.int32, shape, dim).astype(F32)
    chunk = jnp.floor((place + 0.5) * (1.0 / CAP))
    return place - CAP * chunk, chunk


def select_of(routes):
    hits = (routes == 0).astype(F32)
    marked = jnp.sum(hits, axis=0, keepdims=True)
    rows = routes.shape[1]
    before = lax.broadcasted_iota(jnp.int32, (rows, rows), 0) < lax.broadcasted_iota(
        jnp.int32, (rows, rows), 1
    )
    wide = jnp.broadcast_to(marked, (PACKED, rows))
    places = dot(wide.astype(BF16), before.astype(F32).astype(BF16))
    slot, _ = packed_index((PACKED, rows), 0)
    return jnp.where((places == slot) & (wide > 0.5), 1.0, 0.0)


def slot_gates(select, routes, gates):
    weights = jnp.sum(jnp.where(routes == 0, gates, 0.0), axis=0, keepdims=True)
    return jnp.sum(select * weights, axis=1, keepdims=True)


def chunk_of(select, c):
    _, chunk = packed_index(select.shape, 0)
    return jnp.where(chunk == c, select, 0.0).astype(BF16)


def columns(c, width):
    return slice(c * (width // PACK), (c + 1) * (width // PACK))


def pick(select, pieces):
    total = None
    for block, (r0, r1, c0, c1) in pieces:
        width = block.shape[1] // (c1 - c0)
        for c in range(c0, c1):
            columns_here = slice((c - c0) * width, (c - c0 + 1) * width)
            part = dot(chunk_of(select[:, r0:r1], c), block[:, columns_here])
            total = part if total is None else total + part
    return total


def whole_block(block):
    return [(block, (0, block.shape[0], 0, PACK))]


def over_chunks(row_sums):
    slot_r, _ = packed_index((PACKED, PACKED), 0)
    slot_c, _ = packed_index((PACKED, PACKED), 1)
    same = jnp.where(slot_r == slot_c, 1.0, 0.0)
    wide = jnp.broadcast_to(row_sums, (PACKED, 128))
    return jnp.dot(
        same, wide, precision=lax.Precision.HIGHEST, preferred_element_type=F32
    )[:, :1]


def mean_of(values):
    return over_chunks(jnp.sum(values, axis=-1, keepdims=True)) * (1.0 / (PACK * values.shape[1]))


def inv_rms_of(values):
    return lax.rsqrt(mean_of(values * values) + EPSILON)


def merged(select_to, select_from, fresh, old):
    same = dot(select_to.astype(BF16), select_from.astype(BF16), 1, 1)
    _, chunk_r = packed_index(same.shape, 0)
    _, chunk_c = packed_index(same.shape, 1)
    same = jnp.where(chunk_r == chunk_c, same, 0.0)
    taken = jnp.sum(same, axis=1, keepdims=True)
    return jnp.where(taken > 0.5, dot(same.astype(BF16), fresh), old).astype(BF16)


def summed(parts):
    total = parts[0][...].astype(F32)
    for p in parts[1:]:
        total = total + p[...].astype(F32)
    return total


def hit_rows(select):
    ones = jnp.ones((PACKED, 128), BF16)
    return dot(chunk_of(select, 0), ones, 0, 0)[:, :1] > 0.5


def placed(c, old, select, hit, rows):
    return jnp.where(hit, dot(chunk_of(select, c), rows, 0, 0), old.astype(F32)).astype(BF16)


def start_rows(source, target, sems):
    copies = []
    for i in range(source.shape[0] // 16):
        r = pl.ds(16 * i, 16)
        copies.append(pltpu.make_async_copy(source.at[r], target.at[r], sems.at[i]))
        copies[-1].start()
    return copies


def first_rows_kernel(
    tokens, routes_far, gates, raw, normed, early, mask, weight, sems, held, routes
):
    fetch_routes = pltpu.make_async_copy(routes_far, routes, sems.at[sems.shape[0] - 1])
    fetch_routes.start()
    fetches = start_rows(tokens, held, sems)
    fetch_routes.wait()
    select = select_of(routes[0])
    for fetch in fetches:
        fetch.wait()
    mask[...] = select.astype(BF16)
    gate = slot_gates(select, routes[0], gates[0])
    weight[...] = jnp.broadcast_to(gate, weight.shape)
    values = pick(select, whole_block(held))
    raw[...] = values.astype(BF16)
    normed[...] = (values * inv_rms_of(values)).astype(BF16)
    height, width = held.shape
    for c in range(EARLY):
        early[c * height : (c + 1) * height] = held[:, columns(c, width)]


def update0_kernel(n, *refs):
    parts, (raw, mask, weight, tokens, next_routes, upd, onward) = refs[:n], refs[n:]
    select = mask[...]
    select_next = select_of(next_routes[0])
    fresh = (raw[...].astype(F32) + weight[:, :1] * summed(parts)).astype(BF16)
    old = pick(select_next, whole_block(tokens))
    onward[...] = merged(select_next, select, fresh, old)
    upd[...] = fresh


def merge_kernel(tokens, upd, routes, next_routes, out, last):
    select = select_of(routes[0])
    hit = hit_rows(select)
    height, width = tokens.shape
    for c in range(EARLY, PACK):
        value = placed(c, tokens[:, columns(c, width)], select, hit, upd[...])
        out[(c - EARLY) * height : (c - EARLY + 1) * height] = value
    last[...] = jnp.zeros(last.shape, F32)
    last[:CAP] = upd[...].astype(F32)[:CAP]
    last[CAP : CAP + TOP, :height] = routes[0].astype(F32)
    last[CAP : CAP + TOP, height : 2 * height] = next_routes[0].astype(F32)
    out[(PACK - EARLY) * height :] = last[...].astype(BF16)


def release_kernel(*_):
    pass


def grad_rows_kernel(bulk, routes, gates, cot, scaled):
    select = select_of(routes[1])
    values = pick(select, whole_block(bulk))
    cot[...] = values.astype(BF16)
    scaled[...] = (slot_gates(select, routes[1], gates[1]) * values).astype(BF16)


def update1_kernel(n, *refs):
    parts, (h, routes, gates, upd) = refs[:n], refs[n:]
    select = select_of(routes[1])
    weight = slot_gates(select, routes[1], gates[1])
    upd[...] = (h[...].astype(F32) + weight * summed(parts)).astype(BF16)


def enter1_kernel(h, scaled, out):
    values = h[...].astype(F32)
    out[:PACKED] = (values * inv_rms_of(values)).astype(BF16)
    out[PACKED:] = scaled[...]


def state_grad(parts, h, c):
    total = summed(parts)
    values = h.astype(F32)
    inv = inv_rms_of(values)
    inner = mean_of(total * values)
    return (c.astype(F32) + inv * total - inv * inv * inv * values * inner).astype(BF16)


def grad1_kernel(n, *refs):
    parts, (h, cot, upd) = refs[:n], refs[n:]
    upd[...] = state_grad(parts, h[...], cot[...])


def enter0_kernel(upd1, next_routes, routes, gates, bulk, _, c0, out):
    select = select_of(routes[0])
    old = pick(select, whole_block(bulk))
    rows = merged(select, select_of(next_routes[0]), upd1[...], old)
    c0[...] = rows
    out[...] = (slot_gates(select, routes[0], gates[0]) * rows.astype(F32)).astype(BF16)


def finish_grad_kernel(n, *refs):
    parts, (h, c, routes, upd1, next_routes, bulk, out) = refs[:n], refs[n:]
    fresh = state_grad(parts, h[...], c[...])
    first, second = select_of(next_routes[0]), select_of(routes[0])
    hit1, hit2 = hit_rows(first), hit_rows(second)
    for chunk in range(PACK):
        k = columns(chunk, out.shape[1])
        value = placed(chunk, bulk[:, k], first, hit1, upd1[...])
        out[:, k] = placed(chunk, value, second, hit2, fresh)


def prepare_state_kernel(early, rest, out, turned_select, hit, last):
    height, width = out.shape
    at = (PACK - EARLY) * height
    last[...] = rest[at:].astype(F32)
    first = select_of(last[CAP : CAP + TOP, :height])
    second = select_of(last[CAP : CAP + TOP, height : 2 * height])
    rows = jnp.concatenate([last[...], jnp.zeros((PACKED - TAIL, last.shape[1]), F32)], axis=0)
    out[:, columns(0, width)] = placed(0, early[...], first, hit_rows(first), rows.astype(BF16))
    for c in range(EARLY, PACK):
        out[:, columns(c, width)] = rest[(c - EARLY) * height : (c - EARLY + 1) * height]
    turned_select[...] = second.T
    ones = jnp.ones((PACKED, 128), BF16)
    hit[...] = dot(chunk_of(second, 0), ones, 0, 0)


def finish_state_kernel(base, turned_select, hit, upd1, out, outs, sems):
    height, width = out.shape
    _, chunk = packed_index(turned_select.shape, 1)
    copies = []
    for r0 in range(0, height, height // 2):
        r = slice(r0, r0 + height // 2)
        taken = hit[r, :1] > 0.5
        for c in range(PACK):
            k = columns(c, width)
            select = jnp.where(chunk[r] == c, turned_select[r], 0.0).astype(BF16)
            value = jnp.where(taken, dot(select, upd1[...]), base[r, k].astype(F32))
            outs[r, k] = value.astype(BF16)
        for i in range(r0 // 16, r.stop // 16):
            b = pl.ds(16 * i, 16)
            copies.append(pltpu.make_async_copy(outs.at[b], out.at[b], sems.at[i]))
            copies[-1].start()
    for copy in copies:
        copy.wait()


def silu_grads(pre_gate, pre_up, grad_act):
    sig = jax.nn.sigmoid(pre_gate)
    grad_gate = (grad_act * pre_up * sig * (1.0 + pre_gate * (1.0 - sig))).astype(BF16)
    grad_up = (grad_act * (pre_gate * sig)).astype(BF16)
    return grad_gate, grad_up


def gather_rows(blocks, unpacked, whole32, whole):
    width = whole.shape[1]
    used = len(blocks) * CAP
    if used < whole.shape[0]:
        whole32[used:] = jnp.zeros((whole.shape[0] - used, width), F32)
    for i, b in enumerate(blocks):
        unpacked[i] = b[...].astype(F32)
        for c in range(PACK):
            whole32[i * CAP : (i + 1) * CAP, columns(c, width)] = unpacked[
                i, c * CAP : (c + 1) * CAP
            ]
    whole[...] = whole32[...].astype(BF16)


def spread_rows(value, c, n, held, unpacked):
    held[...] = value
    for i in range(n):
        unpacked[i, c * CAP : (c + 1) * CAP] = held[i * CAP : (i + 1) * CAP]


def forward_kernel(n, *refs):
    blocks, (gate, up, down) = refs[:n], refs[n : n + 3]
    x, pre_gate, pre_up, act, gate_v, up_v, down_v = refs[n + 3 : n + 10]
    parts = refs[n + 10 : 2 * n + 10]
    sems, unpacked, whole32, held = refs[2 * n + 10 :]
    width = gate.shape[0]
    fetches = []
    for c in range(PACK):
        k = columns(c, width)
        fetches.append(
            (
                pltpu.make_async_copy(gate.at[k], gate_v.at[k], sems.at[0, c]),
                pltpu.make_async_copy(up.at[k], up_v.at[k], sems.at[1, c]),
                pltpu.make_async_copy(down.at[:, k], down_v.at[:, k], sems.at[2, c]),
            )
        )
    for fetch_g, fetch_u, _ in fetches:
        fetch_g.start()
        fetch_u.start()
    for _, _, fetch_d in fetches:
        fetch_d.start()
    gather_rows(blocks, unpacked, whole32, x)
    acc_g = jnp.zeros(pre_gate.shape, F32)
    acc_u = jnp.zeros(pre_up.shape, F32)
    for c, (fetch_g, fetch_u, _) in enumerate(fetches):
        k = columns(c, width)
        fetch_g.wait()
        acc_g = acc_g + dot(x[:, k], gate_v[k])
        fetch_u.wait()
        acc_u = acc_u + dot(x[:, k], up_v[k])
    pre_gate[...] = acc_g
    pre_up[...] = acc_u
    activated = (acc_g * jax.nn.sigmoid(acc_g) * acc_u).astype(BF16)
    act[...] = activated
    for c, (_, _, fetch_d) in enumerate(fetches):
        fetch_d.wait()
        value = dot(activated, down_v[:, columns(c, width)])
        spread_rows(value, c, n, held.at[c], unpacked)
    for i, p in enumerate(parts):
        p[...] = unpacked[i].astype(BF16)


def out_rows(act, down, held, unpacked, parts):
    n = len(parts)
    for c in range(PACK):
        value = dot(act, down[:, columns(c, down.shape[1])])
        spread_rows(value, c, n, held.at[c], unpacked)
    for i, p in enumerate(parts):
        p[...] = unpacked[i].astype(BF16)


def down_kernel(n, act, down, _, *refs):
    parts, (unpacked, held) = refs[:n], refs[n:]
    hidden, width = down.shape
    out_rows(act[:, 3 * width + hidden : 3 * width + 2 * hidden], down, held, unpacked, parts)


def back_rows(gg, gu, gate, up, held, unpacked, parts):
    n = len(parts)
    for c in range(PACK):
        k = columns(c, gate.shape[0])
        value = dot(gg, gate[k], 1, 1) + dot(gu, up[k], 1, 1)
        spread_rows(value, c, n, held.at[c], unpacked)
    for i, p in enumerate(parts):
        p[...] = unpacked[i].astype(BF16)


def tick1_kernel(n, *refs):
    blocks, (x0, act0, gate, up, down) = refs[:n], refs[n : n + 5]
    (kept,) = refs[n + 5 : n + 6]
    parts = refs[n + 6 : 2 * n + 6]
    unpacked, whole32, held, x, g = refs[2 * n + 6 :]
    gather_rows([b.at[:PACKED] for b in blocks], unpacked, whole32.at[0], x)
    gather_rows([b.at[PACKED:] for b in blocks], unpacked, whole32.at[1], g)
    width, hidden = gate.shape
    kept[:, :width] = x0[...]
    kept[:, width : 2 * width] = x[...]
    kept[:, 2 * width : 3 * width] = g[...]
    narrow = [slice(3 * width + i * hidden, 3 * width + (i + 1) * hidden) for i in range(4)]
    kept[:, narrow[0]] = act0[...]
    acc_g = dot(x[...], gate[...])
    acc_u = dot(x[...], up[...])
    acc_a = dot(g[...], down[...], 1, 1)
    gg, gu = silu_grads(acc_g, acc_u, acc_a)
    kept[:, narrow[1]] = (acc_g * jax.nn.sigmoid(acc_g) * acc_u).astype(BF16)
    kept[:, narrow[2]] = gg
    kept[:, narrow[3]] = gu
    back_rows(gg, gu, gate, up, held, unpacked, parts)


def tick0_kernel(n, *refs):
    blocks, (pre_gate, pre_up, gate, up, down) = refs[:n], refs[n : n + 5]
    (g_grad,) = refs[n + 5 : n + 6]
    parts = refs[n + 6 : 2 * n + 6]
    unpacked, whole32, held, g = refs[2 * n + 6 :]
    gather_rows(blocks, unpacked, whole32, g)
    width, hidden = gate.shape
    g_grad[:, :width] = g[...]
    acc_a = dot(g[...], down[...], 1, 1)
    gg, gu = silu_grads(pre_gate[...], pre_up[...], acc_a)
    g_grad[:, width : width + hidden] = gg
    g_grad[:, width + hidden :] = gu
    back_rows(gg, gu, gate, up, held, unpacked, parts)


def whole_of(blocks):
    return jnp.concatenate([b.astype(F32) for b in blocks], axis=0).astype(BF16)


def turn_kernel(m, *refs):
    x0, x1, act0, act1 = (refs[i * m : (i + 1) * m] for i in range(4))
    x_t, act_t = refs[4 * m :]
    x_t[...] = whole_of([b[...] for b in x0 + x1]).T

    @pl.when(pl.program_id(0) == 0)
    def _():
        act_t[...] = whole_of([b[...] for b in act0 + act1]).T


def down_grad_kernel(m, act_t, *refs):
    g0, g1, (down_out, both) = refs[:m], refs[m : 2 * m], refs[2 * m :]

    @pl.when(pl.program_id(0) == 0)
    def _():
        both[...] = whole_of([b[...] for b in g0 + g1])

    for c in range(PACK):
        k = columns(c, both.shape[1])
        down_out[:, k] = dot(act_t[...], both[:, k]).astype(BF16)


def input_grad_kernel(m, x_t, *refs):
    gates0, ups0, gates1, ups1 = (refs[i * m : (i + 1) * m] for i in range(4))
    gate_out, up_out, both = refs[4 * m :]
    hidden = gate_out.shape[1]

    @pl.when(pl.program_id(0) == 0)
    def _():
        both[:, :hidden] = whole_of([b[...] for b in gates0 + gates1])
        both[:, hidden:] = whole_of([b[...] for b in ups0 + ups1])

    gate_out[...] = dot(x_t[...], both[:, :hidden]).astype(BF16)
    up_out[...] = dot(x_t[...], both[:, hidden:]).astype(BF16)


def chunked_call(kernel, ins, outs, scratch=(), steps=PACK):
    return pl.pallas_call(
        kernel,
        grid=(steps,),
        out_shape=[jax.ShapeDtypeStruct(s, BF16) for s, _, _ in outs],
        in_specs=[pl.BlockSpec(block, index) for _, block, index in ins],
        out_specs=[pl.BlockSpec(block, index) for _, block, index in outs],
        scratch_shapes=list(scratch),
        compiler_params=pltpu.CompilerParams(vmem_limit_bytes=VMEM_SMALL),
        cost_estimate=pl.CostEstimate(flops=0, bytes_accessed=COST_BYTES, transcendentals=0),
    )(*(a for a, _, _ in ins))


def constant(at):
    return lambda c: (0, at)


def chunk_at(at):
    return lambda c: (0, at + c)


def turned(kept, width, hidden):
    m = len(kept)
    rows = kept[0].shape[0]
    step = width // PACK
    first = 3 * width // hidden
    ins = [(a, (rows, step), chunk_at(at)) for at in (0, PACK) for a in kept]
    ins += [(a, (rows, hidden), constant(at)) for at in (first, first + 1) for a in kept]
    outs = [
        ((width, 2 * m * rows), (step, 2 * m * rows), lambda c: (c, 0)),
        ((hidden, 2 * m * rows), (hidden, 2 * m * rows), lambda c: (0, 0)),
    ]
    return chunked_call(functools.partial(turn_kernel, m), ins, outs)


def down_grads(act_t, g_grad0, kept, width, hidden):
    m = len(kept)
    rows = kept[0].shape[0]
    block = max(hidden // 4, 16)
    ins = [(act_t, (block, act_t.shape[1]), lambda c: (c, 0))]
    ins += [(a, (rows, width), constant(0)) for a in g_grad0]
    ins += [(a, (rows, width), constant(2)) for a in kept]
    outs = [((hidden, width), (block, width), lambda c: (c, 0))]
    scratch = [pltpu.VMEM((2 * m * rows, width), BF16)]
    kernel = functools.partial(down_grad_kernel, m)
    return chunked_call(kernel, ins, outs, scratch, hidden // block)


def input_grads(x_t, g_grad0, kept, width, hidden):
    m = len(kept)
    rows = kept[0].shape[0]
    step = width // PACK
    first, second = width // hidden, 3 * width // hidden + 2
    ins = [(x_t, (step, x_t.shape[1]), lambda c: (c, 0))]
    ins += [(a, (rows, hidden), constant(at)) for at in (first, first + 1) for a in g_grad0]
    ins += [(a, (rows, hidden), constant(at)) for at in (second, second + 1) for a in kept]
    tall = ((width, hidden), (step, hidden), lambda c: (c, 0))
    scratch = [pltpu.VMEM((2 * m * rows, 2 * hidden), BF16)]
    return chunked_call(functools.partial(input_grad_kernel, m), ins, [tall, tall], scratch)


def from_group(block):
    n = lax.axis_size("expert")
    return [block] + [shifted(block, "expert", k) for k in range(1, n)]


def to_group(blocks):
    return [blocks[0]] + [shifted(b, "expert", -k) for k, b in enumerate(blocks) if k]


def copies_of(block):
    n = lax.axis_size("dp")
    return [block] + [shifted(block, "dp", k) for k in range(1, n)]


def shards(tokens, cotangent, w_gate, w_up, w_down, routes, gates):
    gate, up, down = w_gate[0], w_up[0], w_down[0]
    width, hidden = gate.shape
    step = width // PACK
    n = lax.axis_size("expert")
    rows = -(-n * CAP // 16) * 16
    routes = jnp.transpose(routes, (0, 2, 1))
    gates = jnp.transpose(gates, (0, 2, 1))
    one = ((PACKED, step), BF16)
    part = functools.partial
    unpacked = pltpu.VMEM((n, PACKED, step), F32)
    flat32 = pltpu.VMEM((rows, width), F32)
    held = pltpu.VMEM((PACK, rows, step), F32)
    flat = pltpu.VMEM((rows, width), BF16)
    wide = ((rows, width + 2 * hidden), BF16)
    dma = [pltpu.SemaphoreType.DMA]

    cot1_all = shifted(cotangent, "section", -1)
    next_routes = shifted(routes[1:], "section", -1)

    raw0, normed0, early, mask0, weight0 = call(
        first_rows_kernel,
        [
            pltpu.VMEM(*one),
            pltpu.VMEM(*one),
            ((EARLY * tokens.shape[0], step), BF16),
            pltpu.VMEM((PACKED, tokens.shape[0]), BF16),
            pltpu.VMEM((PACKED, 128), F32),
        ],
        [tokens, routes, gates],
        any_args=(0, 1),
        scratch=[
            pltpu.SemaphoreType.DMA((tokens.shape[0] // 16 + 1,)),
            pltpu.VMEM(tokens.shape, BF16),
            pltpu.VMEM(routes.shape, jnp.int32),
        ],
        vmem=VMEM_ALL,
    )
    early = shifted(early, "section", 2)
    blocks = from_group(normed0)
    x0, pre_gate0, pre_up0, act0, gate, up, down, *parts = call(
        part(forward_kernel, n),
        [((rows, width), BF16), ((rows, hidden), F32), ((rows, hidden), F32)]
        + [((rows, hidden), BF16)]
        + [pltpu.VMEM(a.shape, BF16) for a in (gate, up, down)]
        + [one] * n,
        [*blocks, gate, up, down],
        any_args=(n, n + 1, n + 2),
        scratch=[pltpu.SemaphoreType.DMA((3, PACK)), unpacked, flat32, held],
        vmem=VMEM_LOAD,
    )
    parts = to_group(parts)
    upd0, h1 = call(
        part(update0_kernel, n),
        [one, one],
        [*parts, raw0, mask0, weight0, tokens, next_routes],
    )
    h1 = shifted(h1, "section", 1)
    (rest,) = call(
        merge_kernel,
        [(((PACK - EARLY) * tokens.shape[0] + TAIL, step), BF16)],
        [tokens, upd0, routes, next_routes],
        scratch=[pltpu.VMEM((TAIL, step), F32)],
    )
    cot1, scaled1 = call(grad_rows_kernel, [one, one], [cot1_all, routes, gates])

    (enter1,) = call(
        enter1_kernel,
        [((2 * PACKED, step), BF16)],
        [h1, scaled1],
    )
    (cot1_all,) = call(
        release_kernel,
        [(tokens.shape, BF16)],
        [cot1_all, h1, scaled1, early],
        any_args=(0, 1, 2, 3),
        any_outs=(0,),
        aliases={0: 0},
    )
    cot0_all = shifted(cot1_all, "section", -1)
    blocks = from_group(enter1)
    kept, *parts = call(
        part(tick1_kernel, n),
        [((rows, 3 * width + 4 * hidden), BF16)] + [one] * n,
        [*blocks, x0, act0, gate, up, down],
        scratch=[unpacked, pltpu.VMEM((2, rows, width), F32), held, flat, flat],
    )
    parts = to_group(parts)
    (upd1,) = call(
        part(grad1_kernel, n),
        [one],
        [*parts, h1, cot1],
    )
    upd1 = shifted(upd1, "section", -1)
    kept_all = copies_of(kept)

    (rest,) = call(
        release_kernel,
        [(rest.shape, BF16)],
        [rest, cot0_all, upd1],
        any_args=(0, 1, 2),
        any_outs=(0,),
        aliases={0: 0},
    )
    c0, enter0 = call(
        enter0_kernel,
        [one, one],
        [upd1, next_routes, routes, gates, cot0_all, rest],
        any_args=(5,),
    )
    rest = shifted(rest, "section", 2)
    blocks = from_group(enter0)
    g_grad0, *parts = call(
        part(tick0_kernel, n),
        [wide] + [one] * n,
        [*blocks, pre_gate0, pre_up0, gate, up, down],
        scratch=[unpacked, flat32, held, flat],
    )
    parts = to_group(parts)
    g_grad0_all = copies_of(g_grad0)
    (grad,) = call(
        part(finish_grad_kernel, n),
        [(tokens.shape, BF16)],
        [*parts, raw0, c0, routes, upd1, next_routes, cot0_all],
    )
    outs = call(
        part(down_kernel, n),
        [one] * n,
        [kept, down, g_grad0],
        any_args=(2,),
        scratch=[unpacked, held],
    )
    outs = to_group(outs)
    (last1,) = call(part(update1_kernel, n), [one], [*outs, h1, routes, gates])
    last1 = shifted(last1, "section", 1)
    x_t, act_t = turned(kept_all, width, hidden)
    (down_out,) = down_grads(act_t, g_grad0_all, kept_all, width, hidden)
    gate_out, up_out = input_grads(x_t, g_grad0_all, kept_all, width, hidden)
    height = tokens.shape[0]
    base, turned_select, hit = call(
        prepare_state_kernel,
        [
            pltpu.VMEM(tokens.shape, BF16),
            pltpu.VMEM((height, PACKED), F32),
            pltpu.VMEM((height, 128), F32),
        ],
        [early, rest],
        scratch=[pltpu.VMEM((TAIL, step), F32)],
    )
    (state,) = call(
        finish_state_kernel,
        [(tokens.shape, BF16)],
        [base, turned_select, hit, last1],
        any_outs=(0,),
        scratch=[pltpu.VMEM(tokens.shape, BF16), pltpu.SemaphoreType.DMA((height // 16,))],
    )
    return (grad, state, gate_out[None], up_out[None], down_out[None])


def solution(mesh):
    rows = P(("section", "expert", "dp"), None)
    slots = P(None, ("section", "expert", "dp"), None)
    cols = P("section", None, "expert")
    hidden = P("section", "expert", None)
    return jax.shard_map(
        shards,
        mesh=mesh,
        in_specs=(rows, rows, cols, cols, hidden, slots, slots),
        out_specs=(rows, rows, cols, cols, hidden),
        check_vma=False,
    )
```
